512 devices in a mesh: bulk: 32 (over z, x_hi), wide: 16 (over y, x_lo, core).
Axes of the slice: x: 4 (x_hi: 2, x_lo: 2; x = x_hi * 2 + x_lo), y: 4, z: 16, core: 2. Of those that a mesh axis runs over, the one named last changes fastest.
Arguments:
- seed_electric: float32 [3, 256, 256, 128], P(None, 'bulk', 'wide'), may hold values from -6 to 6
- seed_magnetic: float32 [3, 256, 256, 128], P(None, 'bulk', 'wide'), may hold values from -6 to 6
- saved_magnetic: bfloat16 [2, 3, 256, 256, 128], P(None, None, 'bulk', 'wide'), may hold values from -6 to 6
- material: int32 [256, 256, 128], P('bulk', 'wide'), may hold values from 0 to 7
- permittivity: float32 [8], replicated, may hold values from 1 to 12
- source_cells: int32 [64], replicated, may hold values from 0 to 8388607
- monitor_cells: int32 [64], replicated, may hold values from 0 to 8388607
- monitor_weights: float32 [2, 64, 3], replicated, may hold values from -24 to 24
- lift_weight: float32 [16, 3], replicated, may hold values from -3.5 to 3.5
- project_weight: float32 [3, 16], replicated, may hold values from -1.5 to 1.5
- mode_mix: bfloat16 [2, 48, 16, 16], replicated, may hold values from -1.5 to 1.5
- gain_first: float32 [16, 48], replicated, may hold values from 0.1 to 1.9
- gain_second: float32 [16, 48], replicated, may hold values from 0.1 to 1.9
Outputs:
- grad_electric: float32 [3, 256, 256, 128], P(None, 'bulk', 'wide')
- grad_magnetic: float32 [3, 256, 256, 128], P(None, 'bulk', 'wide')
- grad_permittivity: float32 [256, 256, 128], P('bulk', 'wide')
- grad_sources: float32 [2, 64, 3], replicated
The draws below stay inside these ranges and needn't reach their ends.
All inputs are finite; a program needn't handle non-finite values.
Results may differ from the reference program's by a relative error of at most 0.02.
Values may be sent and summed in bfloat16 or wider, within the bound.
No kernel may reach another device: no remote copies, remote signals or barrier semaphores. Data moves between devices by JAX's collectives and lax.ppermute only.
A program may use at most 64 MiB of HBM per device.

```python
import math
import jax
import jax.numpy as jnp
from jax import lax

STEPS = 2
CH = 16
K = 48
MATS = 8
NSRC = 64
NMON = 64
NX = 256
NY = 256
NZ = 128


def plant(drawn, stream_key, smallest, top_value):
    extent = drawn.shape
    place = [jax.random.randint(jax.random.fold_in(stream_key, axis), (), 0, extent[axis]) for axis in range(len(extent))]
    drawn = drawn.at[tuple(place)].set(smallest)
    longest = extent.index(max(extent))
    place[longest] = (place[longest] + 1) % extent[longest]
    return drawn.at[tuple(place)].set(top_value)


def steps_of(stream_key, extent, pieces, low, largest):
    factor_of, own = 1.0, jax.random.fold_in(stream_key, 6)
    for position, blocks in pieces:
        steps = jnp.exp(jax.random.uniform(jax.random.fold_in(own, position), (blocks,), jnp.float32, low / len(pieces), largest / len(pieces)))
        factor_of = factor_of * jnp.repeat(steps, extent[position] // blocks).reshape([-1 if axis == position else 1 for axis in range(len(extent))])
    return factor_of


def noise(stream_key, extent, spread, limit, pieces=(), kind=jnp.bfloat16):
    factor_of = steps_of(stream_key, extent, pieces, -0.22, 0.18) if pieces else 1.0
    values = jax.random.normal(stream_key, extent, jnp.float32) * spread * factor_of
    return jnp.minimum(jnp.maximum(values, -limit), limit).astype(kind)


def setup_inputs(seed: int = 0) -> dict:
    seeds = jax.random.split(jax.random.key(seed), 14)
    seed_electric = noise(seeds[0], (3, NX, NY, NZ), 1.0, 6.0, ((1, 32), (2, 16)), jnp.float32)
    seed_magnetic = noise(seeds[1], (3, NX, NY, NZ), 1.0, 6.0, ((1, 32), (2, 16)), jnp.float32)
    saved_magnetic = noise(seeds[2], (STEPS, 3, NX, NY, NZ), 1.0, 6.0, ((2, 32), (3, 16)))
    material = plant(jax.random.randint(seeds[3], (NX, NY, NZ), 0, MATS), jax.random.fold_in(seeds[3], 1), 0, MATS - 1).astype(jnp.int32)
    permittivity = jnp.clip(jnp.exp(jax.random.uniform(seeds[4], (MATS,), jnp.float32, math.log(1.0), math.log(12.0))), 1.0, 12.0)
    source_cells = plant(jax.random.randint(seeds[5], (NSRC,), 0, NX * NY * NZ), jax.random.fold_in(seeds[5], 1), 0, (NX * NY * NZ) - 1).astype(jnp.int32)
    monitor_cells = plant(jax.random.randint(seeds[6], (NMON,), 0, NX * NY * NZ), jax.random.fold_in(seeds[6], 1), 0, (NX * NY * NZ) - 1).astype(jnp.int32)
    monitor_weights = noise(seeds[7], (STEPS, NMON, 3), 4.0, 24.0, (), jnp.float32)
    lift_weight = noise(seeds[8], (CH, 3), 3 ** -0.5, 3.5, (), jnp.float32)
    project_weight = noise(seeds[9], (3, CH), CH ** -0.5, 1.5, (), jnp.float32)
    mode_mix = noise(seeds[10], (2, K, CH, CH), CH ** -0.5, 1.5)
    gain_first = jnp.clip(1.0 + 0.18 * jax.random.normal(seeds[11], (CH, K), jnp.float32), 0.1, 1.9)
    gain_second = jnp.clip(1.0 + 0.18 * jax.random.normal(seeds[12], (CH, K), jnp.float32), 0.1, 1.9)
    return {"seed_electric": seed_electric, "seed_magnetic": seed_magnetic, "saved_magnetic": saved_magnetic, "material": material, "permittivity": permittivity, "source_cells": source_cells, "monitor_cells": monitor_cells, "monitor_weights": monitor_weights, "lift_weight": lift_weight, "project_weight": project_weight, "mode_mix": mode_mix, "gain_first": gain_first, "gain_second": gain_second}


COURANT = 0.5

def waves(freqs, places, total):
    phase = freqs[:, None] * places[None, :] % total
    angle = phase.astype(jnp.float32) * (2.0 * math.pi / total)
    return (jnp.cos(angle), jnp.sin(angle))

def signed_modes(index, count):
    return jnp.where(index < count // 2, index, index - count)

def forward_diff(field, axis):
    size = field.shape[axis]
    ahead = jnp.concatenate([lax.slice_in_dim(field, 1, size, axis=axis), jnp.zeros_like(lax.slice_in_dim(field, 0, 1, axis=axis))], axis)
    return ahead - field

def backward_diff(field, axis):
    size = field.shape[axis]
    behind = jnp.concatenate([jnp.zeros_like(lax.slice_in_dim(field, 0, 1, axis=axis)), lax.slice_in_dim(field, 0, size - 1, axis=axis)], axis)
    return field - behind

def curl_with(field, differ):
    first = differ(field[2], 1) - differ(field[1], 2)
    second = differ(field[0], 2) - differ(field[2], 0)
    third = differ(field[1], 0) - differ(field[0], 1)
    return jnp.stack([first, second, third])

def matmul(spec, left, right):
    return jnp.einsum(spec, left.astype(jnp.float32), right.astype(jnp.float32), precision=lax.Precision.HIGHEST)

def spectral(field, lift_weight, project_weight, mode_mix, gain_first, gain_second):
    modes = jnp.arange(K, dtype=jnp.int32)
    plane_freq = signed_modes(modes, K)
    cos_z, sin_z = waves(modes, jnp.arange(NZ, dtype=jnp.int32), NZ)
    table_z = (jnp.concatenate([cos_z, -sin_z]) * (1.0 / math.sqrt(NX * NY * NZ))).astype(jnp.bfloat16)
    cos_y, sin_y = waves(plane_freq, jnp.arange(NY, dtype=jnp.int32), NY)
    cos_y, sin_y = (cos_y.astype(jnp.bfloat16), sin_y.astype(jnp.bfloat16))
    cos_x, sin_x = waves(plane_freq, jnp.arange(NX, dtype=jnp.int32), NX)
    cos_x, sin_x = (cos_x.astype(jnp.bfloat16), sin_x.astype(jnp.bfloat16))
    back_scale = 1.0 / math.sqrt(K ** 3)
    cos_back = (cos_z * back_scale).astype(jnp.bfloat16)
    sin_back = (sin_z * back_scale).astype(jnp.bfloat16)

    def lift_one(channel):
        lifted = jnp.einsum('d,dxyz->xyz', lift_weight[channel], field, precision=lax.Precision.HIGHEST).astype(jnp.bfloat16)
        along_z = matmul('xyz,mz->xym', lifted, table_z).astype(jnp.bfloat16)
        part_a = matmul('xym,jy->jxm', along_z, cos_y)
        part_b = matmul('xym,jy->jxm', along_z, sin_y)
        real = part_a[..., :K] + part_b[..., K:]
        imag = part_a[..., K:] - part_b[..., :K]
        return jnp.concatenate([real, imag], -1).astype(jnp.bfloat16)
    spectra = lax.map(lift_one, jnp.arange(CH, dtype=jnp.int32))
    y_real, y_imag = (spectra[..., :K], spectra[..., K:])
    mix_real, mix_imag = (mode_mix[0], mode_mix[1])
    gain_y = gain_second[:, :, None, None]
    p_real = ((matmul('cjxk,kco->ojxk', y_real, mix_real) - matmul('cjxk,kco->ojxk', y_imag, mix_imag)) * gain_y).astype(jnp.bfloat16)
    p_imag = ((matmul('cjxk,kco->ojxk', y_real, mix_imag) + matmul('cjxk,kco->ojxk', y_imag, mix_real)) * gain_y).astype(jnp.bfloat16)
    gain_x = gain_first[:, None, :, None]
    q_real = (gain_x * (matmul('ojxk,fx->ojfk', p_real, cos_x) + matmul('ojxk,fx->ojfk', p_imag, sin_x))).astype(jnp.bfloat16)
    q_imag = (gain_x * (matmul('ojxk,fx->ojfk', p_imag, cos_x) - matmul('ojxk,fx->ojfk', p_real, sin_x))).astype(jnp.bfloat16)
    r_real = (matmul('ojfk,fx->ojxk', q_real, cos_x) - matmul('ojfk,fx->ojxk', q_imag, sin_x)).astype(jnp.bfloat16)
    r_imag = (matmul('ojfk,fx->ojxk', q_real, sin_x) + matmul('ojfk,fx->ojxk', q_imag, cos_x)).astype(jnp.bfloat16)

    def out_one(total, channel):
        real_part = r_real[channel]
        imag_part = r_imag[channel]
        w_real = (matmul('jxk,jy->xyk', real_part, cos_y) - matmul('jxk,jy->xyk', imag_part, sin_y)).astype(jnp.bfloat16)
        w_imag = (matmul('jxk,jy->xyk', real_part, sin_y) + matmul('jxk,jy->xyk', imag_part, cos_y)).astype(jnp.bfloat16)
        values = matmul('xyk,kz->xyz', w_real, cos_back) - matmul('xyk,kz->xyz', w_imag, sin_back)
        return (total + project_weight[:, channel][:, None, None, None] * values[None], None)
    result, unused = lax.scan(out_one, jnp.zeros((3, NX, NY, NZ), jnp.float32), jnp.arange(CH, dtype=jnp.int32))
    return result

def cell_coords(flat):
    first = flat // (NY * NZ)
    second = flat // NZ % NY
    third = flat % NZ
    return (first, second, third)

def reference(seed_electric, seed_magnetic, saved_magnetic, material, permittivity, source_cells, monitor_cells, monitor_weights, lift_weight, project_weight, mode_mix, gain_first, gain_second):
    eps_cells = permittivity[material]
    mon_x, mon_y, mon_z = cell_coords(monitor_cells)
    src_x, src_y, src_z = cell_coords(source_cells)

    def inject(index):
        return jnp.zeros((3, NX, NY, NZ), jnp.float32).at[:, mon_x, mon_y, mon_z].add(monitor_weights[index].T)
    adjoint_e = seed_electric + inject(STEPS - 1)
    adjoint_h = seed_magnetic
    grad_eps = jnp.zeros((NX, NY, NZ), jnp.float32)
    sources = [None] * STEPS
    for step in reversed(range(STEPS)):
        sources[step] = adjoint_e[:, src_x, src_y, src_z].T
        scaled = COURANT / eps_cells * adjoint_e
        adjoint_h = adjoint_h + curl_with(scaled, forward_diff)
        saved_curl = curl_with(saved_magnetic[step].astype(jnp.float32), backward_diff)
        grad_eps = grad_eps - lax.optimization_barrier(jnp.sum(scaled / eps_cells * saved_curl, 0))
        updated = adjoint_e - COURANT * curl_with(adjoint_h, backward_diff)
        if step % 2 == 1:
            updated = updated + spectral(adjoint_e, lift_weight, project_weight, mode_mix, gain_first, gain_second)
        adjoint_e = updated
        if step >= 1:
            adjoint_e = adjoint_e + inject(step - 1)
    return (adjoint_e, adjoint_h, grad_eps, jnp.stack(sources))
```

```python
import functools
import math

import jax
import jax.numpy as jnp
import ml_dtypes
import numpy as np
from jax import lax
from jax.experimental import pallas as pl
from jax.experimental.pallas import tpu as pltpu
from jax.sharding import PartitionSpec as P

NX, NY, NZ = 256, 256, 128
K = 48
OWN = 3
WIDE, BULK = 16, 32
RX, RY = 8, 16
LANES = 128
F32, BF16 = jnp.float32, jnp.bfloat16
PARAMS = pltpu.CompilerParams(vmem_limit_bytes=40 * 1024 * 1024)


def waves(freqs, places, total):
    phase = np.mod(np.asarray(freqs)[:, None] * np.asarray(places)[None, :], total)
    angle = phase.astype(np.float32) * np.float32(2.0 * math.pi / total)
    return np.cos(angle).astype(np.float32), np.sin(angle).astype(np.float32)


def rounded(table):
    return np.asarray(table, np.float32).astype(ml_dtypes.bfloat16)


def make_tables():
    mode = np.arange(K)
    plane = np.where(mode < K // 2, mode, mode - K)
    cz, sz = waves(mode, np.arange(NZ), NZ)
    cx, sx = (rounded(t) for t in waves(plane, np.arange(NX), NX))
    cy, sy = (rounded(t) for t in waves(plane, np.arange(NY), NY))
    scale = np.float32(1.0 / math.sqrt(NX * NY * NZ))
    back = np.float32(1.0 / math.sqrt(K**3))
    fz, gz = rounded(cz * scale), rounded(-sz * scale)
    bz, hz = rounded(cz * back), rounded(sz * back)
    out = {}
    lift_z = np.zeros((LANES, LANES), ml_dtypes.bfloat16)
    back_z = np.zeros((LANES, LANES), ml_dtypes.bfloat16)
    for w in range(WIDE):
        for i in range(OWN):
            lift_z[:, w * 8 + i] = fz[w * OWN + i]
            lift_z[:, w * 8 + OWN + i] = gz[w * OWN + i]
            back_z[w * 8 + i] = bz[w * OWN + i]
            back_z[w * 8 + OWN + i] = -hz[w * OWN + i]
    out["lift_z"], out["back_z"] = lift_z, back_z

    lane = np.arange(LANES)
    y_of = np.concatenate([(h * 8 + lane % 8) * RY + lane // 8 for h in range(2)])
    fwd_y = np.zeros((512, 256), ml_dtypes.bfloat16)
    fwd_y[:256, :K] = cy[:, y_of].T
    fwd_y[256:, :K] = sy[:, y_of].T
    fwd_y[:256, 128 : 128 + K] = -sy[:, y_of].T
    fwd_y[256:, 128 : 128 + K] = cy[:, y_of].T
    out["fwd_y"] = fwd_y

    fwd_x = np.zeros((2, LANES, NX), ml_dtypes.bfloat16)
    fwd_x[0, :K], fwd_x[0, 64 : 64 + K] = cx, -sx
    fwd_x[1, :K], fwd_x[1, 64 : 64 + K] = sx, cx
    out["fwd_x"] = fwd_x

    inv_x = np.zeros((BULK, 16, LANES), ml_dtypes.bfloat16)
    for b in range(BULK):
        x_of = (b * RX + np.array([0, 1, 2, 3, 4, 5, 6, 7, 8, -1])) % NX
        inv_x[b, :10, :K] = cx[:, x_of].T
        inv_x[b, :10, 64 : 64 + K] = -sx[:, x_of].T
    out["inv_x"] = inv_x

    inv_y = np.zeros((LANES, 384), ml_dtypes.bfloat16)
    inv_y[:K, :256], inv_y[64 : 64 + K, :256] = cy, -sy
    for w in range(WIDE):
        for h, y in ((0, w * RY + RY), (7, w * RY - 1)):
            inv_y[:K, 256 + w * 8 + h] = cy[:, y % NY]
            inv_y[64 : 64 + K, 256 + w * 8 + h] = -sy[:, y % NY]
    out["inv_y"] = inv_y

    at_x = np.zeros((2, LANES, NX), ml_dtypes.bfloat16)
    at_x[0, :K], at_x[0, 64 : 64 + K] = cx, -sx
    at_x[1, :K], at_x[1, 64 : 64 + K] = sx, cx
    out["at_x"] = at_x
    out["at_y"] = np.stack([cy, sy])
    at_z = np.zeros((WIDE, 2, 8, NZ), ml_dtypes.bfloat16)
    for w in range(WIDE):
        at_z[w, 0, :OWN] = bz[w * OWN : (w + 1) * OWN]
        at_z[w, 1, :OWN] = hz[w * OWN : (w + 1) * OWN]
    out["at_z"] = at_z
    return out


TABLES = make_tables()


def iota(shape, axis):
    return lax.broadcasted_iota(jnp.int32, shape, axis)


def exchange(tiles, block, axis):
    tiles = list(tiles)
    shape = tiles[0].shape
    size = shape[axis]
    place = iota(shape, axis) // block
    step = 1
    while step < len(tiles):
        high = (place // step) % 2 == 1
        new = list(tiles)
        for low in range(len(tiles)):
            if low & step:
                continue
            u, v = tiles[low], tiles[low + step]
            new[low] = jnp.where(high, pltpu.roll(v, step * block, axis), u)
            new[low + step] = jnp.where(high, v, pltpu.roll(u, size - step * block, axis))
        tiles = new
        step *= 2
    return tiles


def z_ahead(v):
    axis = v.ndim - 1
    return jnp.where(iota(v.shape, axis) < NZ - 1, pltpu.roll(v, NZ - 1, axis), 0.0)


def z_behind(v):
    axis = v.ndim - 1
    return jnp.where(iota(v.shape, axis) > 0, pltpu.roll(v, 1, axis), 0.0)


def x_ahead(v):
    return jnp.concatenate([v[1:], v[:1]], 0)


def x_behind(v):
    return jnp.concatenate([v[-1:], v[:-1]], 0)


def y_ahead(v):
    return pltpu.roll(v, v.shape[1] - 1, 1)


def y_behind(v):
    return pltpu.roll(v, 1, 1)


def curl_ahead(fx, fy, fz):
    return (
        (y_ahead(fz) - fz) - (z_ahead(fy) - fy),
        (z_ahead(fx) - fx) - (x_ahead(fz) - fz),
        (x_ahead(fy) - fy) - (y_ahead(fx) - fx),
    )


def curl_behind(fx, fy, fz):
    return (
        (fz - y_behind(fz)) - (fy - z_behind(fy)),
        (fx - z_behind(fx)) - (fz - x_behind(fz)),
        (fy - x_behind(fy)) - (fx - y_behind(fx)),
    )


def place_of(flat):
    return flat >> 15, (flat >> 7) & (NY - 1), flat & (NZ - 1)


def lift_kernel(
    here, mon, src, weights, perm, electric, magnetic, material, table,
    out, taken, inverse, field, scaled, held,
):
    b, w = here[0], here[1]
    eps = jnp.zeros((RX, RY, NZ), F32)
    cells = material[...]
    for level in range(8):
        eps = jnp.where(cells == level, perm[level], eps)
    inv = 1.0 / eps
    inverse[...] = inv
    lane = iota((1, NZ), 1)
    field[...] = electric[...]

    def add(i, carry):
        x, y, z = place_of(mon[i])
        lx, ly = x - b * RX, y - w * RY

        @pl.when((lx >= 0) & (lx < RX) & (ly >= 0) & (ly < RY))
        def _():
            for c in range(3):
                row = field[c, lx, pl.ds(ly, 1), :]
                weight = weights[(64 + i) * 3 + c]
                field[c, lx, pl.ds(ly, 1), :] = row + jnp.where(lane == z, weight, 0.0)

        return carry

    lax.fori_loop(0, 64, add, 0)
    rows = field[...].reshape(3 * RX * RY, NZ).astype(BF16)
    modes = jnp.dot(rows, table[...], preferred_element_type=F32)
    modes = modes.reshape(3, RX, 2, 8, LANES)
    tiles = exchange([modes[:, x].reshape(6, 8, LANES) for x in range(RX)], 1, 1)
    tiles = [t.reshape(3, 2, 8, LANES) for t in tiles]
    tiles = exchange([tiles[y % 8][:, y // 8] for y in range(RY)], 8, 2)
    out[...] = jnp.concatenate([t.reshape(24, LANES) for t in tiles], 0).astype(BF16)

    zero = jnp.zeros((12, 32, NZ), F32)
    for c in range(3):
        scaled[c] = zero
        held[c] = zero
    for c in range(3):
        scaled[c, 2:10, 8:24, :] = 0.5 * inv * field[c]
        held[c, 2:10, 8:24, :] = magnetic[c]
    taken[...] = jnp.zeros((8, LANES), F32)
    spot_row, spot_lane = iota((8, LANES), 0), iota((8, LANES), 1)

    def take(i, carry):
        x, y, z = place_of(src[i])
        lx, ly = x - b * RX, y - w * RY

        @pl.when((lx >= -1) & (lx <= RX) & (ly >= -1) & (ly <= RY))
        def _():
            def a(c, dx, dy):
                return scaled[c, lx + 2 + dx, pl.ds(ly + 8 + dy, 1), :]

            def h(c, dx, dy):
                old = held[c, lx + 2 + dx, pl.ds(ly + 8 + dy, 1), :]
                if c == 0:
                    near = a(1, dx, dy)
                    turn = (a(2, dx, dy + 1) - a(2, dx, dy)) - (z_ahead(near) - near)
                elif c == 1:
                    near = a(0, dx, dy)
                    turn = (z_ahead(near) - near) - (a(2, dx + 1, dy) - a(2, dx, dy))
                else:
                    turn = (a(1, dx + 1, dy) - a(1, dx, dy)) - (a(0, dx, dy + 1) - a(0, dx, dy))
                return old + turn

            left = jnp.where(x > 0, 1.0, 0.0)
            down = jnp.where(y > 0, 1.0, 0.0)
            hx, hy, hz = h(0, 0, 0), h(1, 0, 0), h(2, 0, 0)
            hx_y, hz_y = down * h(0, 0, -1), down * h(2, 0, -1)
            hy_x, hz_x = left * h(1, -1, 0), left * h(2, -1, 0)
            curls = (
                (hz - hz_y) - (hy - z_behind(hy)),
                (hx - z_behind(hx)) - (hz - hz_x),
                (hy - hy_x) - (hx - hx_y),
            )
            mine = jnp.where((lx >= 0) & (lx < RX) & (ly >= 0) & (ly < RY), 1.0, 0.0)
            cx, cy = jnp.clip(lx, 0, RX - 1), jnp.clip(ly, 0, RY - 1)
            got = taken[...]
            for c in range(3):
                old = mine * field[c, cx, pl.ds(cy, 1), :]
                for n, row in ((0, old - 0.5 * curls[c]), (1, old)):
                    value = jnp.sum(jnp.where(lane == z, row, 0.0), axis=1, keepdims=True)
                    spot = (spot_row == n * 3 + c) & (spot_lane == i)
                    got = got + jnp.where(spot, value, 0.0)
            taken[...] = got

        return carry

    lax.fori_loop(0, 64, take, 0)


def middle_kernel(lines, taken, table, out):
    got = lines[...].astype(F32).reshape(WIDE, 24, LANES)
    halves = [exchange([got[h * 8 + i] for i in range(8)], 1, 1) for h in range(2)]
    rows = [
        jnp.concatenate([halves[0][k], halves[1][k], halves[0][OWN + k], halves[1][OWN + k]], 1)
        for k in range(OWN)
    ]
    lhs = jnp.concatenate(rows, 0).astype(BF16)
    found = jnp.dot(lhs, table[...], preferred_element_type=F32)
    lane = iota((8, LANES), 1)
    src = taken[...]
    high = src.astype(BF16).astype(F32)
    extra = (high, src - high)
    parts = []
    for part in range(2):
        tiles = [jnp.zeros((8, LANES), F32) for _ in range(4)]
        for d in range(3):
            for k in range(OWN):
                start = (d * OWN + k) * K
                tile, offset = start // LANES, start % LANES
                row = (k * 3 + d) * 8
                piece = found[row : row + 8, part * LANES : (part + 1) * LANES]
                if offset:
                    piece = pltpu.roll(piece, offset, 1)
                if offset + K <= LANES:
                    tiles[tile] = tiles[tile] + piece
                else:
                    tiles[tile] = tiles[tile] + jnp.where(lane >= offset, piece, 0.0)
                    tiles[tile + 1] = tiles[tile + 1] + jnp.where(lane < offset, piece, 0.0)
        tiles[3] = jnp.where(lane >= 64, pltpu.roll(extra[part], 64, 1), tiles[3])
        parts += tiles
    out[...] = jnp.concatenate(parts, 1).astype(BF16)


def phase_kernel(here, cells, at_x, at_y, at_z, phase_x, phase_yz):
    w = here[1]
    flat = cells[...]
    x, y, z = place_of(flat)
    first = iota((1, LANES), 1) < 64
    hot_x = jnp.where(iota((NX, LANES), 0) == x, 1.0, 0.0)
    real = jnp.where(first, hot_x, 0.0).astype(BF16)
    imag = jnp.where(first, 0.0, hot_x).astype(BF16)
    phase_x[...] = (
        jnp.dot(at_x[0], real, preferred_element_type=F32)
        + jnp.dot(at_x[1], imag, preferred_element_type=F32)
    ).astype(BF16)
    hot_y = jnp.where(iota((NY, LANES), 0) == y, 1.0, 0.0).astype(BF16)
    hot_z = jnp.where(iota((NZ, LANES), 0) == z, 1.0, 0.0).astype(BF16)
    cy = jnp.dot(at_y[0], hot_y, preferred_element_type=F32)
    sy = jnp.dot(at_y[1], hot_y, preferred_element_type=F32)
    cz = jnp.dot(at_z[w, 0].astype(F32).astype(BF16), hot_z, preferred_element_type=F32)
    sz = jnp.dot(at_z[w, 1].astype(F32).astype(BF16), hot_z, preferred_element_type=F32)
    for k in range(OWN):
        ck, sk = cz[k : k + 1], sz[k : k + 1]
        phase_yz[k * K : (k + 1) * K, :] = jnp.where(
            first, cy * ck - sy * sk, -(sy * ck + cy * sk)
        )


def filter_kernel(
    here, spectrum, coef_a, coef_b, fwd_x, inv_x, inv_y, phase_x, phase_yz, out, rows
):
    b = here[0]
    lane = iota((1, LANES), 1)
    got_r, got_i = spectrum[:, 0:512], spectrum[:, 512:1024]
    full = jnp.dot(fwd_x[0], got_r, preferred_element_type=F32) + jnp.dot(
        fwd_x[1], got_i, preferred_element_type=F32
    )
    full = full.T
    size = OWN * K
    field = [full[d * size : (d + 1) * size] for d in range(3)]
    turned = [pltpu.roll(f, 64, 1) for f in field]
    sign = jnp.where(lane < 64, 1.0, -1.0)
    gap = jnp.zeros((16, LANES), F32)
    right = []
    shares = []
    for e in range(3):
        q = jnp.zeros((size, LANES), F32)
        for d in range(3):
            at = (e * 3 + d) * size
            q = q + coef_a[at : at + size] * field[d] + coef_b[at : at + size] * turned[d]
        other = pltpu.roll(q, 64, 1) * sign
        for k in range(OWN):
            right += [q[k * K : (k + 1) * K], gap, other[k * K : (k + 1) * K], gap]
        for k in range(OWN):
            right += [other[k * K : (k + 1) * K], gap, -q[k * K : (k + 1) * K], gap]
        near = jnp.dot(q.astype(BF16), phase_x[...], preferred_element_type=F32)
        line = jnp.sum(near * phase_yz[...], axis=0, keepdims=True)
        shares.append(line + pltpu.roll(line, 64, 1))
    stacked = jnp.concatenate(right, 0).astype(BF16)
    at_b = inv_x[b]
    along = lax.dot_general(
        at_b, stacked, (((1,), (1,)), ((), ())), preferred_element_type=F32
    )
    rows[...] = jnp.zeros((32, 8, LANES), F32)
    for e in range(3):
        for m in range(6):
            tile = (e * 6 + m) * LANES
            for x in range(10):
                rows[e * 10 + x, m : m + 1, :] = along[x : x + 1, tile : tile + LANES]
    lhs = rows[...].reshape(256, LANES).astype(BF16)
    wide = jnp.dot(lhs, inv_y[...], preferred_element_type=F32).reshape(32, 8, 384)
    near = []
    for low in range(8):
        group = [wide[high * 8 + low, :, c * LANES : (c + 1) * LANES] for high in range(4) for c in range(2)]
        near.append(jnp.stack(group))
    near = exchange(near, 16, 2)
    edge = []
    for low in range(16):
        edge.append(jnp.stack([wide[high * 16 + low, :, 256:384] for high in range(2)]))
    edge = exchange(edge, 8, 2)

    extra_r = spectrum[:, 384:512].astype(F32).reshape(BULK, 8, LANES).sum(0)
    extra_i = spectrum[:, 896:1024].astype(F32).reshape(BULK, 8, LANES).sum(0)
    total = pltpu.roll(extra_r + extra_i, 64, 1)
    row = iota((8, LANES), 0)
    for e in range(3):
        total = total + jnp.where(row == e, shares[e], 0.0)
    total = jnp.where(lane < 64, total, 0.0)
    high = total.astype(BF16).astype(F32)
    last = high + pltpu.roll(total - high, 64, 1)
    blocks = []
    for w in range(WIDE):
        tiles = [near[w % 8][high_x * 2 + w // 8] for high_x in range(4)]
        tiles += [edge[w][high_x] for high_x in range(2)] + [last]
        blocks.append(jnp.concatenate(tiles, 1))
    out[...] = jnp.concatenate(blocks, 0).astype(BF16)


def first_kernel(
    here, mon, weights, electric, magnetic, inverse, saved, x_low, x_high, y_low, y_high,
    early, curled, factor, grad, ready, e_ext, h_ext, g_ext,
):
    b, w = here[0], here[1]
    lane = iota((1, NZ), 1)
    for c in range(7):
        to = e_ext.at[c] if c < 3 else (h_ext.at[c - 3] if c < 6 else g_ext)
        own = electric[c] if c < 3 else (magnetic[c - 3] if c < 6 else inverse[...])
        to[0:8, 0:16, :] = own
        to[8:10, 0:16, :] = x_high[c]
        to[10:12, 0:16, :] = x_low[c]
        low, high = y_low[c * 12 : (c + 1) * 12], y_high[c * 12 : (c + 1) * 12]
        to[:, 16:24, :] = jnp.concatenate([high, jnp.zeros((12, 4, NZ), F32), low], 1)

    def inject(ref, which):
        def add(i, carry):
            x, y, z = place_of(mon[i])
            lx, ly = x - b * RX, y - w * RY

            @pl.when((lx >= -2) & (lx < RX + 2) & (ly >= -2) & (ly < RY + 2))
            def _():
                px = jnp.where(lx < 0, lx + 12, lx)
                py = jnp.where(ly < 0, ly + 24, ly)
                for c in range(3):
                    row = ref[c, px, pl.ds(py, 1), :]
                    weight = weights[(which * 64 + i) * 3 + c]
                    ref[c, px, pl.ds(py, 1), :] = row + jnp.where(lane == z, weight, 0.0)

            return carry

        lax.fori_loop(0, 64, add, 0)

    inject(e_ext, 1)
    g = g_ext[...]
    half = 0.5 * g
    a = [half * e_ext[c] for c in range(3)]
    spot_x = iota((12, 24, 1), 0)
    spot_y = iota((12, 24, 1), 1)
    outside = ((spot_x >= 10) & (b == 0)) | ((spot_y >= 22) & (w == 0))
    inside = jnp.where(outside, 0.0, 1.0)
    turned = curl_ahead(*a)
    h = [h_ext[c] + inside * turned[c] for c in range(3)]
    back = curl_behind(*h)
    for c in range(3):
        e_ext[c] = e_ext[c] - 0.5 * back[c]
    inject(e_ext, 0)
    for c in range(3):
        early[c, 0:9] = e_ext[c, 0:9]
        early[c, 9:10] = e_ext[c, 11:12]
        curled[c, 0:9] = h[c][0:9]
        curled[c, 9:10] = h[c][11:12]
    factor[0:9] = half[0:9]
    factor[9:10] = half[11:12]

    near = inverse[...]
    for step in range(2):
        s = [saved[step, c].astype(F32) for c in range(3)]
        before_x = {c: jnp.concatenate([x_low[7 + step, c - 1 : c], s[c][:-1]], 0) for c in (1, 2)}
        at = 84 + step * 8
        before_y = {}
        for c in (0, 2):
            edge = y_low[at : at + 8, c // 2 : c // 2 + 1, :]
            first = iota((RX, RY, NZ), 1) == 0
            before_y[c] = jnp.where(first, edge, pltpu.roll(s[c], 1, 1))
        curls = (
            (s[2] - before_y[2]) - (s[1] - z_behind(s[1])),
            (s[0] - z_behind(s[0])) - (s[2] - before_x[2]),
            (s[1] - before_x[1]) - (s[0] - before_y[0]),
        )
        if step == 0:
            for c in range(3):
                ready[c] = near * curls[c]
        else:
            total = jnp.zeros((RX, RY, NZ), F32)
            for c in range(3):
                total = total + a[c][0:8, 0:16] * near * curls[c]
            grad[...] = -total


def second_kernel(
    here, lines, table, early, curled, factor, first_grad, ready, injected,
    grad_e, grad_h, grad_eps, sources,
):
    b, w = here[0], here[1]
    modes = lines[:, 0:768]
    back = lax.dot_general(
        modes, table[...], (((0,), (0,)), ((), ())), preferred_element_type=F32
    )
    main = back[0:512].reshape(32, 16, NZ)
    edge = back[512:768].reshape(32, 8, NZ)
    half = factor[...]
    e1 = []
    for c in range(3):
        at = slice(c * 10, c * 10 + 10)
        e1.append(early[c] + jnp.concatenate([main[at], edge[at]], 1))
    a = [half * e for e in e1]
    spot_x = iota((10, 24, 1), 0)
    spot_y = iota((10, 24, 1), 1)
    outside = ((spot_x == 9) & (b == 0)) | ((spot_y == 23) & (w == 0))
    inside = jnp.where(outside, 0.0, 1.0)
    turned = curl_ahead(*a)
    h = [curled[c] + inside * turned[c] for c in range(3)]
    backed = curl_behind(*h)
    total = first_grad[...]
    for c in range(3):
        grad_h[c] = h[c][0:8, 0:16]
        grad_e[c] = e1[c][0:8, 0:16] - 0.5 * backed[c][0:8, 0:16]
        total = total - a[c][0:8, 0:16] * ready[c]
    grad_eps[...] = total
    got = lines[:, 768:896].astype(F32).reshape(WIDE, 8, LANES).sum(0)
    got = got + pltpu.roll(got, 64, 1) + injected[...]
    columns = got.T
    sources[0] = columns[0:64, 0:3]
    sources[1] = columns[0:64, 3:6]


def call(kernel, outs, in_smem, count, scratch=(), flops=0, moved=0):
    smem, vmem = pl.BlockSpec(memory_space=pltpu.SMEM), pl.BlockSpec(memory_space=pltpu.VMEM)
    return pl.pallas_call(
        kernel,
        out_shape=outs,
        in_specs=[smem if i in in_smem else vmem for i in range(count)],
        out_specs=jax.tree.map(lambda _: vmem, outs),
        scratch_shapes=list(scratch),
        compiler_params=PARAMS,
        cost_estimate=pl.CostEstimate(flops=flops, bytes_accessed=moved, transcendentals=0),
    )


def shape(*dims, dtype=F32):
    return jax.ShapeDtypeStruct(dims, dtype)


def passed_along(block, axis, distance):
    devices = range(lax.axis_size(axis))
    route = [(i - distance, i) for i in devices if i - distance in devices]
    return lax.ppermute(block, axis, route)


def tables_of(name):
    return jnp.asarray(TABLES[name])


def body(
    seed_electric, seed_magnetic, saved_magnetic, material, permittivity, source_cells,
    monitor_cells, monitor_weights, lift_weight, project_weight, mode_mix, gain_first, gain_second,
):
    bulk, wide = lax.axis_index("bulk"), lax.axis_index("wide")
    here = jnp.stack([bulk, wide]).astype(jnp.int32)
    weights = monitor_weights.reshape(-1)

    payload, taken, inverse = call(
        lift_kernel,
        (shape(384, LANES, dtype=BF16), shape(8, LANES), shape(RX, RY, NZ)),
        range(5),
        9,
        [pltpu.VMEM((3, RX, RY, NZ), F32)] + [pltpu.VMEM((3, 12, 32, NZ), F32)] * 2,
        flops=13_000_000,
        moved=700_000,
    )(
        here, monitor_cells, source_cells, weights, permittivity,
        seed_electric, seed_magnetic, material, tables_of("lift_z"),
    )
    lines = lax.all_to_all(payload, "wide", split_axis=0, concat_axis=0, tiled=True)

    g = inverse[None]
    own = jnp.concatenate([seed_electric, seed_magnetic, g], 0)
    saved = saved_magnetic.astype(F32)
    x_low = passed_along(
        jnp.concatenate([own[:, 6:8], saved[:, 1:3, 7]], 0), "bulk", 1
    )
    x_high = passed_along(own[:, 0:2], "bulk", -1)
    block = jnp.concatenate([own, x_high, x_low[:7]], 1)
    lows = jnp.stack([saved[:, 0, :, 15], saved[:, 2, :, 15]], 2).reshape(16, 2, NZ)
    y_low = passed_along(
        jnp.concatenate([block[:, :, 14:16].reshape(84, 2, NZ), lows], 0), "wide", 1
    )
    y_high = passed_along(block[:, :, 0:2].reshape(84, 2, NZ), "wide", -1)

    spectrum = call(
        middle_kernel,
        shape(8, 1024, dtype=BF16),
        (),
        3,
        flops=20_000_000,
        moved=400_000,
    )(lines, taken, tables_of("fwd_y"))
    gathered = lax.all_gather(spectrum, "bulk", axis=0, tiled=True)

    cells = jnp.concatenate([source_cells, source_cells]).reshape(1, LANES)
    phase_x, phase_yz = call(
        phase_kernel,
        (shape(LANES, LANES, dtype=BF16), shape(OWN * K, LANES)),
        (0,),
        5,
        flops=20_000_000,
        moved=400_000,
    )(here, cells, tables_of("at_x"), tables_of("at_y"), tables_of("at_z"))

    mix = lax.dynamic_slice_in_dim(mode_mix, wide * OWN, OWN, 1).astype(F32)
    mixed = jnp.sum(
        lift_weight.T[None, None, :, :, None] * mix[:, :, None, :, :], axis=3
    )
    joint = (
        project_weight[None, :, None, None, None, :]
        * mixed.transpose(0, 2, 1, 3)[:, None, :, :, None, :]
        * gain_second.T[None, None, None, None, :, :]
    ).reshape(2, 9 * OWN * K, 16)
    blank = jnp.zeros((16, 16), F32)
    gain_a = jnp.concatenate([gain_first, blank, gain_first, blank], 1)
    gain_b = jnp.concatenate([-gain_first, blank, gain_first, blank], 1)
    coef_a = jnp.dot(joint[0], gain_a, precision=lax.Precision.HIGHEST)
    coef_b = jnp.dot(joint[1], gain_b, precision=lax.Precision.HIGHEST)
    injected = jnp.sum(
        jnp.where(
            source_cells[None, :, None] == monitor_cells[None, None, :],
            monitor_weights[0].T[:, None, :],
            0.0,
        ),
        axis=2,
    )
    injected = jnp.pad(injected, ((0, 5), (0, 64)))

    early, curled, factor, first_grad, ready = call(
        first_kernel,
        (
            shape(3, 10, 24, NZ), shape(3, 10, 24, NZ), shape(10, 24, NZ),
            shape(RX, RY, NZ), shape(3, RX, RY, NZ),
        ),
        range(3),
        11,
        [pltpu.VMEM((3, 12, 24, NZ), F32)] * 2 + [pltpu.VMEM((12, 24, NZ), F32)],
        flops=10_000_000,
        moved=3_000_000,
    )(
        here, monitor_cells, weights, seed_electric, seed_magnetic, inverse, saved_magnetic,
        x_low, x_high, y_low, y_high,
    )

    sent = call(
        filter_kernel,
        shape(128, 896, dtype=BF16),
        (0,),
        9,
        [pltpu.VMEM((32, 8, LANES), F32)],
        flops=200_000_000,
        moved=3_000_000,
    )(
        here, gathered, coef_a, coef_b, tables_of("fwd_x"), tables_of("inv_x"),
        tables_of("inv_y"), phase_x, phase_yz,
    )
    returned = lax.all_to_all(sent, "wide", split_axis=0, concat_axis=0, tiled=True)
    return call(
        second_kernel,
        (
            shape(3, RX, RY, NZ), shape(3, RX, RY, NZ), shape(RX, RY, NZ), shape(2, 64, 3),
        ),
        (0,),
        9,
        flops=40_000_000,
        moved=4_000_000,
    )(
        here, returned, tables_of("back_z"), early, curled, factor, first_grad, ready, injected
    )


def solution(mesh):
    field = P(None, "bulk", "wide", None)
    return jax.shard_map(
        body,
        mesh=mesh,
        in_specs=(
            field, field, P(None, None, "bulk", "wide", None), P("bulk", "wide", None),
            P(), P(), P(), P(), P(), P(), P(), P(), P(),
        ),
        out_specs=(field, field, P("bulk", "wide", None), P()),
        check_vma=False,
    )
```

```python
import functools
import math

import jax
import jax.numpy as jnp
import ml_dtypes
import numpy as np
from jax import lax
from jax.experimental import pallas as pl
from jax.experimental.pallas import tpu as pltpu
from jax.sharding import PartitionSpec as P

NX, NY, NZ = 256, 256, 128
K = 48
OWN = 3
WIDE, BULK = 16, 32
RX, RY = 8, 16
NEAR, FAR = 8, 4
SHARE = OWN * K // NEAR
LANES = 128
F32, BF16 = jnp.float32, jnp.bfloat16
PARAMS = pltpu.CompilerParams(vmem_limit_bytes=40 * 1024 * 1024)
HIGHEST = lax.Precision.HIGHEST


def waves(freqs, places, total):
    phase = np.mod(np.asarray(freqs)[:, None] * np.asarray(places)[None, :], total)
    angle = phase.astype(np.float32) * np.float32(2.0 * math.pi / total)
    return np.cos(angle).astype(np.float32), np.sin(angle).astype(np.float32)


def rounded(table):
    return np.asarray(table, np.float32).astype(ml_dtypes.bfloat16)


def make_tables():
    mode = np.arange(K)
    plane = np.where(mode < K // 2, mode, mode - K)
    cz, sz = waves(mode, np.arange(NZ), NZ)
    cx, sx = (rounded(t) for t in waves(plane, np.arange(NX), NX))
    cy, sy = (rounded(t) for t in waves(plane, np.arange(NY), NY))
    scale = np.float32(1.0 / math.sqrt(NX * NY * NZ))
    back = np.float32(1.0 / math.sqrt(K**3))
    fz, gz = rounded(cz * scale), rounded(-sz * scale)
    bz, hz = rounded(cz * back), rounded(sz * back)
    out = {}
    lift_z = np.zeros((LANES, LANES), ml_dtypes.bfloat16)
    back_z = np.zeros((LANES, LANES), ml_dtypes.bfloat16)
    for w in range(WIDE):
        for i in range(OWN):
            lift_z[:, w * 8 + i] = fz[w * OWN + i]
            lift_z[:, w * 8 + OWN + i] = gz[w * OWN + i]
            back_z[w * 8 + i] = bz[w * OWN + i]
            back_z[w * 8 + OWN + i] = -hz[w * OWN + i]
    out["lift_z"], out["back_z"] = lift_z, back_z

    lane = np.arange(LANES)
    y_of = np.concatenate([(h * 8 + lane % 8) * RY + lane // 8 for h in range(2)])
    fwd_y = np.zeros((512, 256), ml_dtypes.bfloat16)
    fwd_y[:256, :K] = cy[:, y_of].T
    fwd_y[256:, :K] = sy[:, y_of].T
    fwd_y[:256, 128 : 128 + K] = -sy[:, y_of].T
    fwd_y[256:, 128 : 128 + K] = cy[:, y_of].T
    out["fwd_y"] = fwd_y

    fwd_x = np.zeros((FAR, 2 * LANES, LANES), ml_dtypes.bfloat16)
    inv_x = np.zeros((FAR, LANES, LANES), ml_dtypes.bfloat16)
    for far in range(FAR):
        for n in range(NEAR):
            start = (far * NEAR + n) * RX
            here, at = slice(start, start + RX), slice(n * 16, n * 16 + RX)
            fwd_x[far, :K, at], fwd_x[far, 64 : 64 + K, at] = cx[:, here], -sx[:, here]
            fwd_x[far, 128 : 128 + K, at], fwd_x[far, 192 : 192 + K, at] = sx[:, here], cx[:, here]
            x_of = (start + np.array([0, 1, 2, 3, 4, 5, 6, 7, 8, -1])) % NX
            inv_x[far, n * 16 : n * 16 + 10, :K] = cx[:, x_of].T
            inv_x[far, n * 16 : n * 16 + 10, 64 : 64 + K] = -sx[:, x_of].T
    out["fwd_x"], out["inv_x"] = fwd_x, inv_x

    inv_y = np.zeros((LANES, 384), ml_dtypes.bfloat16)
    inv_y[:K, :256], inv_y[64 : 64 + K, :256] = cy, -sy
    for w in range(WIDE):
        for h, y in ((0, w * RY + RY), (7, w * RY - 1)):
            inv_y[:K, 256 + w * 8 + h] = cy[:, y % NY]
            inv_y[64 : 64 + K, 256 + w * 8 + h] = -sy[:, y % NY]
    out["inv_y"] = inv_y

    at_x = np.zeros((2, LANES, NX), ml_dtypes.bfloat16)
    at_x[0, :K], at_x[0, 64 : 64 + K] = cx, -sx
    at_x[1, :K], at_x[1, 64 : 64 + K] = sx, cx
    out["at_x"] = at_x
    at_y = np.zeros((NEAR, 2, 32, NY), ml_dtypes.bfloat16)
    for n in range(NEAR):
        j_of = np.arange(n * SHARE, (n + 1) * SHARE) % K
        at_y[n, 0, :SHARE], at_y[n, 1, :SHARE] = cy[j_of], sy[j_of]
    out["at_y"] = at_y
    at_z = np.zeros((WIDE, 2, 16, NZ), ml_dtypes.bfloat16)
    for w in range(WIDE):
        at_z[w, 0, :OWN] = bz[w * OWN : (w + 1) * OWN]
        at_z[w, 1, :OWN] = hz[w * OWN : (w + 1) * OWN]
    out["at_z"] = at_z
    return out


TABLES = make_tables()


def iota(shape, axis):
    return lax.broadcasted_iota(jnp.int32, shape, axis)


def exchange(tiles, block, axis):
    tiles = list(tiles)
    shape = tiles[0].shape
    size = shape[axis]
    place = iota(shape, axis) // block
    step = 1
    while step < len(tiles):
        high = (place // step) % 2 == 1
        new = list(tiles)
        for low in range(len(tiles)):
            if low & step:
                continue
            u, v = tiles[low], tiles[low + step]
            new[low] = jnp.where(high, pltpu.roll(v, step * block, axis), u)
            new[low + step] = jnp.where(high, v, pltpu.roll(u, size - step * block, axis))
        tiles = new
        step *= 2
    return tiles


def z_ahead(v):
    axis = v.ndim - 1
    return jnp.where(iota(v.shape, axis) < NZ - 1, pltpu.roll(v, NZ - 1, axis), 0.0)


def z_behind(v):
    axis = v.ndim - 1
    return jnp.where(iota(v.shape, axis) > 0, pltpu.roll(v, 1, axis), 0.0)


def x_ahead(v):
    return jnp.concatenate([v[1:], v[:1]], 0)


def x_behind(v):
    return jnp.concatenate([v[-1:], v[:-1]], 0)


def y_ahead(v):
    return pltpu.roll(v, v.shape[1] - 1, 1)


def y_behind(v):
    return pltpu.roll(v, 1, 1)


def curl_ahead(fx, fy, fz):
    return (
        (y_ahead(fz) - fz) - (z_ahead(fy) - fy),
        (z_ahead(fx) - fx) - (x_ahead(fz) - fz),
        (x_ahead(fy) - fy) - (y_ahead(fx) - fx),
    )


def curl_behind(fx, fy, fz):
    return (
        (fz - y_behind(fz)) - (fy - z_behind(fy)),
        (fx - z_behind(fx)) - (fz - x_behind(fz)),
        (fy - x_behind(fy)) - (fx - y_behind(fx)),
    )


def place_of(flat):
    return flat >> 15, (flat >> 7) & (NY - 1), flat & (NZ - 1)


def own_block():
    return lax.axis_index("bulk"), lax.axis_index("wide")


def fetch(pairs, sems):
    copies = [pltpu.make_async_copy(a, b, sems.at[i]) for i, (a, b) in enumerate(pairs)]
    for copy in copies:
        copy.start()
    return copies


def scan(cells, hit, act):
    def group(g, carry):
        found = [cells[g * 8 + i] for i in range(8)]
        hits = [hit(*place_of(f)) for f in found]
        some = functools.reduce(jnp.logical_or, hits)

        @pl.when(some)
        def _():
            for i in range(8):
                pl.when(hits[i])(functools.partial(act, g * 8 + i, found[i]))

        return carry

    lax.fori_loop(0, 8, group, 0)


def lift_kernel(mon_in, weights_in, electric, table_in, out, field, mon, weights, table, sems):
    b, w = own_block()
    copies = fetch(
        ((mon_in, mon), (electric, field), (weights_in, weights), (table_in, table)), sems
    )
    for copy in copies:
        copy.wait()
    lane = iota((1, NZ), 1)
    spot = iota((1, 64), 1)

    def hit(x, y, z):
        return ((x >> 3) == b) & ((y >> 4) == w)

    def add(i, flat):
        x, y, z = place_of(flat)
        lx, ly = x & (RX - 1), y & (RY - 1)
        for c in range(3):
            row = field[c, lx, pl.ds(ly, 1), :]
            given = jnp.where(spot == i, weights[c, 1:2, :], 0.0)
            weight = jnp.sum(given, axis=1, keepdims=True)
            field[c, lx, pl.ds(ly, 1), :] = row + jnp.where(lane == z, weight, 0.0)

    scan(mon, hit, add)
    rows = field[...].reshape(3 * RX * RY, NZ).astype(BF16)
    modes = jnp.dot(rows, table[...], preferred_element_type=F32)
    modes = modes.reshape(3, RX, 2, 8, LANES)
    tiles = exchange([modes[:, x].reshape(6, 8, LANES) for x in range(RX)], 1, 1)
    tiles = [t.reshape(3, 2, 8, LANES) for t in tiles]
    tiles = exchange([tiles[y % 8][:, y // 8] for y in range(RY)], 8, 2)
    out[...] = jnp.concatenate([t.reshape(24, LANES) for t in tiles], 0).astype(BF16)


def share_kernel(
    src_in, perm_in, field, magnetic_in, material_in, saved_in,
    taken, inverse, to_low, to_high,
    src, perm, magnetic, material, saved, scaled, held, sems,
):
    b, w = own_block()
    copies = fetch(
        (
            (src_in, src), (perm_in, perm), (magnetic_in, magnetic),
            (material_in, material), (saved_in, saved),
        ),
        sems,
    )
    zero = jnp.zeros((12, 32, NZ), F32)
    for c in range(3):
        scaled[c] = zero
        held[c] = zero
    for copy in copies:
        copy.wait()
    eps = jnp.zeros((RX, RY, NZ), F32)
    cells = material[...]
    for level in range(8):
        eps = jnp.where(cells == level, perm[level], eps)
    inv = 1.0 / eps
    inverse[...] = inv
    lane = iota((1, NZ), 1)
    for c in range(3):
        scaled[c, 2:10, 8:24, :] = 0.5 * inv * field[c]
        held[c, 2:10, 8:24, :] = magnetic[c]
        to_low[c], to_high[c] = field[c, 6:8], field[c, 0:2]
        to_low[3 + c], to_high[3 + c] = magnetic[c, 6:8], magnetic[c, 0:2]
    to_low[6], to_high[6] = inv[6:8], inv[0:2]
    for n in range(2):
        for c in range(2):
            to_low[7 + n, c] = saved[n, 1 + c, 7].astype(F32)
    taken[...] = jnp.zeros((8, LANES), F32)
    spot_row, spot_lane = iota((8, LANES), 0), iota((8, LANES), 1)

    def hit(x, y, z):
        lx, ly = x - b * RX, y - w * RY
        return (lx >= -1) & (lx <= RX) & (ly >= -1) & (ly <= RY)

    def take(i, flat):
        x, y, z = place_of(flat)
        lx, ly = x - b * RX, y - w * RY

        def a(c, dx, dy):
            return scaled[c, lx + 2 + dx, pl.ds(ly + 8 + dy, 1), :]

        def h(c, dx, dy):
            old = held[c, lx + 2 + dx, pl.ds(ly + 8 + dy, 1), :]
            if c == 0:
                near = a(1, dx, dy)
                turn = (a(2, dx, dy + 1) - a(2, dx, dy)) - (z_ahead(near) - near)
            elif c == 1:
                near = a(0, dx, dy)
                turn = (z_ahead(near) - near) - (a(2, dx + 1, dy) - a(2, dx, dy))
            else:
                turn = (a(1, dx + 1, dy) - a(1, dx, dy)) - (a(0, dx, dy + 1) - a(0, dx, dy))
            return old + turn

        left = jnp.where(x > 0, 1.0, 0.0)
        down = jnp.where(y > 0, 1.0, 0.0)
        hx, hy, hz = h(0, 0, 0), h(1, 0, 0), h(2, 0, 0)
        hx_y, hz_y = down * h(0, 0, -1), down * h(2, 0, -1)
        hy_x, hz_x = left * h(1, -1, 0), left * h(2, -1, 0)
        curls = (
            (hz - hz_y) - (hy - z_behind(hy)),
            (hx - z_behind(hx)) - (hz - hz_x),
            (hy - hy_x) - (hx - hx_y),
        )
        mine = jnp.where((lx >= 0) & (lx < RX) & (ly >= 0) & (ly < RY), 1.0, 0.0)
        cx, cy = jnp.clip(lx, 0, RX - 1), jnp.clip(ly, 0, RY - 1)
        got = taken[...]
        for c in range(3):
            old = mine * field[c, cx, pl.ds(cy, 1), :]
            for n, row in ((0, old - 0.5 * curls[c]), (1, old)):
                value = jnp.sum(jnp.where(lane == z, row, 0.0), axis=1, keepdims=True)
                spot = (spot_row == n * 3 + c) & (spot_lane == i)
                got = got + jnp.where(spot, value, 0.0)
        taken[...] = got

    scan(src, hit, take)


def middle_kernel(lines, taken, table, out):
    got = lines[...].astype(F32).reshape(WIDE, 24, LANES)
    halves = [exchange([got[h * 8 + i] for i in range(8)], 1, 1) for h in range(2)]
    rows = [
        jnp.concatenate([halves[0][k], halves[1][k], halves[0][OWN + k], halves[1][OWN + k]], 1)
        for k in range(OWN)
    ]
    lhs = jnp.concatenate(rows, 0).astype(BF16)
    found = jnp.dot(lhs, table[...], preferred_element_type=F32)
    lane = iota((8, LANES), 1)
    parts = [jnp.zeros((8, LANES), F32) for _ in range(NEAR)]
    for part in range(2):
        for d in range(3):
            piece = [
                found[(k * 3 + d) * 8 : (k * 3 + d) * 8 + 8, part * LANES : (part + 1) * LANES]
                for k in range(OWN)
            ]
            last = pltpu.roll(piece[2], 2 * K, 1)
            first = piece[0] + pltpu.roll(piece[1], K, 1) + jnp.where(lane >= 2 * K, last, 0.0)
            rest = jnp.where(lane < 16, last, 0.0)
            to = part * 64 + d * SHARE
            for n in range(NEAR):
                moved = pltpu.roll(first, (to - n * SHARE) % LANES, 1)
                if n == NEAR - 1:
                    moved = jnp.where(lane < to + 2, moved, pltpu.roll(rest, to + 2, 1))
                within = (lane >= to) & (lane < to + SHARE)
                parts[n] = parts[n] + jnp.where(within, moved, 0.0)
    src = taken[...]
    high = src.astype(BF16).astype(F32)
    extra = high + pltpu.roll(src - high, 64, 1)
    out[...] = jnp.concatenate([t for p in parts for t in (p, extra)], 0).astype(BF16)


def param_kernel(
    mon, weights, lift, cells, project, gain_x, gain_y, mix, at_x, at_y, at_z, after,
    coef_a, coef_b, phase_x, phase_yz, injected,
):
    b, w = own_block()
    n = b % NEAR
    flat = cells[...]
    x, y, z = place_of(flat)
    first = iota((1, LANES), 1) < 64
    hot_x = jnp.where(iota((NX, LANES), 0) == x, 1.0, 0.0)
    real = jnp.where(first, hot_x, 0.0).astype(BF16)
    imag = jnp.where(first, 0.0, hot_x).astype(BF16)
    phase_x[...] = (
        jnp.dot(at_x[0], real, preferred_element_type=F32)
        + jnp.dot(at_x[1], imag, preferred_element_type=F32)
    ).astype(BF16)
    hot_y = jnp.where(iota((NY, LANES), 0) == y, 1.0, 0.0).astype(BF16)
    hot_z = jnp.where(iota((NZ, LANES), 0) == z, 1.0, 0.0).astype(BF16)
    cy = jnp.dot(at_y[n, 0], hot_y, preferred_element_type=F32)[:24]
    sy = jnp.dot(at_y[n, 1], hot_y, preferred_element_type=F32)[:24]
    cz = jnp.dot(at_z[w, 0], hot_z, preferred_element_type=F32)
    sz = jnp.dot(at_z[w, 1], hot_z, preferred_element_type=F32)
    mode = n * SHARE + iota((24, 1), 0)
    ck = jnp.where(mode < K, cz[0:1], jnp.where(mode < 2 * K, cz[1:2], cz[2:3]))
    sk = jnp.where(mode < K, sz[0:1], jnp.where(mode < 2 * K, sz[1:2], sz[2:3]))
    phase_yz[...] = jnp.where(first, cy * ck - sy * sk, -(sy * ck + cy * sk))

    place = iota((K, 24), 1)
    mode = n * SHARE + place
    depth = jnp.where(mode < K, 0, jnp.where(mode < 2 * K, 1, 2))
    live = place < SHARE
    hot_j = jnp.where((iota((K, 24), 0) == mode - depth * K) & live, 1.0, 0.0)
    hot_k = jnp.where((iota((K, 24), 0) == w * OWN + depth) & live, 1.0, 0.0)
    gains = jnp.dot(gain_y[...], hot_j, precision=HIGHEST, preferred_element_type=F32)
    diagonal = iota((16, 16), 0) == iota((16, 16), 1)
    columns = [
        jnp.sum(jnp.where(diagonal, project[e : e + 1, :], 0.0), axis=1, keepdims=True)
        for e in range(3)
    ]
    blank = jnp.zeros((16, 16), F32)
    along = gain_x[...]
    for part, to in ((0, coef_a), (1, coef_b)):
        joined = []
        for d in range(3):
            total = jnp.zeros((16, K), F32)
            for c in range(16):
                total = total + lift[d, c] * mix[part, c].astype(F32)
            joined.append(
                gains * jnp.dot(total, hot_k, precision=HIGHEST, preferred_element_type=F32)
            )
        sign = 1.0 if part == 0 else -1.0
        right = jnp.concatenate([sign * along, blank, along, blank], 1)
        for e in range(3):
            for d in range(3):
                left = (columns[e] * joined[d]).T
                to[(e * 3 + d) * 24 : (e * 3 + d + 1) * 24, :] = jnp.dot(
                    left, right, precision=HIGHEST, preferred_element_type=F32
                )
    row = iota((8, LANES), 0)
    total = jnp.zeros((8, LANES), F32)
    for i in range(64):
        given = jnp.where(
            row == 0, weights[0, 0, i], jnp.where(row == 1, weights[1, 0, i], weights[2, 0, i])
        )
        total = total + jnp.where((flat == mon[i]) & (row < 3), given, 0.0)
    injected[...] = jnp.where(iota((8, LANES), 1) < 64, total, 0.0)


def filter_kernel(
    own, far_1, far_2, far_3, coef_a, coef_b, fwd_x, inv_x, phase_x, phase_yz, after, out, pre
):
    b, w = own_block()
    far = b // NEAR
    lane = iota((1, LANES), 1)
    both = jnp.zeros((2 * LANES, LANES), F32)
    total = jnp.zeros((8, LANES), F32)
    for t, ref in enumerate((own, far_1, far_2, far_3)):
        got = ref[...]
        both = both + jnp.dot(fwd_x[(far + FAR - t) % FAR], got, preferred_element_type=F32)
        total = total + got.astype(F32).reshape(NEAR, 2, 8, LANES)[:, 1].sum(0)
    pre[...] = jnp.where(lane < 64, total + pltpu.roll(total, 64, 1), 0.0)
    full = (both[:LANES] + pltpu.roll(both[LANES:], 64, 1)).T
    field = [full[d * SHARE : d * SHARE + 24] for d in range(3)]
    turned = [pltpu.roll(f, 64, 1) for f in field]
    sign = jnp.where(lane < 64, 1.0, -1.0)
    real = []
    for e in range(3):
        q = jnp.zeros((24, LANES), F32)
        for d in range(3):
            at = (e * 3 + d) * 24
            q = q + coef_a[at : at + 24] * field[d] + coef_b[at : at + 24] * turned[d]
        real.append(q)
    near = jnp.dot(
        jnp.concatenate(real, 0).astype(BF16), phase_x[...], preferred_element_type=F32
    )
    gap = jnp.zeros((10, LANES), F32)
    packed = jnp.concatenate([q[:SHARE] for q in real] + [gap], 0)
    right = jnp.concatenate([packed, pltpu.roll(packed, 64, 1) * sign], 0).astype(BF16)
    back = lax.dot_general(
        inv_x[far], right, (((1,), (1,)), ((), ())), preferred_element_type=F32
    ).reshape(NEAR, 2, 8, LANES)
    row = iota((8, LANES), 0)
    extra = jnp.zeros((8, LANES), F32)
    for e in range(3):
        line = jnp.sum(near[e * 24 : (e + 1) * 24] * phase_yz[...], axis=0, keepdims=True)
        line = line + pltpu.roll(line, 64, 1)
        high = line.astype(BF16).astype(F32)
        extra = extra + jnp.where(row == 2 + e, jnp.where(lane < 64, high, line - high), 0.0)
    tiles = []
    for n in range(NEAR):
        tiles += [back[n, 0], back[n, 1] + extra]
    out[...] = jnp.concatenate(tiles, 0).astype(BF16)


def spread_kernel(shares, pre, inv_y, out, rows):
    lane = iota((1, LANES), 1)
    got = shares[...].astype(F32).reshape(NEAR, 16, LANES)
    rows[...] = jnp.zeros((32, 8, LANES), F32)
    for e in range(3):
        flat = []
        for part in range(2):
            start = part * 64 + e * SHARE
            first, rest = jnp.zeros((16, LANES), F32), None
            for n in range(NEAR):
                moved = pltpu.roll(got[n], (n * SHARE - start) % LANES, 1)
                within = (lane >= n * SHARE) & (lane < (n + 1) * SHARE)
                first = first + jnp.where(within, moved, 0.0)
                if n == NEAR - 1:
                    rest = jnp.where(lane < 16, moved, 0.0)
            flat.append((first, rest))

        def mode_rows(part, k, to):
            first, rest = flat[part]
            moved = pltpu.roll(first, (to - k * K) % LANES, 1)
            if k < 2:
                return jnp.where((lane >= to) & (lane < to + K), moved, 0.0)
            tail = pltpu.roll(rest, to + 32, 1)
            return jnp.where((lane >= to) & (lane < to + 32), moved, 0.0) + jnp.where(
                (lane >= to + 32) & (lane < to + K), tail, 0.0
            )

        for k in range(OWN):
            real = mode_rows(0, k, 0) + mode_rows(1, k, 64)
            imag = mode_rows(1, k, 0) - mode_rows(0, k, 64)
            for x in range(10):
                rows[e * 10 + x, k : k + 1, :] = real[x : x + 1]
                rows[e * 10 + x, OWN + k : OWN + k + 1, :] = imag[x : x + 1]
    lhs = rows[...].reshape(256, LANES).astype(BF16)
    wide = jnp.dot(lhs, inv_y[...], preferred_element_type=F32).reshape(32, 8, 384)
    near = []
    for low in range(8):
        group = [wide[high * 8 + low, :, c * LANES : (c + 1) * LANES] for high in range(4) for c in range(2)]
        near.append(jnp.stack(group))
    near = exchange(near, 16, 2)
    edge = []
    for low in range(16):
        edge.append(jnp.stack([wide[high * 16 + low, :, 256:384] for high in range(2)]))
    edge = exchange(edge, 8, 2)
    row = iota((8, LANES), 0)
    spectral = pltpu.roll(got[:, 8:16].sum(0), 6, 0)
    spectral = jnp.where((row < 3) & (lane < 64), spectral + pltpu.roll(spectral, 64, 1), 0.0)
    total = pre[...] + spectral
    high = total.astype(BF16).astype(F32)
    last = high + pltpu.roll(total - high, 64, 1)
    blocks = []
    for w in range(WIDE):
        tiles = [near[w % 8][high_x * 2 + w // 8] for high_x in range(4)]
        tiles += [edge[w][high_x] for high_x in range(2)] + [last]
        blocks.append(jnp.concatenate(tiles, 1))
    out[...] = jnp.concatenate(blocks, 0).astype(BF16)


def corner_kernel(electric, magnetic, inverse, saved, x_low, x_high, after, to_low, to_high):
    for c in range(7):
        own = electric.at[c] if c < 3 else (magnetic.at[c - 3] if c < 6 else inverse)
        for to, rows in ((to_low, slice(14, 16)), (to_high, slice(0, 2))):
            to[c * 12 : c * 12 + 8] = own[:, rows, :]
            to[c * 12 + 8 : c * 12 + 10] = x_high[c, :, rows, :]
            to[c * 12 + 10 : c * 12 + 12] = x_low[c, :, rows, :]
    for n in range(2):
        for i, c in enumerate((0, 2)):
            edge = saved[n, c].astype(F32)[:, RY - 1 : RY, :]
            to_low[84 + n * 8 : 92 + n * 8, i : i + 1, :] = edge


def first_kernel(
    mon, weights, electric, magnetic, inverse, saved, x_low, x_high, y_low, y_high, after,
    early, curled, factor, grad, ready, e_ext, h_ext, g_ext,
):
    b, w = own_block()
    lane = iota((1, NZ), 1)
    for c in range(7):
        to = e_ext.at[c] if c < 3 else (h_ext.at[c - 3] if c < 6 else g_ext)
        own = electric[c] if c < 3 else (magnetic[c - 3] if c < 6 else inverse[...])
        to[0:8, 0:16, :] = own
        to[8:10, 0:16, :] = x_high[c]
        to[10:12, 0:16, :] = x_low[c]
        low, high = y_low[c * 12 : (c + 1) * 12], y_high[c * 12 : (c + 1) * 12]
        to[:, 16:24, :] = jnp.concatenate([high, jnp.zeros((12, 4, NZ), F32), low], 1)

    g = g_ext[...]
    half = 0.5 * g
    a = [half * e_ext[c] for c in range(3)]
    spot_x = iota((12, 24, 1), 0)
    spot_y = iota((12, 24, 1), 1)
    outside = ((spot_x >= 10) & (b == 0)) | ((spot_y >= 22) & (w == 0))
    inside = jnp.where(outside, 0.0, 1.0)
    turned = curl_ahead(*a)
    h = [h_ext[c] + inside * turned[c] for c in range(3)]
    back = curl_behind(*h)
    for c in range(3):
        e_ext[c] = e_ext[c] - 0.5 * back[c]

    def hit(x, y, z):
        lx, ly = x - b * RX, y - w * RY
        return (lx >= -2) & (lx < RX + 2) & (ly >= -2) & (ly < RY + 2)

    def add(i, flat):
        x, y, z = place_of(flat)
        lx, ly = x - b * RX, y - w * RY
        px = jnp.where(lx < 0, lx + 12, lx)
        py = jnp.where(ly < 0, ly + 24, ly)
        for c in range(3):
            row = e_ext[c, px, pl.ds(py, 1), :]
            e_ext[c, px, pl.ds(py, 1), :] = row + jnp.where(lane == z, weights[c, 0, i], 0.0)

    scan(mon, hit, add)
    for c in range(3):
        early[c, 0:9] = e_ext[c, 0:9]
        early[c, 9:10] = e_ext[c, 11:12]
        curled[c, 0:9] = h[c][0:9]
        curled[c, 9:10] = h[c][11:12]
    factor[0:9] = half[0:9]
    factor[9:10] = half[11:12]

    near = inverse[...]
    for step in range(2):
        s = [saved[step, c].astype(F32) for c in range(3)]
        before_x = {c: jnp.concatenate([x_low[7 + step, c - 1 : c], s[c][:-1]], 0) for c in (1, 2)}
        at = 84 + step * 8
        before_y = {}
        for c in (0, 2):
            edge = y_low[at : at + 8, c // 2 : c // 2 + 1, :]
            first = iota((RX, RY, NZ), 1) == 0
            before_y[c] = jnp.where(first, edge, pltpu.roll(s[c], 1, 1))
        curls = (
            (s[2] - before_y[2]) - (s[1] - z_behind(s[1])),
            (s[0] - z_behind(s[0])) - (s[2] - before_x[2]),
            (s[1] - before_x[1]) - (s[0] - before_y[0]),
        )
        if step == 0:
            for c in range(3):
                ready[c] = near * curls[c]
        else:
            total = jnp.zeros((RX, RY, NZ), F32)
            for c in range(3):
                total = total + a[c][0:8, 0:16] * near * curls[c]
            grad[...] = -total


def second_kernel(
    lines, table, early, curled, factor, first_grad, ready, injected,
    grad_e, grad_h, grad_eps, sources,
):
    b, w = own_block()
    modes = lines[:, 0:768]
    back = lax.dot_general(
        modes, table[...], (((0,), (0,)), ((), ())), preferred_element_type=F32
    )
    main = back[0:512].reshape(32, 16, NZ)
    edge = back[512:768].reshape(32, 8, NZ)
    half = factor[...]
    e1 = []
    for c in range(3):
        at = slice(c * 10, c * 10 + 10)
        e1.append(early[c] + jnp.concatenate([main[at], edge[at]], 1))
    a = [half * e for e in e1]
    spot_x = iota((10, 24, 1), 0)
    spot_y = iota((10, 24, 1), 1)
    outside = ((spot_x == 9) & (b == 0)) | ((spot_y == 23) & (w == 0))
    inside = jnp.where(outside, 0.0, 1.0)
    turned = curl_ahead(*a)
    h = [curled[c] + inside * turned[c] for c in range(3)]
    backed = curl_behind(*h)
    total = first_grad[...]
    for c in range(3):
        grad_h[c] = h[c][0:8, 0:16]
        grad_e[c] = e1[c][0:8, 0:16] - 0.5 * backed[c][0:8, 0:16]
        total = total - a[c][0:8, 0:16] * ready[c]
    grad_eps[...] = total
    got = lines[:, 768:896].astype(F32).reshape(WIDE, 8, LANES).sum(0)
    got = got + pltpu.roll(got, 64, 1) + injected[...]
    for n in range(2):
        for c in range(3):
            sources[c, n : n + 1, :] = got[n * 3 + c : n * 3 + c + 1, 0:64]


def call(kernel, outs, places, scratch=(), flops=0, moved=0, params=PARAMS):
    spaces = {"s": pltpu.SMEM, "v": pltpu.VMEM, "a": pl.ANY}
    return pl.pallas_call(
        kernel,
        out_shape=outs,
        in_specs=[pl.BlockSpec(memory_space=spaces[p]) for p in places],
        out_specs=jax.tree.map(lambda _: pl.BlockSpec(memory_space=pltpu.VMEM), outs),
        scratch_shapes=list(scratch),
        compiler_params=params,
        cost_estimate=pl.CostEstimate(flops=flops, bytes_accessed=moved, transcendentals=0),
    )


def shape(*dims, dtype=F32):
    return jax.ShapeDtypeStruct(dims, dtype)


def passed_along(block, axis, distance):
    devices = range(lax.axis_size(axis))
    route = [(i - distance, i) for i in devices if i - distance in devices]
    return lax.ppermute(block, axis, route)


def passed_far(block, distance):
    route = [(i, (i + distance * NEAR) % BULK) for i in range(BULK)]
    return lax.ppermute(block, "bulk", route)


def dealt_near(block):
    groups = [[f * NEAR + n for n in range(NEAR)] for f in range(FAR)]
    return lax.all_to_all(
        block, "bulk", split_axis=0, concat_axis=0, axis_index_groups=groups, tiled=True
    )


def tables_of(name):
    return jnp.asarray(TABLES[name])


def body(
    seed_electric, seed_magnetic, saved_magnetic, material, permittivity, source_cells,
    monitor_cells, monitor_weights, lift_weight, project_weight, mode_mix, gain_first, gain_second,
):
    weights = monitor_weights.transpose(2, 0, 1)
    big, dma = pltpu.CompilerParams(vmem_limit_bytes=56 * 1024 * 1024), pltpu.SemaphoreType.DMA
    block = (RX, RY, NZ)

    payload, field = call(
        lift_kernel,
        (shape(384, LANES, dtype=BF16), shape(3, *block)),
        "aaaa",
        [
            pltpu.SMEM((64,), jnp.int32), pltpu.VMEM((3, 2, 64), F32),
            pltpu.VMEM((LANES, LANES), BF16), dma((4,)),
        ],
        13_000_000,
        500_000,
        big,
    )(monitor_cells, weights, seed_electric, tables_of("lift_z"))
    lines = lax.all_to_all(payload, "wide", split_axis=0, concat_axis=0, tiled=True)

    taken, inverse, to_low, to_high = call(
        share_kernel,
        (shape(8, LANES), shape(*block), shape(9, 2, RY, NZ), shape(7, 2, RY, NZ)),
        "aavaaa",
        [
            pltpu.SMEM((64,), jnp.int32), pltpu.SMEM((8,), F32), pltpu.VMEM((3, *block), F32),
            pltpu.VMEM(block, jnp.int32), pltpu.VMEM((2, 3, *block), BF16),
            pltpu.VMEM((3, 12, 32, NZ), F32), pltpu.VMEM((3, 12, 32, NZ), F32), dma((5,)),
        ],
        3_000_000,
        1_500_000,
        big,
    )(source_cells, permittivity, field, seed_magnetic, material, saved_magnetic)
    x_low = passed_along(to_low, "bulk", 1)
    x_high = passed_along(to_high, "bulk", -1)

    dealt = call(
        middle_kernel, shape(LANES, LANES, dtype=BF16), "vvv", (), 20_000_000, 400_000
    )(lines, taken, tables_of("fwd_y"))
    own = dealt_near(dealt)

    cells = jnp.concatenate([source_cells, source_cells]).reshape(1, LANES)
    coef_a, coef_b, phase_x, phase_yz, injected = call(
        param_kernel,
        (
            shape(216, LANES), shape(216, LANES), shape(LANES, LANES, dtype=BF16),
            shape(24, LANES), shape(8, LANES),
        ),
        "sssvvvvvvvva",
        (),
        20_000_000,
        1_000_000,
    )(
        monitor_cells, weights, lift_weight.T, cells, project_weight, gain_first, gain_second,
        mode_mix.transpose(0, 2, 3, 1), tables_of("at_x"), tables_of("at_y"), tables_of("at_z"),
        dealt,
    )

    far = [passed_far(own, t) for t in (1, 2, 3)]
    low_part, high_part = call(
        corner_kernel, (shape(100, 2, NZ), shape(84, 2, NZ)), "vvvvvva", (), 0, 1_000_000
    )(field, seed_magnetic, inverse, saved_magnetic, x_low, x_high, own)
    y_low = passed_along(low_part, "wide", 1)
    y_high = passed_along(high_part, "wide", -1)

    shares, pre = call(
        filter_kernel,
        (shape(LANES, LANES, dtype=BF16), shape(8, LANES)),
        "vvvvvvvvvva",
        (),
        40_000_000,
        600_000,
    )(
        own, *far, coef_a, coef_b, tables_of("fwd_x"), tables_of("inv_x"), phase_x, phase_yz,
        low_part,
    )
    back = dealt_near(shares)

    early, curled, factor, first_grad, ready = call(
        first_kernel,
        (
            shape(3, 10, 24, NZ), shape(3, 10, 24, NZ), shape(10, 24, NZ), shape(*block),
            shape(3, *block),
        ),
        "ssvvvvvvvva",
        [pltpu.VMEM((3, 12, 24, NZ), F32)] * 2 + [pltpu.VMEM((12, 24, NZ), F32)],
        10_000_000,
        3_000_000,
    )(
        monitor_cells, weights, field, seed_magnetic, inverse, saved_magnetic,
        x_low, x_high, y_low, y_high, shares,
    )

    sent = call(
        spread_kernel,
        shape(128, 896, dtype=BF16),
        "vvv",
        [pltpu.VMEM((32, 8, LANES), F32)],
        40_000_000,
        600_000,
    )(back, pre, tables_of("inv_y"))
    returned = lax.all_to_all(sent, "wide", split_axis=0, concat_axis=0, tiled=True)
    grad_e, grad_h, grad_eps, sources = call(
        second_kernel,
        (shape(3, *block), shape(3, *block), shape(*block), shape(3, 2, 64)),
        "vvvvvvvv",
        (),
        40_000_000,
        4_000_000,
    )(returned, tables_of("back_z"), early, curled, factor, first_grad, ready, injected)
    return grad_e, grad_h, grad_eps, sources.transpose(1, 2, 0)


def solution(mesh):
    field = P(None, "bulk", "wide", None)
    return jax.shard_map(
        body,
        mesh=mesh,
        in_specs=(
            field, field, P(None, None, "bulk", "wide", None), P("bulk", "wide", None),
            P(), P(), P(), P(), P(), P(), P(), P(), P(),
        ),
        out_specs=(field, field, P("bulk", "wide", None), P()),
        check_vma=False,
    )
```

```python
import functools
import math

import jax
import jax.numpy as jnp
import ml_dtypes
import numpy as np
from jax import lax
from jax.experimental import pallas as pl
from jax.experimental.pallas import tpu as pltpu
from jax.sharding import PartitionSpec as P

NX, NY, NZ = 256, 256, 128
K = 48
OWN = 3
WIDE, BULK = 16, 32
RX, RY = 8, 16
NEAR, FAR = 8, 4
SHARE = OWN * K // NEAR
LANES = 128
F32, BF16 = jnp.float32, jnp.bfloat16
PARAMS = pltpu.CompilerParams(vmem_limit_bytes=40 * 1024 * 1024)
HIGHEST = lax.Precision.HIGHEST


def waves(freqs, places, total):
    phase = np.mod(np.asarray(freqs)[:, None] * np.asarray(places)[None, :], total)
    angle = phase.astype(np.float32) * np.float32(2.0 * math.pi / total)
    return np.cos(angle).astype(np.float32), np.sin(angle).astype(np.float32)


def rounded(table):
    return np.asarray(table, np.float32).astype(ml_dtypes.bfloat16)


def make_tables():
    mode = np.arange(K)
    plane = np.where(mode < K // 2, mode, mode - K)
    cz, sz = waves(mode, np.arange(NZ), NZ)
    cx, sx = (rounded(t) for t in waves(plane, np.arange(NX), NX))
    cy, sy = (rounded(t) for t in waves(plane, np.arange(NY), NY))
    scale = np.float32(1.0 / math.sqrt(NX * NY * NZ))
    back = np.float32(1.0 / math.sqrt(K**3))
    fz, gz = rounded(cz * scale), rounded(-sz * scale)
    bz, hz = rounded(cz * back), rounded(sz * back)
    out = {}
    lift_z = np.zeros((LANES, LANES), ml_dtypes.bfloat16)
    back_z = np.zeros((LANES, LANES), ml_dtypes.bfloat16)
    for w in range(WIDE):
        for i in range(OWN):
            lift_z[:, w * 8 + i] = fz[w * OWN + i]
            lift_z[:, w * 8 + OWN + i] = gz[w * OWN + i]
            back_z[w * 8 + i] = bz[w * OWN + i]
            back_z[w * 8 + OWN + i] = -hz[w * OWN + i]
    out["lift_z"], out["back_z"] = lift_z, back_z

    lane = np.arange(LANES)
    y_of = np.concatenate([(h * 8 + lane % 8) * RY + lane // 8 for h in range(2)])
    fwd_y = np.zeros((512, 256), ml_dtypes.bfloat16)
    fwd_y[:256, :K] = cy[:, y_of].T
    fwd_y[256:, :K] = sy[:, y_of].T
    fwd_y[:256, 128 : 128 + K] = -sy[:, y_of].T
    fwd_y[256:, 128 : 128 + K] = cy[:, y_of].T
    out["fwd_y"] = fwd_y

    fwd_x = np.zeros((2 * LANES, NX), ml_dtypes.bfloat16)
    fwd_x[:K], fwd_x[64 : 64 + K] = cx, -sx
    fwd_x[128 : 128 + K], fwd_x[192 : 192 + K] = sx, cx
    inv_x = np.zeros((FAR, LANES, LANES), ml_dtypes.bfloat16)
    for far in range(FAR):
        for n in range(NEAR):
            start = (far * NEAR + n) * RX
            x_of = (start + np.array([0, 1, 2, 3, 4, 5, 6, 7, 8, -1])) % NX
            inv_x[far, n * 16 : n * 16 + 10, :K] = cx[:, x_of].T
            inv_x[far, n * 16 : n * 16 + 10, 64 : 64 + K] = -sx[:, x_of].T
    out["fwd_x"], out["inv_x"] = fwd_x, inv_x

    inv_y = np.zeros((LANES, 384), ml_dtypes.bfloat16)
    inv_y[:K, :256], inv_y[64 : 64 + K, :256] = cy, -sy
    for w in range(WIDE):
        for h, y in ((0, w * RY + RY), (7, w * RY - 1)):
            inv_y[:K, 256 + w * 8 + h] = cy[:, y % NY]
            inv_y[64 : 64 + K, 256 + w * 8 + h] = -sy[:, y % NY]
    out["inv_y"] = inv_y

    at_x = np.zeros((2, LANES, NX), ml_dtypes.bfloat16)
    at_x[0, :K], at_x[0, 64 : 64 + K] = cx, -sx
    at_x[1, :K], at_x[1, 64 : 64 + K] = sx, cx
    out["at_x"] = at_x
    at_y = np.zeros((NEAR, 2, 32, NY), ml_dtypes.bfloat16)
    for n in range(NEAR):
        j_of = np.arange(n * SHARE, (n + 1) * SHARE) % K
        at_y[n, 0, :SHARE], at_y[n, 1, :SHARE] = cy[j_of], sy[j_of]
    out["at_y"] = at_y
    at_z = np.zeros((WIDE, 2, 16, NZ), ml_dtypes.bfloat16)
    for w in range(WIDE):
        at_z[w, 0, :OWN] = bz[w * OWN : (w + 1) * OWN]
        at_z[w, 1, :OWN] = hz[w * OWN : (w + 1) * OWN]
    out["at_z"] = at_z
    return out


TABLES = make_tables()


def iota(shape, axis):
    return lax.broadcasted_iota(jnp.int32, shape, axis)


def exchange(tiles, block, axis):
    tiles = list(tiles)
    shape = tiles[0].shape
    size = shape[axis]
    place = iota(shape, axis) // block
    step = 1
    while step < len(tiles):
        high = (place // step) % 2 == 1
        new = list(tiles)
        for low in range(len(tiles)):
            if low & step:
                continue
            u, v = tiles[low], tiles[low + step]
            new[low] = jnp.where(high, pltpu.roll(v, step * block, axis), u)
            new[low + step] = jnp.where(high, v, pltpu.roll(u, size - step * block, axis))
        tiles = new
        step *= 2
    return tiles


def z_ahead(v):
    axis = v.ndim - 1
    return jnp.where(iota(v.shape, axis) < NZ - 1, pltpu.roll(v, NZ - 1, axis), 0.0)


def z_behind(v):
    axis = v.ndim - 1
    return jnp.where(iota(v.shape, axis) > 0, pltpu.roll(v, 1, axis), 0.0)


def x_ahead(v):
    return jnp.concatenate([v[1:], v[:1]], 0)


def x_behind(v):
    return jnp.concatenate([v[-1:], v[:-1]], 0)


def y_ahead(v):
    return pltpu.roll(v, v.shape[1] - 1, 1)


def y_behind(v):
    return pltpu.roll(v, 1, 1)


def curl_ahead(fx, fy, fz):
    return (
        (y_ahead(fz) - fz) - (z_ahead(fy) - fy),
        (z_ahead(fx) - fx) - (x_ahead(fz) - fz),
        (x_ahead(fy) - fy) - (y_ahead(fx) - fx),
    )


def curl_behind(fx, fy, fz):
    return (
        (fz - y_behind(fz)) - (fy - z_behind(fy)),
        (fx - z_behind(fx)) - (fz - x_behind(fz)),
        (fy - x_behind(fy)) - (fx - y_behind(fx)),
    )


def place_of(flat):
    return flat >> 15, (flat >> 7) & (NY - 1), flat & (NZ - 1)


def own_block():
    return lax.axis_index("bulk"), lax.axis_index("wide")


def fetch(pairs, sems):
    copies = [pltpu.make_async_copy(a, b, sems.at[i]) for i, (a, b) in enumerate(pairs)]
    for copy in copies:
        copy.start()
    return copies


def scan(cells, hit, act):
    def group(g, carry):
        found = [cells[g * 8 + i] for i in range(8)]
        hits = [hit(*place_of(f)) for f in found]
        some = functools.reduce(jnp.logical_or, hits)

        @pl.when(some)
        def _():
            for i in range(8):
                pl.when(hits[i])(functools.partial(act, g * 8 + i, found[i]))

        return carry

    lax.fori_loop(0, 8, group, 0)


def lift_kernel(mon_in, weights_in, electric, table_in, out, field, mon, weights, table, sems):
    b, w = own_block()
    copies = fetch(
        ((mon_in, mon), (electric, field), (weights_in, weights), (table_in, table)), sems
    )
    for copy in copies:
        copy.wait()
    lane = iota((1, NZ), 1)
    spot = iota((1, 64), 1)

    def hit(x, y, z):
        return ((x >> 3) == b) & ((y >> 4) == w)

    def add(i, flat):
        x, y, z = place_of(flat)
        lx, ly = x & (RX - 1), y & (RY - 1)
        for c in range(3):
            row = field[c, lx, pl.ds(ly, 1), :]
            given = jnp.where(spot == i, weights[c, 1:2, :], 0.0)
            weight = jnp.sum(given, axis=1, keepdims=True)
            field[c, lx, pl.ds(ly, 1), :] = row + jnp.where(lane == z, weight, 0.0)

    scan(mon, hit, add)
    rows = field[...].reshape(3 * RX * RY, NZ).astype(BF16)
    modes = jnp.dot(rows, table[...], preferred_element_type=F32)
    modes = modes.reshape(3, RX, 2, 8, LANES)
    tiles = exchange([modes[:, x].reshape(6, 8, LANES) for x in range(RX)], 1, 1)
    tiles = [t.reshape(3, 2, 8, LANES) for t in tiles]
    tiles = exchange([tiles[y % 8][:, y // 8] for y in range(RY)], 8, 2)
    out[...] = jnp.concatenate([t.reshape(24, LANES) for t in tiles], 0).astype(BF16)


def share_kernel(
    src_in, perm_in, field, magnetic_in, material_in,
    taken, inverse,
    src, perm, magnetic, material, scaled, held, sems,
):
    b, w = own_block()
    copies = fetch(
        (
            (src_in, src), (perm_in, perm), (magnetic_in, magnetic),
            (material_in, material),
        ),
        sems,
    )
    zero = jnp.zeros((12, 32, NZ), F32)
    for c in range(3):
        scaled[c] = zero
        held[c] = zero
    for copy in copies:
        copy.wait()
    eps = jnp.zeros((RX, RY, NZ), F32)
    cells = material[...]
    for level in range(8):
        eps = jnp.where(cells == level, perm[level], eps)
    inv = 1.0 / eps
    inverse[...] = inv
    lane = iota((1, NZ), 1)
    for c in range(3):
        scaled[c, 2:10, 8:24, :] = 0.5 * inv * field[c]
        held[c, 2:10, 8:24, :] = magnetic[c]
    taken[...] = jnp.zeros((8, LANES), F32)
    spot_row, spot_lane = iota((8, LANES), 0), iota((8, LANES), 1)

    def hit(x, y, z):
        lx, ly = x - b * RX, y - w * RY
        return (lx >= -1) & (lx <= RX) & (ly >= -1) & (ly <= RY)

    def take(i, flat):
        x, y, z = place_of(flat)
        lx, ly = x - b * RX, y - w * RY

        def a(c, dx, dy):
            return scaled[c, lx + 2 + dx, pl.ds(ly + 8 + dy, 1), :]

        def h(c, dx, dy):
            old = held[c, lx + 2 + dx, pl.ds(ly + 8 + dy, 1), :]
            if c == 0:
                near = a(1, dx, dy)
                turn = (a(2, dx, dy + 1) - a(2, dx, dy)) - (z_ahead(near) - near)
            elif c == 1:
                near = a(0, dx, dy)
                turn = (z_ahead(near) - near) - (a(2, dx + 1, dy) - a(2, dx, dy))
            else:
                turn = (a(1, dx + 1, dy) - a(1, dx, dy)) - (a(0, dx, dy + 1) - a(0, dx, dy))
            return old + turn

        left = jnp.where(x > 0, 1.0, 0.0)
        down = jnp.where(y > 0, 1.0, 0.0)
        hx, hy, hz = h(0, 0, 0), h(1, 0, 0), h(2, 0, 0)
        hx_y, hz_y = down * h(0, 0, -1), down * h(2, 0, -1)
        hy_x, hz_x = left * h(1, -1, 0), left * h(2, -1, 0)
        curls = (
            (hz - hz_y) - (hy - z_behind(hy)),
            (hx - z_behind(hx)) - (hz - hz_x),
            (hy - hy_x) - (hx - hx_y),
        )
        mine = jnp.where((lx >= 0) & (lx < RX) & (ly >= 0) & (ly < RY), 1.0, 0.0)
        cx, cy = jnp.clip(lx, 0, RX - 1), jnp.clip(ly, 0, RY - 1)
        got = taken[...]
        for c in range(3):
            old = mine * field[c, cx, pl.ds(cy, 1), :]
            for n, row in ((0, old - 0.5 * curls[c]), (1, old)):
                value = jnp.sum(jnp.where(lane == z, row, 0.0), axis=1, keepdims=True)
                spot = (spot_row == n * 3 + c) & (spot_lane == i)
                got = got + jnp.where(spot, value, 0.0)
        taken[...] = got

    scan(src, hit, take)


def middle_kernel(lines, taken, table, out):
    got = lines[...].astype(F32).reshape(WIDE, 24, LANES)
    halves = [exchange([got[h * 8 + i] for i in range(8)], 1, 1) for h in range(2)]
    rows = [
        jnp.concatenate([halves[0][k], halves[1][k], halves[0][OWN + k], halves[1][OWN + k]], 1)
        for k in range(OWN)
    ]
    lhs = jnp.concatenate(rows, 0).astype(BF16)
    found = jnp.dot(lhs, table[...], preferred_element_type=F32)
    lane = iota((8, LANES), 1)
    parts = [jnp.zeros((8, LANES), F32) for _ in range(NEAR)]
    for part in range(2):
        for d in range(3):
            piece = [
                found[(k * 3 + d) * 8 : (k * 3 + d) * 8 + 8, part * LANES : (part + 1) * LANES]
                for k in range(OWN)
            ]
            last = pltpu.roll(piece[2], 2 * K, 1)
            first = piece[0] + pltpu.roll(piece[1], K, 1) + jnp.where(lane >= 2 * K, last, 0.0)
            rest = jnp.where(lane < 16, last, 0.0)
            to = part * 64 + d * SHARE
            for n in range(NEAR):
                moved = pltpu.roll(first, (to - n * SHARE) % LANES, 1)
                if n == NEAR - 1:
                    moved = jnp.where(lane < to + 2, moved, pltpu.roll(rest, to + 2, 1))
                within = (lane >= to) & (lane < to + SHARE)
                parts[n] = parts[n] + jnp.where(within, moved, 0.0)
    src = jnp.concatenate([taken[...], jnp.zeros((LANES - 8, LANES), F32)], 0).T
    high = src.astype(BF16).astype(F32)
    extra = pltpu.roll(high, 54, 1) + pltpu.roll(src - high, 118, 1)
    out[...] = (jnp.concatenate(parts, 0) + extra[: NEAR * 8]).astype(BF16)


def param_kernel(
    mon, weights, lift, cells, project, gain_x, gain_y, mix, at_x, at_y, at_z, after,
    coef_a, coef_b, phase_x, phase_yz, injected,
):
    b, w = own_block()
    n = b % NEAR
    flat = cells[...]
    x, y, z = place_of(flat)
    first = iota((1, LANES), 1) < 64
    hot_x = jnp.where(iota((NX, LANES), 0) == x, 1.0, 0.0)
    real = jnp.where(first, hot_x, 0.0).astype(BF16)
    imag = jnp.where(first, 0.0, hot_x).astype(BF16)
    phase_x[...] = (
        jnp.dot(at_x[0], real, preferred_element_type=F32)
        + jnp.dot(at_x[1], imag, preferred_element_type=F32)
    ).astype(BF16)
    hot_y = jnp.where(iota((NY, LANES), 0) == y, 1.0, 0.0).astype(BF16)
    hot_z = jnp.where(iota((NZ, LANES), 0) == z, 1.0, 0.0).astype(BF16)
    cy = jnp.dot(at_y[n, 0], hot_y, preferred_element_type=F32)[:24]
    sy = jnp.dot(at_y[n, 1], hot_y, preferred_element_type=F32)[:24]
    cz = jnp.dot(at_z[w, 0], hot_z, preferred_element_type=F32)
    sz = jnp.dot(at_z[w, 1], hot_z, preferred_element_type=F32)
    mode = n * SHARE + iota((24, 1), 0)
    ck = jnp.where(mode < K, cz[0:1], jnp.where(mode < 2 * K, cz[1:2], cz[2:3]))
    sk = jnp.where(mode < K, sz[0:1], jnp.where(mode < 2 * K, sz[1:2], sz[2:3]))
    phase_yz[...] = jnp.where(first, cy * ck - sy * sk, -(sy * ck + cy * sk))

    place = iota((K, 24), 1)
    mode = n * SHARE + place
    depth = jnp.where(mode < K, 0, jnp.where(mode < 2 * K, 1, 2))
    live = place < SHARE
    hot_j = jnp.where((iota((K, 24), 0) == mode - depth * K) & live, 1.0, 0.0)
    hot_k = jnp.where((iota((K, 24), 0) == w * OWN + depth) & live, 1.0, 0.0)
    gains = jnp.dot(gain_y[...], hot_j, precision=HIGHEST, preferred_element_type=F32)
    diagonal = iota((16, 16), 0) == iota((16, 16), 1)
    columns = [
        jnp.sum(jnp.where(diagonal, project[e : e + 1, :], 0.0), axis=1, keepdims=True)
        for e in range(3)
    ]
    blank = jnp.zeros((16, 16), F32)
    along = gain_x[...]
    for part, to in ((0, coef_a), (1, coef_b)):
        joined = []
        for d in range(3):
            total = jnp.zeros((16, K), F32)
            for c in range(16):
                total = total + lift[d, c] * mix[part, c].astype(F32)
            joined.append(
                gains * jnp.dot(total, hot_k, precision=HIGHEST, preferred_element_type=F32)
            )
        sign = 1.0 if part == 0 else -1.0
        right = jnp.concatenate([sign * along, blank, along, blank], 1)
        for e in range(3):
            for d in range(3):
                left = (columns[e] * joined[d]).T
                to[(e * 3 + d) * 24 : (e * 3 + d + 1) * 24, :] = jnp.dot(
                    left, right, precision=HIGHEST, preferred_element_type=F32
                )
    row = iota((8, LANES), 0)
    total = jnp.zeros((8, LANES), F32)
    for i in range(64):
        given = jnp.where(
            row == 0, weights[0, 0, i], jnp.where(row == 1, weights[1, 0, i], weights[2, 0, i])
        )
        total = total + jnp.where((flat == mon[i]) & (row < 3), given, 0.0)
    injected[...] = jnp.where(iota((8, LANES), 1) < 64, total, 0.0)


def filter_kernel(
    gathered, coef_a, coef_b, fwd_x, inv_x, phase_x, phase_yz, out
):
    b, w = own_block()
    far = b // NEAR
    lane = iota((1, LANES), 1)
    got = gathered[...]
    both = jnp.dot(fwd_x[...], got, preferred_element_type=F32)
    total = got.astype(F32).reshape(BULK, 8, LANES).sum(0)
    total = total + pltpu.roll(total, 64, 1)
    total = jnp.where(lane < 6, pltpu.roll(total, LANES - 54, 1), 0.0)
    total = jnp.concatenate([total, jnp.zeros((LANES - 8, LANES), F32)], 0).T[:8]
    total = pltpu.roll(total, (b % NEAR) * 8, 1)
    full = (both[:LANES] + pltpu.roll(both[LANES:], 64, 1)).T
    field = [full[d * SHARE : d * SHARE + 24] for d in range(3)]
    turned = [pltpu.roll(f, 64, 1) for f in field]
    sign = jnp.where(lane < 64, 1.0, -1.0)
    real = []
    for e in range(3):
        q = jnp.zeros((24, LANES), F32)
        for d in range(3):
            at = (e * 3 + d) * 24
            q = q + coef_a[at : at + 24] * field[d] + coef_b[at : at + 24] * turned[d]
        real.append(q)
    near = jnp.dot(
        jnp.concatenate(real, 0).astype(BF16), phase_x[...], preferred_element_type=F32
    )
    gap = jnp.zeros((10, LANES), F32)
    packed = jnp.concatenate([q[:SHARE] for q in real] + [gap], 0)
    right = jnp.concatenate([packed, pltpu.roll(packed, 64, 1) * sign], 0).astype(BF16)
    back = lax.dot_general(
        inv_x[far], right, (((1,), (1,)), ((), ())), preferred_element_type=F32
    ).reshape(NEAR, 2, 8, LANES)
    row = iota((8, LANES), 0)
    for e in range(3):
        line = jnp.sum(near[e * 24 : (e + 1) * 24] * phase_yz[...], axis=0, keepdims=True)
        line = line + pltpu.roll(line, 64, 1)
        total = total + jnp.where((row == e) & (lane < 64), line, 0.0)
    high = total.astype(BF16).astype(F32)
    extra = pltpu.roll(high + pltpu.roll(total - high, 64, 1), 2, 0)
    tiles = []
    for n in range(NEAR):
        tiles += [back[n, 0], back[n, 1] + extra]
    out[...] = jnp.concatenate(tiles, 0).astype(BF16)


def spread_kernel(shares, inv_y, after, out, rows):
    lane = iota((1, LANES), 1)
    got = shares[...].astype(F32).reshape(NEAR, 16, LANES)
    rows[...] = jnp.zeros((32, 8, LANES), F32)
    for e in range(3):
        flat = []
        for part in range(2):
            start = part * 64 + e * SHARE
            first, rest = jnp.zeros((16, LANES), F32), None
            for n in range(NEAR):
                moved = pltpu.roll(got[n], (n * SHARE - start) % LANES, 1)
                within = (lane >= n * SHARE) & (lane < (n + 1) * SHARE)
                first = first + jnp.where(within, moved, 0.0)
                if n == NEAR - 1:
                    rest = jnp.where(lane < 16, moved, 0.0)
            flat.append((first, rest))

        def mode_rows(part, k, to):
            first, rest = flat[part]
            moved = pltpu.roll(first, (to - k * K) % LANES, 1)
            if k < 2:
                return jnp.where((lane >= to) & (lane < to + K), moved, 0.0)
            tail = pltpu.roll(rest, to + 32, 1)
            return jnp.where((lane >= to) & (lane < to + 32), moved, 0.0) + jnp.where(
                (lane >= to + 32) & (lane < to + K), tail, 0.0
            )

        for k in range(OWN):
            real = mode_rows(0, k, 0) + mode_rows(1, k, 64)
            imag = mode_rows(1, k, 0) - mode_rows(0, k, 64)
            for x in range(10):
                rows[e * 10 + x, k : k + 1, :] = real[x : x + 1]
                rows[e * 10 + x, OWN + k : OWN + k + 1, :] = imag[x : x + 1]
    lhs = rows[...].reshape(256, LANES).astype(BF16)
    wide = jnp.dot(lhs, inv_y[...], preferred_element_type=F32).reshape(32, 8, 384)
    near = []
    for low in range(8):
        group = [wide[high * 8 + low, :, c * LANES : (c + 1) * LANES] for high in range(4) for c in range(2)]
        near.append(jnp.stack(group))
    near = exchange(near, 16, 2)
    edge = []
    for low in range(16):
        edge.append(jnp.stack([wide[high * 16 + low, :, 256:384] for high in range(2)]))
    edge = exchange(edge, 8, 2)
    row = iota((8, LANES), 0)
    total = pltpu.roll(got[:, 8:16].sum(0), 6, 0)
    total = jnp.where((row < 6) & (lane < 64), total + pltpu.roll(total, 64, 1), 0.0)
    high = total.astype(BF16).astype(F32)
    last = high + pltpu.roll(total - high, 64, 1)
    blocks = []
    for w in range(WIDE):
        tiles = [near[w % 8][high_x * 2 + w // 8] for high_x in range(4)]
        tiles += [edge[w][high_x] for high_x in range(2)] + [last]
        blocks.append(jnp.concatenate(tiles, 1))
    out[...] = jnp.concatenate(blocks, 0).astype(BF16)


def edge_kernel(electric, magnetic, inverse, saved, after, to_low, to_high):
    for c in range(3):
        to_low[c], to_high[c] = electric[c, 6:8], electric[c, 0:2]
        to_low[3 + c], to_high[3 + c] = magnetic[c, 6:8], magnetic[c, 0:2]
    to_low[6], to_high[6] = inverse[6:8], inverse[0:2]
    for n in range(2):
        for c in range(2):
            to_low[7 + n, c] = saved[n, 1 + c, 7].astype(F32)


def corner_kernel(electric, magnetic, inverse, saved, x_low, x_high, after, to_low, to_high):
    for c in range(7):
        own = electric.at[c] if c < 3 else (magnetic.at[c - 3] if c < 6 else inverse)
        for to, rows in ((to_low, slice(14, 16)), (to_high, slice(0, 2))):
            to[c * 12 : c * 12 + 8] = own[:, rows, :]
            to[c * 12 + 8 : c * 12 + 10] = x_high[c, :, rows, :]
            to[c * 12 + 10 : c * 12 + 12] = x_low[c, :, rows, :]
    for n in range(2):
        for i, c in enumerate((0, 2)):
            edge = saved[n, c].astype(F32)[:, RY - 1 : RY, :]
            to_low[84 + n * 8 : 92 + n * 8, i : i + 1, :] = edge


def first_kernel(
    mon, weights, electric, magnetic, inverse, saved, x_low, x_high, y_low, y_high, after,
    early, curled, factor, grad, ready, e_ext, h_ext, g_ext,
):
    b, w = own_block()
    lane = iota((1, NZ), 1)
    for c in range(7):
        to = e_ext.at[c] if c < 3 else (h_ext.at[c - 3] if c < 6 else g_ext)
        own = electric[c] if c < 3 else (magnetic[c - 3] if c < 6 else inverse[...])
        to[0:8, 0:16, :] = own
        to[8:10, 0:16, :] = x_high[c]
        to[10:12, 0:16, :] = x_low[c]
        low, high = y_low[c * 12 : (c + 1) * 12], y_high[c * 12 : (c + 1) * 12]
        to[:, 16:24, :] = jnp.concatenate([high, jnp.zeros((12, 4, NZ), F32), low], 1)

    g = g_ext[...]
    half = 0.5 * g
    a = [half * e_ext[c] for c in range(3)]
    spot_x = iota((12, 24, 1), 0)
    spot_y = iota((12, 24, 1), 1)
    outside = ((spot_x >= 10) & (b == 0)) | ((spot_y >= 22) & (w == 0))
    inside = jnp.where(outside, 0.0, 1.0)
    turned = curl_ahead(*a)
    h = [h_ext[c] + inside * turned[c] for c in range(3)]
    back = curl_behind(*h)
    for c in range(3):
        e_ext[c] = e_ext[c] - 0.5 * back[c]

    def hit(x, y, z):
        lx, ly = x - b * RX, y - w * RY
        return (lx >= -2) & (lx < RX + 2) & (ly >= -2) & (ly < RY + 2)

    def add(i, flat):
        x, y, z = place_of(flat)
        lx, ly = x - b * RX, y - w * RY
        px = jnp.where(lx < 0, lx + 12, lx)
        py = jnp.where(ly < 0, ly + 24, ly)
        for c in range(3):
            row = e_ext[c, px, pl.ds(py, 1), :]
            e_ext[c, px, pl.ds(py, 1), :] = row + jnp.where(lane == z, weights[c, 0, i], 0.0)

    scan(mon, hit, add)
    for c in range(3):
        early[c, 0:9] = e_ext[c, 0:9]
        early[c, 9:10] = e_ext[c, 11:12]
        curled[c, 0:9] = h[c][0:9]
        curled[c, 9:10] = h[c][11:12]
    factor[0:9] = half[0:9]
    factor[9:10] = half[11:12]

    near = inverse[...]
    for step in range(2):
        s = [saved[step, c].astype(F32) for c in range(3)]
        before_x = {c: jnp.concatenate([x_low[7 + step, c - 1 : c], s[c][:-1]], 0) for c in (1, 2)}
        at = 84 + step * 8
        before_y = {}
        for c in (0, 2):
            edge = y_low[at : at + 8, c // 2 : c // 2 + 1, :]
            first = iota((RX, RY, NZ), 1) == 0
            before_y[c] = jnp.where(first, edge, pltpu.roll(s[c], 1, 1))
        curls = (
            (s[2] - before_y[2]) - (s[1] - z_behind(s[1])),
            (s[0] - z_behind(s[0])) - (s[2] - before_x[2]),
            (s[1] - before_x[1]) - (s[0] - before_y[0]),
        )
        if step == 0:
            for c in range(3):
                ready[c] = near * curls[c]
        else:
            total = jnp.zeros((RX, RY, NZ), F32)
            for c in range(3):
                total = total + a[c][0:8, 0:16] * near * curls[c]
            grad[...] = -total


def second_kernel(
    lines, table, early, curled, factor, first_grad, ready, injected,
    grad_e, grad_h, grad_eps, sources,
):
    b, w = own_block()
    modes = lines[:, 0:768]
    back = lax.dot_general(
        modes, table[...], (((0,), (0,)), ((), ())), preferred_element_type=F32
    )
    main = back[0:512].reshape(32, 16, NZ)
    edge = back[512:768].reshape(32, 8, NZ)
    half = factor[...]
    e1 = []
    for c in range(3):
        at = slice(c * 10, c * 10 + 10)
        e1.append(early[c] + jnp.concatenate([main[at], edge[at]], 1))
    a = [half * e for e in e1]
    spot_x = iota((10, 24, 1), 0)
    spot_y = iota((10, 24, 1), 1)
    outside = ((spot_x == 9) & (b == 0)) | ((spot_y == 23) & (w == 0))
    inside = jnp.where(outside, 0.0, 1.0)
    turned = curl_ahead(*a)
    h = [curled[c] + inside * turned[c] for c in range(3)]
    backed = curl_behind(*h)
    total = first_grad[...]
    for c in range(3):
        grad_h[c] = h[c][0:8, 0:16]
        grad_e[c] = e1[c][0:8, 0:16] - 0.5 * backed[c][0:8, 0:16]
        total = total - a[c][0:8, 0:16] * ready[c]
    grad_eps[...] = total
    got = lines[:, 768:896].astype(F32).reshape(WIDE, 8, LANES).sum(0)
    got = got + pltpu.roll(got, 64, 1) + injected[...]
    for n in range(2):
        for c in range(3):
            sources[c, n : n + 1, :] = got[n * 3 + c : n * 3 + c + 1, 0:64]


def call(kernel, outs, places, scratch=(), flops=0, moved=0, params=PARAMS):
    spaces = {"s": pltpu.SMEM, "v": pltpu.VMEM, "a": pl.ANY}
    return pl.pallas_call(
        kernel,
        out_shape=outs,
        in_specs=[pl.BlockSpec(memory_space=spaces[p]) for p in places],
        out_specs=jax.tree.map(lambda _: pl.BlockSpec(memory_space=pltpu.VMEM), outs),
        scratch_shapes=list(scratch),
        compiler_params=params,
        cost_estimate=pl.CostEstimate(flops=flops, bytes_accessed=moved, transcendentals=0),
    )


def shape(*dims, dtype=F32):
    return jax.ShapeDtypeStruct(dims, dtype)


def passed_along(block, axis, distance):
    devices = range(lax.axis_size(axis))
    route = [(i - distance, i) for i in devices if i - distance in devices]
    return lax.ppermute(block, axis, route)


def joined_far(block):
    groups = [[f * NEAR + n for f in range(FAR)] for n in range(NEAR)]
    copies = jnp.concatenate([block] * FAR, 0)
    return lax.all_to_all(
        copies, "bulk", split_axis=0, concat_axis=0, axis_index_groups=groups, tiled=True
    )


def dealt_near(block):
    groups = [[f * NEAR + n for n in range(NEAR)] for f in range(FAR)]
    return lax.all_to_all(
        block, "bulk", split_axis=0, concat_axis=0, axis_index_groups=groups, tiled=True
    )


def tables_of(name):
    return jnp.asarray(TABLES[name])


def body(
    seed_electric, seed_magnetic, saved_magnetic, material, permittivity, source_cells,
    monitor_cells, monitor_weights, lift_weight, project_weight, mode_mix, gain_first, gain_second,
):
    weights = monitor_weights.transpose(2, 0, 1)
    big, dma = pltpu.CompilerParams(vmem_limit_bytes=56 * 1024 * 1024), pltpu.SemaphoreType.DMA
    block = (RX, RY, NZ)

    payload, field = call(
        lift_kernel,
        (shape(384, LANES, dtype=BF16), shape(3, *block)),
        "aaaa",
        [
            pltpu.SMEM((64,), jnp.int32), pltpu.VMEM((3, 2, 64), F32),
            pltpu.VMEM((LANES, LANES), BF16), dma((4,)),
        ],
        13_000_000,
        500_000,
        big,
    )(monitor_cells, weights, seed_electric, tables_of("lift_z"))
    lines = lax.all_to_all(payload, "wide", split_axis=0, concat_axis=0, tiled=True)

    taken, inverse = call(
        share_kernel,
        (shape(8, LANES), shape(*block)),
        "aavaa",
        [
            pltpu.SMEM((64,), jnp.int32), pltpu.SMEM((8,), F32), pltpu.VMEM((3, *block), F32),
            pltpu.VMEM(block, jnp.int32), pltpu.VMEM((3, 12, 32, NZ), F32),
            pltpu.VMEM((3, 12, 32, NZ), F32), dma((4,)),
        ],
        3_000_000,
        1_500_000,
    )(source_cells, permittivity, field, seed_magnetic, material)

    dealt = call(
        middle_kernel, shape(NEAR * 8, LANES, dtype=BF16), "vvv", (), 20_000_000, 400_000
    )(lines, taken, tables_of("fwd_y"))
    own = dealt_near(dealt)

    cells = jnp.concatenate([source_cells, source_cells]).reshape(1, LANES)
    coef_a, coef_b, phase_x, phase_yz, injected = call(
        param_kernel,
        (
            shape(216, LANES), shape(216, LANES), shape(LANES, LANES, dtype=BF16),
            shape(24, LANES), shape(8, LANES),
        ),
        "sssvvvvvvvva",
        (),
        20_000_000,
        1_000_000,
    )(
        monitor_cells, weights, lift_weight.T, cells, project_weight, gain_first, gain_second,
        mode_mix.transpose(0, 2, 3, 1), tables_of("at_x"), tables_of("at_y"), tables_of("at_z"),
        dealt,
    )

    gathered = joined_far(own)
    to_low, to_high = call(
        edge_kernel, (shape(9, 2, RY, NZ), shape(7, 2, RY, NZ)), "vvvva", (), 0, 500_000
    )(field, seed_magnetic, inverse, saved_magnetic, own)
    x_low = passed_along(to_low, "bulk", 1)
    x_high = passed_along(to_high, "bulk", -1)

    shares = call(
        filter_kernel, shape(LANES, LANES, dtype=BF16), "vvvvvvv", (), 40_000_000, 600_000
    )(gathered, coef_a, coef_b, tables_of("fwd_x"), tables_of("inv_x"), phase_x, phase_yz)
    back = dealt_near(shares)

    low_part, high_part = call(
        corner_kernel, (shape(100, 2, NZ), shape(84, 2, NZ)), "vvvvvva", (), 0, 1_000_000
    )(field, seed_magnetic, inverse, saved_magnetic, x_low, x_high, shares)
    y_low = passed_along(low_part, "wide", 1)
    y_high = passed_along(high_part, "wide", -1)

    early, curled, factor, first_grad, ready = call(
        first_kernel,
        (
            shape(3, 10, 24, NZ), shape(3, 10, 24, NZ), shape(10, 24, NZ), shape(*block),
            shape(3, *block),
        ),
        "ssvvvvvvvva",
        [pltpu.VMEM((3, 12, 24, NZ), F32)] * 2 + [pltpu.VMEM((12, 24, NZ), F32)],
        10_000_000,
        3_000_000,
    )(
        monitor_cells, weights, field, seed_magnetic, inverse, saved_magnetic,
        x_low, x_high, y_low, y_high, shares,
    )

    sent = call(
        spread_kernel,
        shape(128, 896, dtype=BF16),
        "vva",
        [pltpu.VMEM((32, 8, LANES), F32)],
        40_000_000,
        600_000,
    )(back, tables_of("inv_y"), factor)
    returned = lax.all_to_all(sent, "wide", split_axis=0, concat_axis=0, tiled=True)
    grad_e, grad_h, grad_eps, sources = call(
        second_kernel,
        (shape(3, *block), shape(3, *block), shape(*block), shape(3, 2, 64)),
        "vvvvvvvv",
        (),
        40_000_000,
        4_000_000,
    )(returned, tables_of("back_z"), early, curled, factor, first_grad, ready, injected)
    return grad_e, grad_h, grad_eps, sources.transpose(1, 2, 0)


def solution(mesh):
    field = P(None, "bulk", "wide", None)
    return jax.shard_map(
        body,
        mesh=mesh,
        in_specs=(
            field, field, P(None, None, "bulk", "wide", None), P("bulk", "wide", None),
            P(), P(), P(), P(), P(), P(), P(), P(), P(),
        ),
        out_specs=(field, field, P("bulk", "wide", None), P()),
        check_vma=False,
    )
```

```python
import functools
import math

import jax
import jax.numpy as jnp
import ml_dtypes
import numpy as np
from jax import lax
from jax.experimental import pallas as pl
from jax.experimental.pallas import tpu as pltpu
from jax.sharding import PartitionSpec as P

NX, NY, NZ = 256, 256, 128
K = 48
OWN = 3
WIDE, BULK = 16, 32
RX, RY = 8, 16
NEAR, FAR = 8, 4
SHARE = OWN * K // NEAR
LANES = 128
F32, BF16 = jnp.float32, jnp.bfloat16
PARAMS = pltpu.CompilerParams(vmem_limit_bytes=40 * 1024 * 1024)
HIGHEST = lax.Precision.HIGHEST


def waves(freqs, places, total):
    phase = np.mod(np.asarray(freqs)[:, None] * np.asarray(places)[None, :], total)
    angle = phase.astype(np.float32) * np.float32(2.0 * math.pi / total)
    return np.cos(angle).astype(np.float32), np.sin(angle).astype(np.float32)


def rounded(table):
    return np.asarray(table, np.float32).astype(ml_dtypes.bfloat16)


def make_tables():
    mode = np.arange(K)
    plane = np.where(mode < K // 2, mode, mode - K)
    cz, sz = waves(mode, np.arange(NZ), NZ)
    cx, sx = (rounded(t) for t in waves(plane, np.arange(NX), NX))
    cy, sy = (rounded(t) for t in waves(plane, np.arange(NY), NY))
    scale = np.float32(1.0 / math.sqrt(NX * NY * NZ))
    back = np.float32(1.0 / math.sqrt(K**3))
    fz, gz = rounded(cz * scale), rounded(-sz * scale)
    bz, hz = rounded(cz * back), rounded(sz * back)
    out = {}
    lift_z = np.zeros((LANES, LANES), ml_dtypes.bfloat16)
    back_z = np.zeros((LANES, LANES), ml_dtypes.bfloat16)
    for w in range(WIDE):
        for i in range(OWN):
            lift_z[:, w * 8 + i] = fz[w * OWN + i]
            lift_z[:, w * 8 + OWN + i] = gz[w * OWN + i]
            back_z[w * 8 + i] = bz[w * OWN + i]
            back_z[w * 8 + OWN + i] = -hz[w * OWN + i]
    out["lift_z"], out["back_z"] = lift_z, back_z

    lane = np.arange(LANES)
    y_of = np.concatenate([(h * 8 + lane % 8) * RY + lane // 8 for h in range(2)])
    fwd_y = np.zeros((512, 256), ml_dtypes.bfloat16)
    fwd_y[:256, :K] = cy[:, y_of].T
    fwd_y[256:, :K] = sy[:, y_of].T
    fwd_y[:256, 128 : 128 + K] = -sy[:, y_of].T
    fwd_y[256:, 128 : 128 + K] = cy[:, y_of].T
    out["fwd_y"] = fwd_y

    fwd_x = np.zeros((2 * LANES, NX), ml_dtypes.bfloat16)
    fwd_x[:K], fwd_x[64 : 64 + K] = cx, -sx
    fwd_x[128 : 128 + K], fwd_x[192 : 192 + K] = sx, cx
    inv_x = np.zeros((FAR, LANES, LANES), ml_dtypes.bfloat16)
    for far in range(FAR):
        for n in range(NEAR):
            start = (far * NEAR + n) * RX
            x_of = (start + np.array([0, 1, 2, 3, 4, 5, 6, 7, 8, -1])) % NX
            inv_x[far, n * 16 : n * 16 + 10, :K] = cx[:, x_of].T
            inv_x[far, n * 16 : n * 16 + 10, 64 : 64 + K] = -sx[:, x_of].T
    out["fwd_x"], out["inv_x"] = fwd_x, inv_x

    inv_y = np.zeros((LANES, 384), ml_dtypes.bfloat16)
    inv_y[:K, :256], inv_y[64 : 64 + K, :256] = cy, -sy
    for w in range(WIDE):
        for h, y in ((0, w * RY + RY), (7, w * RY - 1)):
            inv_y[:K, 256 + w * 8 + h] = cy[:, y % NY]
            inv_y[64 : 64 + K, 256 + w * 8 + h] = -sy[:, y % NY]
    out["inv_y"] = inv_y

    at_x = np.zeros((2, LANES, NX), ml_dtypes.bfloat16)
    at_x[0, :K], at_x[0, 64 : 64 + K] = cx, -sx
    at_x[1, :K], at_x[1, 64 : 64 + K] = sx, cx
    out["at_x"] = at_x
    at_y = np.zeros((NEAR, 2, 32, NY), ml_dtypes.bfloat16)
    for n in range(NEAR):
        j_of = np.arange(n * SHARE, (n + 1) * SHARE) % K
        at_y[n, 0, :SHARE], at_y[n, 1, :SHARE] = cy[j_of], sy[j_of]
    out["at_y"] = at_y
    at_z = np.zeros((WIDE, 2, 16, NZ), ml_dtypes.bfloat16)
    for w in range(WIDE):
        at_z[w, 0, :OWN] = bz[w * OWN : (w + 1) * OWN]
        at_z[w, 1, :OWN] = hz[w * OWN : (w + 1) * OWN]
    out["at_z"] = at_z
    return out


TABLES = make_tables()


def iota(shape, axis):
    return lax.broadcasted_iota(jnp.int32, shape, axis)


def exchange(tiles, block, axis):
    tiles = list(tiles)
    shape = tiles[0].shape
    size = shape[axis]
    place = iota(shape, axis) // block
    step = 1
    while step < len(tiles):
        high = (place // step) % 2 == 1
        new = list(tiles)
        for low in range(len(tiles)):
            if low & step:
                continue
            u, v = tiles[low], tiles[low + step]
            new[low] = jnp.where(high, pltpu.roll(v, step * block, axis), u)
            new[low + step] = jnp.where(high, v, pltpu.roll(u, size - step * block, axis))
        tiles = new
        step *= 2
    return tiles


def z_ahead(v):
    axis = v.ndim - 1
    return jnp.where(iota(v.shape, axis) < NZ - 1, pltpu.roll(v, NZ - 1, axis), 0.0)


def z_behind(v):
    axis = v.ndim - 1
    return jnp.where(iota(v.shape, axis) > 0, pltpu.roll(v, 1, axis), 0.0)


def x_ahead(v):
    return jnp.concatenate([v[1:], v[:1]], 0)


def x_behind(v):
    return jnp.concatenate([v[-1:], v[:-1]], 0)


def y_ahead(v):
    return pltpu.roll(v, v.shape[1] - 1, 1)


def y_behind(v):
    return pltpu.roll(v, 1, 1)


def curl_ahead(fx, fy, fz):
    return (
        (y_ahead(fz) - fz) - (z_ahead(fy) - fy),
        (z_ahead(fx) - fx) - (x_ahead(fz) - fz),
        (x_ahead(fy) - fy) - (y_ahead(fx) - fx),
    )


def curl_behind(fx, fy, fz):
    return (
        (fz - y_behind(fz)) - (fy - z_behind(fy)),
        (fx - z_behind(fx)) - (fz - x_behind(fz)),
        (fy - x_behind(fy)) - (fx - y_behind(fx)),
    )


def place_of(flat):
    return flat >> 15, (flat >> 7) & (NY - 1), flat & (NZ - 1)


def own_block():
    return lax.axis_index("bulk"), lax.axis_index("wide")


def fetch(pairs, sems):
    copies = [pltpu.make_async_copy(a, b, sems.at[i]) for i, (a, b) in enumerate(pairs)]
    for copy in copies:
        copy.start()
    return copies


def scan(cells, hit, act):
    def group(g, carry):
        found = [cells[g * 8 + i] for i in range(8)]
        hits = [hit(*place_of(f)) for f in found]
        some = functools.reduce(jnp.logical_or, hits)

        @pl.when(some)
        def _():
            for i in range(8):
                pl.when(hits[i])(functools.partial(act, g * 8 + i, found[i]))

        return carry

    lax.fori_loop(0, 8, group, 0)


def lift_kernel(mon_in, weights_in, electric, table_in, out, field, mon, weights, table, sems):
    b, w = own_block()
    copies = fetch(
        ((mon_in, mon), (electric, field), (weights_in, weights), (table_in, table)), sems
    )
    for copy in copies:
        copy.wait()
    lane = iota((1, NZ), 1)
    spot = iota((1, 64), 1)

    def hit(x, y, z):
        return ((x >> 3) == b) & ((y >> 4) == w)

    def add(i, flat):
        x, y, z = place_of(flat)
        lx, ly = x & (RX - 1), y & (RY - 1)
        for c in range(3):
            row = field[c, lx, pl.ds(ly, 1), :]
            given = jnp.where(spot == i, weights[c, 1:2, :], 0.0)
            weight = jnp.sum(given, axis=1, keepdims=True)
            field[c, lx, pl.ds(ly, 1), :] = row + jnp.where(lane == z, weight, 0.0)

    scan(mon, hit, add)
    rows = field[...].reshape(3 * RX * RY, NZ).astype(BF16)
    modes = jnp.dot(rows, table[...], preferred_element_type=F32)
    modes = modes.reshape(3, RX, 2, 8, LANES)
    tiles = exchange([modes[:, x].reshape(6, 8, LANES) for x in range(RX)], 1, 1)
    tiles = [t.reshape(3, 2, 8, LANES) for t in tiles]
    tiles = exchange([tiles[y % 8][:, y // 8] for y in range(RY)], 8, 2)
    out[...] = jnp.concatenate([t.reshape(24, LANES) for t in tiles], 0).astype(BF16)


def share_kernel(
    src_in, perm_in, field, magnetic_in, material_in,
    taken, inverse,
    src, perm, magnetic, material, scaled, held, sems,
):
    b, w = own_block()
    copies = fetch(
        (
            (src_in, src), (perm_in, perm), (magnetic_in, magnetic),
            (material_in, material),
        ),
        sems,
    )
    zero = jnp.zeros((12, 32, NZ), F32)
    for c in range(3):
        scaled[c] = zero
        held[c] = zero
    for copy in copies:
        copy.wait()
    eps = jnp.zeros((RX, RY, NZ), F32)
    cells = material[...]
    for level in range(8):
        eps = jnp.where(cells == level, perm[level], eps)
    inv = 1.0 / eps
    inverse[...] = inv
    lane = iota((1, NZ), 1)
    for c in range(3):
        scaled[c, 2:10, 8:24, :] = 0.5 * inv * field[c]
        held[c, 2:10, 8:24, :] = magnetic[c]
    taken[...] = jnp.zeros((8, LANES), F32)
    spot_row, spot_lane = iota((8, LANES), 0), iota((8, LANES), 1)

    def hit(x, y, z):
        lx, ly = x - b * RX, y - w * RY
        return (lx >= -1) & (lx <= RX) & (ly >= -1) & (ly <= RY)

    def take(i, flat):
        x, y, z = place_of(flat)
        lx, ly = x - b * RX, y - w * RY

        def a(c, dx, dy):
            return scaled[c, lx + 2 + dx, pl.ds(ly + 8 + dy, 1), :]

        def h(c, dx, dy):
            old = held[c, lx + 2 + dx, pl.ds(ly + 8 + dy, 1), :]
            if c == 0:
                near = a(1, dx, dy)
                turn = (a(2, dx, dy + 1) - a(2, dx, dy)) - (z_ahead(near) - near)
            elif c == 1:
                near = a(0, dx, dy)
                turn = (z_ahead(near) - near) - (a(2, dx + 1, dy) - a(2, dx, dy))
            else:
                turn = (a(1, dx + 1, dy) - a(1, dx, dy)) - (a(0, dx, dy + 1) - a(0, dx, dy))
            return old + turn

        left = jnp.where(x > 0, 1.0, 0.0)
        down = jnp.where(y > 0, 1.0, 0.0)
        hx, hy, hz = h(0, 0, 0), h(1, 0, 0), h(2, 0, 0)
        hx_y, hz_y = down * h(0, 0, -1), down * h(2, 0, -1)
        hy_x, hz_x = left * h(1, -1, 0), left * h(2, -1, 0)
        curls = (
            (hz - hz_y) - (hy - z_behind(hy)),
            (hx - z_behind(hx)) - (hz - hz_x),
            (hy - hy_x) - (hx - hx_y),
        )
        mine = jnp.where((lx >= 0) & (lx < RX) & (ly >= 0) & (ly < RY), 1.0, 0.0)
        cx, cy = jnp.clip(lx, 0, RX - 1), jnp.clip(ly, 0, RY - 1)
        got = taken[...]
        for c in range(3):
            old = mine * field[c, cx, pl.ds(cy, 1), :]
            for n, row in ((0, old - 0.5 * curls[c]), (1, old)):
                value = jnp.sum(jnp.where(lane == z, row, 0.0), axis=1, keepdims=True)
                spot = (spot_row == n * 3 + c) & (spot_lane == i)
                got = got + jnp.where(spot, value, 0.0)
        taken[...] = got

    scan(src, hit, take)


def middle_kernel(lines, taken, table, out):
    got = lines[...].astype(F32).reshape(WIDE, 24, LANES)
    halves = [exchange([got[h * 8 + i] for i in range(8)], 1, 1) for h in range(2)]
    rows = [
        jnp.concatenate([halves[0][k], halves[1][k], halves[0][OWN + k], halves[1][OWN + k]], 1)
        for k in range(OWN)
    ]
    lhs = jnp.concatenate(rows, 0).astype(BF16)
    found = jnp.dot(lhs, table[...], preferred_element_type=F32)
    lane = iota((8, LANES), 1)
    parts = [jnp.zeros((8, LANES), F32) for _ in range(NEAR)]
    for part in range(2):
        for d in range(3):
            piece = [
                found[(k * 3 + d) * 8 : (k * 3 + d) * 8 + 8, part * LANES : (part + 1) * LANES]
                for k in range(OWN)
            ]
            last = pltpu.roll(piece[2], 2 * K, 1)
            first = piece[0] + pltpu.roll(piece[1], K, 1) + jnp.where(lane >= 2 * K, last, 0.0)
            rest = jnp.where(lane < 16, last, 0.0)
            to = part * 64 + d * SHARE
            for n in range(NEAR):
                moved = pltpu.roll(first, (to - n * SHARE) % LANES, 1)
                if n == NEAR - 1:
                    moved = jnp.where(lane < to + 2, moved, pltpu.roll(rest, to + 2, 1))
                within = (lane >= to) & (lane < to + SHARE)
                parts[n] = parts[n] + jnp.where(within, moved, 0.0)
    src = jnp.concatenate([taken[...], jnp.zeros((LANES - 8, LANES), F32)], 0).T
    high = src.astype(BF16).astype(F32)
    extra = pltpu.roll(high, 54, 1) + pltpu.roll(src - high, 118, 1)
    deal = (jnp.concatenate(parts, 0) + extra[: NEAR * 8]).astype(BF16)
    for f in range(FAR):
        out[f * NEAR * 8 : (f + 1) * NEAR * 8, :] = deal


def param_kernel(
    mon, weights, lift, cells, project, gain_x, gain_y, mix, at_x, at_y, at_z, after,
    coef_a, coef_b, phase_x, phase_yz, injected,
):
    b, w = own_block()
    n = b % NEAR
    flat = cells[...]
    x, y, z = place_of(flat)
    first = iota((1, LANES), 1) < 64
    hot_x = jnp.where(iota((NX, LANES), 0) == x, 1.0, 0.0)
    real = jnp.where(first, hot_x, 0.0).astype(BF16)
    imag = jnp.where(first, 0.0, hot_x).astype(BF16)
    phase_x[...] = (
        jnp.dot(at_x[0], real, preferred_element_type=F32)
        + jnp.dot(at_x[1], imag, preferred_element_type=F32)
    ).astype(BF16)
    hot_y = jnp.where(iota((NY, LANES), 0) == y, 1.0, 0.0).astype(BF16)
    hot_z = jnp.where(iota((NZ, LANES), 0) == z, 1.0, 0.0).astype(BF16)
    cy = jnp.dot(at_y[n, 0], hot_y, preferred_element_type=F32)[:24]
    sy = jnp.dot(at_y[n, 1], hot_y, preferred_element_type=F32)[:24]
    cz = jnp.dot(at_z[w, 0], hot_z, preferred_element_type=F32)
    sz = jnp.dot(at_z[w, 1], hot_z, preferred_element_type=F32)
    mode = n * SHARE + iota((24, 1), 0)
    ck = jnp.where(mode < K, cz[0:1], jnp.where(mode < 2 * K, cz[1:2], cz[2:3]))
    sk = jnp.where(mode < K, sz[0:1], jnp.where(mode < 2 * K, sz[1:2], sz[2:3]))
    phase_yz[...] = jnp.where(first, cy * ck - sy * sk, -(sy * ck + cy * sk))

    place = iota((K, 24), 1)
    mode = n * SHARE + place
    depth = jnp.where(mode < K, 0, jnp.where(mode < 2 * K, 1, 2))
    live = place < SHARE
    hot_j = jnp.where((iota((K, 24), 0) == mode - depth * K) & live, 1.0, 0.0)
    hot_k = jnp.where((iota((K, 24), 0) == w * OWN + depth) & live, 1.0, 0.0)
    gains = jnp.dot(gain_y[...], hot_j, precision=HIGHEST, preferred_element_type=F32)
    diagonal = iota((16, 16), 0) == iota((16, 16), 1)
    columns = [
        jnp.sum(jnp.where(diagonal, project[e : e + 1, :], 0.0), axis=1, keepdims=True)
        for e in range(3)
    ]
    blank = jnp.zeros((16, 16), F32)
    along = gain_x[...]
    for part, to in ((0, coef_a), (1, coef_b)):
        joined = []
        for d in range(3):
            total = jnp.zeros((16, K), F32)
            for c in range(16):
                total = total + lift[d, c] * mix[part, c].astype(F32)
            joined.append(
                gains * jnp.dot(total, hot_k, precision=HIGHEST, preferred_element_type=F32)
            )
        sign = 1.0 if part == 0 else -1.0
        right = jnp.concatenate([sign * along, blank, along, blank], 1)
        for e in range(3):
            for d in range(3):
                left = (columns[e] * joined[d]).T
                to[(e * 3 + d) * 24 : (e * 3 + d + 1) * 24, :] = jnp.dot(
                    left, right, precision=HIGHEST, preferred_element_type=F32
                )
    row = iota((8, LANES), 0)
    total = jnp.zeros((8, LANES), F32)
    for i in range(64):
        given = jnp.where(
            row == 0, weights[0, 0, i], jnp.where(row == 1, weights[1, 0, i], weights[2, 0, i])
        )
        total = total + jnp.where((flat == mon[i]) & (row < 3), given, 0.0)
    injected[...] = jnp.where(iota((8, LANES), 1) < 64, total, 0.0)


def filter_kernel(
    gathered, coef_a, coef_b, fwd_x, inv_x, phase_x, phase_yz, after, out
):
    b, w = own_block()
    far = b // NEAR
    lane = iota((1, LANES), 1)
    got = gathered[...]
    both = jnp.dot(fwd_x[...], got, preferred_element_type=F32)
    total = got.astype(F32).reshape(BULK, 8, LANES).sum(0)
    total = total + pltpu.roll(total, 64, 1)
    total = jnp.where(lane < 6, pltpu.roll(total, LANES - 54, 1), 0.0)
    total = jnp.concatenate([total, jnp.zeros((LANES - 8, LANES), F32)], 0).T[:8]
    total = pltpu.roll(total, (b % NEAR) * 8, 1)
    full = (both[:LANES] + pltpu.roll(both[LANES:], 64, 1)).T
    field = [full[d * SHARE : d * SHARE + 24] for d in range(3)]
    turned = [pltpu.roll(f, 64, 1) for f in field]
    sign = jnp.where(lane < 64, 1.0, -1.0)
    real = []
    for e in range(3):
        q = jnp.zeros((24, LANES), F32)
        for d in range(3):
            at = (e * 3 + d) * 24
            q = q + coef_a[at : at + 24] * field[d] + coef_b[at : at + 24] * turned[d]
        real.append(q)
    near = jnp.dot(
        jnp.concatenate(real, 0).astype(BF16), phase_x[...], preferred_element_type=F32
    )
    gap = jnp.zeros((10, LANES), F32)
    packed = jnp.concatenate([q[:SHARE] for q in real] + [gap], 0)
    right = jnp.concatenate([packed, pltpu.roll(packed, 64, 1) * sign], 0).astype(BF16)
    back = lax.dot_general(
        inv_x[far], right, (((1,), (1,)), ((), ())), preferred_element_type=F32
    ).reshape(NEAR, 2, 8, LANES)
    row = iota((8, LANES), 0)
    for e in range(3):
        line = jnp.sum(near[e * 24 : (e + 1) * 24] * phase_yz[...], axis=0, keepdims=True)
        line = line + pltpu.roll(line, 64, 1)
        total = total + jnp.where((row == e) & (lane < 64), line, 0.0)
    high = total.astype(BF16).astype(F32)
    extra = pltpu.roll(high + pltpu.roll(total - high, 64, 1), 2, 0)
    tiles = []
    for n in range(NEAR):
        tiles += [back[n, 0], back[n, 1] + extra]
    out[...] = jnp.concatenate(tiles, 0).astype(BF16)


def spread_kernel(shares, inv_y, after_low, after_high, out, rows):
    lane = iota((1, LANES), 1)
    got = shares[...].astype(F32).reshape(NEAR, 16, LANES)
    rows[...] = jnp.zeros((32, 8, LANES), F32)
    for e in range(3):
        flat = []
        for part in range(2):
            start = part * 64 + e * SHARE
            first, rest = jnp.zeros((16, LANES), F32), None
            for n in range(NEAR):
                moved = pltpu.roll(got[n], (n * SHARE - start) % LANES, 1)
                within = (lane >= n * SHARE) & (lane < (n + 1) * SHARE)
                first = first + jnp.where(within, moved, 0.0)
                if n == NEAR - 1:
                    rest = jnp.where(lane < 16, moved, 0.0)
            flat.append((first, rest))

        def mode_rows(part, k, to):
            first, rest = flat[part]
            moved = pltpu.roll(first, (to - k * K) % LANES, 1)
            if k < 2:
                return jnp.where((lane >= to) & (lane < to + K), moved, 0.0)
            tail = pltpu.roll(rest, to + 32, 1)
            return jnp.where((lane >= to) & (lane < to + 32), moved, 0.0) + jnp.where(
                (lane >= to + 32) & (lane < to + K), tail, 0.0
            )

        for k in range(OWN):
            real = mode_rows(0, k, 0) + mode_rows(1, k, 64)
            imag = mode_rows(1, k, 0) - mode_rows(0, k, 64)
            for x in range(10):
                rows[e * 10 + x, k : k + 1, :] = real[x : x + 1]
                rows[e * 10 + x, OWN + k : OWN + k + 1, :] = imag[x : x + 1]
    lhs = rows[...].reshape(256, LANES).astype(BF16)
    wide = jnp.dot(lhs, inv_y[...], preferred_element_type=F32).reshape(32, 8, 384)
    near = []
    for low in range(8):
        group = [wide[high * 8 + low, :, c * LANES : (c + 1) * LANES] for high in range(4) for c in range(2)]
        near.append(jnp.stack(group))
    near = exchange(near, 16, 2)
    edge = []
    for low in range(16):
        edge.append(jnp.stack([wide[high * 16 + low, :, 256:384] for high in range(2)]))
    edge = exchange(edge, 8, 2)
    row = iota((8, LANES), 0)
    total = pltpu.roll(got[:, 8:16].sum(0), 6, 0)
    total = jnp.where((row < 6) & (lane < 64), total + pltpu.roll(total, 64, 1), 0.0)
    high = total.astype(BF16).astype(F32)
    last = high + pltpu.roll(total - high, 64, 1)
    blocks = []
    for w in range(WIDE):
        tiles = [near[w % 8][high_x * 2 + w // 8] for high_x in range(4)]
        tiles += [edge[w][high_x] for high_x in range(2)] + [last]
        blocks.append(jnp.concatenate(tiles, 1))
    out[...] = jnp.concatenate(blocks, 0).astype(BF16)


def edge_kernel(electric, magnetic, inverse, saved, after, to_low, to_high):
    for c in range(3):
        to_low[c], to_high[c] = electric[c, 6:8], electric[c, 0:2]
        to_low[3 + c], to_high[3 + c] = magnetic[c, 6:8], magnetic[c, 0:2]
    to_low[6], to_high[6] = inverse[6:8], inverse[0:2]
    for n in range(2):
        for c in range(2):
            to_low[7 + n, c] = saved[n, 1 + c, 7].astype(F32)


def corner_kernel(electric, magnetic, inverse, saved, x_low, x_high, after, to_low, to_high):
    for c in range(7):
        own = electric.at[c] if c < 3 else (magnetic.at[c - 3] if c < 6 else inverse)
        for to, rows in ((to_low, slice(14, 16)), (to_high, slice(0, 2))):
            to[c * 12 : c * 12 + 8] = own[:, rows, :]
            to[c * 12 + 8 : c * 12 + 10] = x_high[c, :, rows, :]
            to[c * 12 + 10 : c * 12 + 12] = x_low[c, :, rows, :]
    for n in range(2):
        for i, c in enumerate((0, 2)):
            edge = saved[n, c].astype(F32)[:, RY - 1 : RY, :]
            to_low[84 + n * 8 : 92 + n * 8, i : i + 1, :] = edge


def first_kernel(
    mon, weights, electric, magnetic, inverse, saved, x_low, x_high, y_low, y_high, after,
    early, curled, factor, grad, ready, e_ext, h_ext, g_ext,
):
    b, w = own_block()
    lane = iota((1, NZ), 1)
    for c in range(7):
        to = e_ext.at[c] if c < 3 else (h_ext.at[c - 3] if c < 6 else g_ext)
        own = electric[c] if c < 3 else (magnetic[c - 3] if c < 6 else inverse[...])
        to[0:8, 0:16, :] = own
        to[8:10, 0:16, :] = x_high[c]
        to[10:12, 0:16, :] = x_low[c]
        low, high = y_low[c * 12 : (c + 1) * 12], y_high[c * 12 : (c + 1) * 12]
        to[:, 16:24, :] = jnp.concatenate([high, jnp.zeros((12, 4, NZ), F32), low], 1)

    g = g_ext[...]
    half = 0.5 * g
    a = [half * e_ext[c] for c in range(3)]
    spot_x = iota((12, 24, 1), 0)
    spot_y = iota((12, 24, 1), 1)
    outside = ((spot_x >= 10) & (b == 0)) | ((spot_y >= 22) & (w == 0))
    inside = jnp.where(outside, 0.0, 1.0)
    turned = curl_ahead(*a)
    h = [h_ext[c] + inside * turned[c] for c in range(3)]
    back = curl_behind(*h)
    for c in range(3):
        e_ext[c] = e_ext[c] - 0.5 * back[c]

    def hit(x, y, z):
        lx, ly = x - b * RX, y - w * RY
        return (lx >= -2) & (lx < RX + 2) & (ly >= -2) & (ly < RY + 2)

    def add(i, flat):
        x, y, z = place_of(flat)
        lx, ly = x - b * RX, y - w * RY
        px = jnp.where(lx < 0, lx + 12, lx)
        py = jnp.where(ly < 0, ly + 24, ly)
        for c in range(3):
            row = e_ext[c, px, pl.ds(py, 1), :]
            e_ext[c, px, pl.ds(py, 1), :] = row + jnp.where(lane == z, weights[c, 0, i], 0.0)

    scan(mon, hit, add)
    for c in range(3):
        early[c, 0:9] = e_ext[c, 0:9]
        early[c, 9:10] = e_ext[c, 11:12]
        curled[c, 0:9] = h[c][0:9]
        curled[c, 9:10] = h[c][11:12]
    factor[0:9] = half[0:9]
    factor[9:10] = half[11:12]

    near = inverse[...]
    for step in range(2):
        s = [saved[step, c].astype(F32) for c in range(3)]
        before_x = {c: jnp.concatenate([x_low[7 + step, c - 1 : c], s[c][:-1]], 0) for c in (1, 2)}
        at = 84 + step * 8
        before_y = {}
        for c in (0, 2):
            edge = y_low[at : at + 8, c // 2 : c // 2 + 1, :]
            first = iota((RX, RY, NZ), 1) == 0
            before_y[c] = jnp.where(first, edge, pltpu.roll(s[c], 1, 1))
        curls = (
            (s[2] - before_y[2]) - (s[1] - z_behind(s[1])),
            (s[0] - z_behind(s[0])) - (s[2] - before_x[2]),
            (s[1] - before_x[1]) - (s[0] - before_y[0]),
        )
        if step == 0:
            for c in range(3):
                ready[c] = near * curls[c]
        else:
            total = jnp.zeros((RX, RY, NZ), F32)
            for c in range(3):
                total = total + a[c][0:8, 0:16] * near * curls[c]
            grad[...] = -total


def second_kernel(
    lines, table, early, curled, factor, first_grad, ready, injected,
    grad_e, grad_h, grad_eps, sources,
):
    b, w = own_block()
    modes = lines[:, 0:768]
    back = lax.dot_general(
        modes, table[...], (((0,), (0,)), ((), ())), preferred_element_type=F32
    )
    main = back[0:512].reshape(32, 16, NZ)
    edge = back[512:768].reshape(32, 8, NZ)
    half = factor[...]
    e1 = []
    for c in range(3):
        at = slice(c * 10, c * 10 + 10)
        e1.append(early[c] + jnp.concatenate([main[at], edge[at]], 1))
    a = [half * e for e in e1]
    spot_x = iota((10, 24, 1), 0)
    spot_y = iota((10, 24, 1), 1)
    outside = ((spot_x == 9) & (b == 0)) | ((spot_y == 23) & (w == 0))
    inside = jnp.where(outside, 0.0, 1.0)
    turned = curl_ahead(*a)
    h = [curled[c] + inside * turned[c] for c in range(3)]
    backed = curl_behind(*h)
    total = first_grad[...]
    for c in range(3):
        grad_h[c] = h[c][0:8, 0:16]
        grad_e[c] = e1[c][0:8, 0:16] - 0.5 * backed[c][0:8, 0:16]
        total = total - a[c][0:8, 0:16] * ready[c]
    grad_eps[...] = total
    got = lines[:, 768:896].astype(F32).reshape(WIDE, 8, LANES).sum(0)
    got = got + pltpu.roll(got, 64, 1) + injected[...]
    for n in range(2):
        for c in range(3):
            sources[c, n : n + 1, :] = got[n * 3 + c : n * 3 + c + 1, 0:64]


def call(kernel, outs, places, scratch=(), flops=0, moved=0, params=PARAMS):
    spaces = {"s": pltpu.SMEM, "v": pltpu.VMEM, "a": pl.ANY}
    return pl.pallas_call(
        kernel,
        out_shape=outs,
        in_specs=[pl.BlockSpec(memory_space=spaces[p]) for p in places],
        out_specs=jax.tree.map(lambda _: pl.BlockSpec(memory_space=pltpu.VMEM), outs),
        scratch_shapes=list(scratch),
        compiler_params=params,
        cost_estimate=pl.CostEstimate(flops=flops, bytes_accessed=moved, transcendentals=0),
    )


def shape(*dims, dtype=F32):
    return jax.ShapeDtypeStruct(dims, dtype)


def passed_along(block, axis, distance):
    devices = range(lax.axis_size(axis))
    route = [(i - distance, i) for i in devices if i - distance in devices]
    return lax.ppermute(block, axis, route)


def dealt_near(block):
    groups = [[f * NEAR + n for n in range(NEAR)] for f in range(FAR)]
    return lax.all_to_all(
        block, "bulk", split_axis=0, concat_axis=0, axis_index_groups=groups, tiled=True
    )


def tables_of(name):
    return jnp.asarray(TABLES[name])


def body(
    seed_electric, seed_magnetic, saved_magnetic, material, permittivity, source_cells,
    monitor_cells, monitor_weights, lift_weight, project_weight, mode_mix, gain_first, gain_second,
):
    weights = monitor_weights.transpose(2, 0, 1)
    big, dma = pltpu.CompilerParams(vmem_limit_bytes=56 * 1024 * 1024), pltpu.SemaphoreType.DMA
    block = (RX, RY, NZ)

    payload, field = call(
        lift_kernel,
        (shape(384, LANES, dtype=BF16), shape(3, *block)),
        "aaaa",
        [
            pltpu.SMEM((64,), jnp.int32), pltpu.VMEM((3, 2, 64), F32),
            pltpu.VMEM((LANES, LANES), BF16), dma((4,)),
        ],
        13_000_000,
        500_000,
        big,
    )(monitor_cells, weights, seed_electric, tables_of("lift_z"))
    lines = lax.all_to_all(payload, "wide", split_axis=0, concat_axis=0, tiled=True)

    taken, inverse = call(
        share_kernel,
        (shape(8, LANES), shape(*block)),
        "aavaa",
        [
            pltpu.SMEM((64,), jnp.int32), pltpu.SMEM((8,), F32), pltpu.VMEM((3, *block), F32),
            pltpu.VMEM(block, jnp.int32), pltpu.VMEM((3, 12, 32, NZ), F32),
            pltpu.VMEM((3, 12, 32, NZ), F32), dma((4,)),
        ],
        3_000_000,
        1_500_000,
    )(source_cells, permittivity, field, seed_magnetic, material)

    dealt = call(
        middle_kernel, shape(BULK * 8, LANES, dtype=BF16), "vvv", (), 20_000_000, 400_000
    )(lines, taken, tables_of("fwd_y"))
    gathered = lax.all_to_all(dealt, "bulk", split_axis=0, concat_axis=0, tiled=True)

    cells = jnp.concatenate([source_cells, source_cells]).reshape(1, LANES)
    coef_a, coef_b, phase_x, phase_yz, injected = call(
        param_kernel,
        (
            shape(216, LANES), shape(216, LANES), shape(LANES, LANES, dtype=BF16),
            shape(24, LANES), shape(8, LANES),
        ),
        "sssvvvvvvvva",
        (),
        20_000_000,
        1_000_000,
    )(
        monitor_cells, weights, lift_weight.T, cells, project_weight, gain_first, gain_second,
        mode_mix.transpose(0, 2, 3, 1), tables_of("at_x"), tables_of("at_y"), tables_of("at_z"),
        dealt,
    )

    to_low, to_high = call(
        edge_kernel, (shape(9, 2, RY, NZ), shape(7, 2, RY, NZ)), "vvvva", (), 0, 500_000
    )(field, seed_magnetic, inverse, saved_magnetic, dealt)
    x_low = passed_along(to_low, "bulk", 1)
    x_high = passed_along(to_high, "bulk", -1)

    low_part, high_part = call(
        corner_kernel, (shape(100, 2, NZ), shape(84, 2, NZ)), "vvvvvva", (), 0, 1_000_000
    )(field, seed_magnetic, inverse, saved_magnetic, x_low, x_high, coef_a)
    shares = call(
        filter_kernel, shape(LANES, LANES, dtype=BF16), "vvvvvvva", (), 40_000_000, 600_000
    )(
        gathered, coef_a, coef_b, tables_of("fwd_x"), tables_of("inv_x"), phase_x, phase_yz,
        low_part,
    )
    back = dealt_near(shares)

    y_low = passed_along(low_part, "wide", 1)
    y_high = passed_along(high_part, "wide", -1)

    sent = call(
        spread_kernel,
        shape(128, 896, dtype=BF16),
        "vvaa",
        [pltpu.VMEM((32, 8, LANES), F32)],
        40_000_000,
        600_000,
    )(back, tables_of("inv_y"), y_low, y_high)
    returned = lax.all_to_all(sent, "wide", split_axis=0, concat_axis=0, tiled=True)
    early, curled, factor, first_grad, ready = call(
        first_kernel,
        (
            shape(3, 10, 24, NZ), shape(3, 10, 24, NZ), shape(10, 24, NZ), shape(*block),
            shape(3, *block),
        ),
        "ssvvvvvvvva",
        [pltpu.VMEM((3, 12, 24, NZ), F32)] * 2 + [pltpu.VMEM((12, 24, NZ), F32)],
        10_000_000,
        3_000_000,
    )(
        monitor_cells, weights, field, seed_magnetic, inverse, saved_magnetic,
        x_low, x_high, y_low, y_high, sent,
    )

    grad_e, grad_h, grad_eps, sources = call(
        second_kernel,
        (shape(3, *block), shape(3, *block), shape(*block), shape(3, 2, 64)),
        "vvvvvvvv",
        (),
        40_000_000,
        4_000_000,
    )(returned, tables_of("back_z"), early, curled, factor, first_grad, ready, injected)
    return grad_e, grad_h, grad_eps, sources.transpose(1, 2, 0)


def solution(mesh):
    field = P(None, "bulk", "wide", None)
    return jax.shard_map(
        body,
        mesh=mesh,
        in_specs=(
            field, field, P(None, None, "bulk", "wide", None), P("bulk", "wide", None),
            P(), P(), P(), P(), P(), P(), P(), P(), P(),
        ),
        out_specs=(field, field, P("bulk", "wide", None), P()),
        check_vma=False,
    )
```

```python
import functools
import math

import jax
import jax.numpy as jnp
import ml_dtypes
import numpy as np
from jax import lax
from jax.experimental import pallas as pl
from jax.experimental.pallas import tpu as pltpu
from jax.sharding import PartitionSpec as P

NX, NY, NZ = 256, 256, 128
K = 48
OWN = 3
WIDE, BULK = 16, 32
RX, RY = 8, 16
NEAR, FAR = 8, 4
SHARE = OWN * K // NEAR
LANES = 128
F32, BF16 = jnp.float32, jnp.bfloat16
PARAMS = pltpu.CompilerParams(vmem_limit_bytes=40 * 1024 * 1024)
HIGHEST = lax.Precision.HIGHEST


def waves(freqs, places, total):
    phase = np.mod(np.asarray(freqs)[:, None] * np.asarray(places)[None, :], total)
    angle = phase.astype(np.float32) * np.float32(2.0 * math.pi / total)
    return np.cos(angle).astype(np.float32), np.sin(angle).astype(np.float32)


def rounded(table):
    return np.asarray(table, np.float32).astype(ml_dtypes.bfloat16)


def make_tables():
    mode = np.arange(K)
    plane = np.where(mode < K // 2, mode, mode - K)
    cz, sz = waves(mode, np.arange(NZ), NZ)
    cx, sx = (rounded(t) for t in waves(plane, np.arange(NX), NX))
    cy, sy = (rounded(t) for t in waves(plane, np.arange(NY), NY))
    scale = np.float32(1.0 / math.sqrt(NX * NY * NZ))
    back = np.float32(1.0 / math.sqrt(K**3))
    fz, gz = rounded(cz * scale), rounded(-sz * scale)
    bz, hz = rounded(cz * back), rounded(sz * back)
    out = {}
    lift_z = np.zeros((LANES, LANES), ml_dtypes.bfloat16)
    back_z = np.zeros((LANES, LANES), ml_dtypes.bfloat16)
    for w in range(WIDE):
        for i in range(OWN):
            lift_z[:, w * 8 + i] = fz[w * OWN + i]
            lift_z[:, w * 8 + OWN + i] = gz[w * OWN + i]
            back_z[w * 8 + i] = bz[w * OWN + i]
            back_z[w * 8 + OWN + i] = -hz[w * OWN + i]
    out["lift_z"], out["back_z"] = lift_z, back_z

    lane = np.arange(LANES)
    y_of = np.concatenate([(h * 8 + lane % 8) * RY + lane // 8 for h in range(2)])
    fwd_y = np.zeros((512, 256), ml_dtypes.bfloat16)
    fwd_y[:256, :K] = cy[:, y_of].T
    fwd_y[256:, :K] = sy[:, y_of].T
    fwd_y[:256, 128 : 128 + K] = -sy[:, y_of].T
    fwd_y[256:, 128 : 128 + K] = cy[:, y_of].T
    out["fwd_y"] = fwd_y

    fwd_x = np.zeros((2 * LANES, NX), ml_dtypes.bfloat16)
    fwd_x[:K], fwd_x[64 : 64 + K] = cx, -sx
    fwd_x[128 : 128 + K], fwd_x[192 : 192 + K] = sx, cx
    inv_x = np.zeros((FAR, LANES, LANES), ml_dtypes.bfloat16)
    for far in range(FAR):
        for n in range(NEAR):
            start = (far * NEAR + n) * RX
            x_of = (start + np.array([0, 1, 2, 3, 4, 5, 6, 7, 8, -1])) % NX
            inv_x[far, n * 16 : n * 16 + 10, :K] = cx[:, x_of].T
            inv_x[far, n * 16 : n * 16 + 10, 64 : 64 + K] = -sx[:, x_of].T
    out["fwd_x"], out["inv_x"] = fwd_x, inv_x

    inv_y = np.zeros((LANES, 384), ml_dtypes.bfloat16)
    inv_y[:K, :256], inv_y[64 : 64 + K, :256] = cy, -sy
    for w in range(WIDE):
        for h, y in enumerate((w * RY + RY, w * RY - 1)):
            inv_y[:K, 256 + w * 2 + h] = cy[:, y % NY]
            inv_y[64 : 64 + K, 256 + w * 2 + h] = -sy[:, y % NY]
    out["inv_y"] = inv_y
    apart = np.zeros((LANES, 256), ml_dtypes.bfloat16)
    for cell in range(32):
        apart[cell * 2, cell * 8] = 1
        apart[cell * 2 + 1, cell * 8 + 7] = 1
    out["apart"] = apart

    at_x = np.zeros((2, LANES, NX), ml_dtypes.bfloat16)
    at_x[0, :K], at_x[0, 64 : 64 + K] = cx, -sx
    at_x[1, :K], at_x[1, 64 : 64 + K] = sx, cx
    out["at_x"] = at_x
    at_y = np.zeros((NEAR, 2, 32, NY), ml_dtypes.bfloat16)
    for n in range(NEAR):
        j_of = np.arange(n * SHARE, (n + 1) * SHARE) % K
        at_y[n, 0, :SHARE], at_y[n, 1, :SHARE] = cy[j_of], sy[j_of]
    out["at_y"] = at_y
    at_z = np.zeros((WIDE, 2, 16, NZ), ml_dtypes.bfloat16)
    for w in range(WIDE):
        at_z[w, 0, :OWN] = bz[w * OWN : (w + 1) * OWN]
        at_z[w, 1, :OWN] = hz[w * OWN : (w + 1) * OWN]
    out["at_z"] = at_z
    return out


TABLES = make_tables()


def iota(shape, axis):
    return lax.broadcasted_iota(jnp.int32, shape, axis)


def exchange(tiles, block, axis):
    tiles = list(tiles)
    shape = tiles[0].shape
    size = shape[axis]
    place = iota(shape, axis) // block
    step = 1
    while step < len(tiles):
        high = (place // step) % 2 == 1
        new = list(tiles)
        for low in range(len(tiles)):
            if low & step:
                continue
            u, v = tiles[low], tiles[low + step]
            new[low] = jnp.where(high, pltpu.roll(v, step * block, axis), u)
            new[low + step] = jnp.where(high, v, pltpu.roll(u, size - step * block, axis))
        tiles = new
        step *= 2
    return tiles


def z_ahead(v):
    axis = v.ndim - 1
    return jnp.where(iota(v.shape, axis) < NZ - 1, pltpu.roll(v, NZ - 1, axis), 0.0)


def z_behind(v):
    axis = v.ndim - 1
    return jnp.where(iota(v.shape, axis) > 0, pltpu.roll(v, 1, axis), 0.0)


def x_ahead(v):
    return jnp.concatenate([v[1:], v[:1]], 0)


def x_behind(v):
    return jnp.concatenate([v[-1:], v[:-1]], 0)


def y_ahead(v):
    return pltpu.roll(v, v.shape[1] - 1, 1)


def y_behind(v):
    return pltpu.roll(v, 1, 1)


def curl_ahead(fx, fy, fz):
    return (
        (y_ahead(fz) - fz) - (z_ahead(fy) - fy),
        (z_ahead(fx) - fx) - (x_ahead(fz) - fz),
        (x_ahead(fy) - fy) - (y_ahead(fx) - fx),
    )


def curl_behind(fx, fy, fz):
    return (
        (fz - y_behind(fz)) - (fy - z_behind(fy)),
        (fx - z_behind(fx)) - (fz - x_behind(fz)),
        (fy - x_behind(fy)) - (fx - y_behind(fx)),
    )


def place_of(flat):
    return flat >> 15, (flat >> 7) & (NY - 1), flat & (NZ - 1)


def own_block():
    return lax.axis_index("bulk"), lax.axis_index("wide")


def fetch(pairs, sems):
    copies = [pltpu.make_async_copy(a, b, sems.at[i]) for i, (a, b) in enumerate(pairs)]
    for copy in copies:
        copy.start()
    return copies


def scan(cells, hit, act):
    def group(g, carry):
        found = [cells[g * 8 + i] for i in range(8)]
        hits = [hit(*place_of(f)) for f in found]
        some = functools.reduce(jnp.logical_or, hits)

        @pl.when(some)
        def _():
            for i in range(8):
                pl.when(hits[i])(functools.partial(act, g * 8 + i, found[i]))

        return carry

    lax.fori_loop(0, 8, group, 0)


def lift_kernel(mon_in, weights_in, electric, table_in, out, field, mon, weights, table, sems):
    b, w = own_block()
    copies = fetch(
        ((mon_in, mon), (electric, field), (weights_in, weights), (table_in, table)), sems
    )
    for copy in copies:
        copy.wait()
    lane = iota((1, NZ), 1)
    spot = iota((1, 64), 1)

    def hit(x, y, z):
        return ((x >> 3) == b) & ((y >> 4) == w)

    def add(i, flat):
        x, y, z = place_of(flat)
        lx, ly = x & (RX - 1), y & (RY - 1)
        for c in range(3):
            row = field[c, lx, pl.ds(ly, 1), :]
            given = jnp.where(spot == i, weights[c, 1:2, :], 0.0)
            weight = jnp.sum(given, axis=1, keepdims=True)
            field[c, lx, pl.ds(ly, 1), :] = row + jnp.where(lane == z, weight, 0.0)

    scan(mon, hit, add)
    rows = field[...].reshape(3 * RX * RY, NZ).astype(BF16)
    modes = jnp.dot(rows, table[...], preferred_element_type=F32)
    modes = modes.reshape(3, RX, 2, 8, LANES)
    tiles = exchange([modes[:, x].reshape(6, 8, LANES) for x in range(RX)], 1, 1)
    tiles = [t.reshape(3, 2, 8, LANES) for t in tiles]
    tiles = exchange([tiles[y % 8][:, y // 8] for y in range(RY)], 8, 2)
    out[...] = jnp.concatenate([t.reshape(24, LANES) for t in tiles], 0).astype(BF16)


def share_kernel(
    src_in, perm_in, field, magnetic_in, material_in,
    taken, inverse,
    src, perm, magnetic, material, scaled, held, sems,
):
    b, w = own_block()
    copies = fetch(
        (
            (src_in, src), (perm_in, perm), (magnetic_in, magnetic),
            (material_in, material),
        ),
        sems,
    )
    zero = jnp.zeros((12, 32, NZ), F32)
    for c in range(3):
        scaled[c] = zero
        held[c] = zero
    for copy in copies:
        copy.wait()
    eps = jnp.zeros((RX, RY, NZ), F32)
    cells = material[...]
    for level in range(8):
        eps = jnp.where(cells == level, perm[level], eps)
    inv = 1.0 / eps
    inverse[...] = inv
    lane = iota((1, NZ), 1)
    for c in range(3):
        scaled[c, 2:10, 8:24, :] = 0.5 * inv * field[c]
        held[c, 2:10, 8:24, :] = magnetic[c]
    taken[...] = jnp.zeros((8, LANES), F32)
    spot_row, spot_lane = iota((8, LANES), 0), iota((8, LANES), 1)

    def hit(x, y, z):
        lx, ly = x - b * RX, y - w * RY
        return (lx >= -1) & (lx <= RX) & (ly >= -1) & (ly <= RY)

    def take(i, flat):
        x, y, z = place_of(flat)
        lx, ly = x - b * RX, y - w * RY

        def a(c, dx, dy):
            return scaled[c, lx + 2 + dx, pl.ds(ly + 8 + dy, 1), :]

        def h(c, dx, dy):
            old = held[c, lx + 2 + dx, pl.ds(ly + 8 + dy, 1), :]
            if c == 0:
                near = a(1, dx, dy)
                turn = (a(2, dx, dy + 1) - a(2, dx, dy)) - (z_ahead(near) - near)
            elif c == 1:
                near = a(0, dx, dy)
                turn = (z_ahead(near) - near) - (a(2, dx + 1, dy) - a(2, dx, dy))
            else:
                turn = (a(1, dx + 1, dy) - a(1, dx, dy)) - (a(0, dx, dy + 1) - a(0, dx, dy))
            return old + turn

        left = jnp.where(x > 0, 1.0, 0.0)
        down = jnp.where(y > 0, 1.0, 0.0)
        hx, hy, hz = h(0, 0, 0), h(1, 0, 0), h(2, 0, 0)
        hx_y, hz_y = down * h(0, 0, -1), down * h(2, 0, -1)
        hy_x, hz_x = left * h(1, -1, 0), left * h(2, -1, 0)
        curls = (
            (hz - hz_y) - (hy - z_behind(hy)),
            (hx - z_behind(hx)) - (hz - hz_x),
            (hy - hy_x) - (hx - hx_y),
        )
        mine = jnp.where((lx >= 0) & (lx < RX) & (ly >= 0) & (ly < RY), 1.0, 0.0)
        cx, cy = jnp.clip(lx, 0, RX - 1), jnp.clip(ly, 0, RY - 1)
        got = taken[...]
        for c in range(3):
            old = mine * field[c, cx, pl.ds(cy, 1), :]
            for n, row in ((0, old - 0.5 * curls[c]), (1, old)):
                value = jnp.sum(jnp.where(lane == z, row, 0.0), axis=1, keepdims=True)
                spot = (spot_row == n * 3 + c) & (spot_lane == i)
                got = got + jnp.where(spot, value, 0.0)
        taken[...] = got

    scan(src, hit, take)


def middle_kernel(lines, taken, table, out):
    got = lines[...].astype(F32).reshape(WIDE, 24, LANES)
    halves = [exchange([got[h * 8 + i] for i in range(8)], 1, 1) for h in range(2)]
    rows = [
        jnp.concatenate([halves[0][k], halves[1][k], halves[0][OWN + k], halves[1][OWN + k]], 1)
        for k in range(OWN)
    ]
    lhs = jnp.concatenate(rows, 0).astype(BF16)
    found = jnp.dot(lhs, table[...], preferred_element_type=F32)
    lane = iota((8, LANES), 1)
    parts = [jnp.zeros((8, LANES), F32) for _ in range(NEAR)]
    for part in range(2):
        for d in range(3):
            piece = [
                found[(k * 3 + d) * 8 : (k * 3 + d) * 8 + 8, part * LANES : (part + 1) * LANES]
                for k in range(OWN)
            ]
            last = pltpu.roll(piece[2], 2 * K, 1)
            first = piece[0] + pltpu.roll(piece[1], K, 1) + jnp.where(lane >= 2 * K, last, 0.0)
            rest = jnp.where(lane < 16, last, 0.0)
            to = part * 64 + d * SHARE
            for n in range(NEAR):
                moved = pltpu.roll(first, (to - n * SHARE) % LANES, 1)
                if n == NEAR - 1:
                    moved = jnp.where(lane < to + 2, moved, pltpu.roll(rest, to + 2, 1))
                within = (lane >= to) & (lane < to + SHARE)
                parts[n] = parts[n] + jnp.where(within, moved, 0.0)
    src = jnp.concatenate([taken[...], jnp.zeros((LANES - 8, LANES), F32)], 0).T
    high = src.astype(BF16).astype(F32)
    extra = pltpu.roll(high, 54, 1) + pltpu.roll(src - high, 118, 1)
    deal = (jnp.concatenate(parts, 0) + extra[: NEAR * 8]).astype(BF16)
    for f in range(FAR):
        out[f * NEAR * 8 : (f + 1) * NEAR * 8, :] = deal


def param_kernel(
    mon, weights, lift, cells, project, gain_x, gain_y, mix, at_x, at_y, at_z, after,
    coef_a, coef_b, phase_x, phase_yz, injected,
):
    b, w = own_block()
    n = b % NEAR
    flat = cells[...]
    x, y, z = place_of(flat)
    first = iota((1, LANES), 1) < 64
    hot_x = jnp.where(iota((NX, LANES), 0) == x, 1.0, 0.0)
    real = jnp.where(first, hot_x, 0.0).astype(BF16)
    imag = jnp.where(first, 0.0, hot_x).astype(BF16)
    phase_x[...] = (
        jnp.dot(at_x[0], real, preferred_element_type=F32)
        + jnp.dot(at_x[1], imag, preferred_element_type=F32)
    ).astype(BF16)
    hot_y = jnp.where(iota((NY, LANES), 0) == y, 1.0, 0.0).astype(BF16)
    hot_z = jnp.where(iota((NZ, LANES), 0) == z, 1.0, 0.0).astype(BF16)
    cy = jnp.dot(at_y[n, 0], hot_y, preferred_element_type=F32)[:24]
    sy = jnp.dot(at_y[n, 1], hot_y, preferred_element_type=F32)[:24]
    cz = jnp.dot(at_z[w, 0], hot_z, preferred_element_type=F32)
    sz = jnp.dot(at_z[w, 1], hot_z, preferred_element_type=F32)
    mode = n * SHARE + iota((24, 1), 0)
    ck = jnp.where(mode < K, cz[0:1], jnp.where(mode < 2 * K, cz[1:2], cz[2:3]))
    sk = jnp.where(mode < K, sz[0:1], jnp.where(mode < 2 * K, sz[1:2], sz[2:3]))
    phase_yz[...] = jnp.where(first, cy * ck - sy * sk, -(sy * ck + cy * sk))

    place = iota((K, 24), 1)
    mode = n * SHARE + place
    depth = jnp.where(mode < K, 0, jnp.where(mode < 2 * K, 1, 2))
    live = place < SHARE
    hot_j = jnp.where((iota((K, 24), 0) == mode - depth * K) & live, 1.0, 0.0)
    hot_k = jnp.where((iota((K, 24), 0) == w * OWN + depth) & live, 1.0, 0.0)
    gains = jnp.dot(gain_y[...], hot_j, precision=HIGHEST, preferred_element_type=F32)
    diagonal = iota((16, 16), 0) == iota((16, 16), 1)
    columns = [
        jnp.sum(jnp.where(diagonal, project[e : e + 1, :], 0.0), axis=1, keepdims=True)
        for e in range(3)
    ]
    blank = jnp.zeros((16, 16), F32)
    along = gain_x[...]
    for part, to in ((0, coef_a), (1, coef_b)):
        joined = []
        for d in range(3):
            total = jnp.zeros((16, K), F32)
            for c in range(16):
                total = total + lift[d, c] * mix[part, c].astype(F32)
            joined.append(
                gains * jnp.dot(total, hot_k, precision=HIGHEST, preferred_element_type=F32)
            )
        sign = 1.0 if part == 0 else -1.0
        right = jnp.concatenate([sign * along, blank, along, blank], 1)
        for e in range(3):
            for d in range(3):
                left = (columns[e] * joined[d]).T
                to[(e * 3 + d) * 24 : (e * 3 + d + 1) * 24, :] = jnp.dot(
                    left, right, precision=HIGHEST, preferred_element_type=F32
                )
    row = iota((8, LANES), 0)
    total = jnp.zeros((8, LANES), F32)
    for i in range(64):
        given = jnp.where(
            row == 0, weights[0, 0, i], jnp.where(row == 1, weights[1, 0, i], weights[2, 0, i])
        )
        total = total + jnp.where((flat == mon[i]) & (row < 3), given, 0.0)
    injected[...] = jnp.where(iota((8, LANES), 1) < 64, total, 0.0)


def filter_kernel(
    gathered, coef_a, coef_b, fwd_x, inv_x, phase_x, phase_yz, after, out
):
    b, w = own_block()
    far = b // NEAR
    lane = iota((1, LANES), 1)
    got = gathered[...]
    both = jnp.dot(fwd_x[...], got, preferred_element_type=F32)
    total = got.astype(F32).reshape(BULK, 8, LANES).sum(0)
    total = total + pltpu.roll(total, 64, 1)
    total = jnp.where(lane < 6, pltpu.roll(total, LANES - 54, 1), 0.0)
    total = jnp.concatenate([total, jnp.zeros((LANES - 8, LANES), F32)], 0).T[:8]
    total = pltpu.roll(total, (b % NEAR) * 8, 1)
    full = (both[:LANES] + pltpu.roll(both[LANES:], 64, 1)).T
    field = [full[d * SHARE : d * SHARE + 24] for d in range(3)]
    turned = [pltpu.roll(f, 64, 1) for f in field]
    sign = jnp.where(lane < 64, 1.0, -1.0)
    real = []
    for e in range(3):
        q = jnp.zeros((24, LANES), F32)
        for d in range(3):
            at = (e * 3 + d) * 24
            q = q + coef_a[at : at + 24] * field[d] + coef_b[at : at + 24] * turned[d]
        real.append(q)
    near = jnp.dot(
        jnp.concatenate(real, 0).astype(BF16), phase_x[...], preferred_element_type=F32
    )
    gap = jnp.zeros((10, LANES), F32)
    packed = jnp.concatenate([q[:SHARE] for q in real] + [gap], 0)
    right = jnp.concatenate([packed, pltpu.roll(packed, 64, 1) * sign], 0).astype(BF16)
    back = lax.dot_general(
        inv_x[far], right, (((1,), (1,)), ((), ())), preferred_element_type=F32
    ).reshape(NEAR, 2, 8, LANES)
    row = iota((8, LANES), 0)
    for e in range(3):
        line = jnp.sum(near[e * 24 : (e + 1) * 24] * phase_yz[...], axis=0, keepdims=True)
        line = line + pltpu.roll(line, 64, 1)
        total = total + jnp.where((row == e) & (lane < 64), line, 0.0)
    high = total.astype(BF16).astype(F32)
    extra = pltpu.roll(high + pltpu.roll(total - high, 64, 1), 2, 0)
    tiles = []
    for n in range(NEAR):
        tiles += [back[n, 0], back[n, 1] + extra]
    out[...] = jnp.concatenate(tiles, 0).astype(BF16)


def spread_kernel(shares, inv_y, after_low, after_high, out, rows):
    lane = iota((1, LANES), 1)
    got = shares[...].astype(F32).reshape(NEAR, 16, LANES)
    rows[...] = jnp.zeros((32, 8, LANES), F32)
    for e in range(3):
        flat = []
        for part in range(2):
            start = part * 64 + e * SHARE
            first, rest = jnp.zeros((16, LANES), F32), None
            for n in range(NEAR):
                moved = pltpu.roll(got[n], (n * SHARE - start) % LANES, 1)
                within = (lane >= n * SHARE) & (lane < (n + 1) * SHARE)
                first = first + jnp.where(within, moved, 0.0)
                if n == NEAR - 1:
                    rest = jnp.where(lane < 16, moved, 0.0)
            flat.append((first, rest))

        def mode_rows(part, k, to):
            first, rest = flat[part]
            moved = pltpu.roll(first, (to - k * K) % LANES, 1)
            if k < 2:
                return jnp.where((lane >= to) & (lane < to + K), moved, 0.0)
            tail = pltpu.roll(rest, to + 32, 1)
            return jnp.where((lane >= to) & (lane < to + 32), moved, 0.0) + jnp.where(
                (lane >= to + 32) & (lane < to + K), tail, 0.0
            )

        for k in range(OWN):
            real = mode_rows(0, k, 0) + mode_rows(1, k, 64)
            imag = mode_rows(1, k, 0) - mode_rows(0, k, 64)
            for x in range(10):
                rows[e * 10 + x, k : k + 1, :] = real[x : x + 1]
                rows[e * 10 + x, OWN + k : OWN + k + 1, :] = imag[x : x + 1]
    lhs = rows[...].reshape(256, LANES).astype(BF16)
    wide = jnp.dot(lhs, inv_y[...], preferred_element_type=F32).reshape(32, 8, 384)
    near = []
    for low in range(8):
        group = [wide[high * 8 + low, :, c * LANES : (c + 1) * LANES] for high in range(4) for c in range(2)]
        near.append(jnp.stack(group))
    near = exchange(near, 16, 2)
    edge = []
    for low in range(16):
        edge.append(jnp.stack([wide[high * 16 + low, :, 256:384] for high in range(2)]))
    edge = exchange(edge, 2, 2)
    row = iota((8, LANES), 0)
    total = pltpu.roll(got[:, 8:16].sum(0), 6, 0)
    total = jnp.where((row < 6) & (lane < 64), total + pltpu.roll(total, 64, 1), 0.0)
    high = total.astype(BF16).astype(F32)
    other = pltpu.roll(total - high, 64, 1)
    moved = pltpu.roll(high, 64, 1)
    low = total - high
    extra = []
    for t in range(3):
        first = jnp.where(lane < 64, high[2 * t : 2 * t + 1], moved[2 * t + 1 : 2 * t + 2])
        second = jnp.where(lane < 64, low[2 * t : 2 * t + 1], other[2 * t + 1 : 2 * t + 2])
        extra.append(jnp.where(row == 6, first, jnp.where(row == 7, second, 0.0)))
    blocks = []
    for w in range(WIDE):
        tiles = [near[w % 8][high_x * 2 + w // 8] for high_x in range(4)]
        for t in range(3):
            tiles[t] = tiles[t] + extra[t]
        pair = jnp.where(lane < 32, edge[w], 0.0)
        tiles.append(pair[0] + pltpu.roll(pair[1], 32, 1))
        blocks.append(jnp.concatenate(tiles, 1))
    out[...] = jnp.concatenate(blocks, 0).astype(BF16)


def high_planes(across):
    first, second = [c for c in range(3) if c != across]
    planes = [(c, 0) for c in range(3)] + [(first, 1), (second, 1), (6, 0), (6, 1)]
    return planes + [(3 + c, 0) for c in range(3)]


def low_planes(across):
    first, second = [c for c in range(3) if c != across]
    planes = [(c, i) for i in range(2) for c in range(3)] + [(6, 0), (6, 1)]
    return planes + [(3 + first, 0), (3 + second, 0)] + [(3 + c, 1) for c in range(3)]


def edge_kernel(electric, magnetic, inverse, saved, after, to_low, to_high):
    def own(f):
        return electric.at[f] if f < 3 else (magnetic.at[f - 3] if f < 6 else inverse)

    for p, (f, i) in enumerate(low_planes(0)):
        to_low[p] = own(f)[6 + i].astype(BF16)
    for n in range(2):
        for c in range(2):
            to_low[13 + 2 * n + c] = saved[n, 1 + c, 7]
    for p, (f, i) in enumerate(high_planes(0)):
        to_high[p] = own(f)[i].astype(BF16)


def corner_kernel(
    electric, magnetic, inverse, saved, x_low, x_high, after, to_low, to_high, low, high
):
    x_of = [{}, {}]
    for p, key in enumerate(low_planes(0)):
        x_of[0][key] = x_low[p].astype(F32)
    for p, key in enumerate(high_planes(0)):
        x_of[1][key] = x_high[p].astype(F32)
    low[...] = jnp.zeros(low.shape, F32)
    high[...] = jnp.zeros(high.shape, F32)
    for to, planes, start in ((low, low_planes(1), 14), (high, high_planes(1), 0)):
        for p, (f, i) in enumerate(planes):
            own = electric.at[f] if f < 3 else (magnetic.at[f - 3] if f < 6 else inverse)
            row = start + i
            to[p, 0:8, :] = own[:, row, :]
            for side, at in ((1, 8), (0, 10)):
                for layer in range(2):
                    if (f, layer) in x_of[side]:
                        got = x_of[side][(f, layer)]
                        to[p, at + layer : at + layer + 1, :] = got[row : row + 1]
    for n in range(2):
        for i, c in enumerate((0, 2)):
            low[13 + 2 * n + i, 0:8, :] = saved[n, c].astype(F32)[:, RY - 1, :]
    to_low[...] = low[...].astype(BF16)
    to_high[...] = high[...].astype(BF16)


def first_kernel(
    mon, weights, electric, magnetic, inverse, saved, x_low, x_high, y_low, y_high, after,
    early, curled, factor, grad, ready, e_ext, h_ext, g_ext,
):
    b, w = own_block()
    lane = iota((1, NZ), 1)
    zero = jnp.zeros((12, 24, NZ), F32)
    for c in range(7):
        to = e_ext.at[c] if c < 3 else (h_ext.at[c - 3] if c < 6 else g_ext)
        to[...] = zero
        own = electric[c] if c < 3 else (magnetic[c - 3] if c < 6 else inverse[...])
        to[0:8, 0:16, :] = own
        for planes, ref, at in ((high_planes(0), x_high, 8), (low_planes(0), x_low, 10)):
            for p, (f, i) in enumerate(planes):
                if f == c:
                    to[at + i, 0:16, :] = ref[p].astype(F32)
        for planes, ref, at in ((high_planes(1), y_high, 16), (low_planes(1), y_low, 22)):
            for p, (f, i) in enumerate(planes):
                if f == c:
                    to[:, at + i : at + i + 1, :] = ref[p].astype(F32)[0:12][:, None, :]

    g = g_ext[...]
    half = 0.5 * g
    a = [half * e_ext[c] for c in range(3)]
    spot_x = iota((12, 24, 1), 0)
    spot_y = iota((12, 24, 1), 1)
    outside = ((spot_x >= 10) & (b == 0)) | ((spot_y >= 22) & (w == 0))
    inside = jnp.where(outside, 0.0, 1.0)
    turned = curl_ahead(*a)
    h = [h_ext[c] + inside * turned[c] for c in range(3)]
    back = curl_behind(*h)
    for c in range(3):
        e_ext[c] = e_ext[c] - 0.5 * back[c]

    def hit(x, y, z):
        lx, ly = x - b * RX, y - w * RY
        return (lx >= -2) & (lx < RX + 2) & (ly >= -2) & (ly < RY + 2)

    def add(i, flat):
        x, y, z = place_of(flat)
        lx, ly = x - b * RX, y - w * RY
        px = jnp.where(lx < 0, lx + 12, lx)
        py = jnp.where(ly < 0, ly + 24, ly)
        for c in range(3):
            row = e_ext[c, px, pl.ds(py, 1), :]
            e_ext[c, px, pl.ds(py, 1), :] = row + jnp.where(lane == z, weights[c, 0, i], 0.0)

    scan(mon, hit, add)
    for c in range(3):
        early[c, 0:9] = e_ext[c, 0:9]
        early[c, 9:10] = e_ext[c, 11:12]
        curled[c, 0:9] = h[c][0:9]
        curled[c, 9:10] = h[c][11:12]
    factor[0:9] = half[0:9]
    factor[9:10] = half[11:12]

    near = inverse[...]
    for step in range(2):
        s = [saved[step, c].astype(F32) for c in range(3)]
        before_x = {c: jnp.concatenate([x_low[12 + 2 * step + c].astype(F32)[None], s[c][:-1]], 0) for c in (1, 2)}
        before_y = {}
        for c in (0, 2):
            edge = y_low[13 + 2 * step + c // 2].astype(F32)[0:8][:, None, :]
            first = iota((RX, RY, NZ), 1) == 0
            before_y[c] = jnp.where(first, edge, pltpu.roll(s[c], 1, 1))
        curls = (
            (s[2] - before_y[2]) - (s[1] - z_behind(s[1])),
            (s[0] - z_behind(s[0])) - (s[2] - before_x[2]),
            (s[1] - before_x[1]) - (s[0] - before_y[0]),
        )
        if step == 0:
            for c in range(3):
                ready[c] = near * curls[c]
        else:
            total = jnp.zeros((RX, RY, NZ), F32)
            for c in range(3):
                total = total + a[c][0:8, 0:16] * near * curls[c]
            grad[...] = -total


def second_kernel(
    lines, table, apart, early, curled, factor, first_grad, ready, injected,
    grad_e, grad_h, grad_eps, sources,
):
    b, w = own_block()
    turn = (((0,), (0,)), ((), ()))
    main = lax.dot_general(lines[:, 0:512], table[...], turn, preferred_element_type=F32)
    main = main.reshape(32, 16, NZ)
    edge = jnp.dot(lines[:, 512:640], apart[...], preferred_element_type=F32).astype(BF16)
    edge = lax.dot_general(edge, table[...], turn, preferred_element_type=F32)
    edge = edge.reshape(32, 8, NZ)
    half = factor[...]
    e1 = []
    for c in range(3):
        at = slice(c * 10, c * 10 + 10)
        e1.append(early[c] + jnp.concatenate([main[at], edge[at]], 1))
    a = [half * e for e in e1]
    spot_x = iota((10, 24, 1), 0)
    spot_y = iota((10, 24, 1), 1)
    outside = ((spot_x == 9) & (b == 0)) | ((spot_y == 23) & (w == 0))
    inside = jnp.where(outside, 0.0, 1.0)
    turned = curl_ahead(*a)
    h = [curled[c] + inside * turned[c] for c in range(3)]
    backed = curl_behind(*h)
    total = first_grad[...]
    for c in range(3):
        grad_h[c] = h[c][0:8, 0:16]
        grad_e[c] = e1[c][0:8, 0:16] - 0.5 * backed[c][0:8, 0:16]
        total = total - a[c][0:8, 0:16] * ready[c]
    grad_eps[...] = total
    got = lines[:, 0:384].astype(F32).reshape(WIDE, 8, 384).sum(0)
    got = got[6:7] + got[7:8]
    moved = pltpu.roll(got, 384 - 64, 1)
    for n in range(2):
        for c in range(3):
            at = n * 3 + c
            line = got if at % 2 == 0 else moved
            line = line[:, at // 2 * LANES : (at // 2 + 1) * LANES]
            if n == 0:
                line = line + injected[c : c + 1, :]
            sources[c, n : n + 1, :] = line[:, 0:64]


def call(kernel, outs, places, scratch=(), flops=0, moved=0, params=PARAMS):
    spaces = {"s": pltpu.SMEM, "v": pltpu.VMEM, "a": pl.ANY}
    return pl.pallas_call(
        kernel,
        out_shape=outs,
        in_specs=[pl.BlockSpec(memory_space=spaces[p]) for p in places],
        out_specs=jax.tree.map(lambda _: pl.BlockSpec(memory_space=pltpu.VMEM), outs),
        scratch_shapes=list(scratch),
        compiler_params=params,
        cost_estimate=pl.CostEstimate(flops=flops, bytes_accessed=moved, transcendentals=0),
    )


def shape(*dims, dtype=F32):
    return jax.ShapeDtypeStruct(dims, dtype)


def passed_along(block, axis, distance):
    devices = range(lax.axis_size(axis))
    route = [(i - distance, i) for i in devices if i - distance in devices]
    return lax.ppermute(block, axis, route)


def dealt_near(block):
    groups = [[f * NEAR + n for n in range(NEAR)] for f in range(FAR)]
    return lax.all_to_all(
        block, "bulk", split_axis=0, concat_axis=0, axis_index_groups=groups, tiled=True
    )


def tables_of(name):
    return jnp.asarray(TABLES[name])


def body(
    seed_electric, seed_magnetic, saved_magnetic, material, permittivity, source_cells,
    monitor_cells, monitor_weights, lift_weight, project_weight, mode_mix, gain_first, gain_second,
):
    weights = monitor_weights.transpose(2, 0, 1)
    big, dma = pltpu.CompilerParams(vmem_limit_bytes=56 * 1024 * 1024), pltpu.SemaphoreType.DMA
    block = (RX, RY, NZ)

    payload, field = call(
        lift_kernel,
        (shape(384, LANES, dtype=BF16), shape(3, *block)),
        "aaaa",
        [
            pltpu.SMEM((64,), jnp.int32), pltpu.VMEM((3, 2, 64), F32),
            pltpu.VMEM((LANES, LANES), BF16), dma((4,)),
        ],
        13_000_000,
        500_000,
        big,
    )(monitor_cells, weights, seed_electric, tables_of("lift_z"))
    lines = lax.all_to_all(payload, "wide", split_axis=0, concat_axis=0, tiled=True)

    taken, inverse = call(
        share_kernel,
        (shape(8, LANES), shape(*block)),
        "aavaa",
        [
            pltpu.SMEM((64,), jnp.int32), pltpu.SMEM((8,), F32), pltpu.VMEM((3, *block), F32),
            pltpu.VMEM(block, jnp.int32), pltpu.VMEM((3, 12, 32, NZ), F32),
            pltpu.VMEM((3, 12, 32, NZ), F32), dma((4,)),
        ],
        3_000_000,
        1_500_000,
    )(source_cells, permittivity, field, seed_magnetic, material)

    dealt = call(
        middle_kernel, shape(BULK * 8, LANES, dtype=BF16), "vvv", (), 20_000_000, 400_000
    )(lines, taken, tables_of("fwd_y"))
    gathered = lax.all_to_all(dealt, "bulk", split_axis=0, concat_axis=0, tiled=True)

    cells = jnp.concatenate([source_cells, source_cells]).reshape(1, LANES)
    coef_a, coef_b, phase_x, phase_yz, injected = call(
        param_kernel,
        (
            shape(216, LANES), shape(216, LANES), shape(LANES, LANES, dtype=BF16),
            shape(24, LANES), shape(8, LANES),
        ),
        "sssvvvvvvvva",
        (),
        20_000_000,
        1_000_000,
    )(
        monitor_cells, weights, lift_weight.T, cells, project_weight, gain_first, gain_second,
        mode_mix.transpose(0, 2, 3, 1), tables_of("at_x"), tables_of("at_y"), tables_of("at_z"),
        dealt,
    )

    to_low, to_high = call(
        edge_kernel,
        (shape(17, RY, NZ, dtype=BF16), shape(10, RY, NZ, dtype=BF16)),
        "vvvva",
        (),
        0,
        500_000,
    )(field, seed_magnetic, inverse, saved_magnetic, dealt)
    x_low = passed_along(to_low, "bulk", 1)
    x_high = passed_along(to_high, "bulk", -1)

    low_part, high_part = call(
        corner_kernel,
        (shape(17, 16, NZ, dtype=BF16), shape(10, 16, NZ, dtype=BF16)),
        "vvvvvva",
        [pltpu.VMEM((17, 16, NZ), F32), pltpu.VMEM((10, 16, NZ), F32)],
        0,
        1_000_000,
    )(field, seed_magnetic, inverse, saved_magnetic, x_low, x_high, coef_a)
    shares = call(
        filter_kernel, shape(LANES, LANES, dtype=BF16), "vvvvvvva", (), 40_000_000, 600_000
    )(
        gathered, coef_a, coef_b, tables_of("fwd_x"), tables_of("inv_x"), phase_x, phase_yz,
        low_part,
    )
    back = dealt_near(shares)

    y_low = passed_along(low_part, "wide", 1)
    y_high = passed_along(high_part, "wide", -1)

    sent = call(
        spread_kernel,
        shape(128, 640, dtype=BF16),
        "vvaa",
        [pltpu.VMEM((32, 8, LANES), F32)],
        40_000_000,
        600_000,
    )(back, tables_of("inv_y"), y_low, y_high)
    returned = lax.all_to_all(sent, "wide", split_axis=0, concat_axis=0, tiled=True)
    early, curled, factor, first_grad, ready = call(
        first_kernel,
        (
            shape(3, 10, 24, NZ), shape(3, 10, 24, NZ), shape(10, 24, NZ), shape(*block),
            shape(3, *block),
        ),
        "ssvvvvvvvva",
        [pltpu.VMEM((3, 12, 24, NZ), F32)] * 2 + [pltpu.VMEM((12, 24, NZ), F32)],
        10_000_000,
        3_000_000,
    )(
        monitor_cells, weights, field, seed_magnetic, inverse, saved_magnetic,
        x_low, x_high, y_low, y_high, sent,
    )

    grad_e, grad_h, grad_eps, sources = call(
        second_kernel,
        (shape(3, *block), shape(3, *block), shape(*block), shape(3, 2, 64)),
        "vvvvvvvvv",
        (),
        40_000_000,
        4_000_000,
    )(
        returned, tables_of("back_z"), tables_of("apart"), early, curled, factor, first_grad,
        ready, injected,
    )
    return grad_e, grad_h, grad_eps, sources.transpose(1, 2, 0)


def solution(mesh):
    field = P(None, "bulk", "wide", None)
    return jax.shard_map(
        body,
        mesh=mesh,
        in_specs=(
            field, field, P(None, None, "bulk", "wide", None), P("bulk", "wide", None),
            P(), P(), P(), P(), P(), P(), P(), P(), P(),
        ),
        out_specs=(field, field, P("bulk", "wide", None), P()),
        check_vma=False,
    )
```

```python
import functools
import math

import jax
import jax.numpy as jnp
import ml_dtypes
import numpy as np
from jax import lax
from jax.experimental import pallas as pl
from jax.experimental.pallas import tpu as pltpu
from jax.sharding import PartitionSpec as P

NX, NY, NZ = 256, 256, 128
K = 48
OWN = 3
WIDE, BULK = 16, 32
RX, RY = 8, 16
NEAR, DEPTH, HALVES = 4, 16, 2
SHARE = OWN * K // NEAR
PAD = 40
LANES = 128
F32, BF16 = jnp.float32, jnp.bfloat16
PARAMS = pltpu.CompilerParams(vmem_limit_bytes=40 * 1024 * 1024)
HIGHEST = lax.Precision.HIGHEST


def waves(freqs, places, total):
    phase = np.mod(np.asarray(freqs)[:, None] * np.asarray(places)[None, :], total)
    angle = phase.astype(np.float32) * np.float32(2.0 * math.pi / total)
    return np.cos(angle).astype(np.float32), np.sin(angle).astype(np.float32)


def rounded(table):
    return np.asarray(table, np.float32).astype(ml_dtypes.bfloat16)


def make_tables():
    mode = np.arange(K)
    plane = np.where(mode < K // 2, mode, mode - K)
    cz, sz = waves(mode, np.arange(NZ), NZ)
    cx, sx = (rounded(t) for t in waves(plane, np.arange(NX), NX))
    cy, sy = (rounded(t) for t in waves(plane, np.arange(NY), NY))
    scale = np.float32(1.0 / math.sqrt(NX * NY * NZ))
    back = np.float32(1.0 / math.sqrt(K**3))
    fz, gz = rounded(cz * scale), rounded(-sz * scale)
    bz, hz = rounded(cz * back), rounded(sz * back)
    out = {}
    lift_z = np.zeros((LANES, LANES), ml_dtypes.bfloat16)
    back_z = np.zeros((LANES, LANES), ml_dtypes.bfloat16)
    for w in range(WIDE):
        for i in range(OWN):
            lift_z[:, w * 8 + i] = fz[w * OWN + i]
            lift_z[:, w * 8 + OWN + i] = gz[w * OWN + i]
            back_z[w * 8 + i] = bz[w * OWN + i]
            back_z[w * 8 + OWN + i] = -hz[w * OWN + i]
    out["lift_z"], out["back_z"] = lift_z, back_z

    lane = np.arange(LANES)
    y_of = np.concatenate([(h * 8 + lane % 8) * RY + lane // 8 for h in range(2)])
    fwd_y = np.zeros((512, 256), ml_dtypes.bfloat16)
    fwd_y[:256, :K] = cy[:, y_of].T
    fwd_y[256:, :K] = sy[:, y_of].T
    fwd_y[:256, 128 : 128 + K] = -sy[:, y_of].T
    fwd_y[256:, 128 : 128 + K] = cy[:, y_of].T
    out["fwd_y"] = fwd_y

    fwd_x = np.zeros((HALVES, 2 * LANES, DEPTH * RX), ml_dtypes.bfloat16)
    inv_x = np.zeros((DEPTH // NEAR, HALVES, NEAR * 16, LANES), ml_dtypes.bfloat16)
    for half in range(HALVES):
        for z in range(DEPTH):
            start = (z * HALVES + half) * RX
            here, at = slice(start, start + RX), slice(z * RX, (z + 1) * RX)
            fwd_x[half, :K, at], fwd_x[half, 64 : 64 + K, at] = cx[:, here], -sx[:, here]
            fwd_x[half, 128 : 128 + K, at] = sx[:, here]
            fwd_x[half, 192 : 192 + K, at] = cx[:, here]
            x_of = (start + np.array([0, 1, 2, 3, 4, 5, 6, 7, 8, -1])) % NX
            at = slice(z % NEAR * 16, z % NEAR * 16 + 10)
            inv_x[z // NEAR, half, at, :K] = cx[:, x_of].T
            inv_x[z // NEAR, half, at, 64 : 64 + K] = -sx[:, x_of].T
    out["fwd_x"], out["inv_x"] = fwd_x, inv_x

    inv_y = np.zeros((LANES, 384), ml_dtypes.bfloat16)
    inv_y[:K, :256], inv_y[64 : 64 + K, :256] = cy, -sy
    for w in range(WIDE):
        for h, y in enumerate((w * RY + RY, w * RY - 1)):
            inv_y[:K, 256 + w * 2 + h] = cy[:, y % NY]
            inv_y[64 : 64 + K, 256 + w * 2 + h] = -sy[:, y % NY]
    out["inv_y"] = inv_y
    apart = np.zeros((LANES, 256), ml_dtypes.bfloat16)
    for cell in range(32):
        apart[cell * 2, cell * 8] = 1
        apart[cell * 2 + 1, cell * 8 + 7] = 1
    out["apart"] = apart

    at_x = np.zeros((2, LANES, NX), ml_dtypes.bfloat16)
    at_x[0, :K], at_x[0, 64 : 64 + K] = cx, -sx
    at_x[1, :K], at_x[1, 64 : 64 + K] = sx, cx
    out["at_x"] = at_x
    at_y = np.zeros((NEAR, 2, 48, NY), ml_dtypes.bfloat16)
    for n in range(NEAR):
        j_of = np.arange(n * SHARE, (n + 1) * SHARE) % K
        at_y[n, 0, :SHARE], at_y[n, 1, :SHARE] = cy[j_of], sy[j_of]
    out["at_y"] = at_y
    at_z = np.zeros((WIDE, 2, 16, NZ), ml_dtypes.bfloat16)
    for w in range(WIDE):
        at_z[w, 0, :OWN] = bz[w * OWN : (w + 1) * OWN]
        at_z[w, 1, :OWN] = hz[w * OWN : (w + 1) * OWN]
    out["at_z"] = at_z
    return out


TABLES = make_tables()


def iota(shape, axis):
    return lax.broadcasted_iota(jnp.int32, shape, axis)


def exchange(tiles, block, axis):
    tiles = list(tiles)
    shape = tiles[0].shape
    size = shape[axis]
    place = iota(shape, axis) // block
    step = 1
    while step < len(tiles):
        high = (place // step) % 2 == 1
        new = list(tiles)
        for low in range(len(tiles)):
            if low & step:
                continue
            u, v = tiles[low], tiles[low + step]
            new[low] = jnp.where(high, pltpu.roll(v, step * block, axis), u)
            new[low + step] = jnp.where(high, v, pltpu.roll(u, size - step * block, axis))
        tiles = new
        step *= 2
    return tiles


def z_ahead(v):
    axis = v.ndim - 1
    return jnp.where(iota(v.shape, axis) < NZ - 1, pltpu.roll(v, NZ - 1, axis), 0.0)


def z_behind(v):
    axis = v.ndim - 1
    return jnp.where(iota(v.shape, axis) > 0, pltpu.roll(v, 1, axis), 0.0)


def x_ahead(v):
    return jnp.concatenate([v[1:], v[:1]], 0)


def x_behind(v):
    return jnp.concatenate([v[-1:], v[:-1]], 0)


def y_ahead(v):
    return pltpu.roll(v, v.shape[1] - 1, 1)


def y_behind(v):
    return pltpu.roll(v, 1, 1)


def curl_ahead(fx, fy, fz):
    return (
        (y_ahead(fz) - fz) - (z_ahead(fy) - fy),
        (z_ahead(fx) - fx) - (x_ahead(fz) - fz),
        (x_ahead(fy) - fy) - (y_ahead(fx) - fx),
    )


def curl_behind(fx, fy, fz):
    return (
        (fz - y_behind(fz)) - (fy - z_behind(fy)),
        (fx - z_behind(fx)) - (fz - x_behind(fz)),
        (fy - x_behind(fy)) - (fx - y_behind(fx)),
    )


def place_of(flat):
    return flat >> 15, (flat >> 7) & (NY - 1), flat & (NZ - 1)


def own_block():
    return lax.axis_index("bulk"), lax.axis_index("wide")


def fetch(pairs, sems):
    copies = [pltpu.make_async_copy(a, b, sems.at[i]) for i, (a, b) in enumerate(pairs)]
    for copy in copies:
        copy.start()
    return copies


def scan(cells, hit, act):
    def group(g, carry):
        found = [cells[g * 8 + i] for i in range(8)]
        hits = [hit(*place_of(f)) for f in found]
        some = functools.reduce(jnp.logical_or, hits)

        @pl.when(some)
        def _():
            for i in range(8):
                pl.when(hits[i])(functools.partial(act, g * 8 + i, found[i]))

        return carry

    lax.fori_loop(0, 8, group, 0)


def lift_kernel(mon_in, weights_in, electric, table_in, out, field, mon, weights, table, sems):
    b, w = own_block()
    copies = fetch(
        ((mon_in, mon), (electric, field), (weights_in, weights), (table_in, table)), sems
    )
    for copy in copies:
        copy.wait()
    lane = iota((1, NZ), 1)
    spot = iota((1, 64), 1)

    def hit(x, y, z):
        return ((x >> 3) == b) & ((y >> 4) == w)

    def add(i, flat):
        x, y, z = place_of(flat)
        lx, ly = x & (RX - 1), y & (RY - 1)
        for c in range(3):
            row = field[c, lx, pl.ds(ly, 1), :]
            given = jnp.where(spot == i, weights[c, 1:2, :], 0.0)
            weight = jnp.sum(given, axis=1, keepdims=True)
            field[c, lx, pl.ds(ly, 1), :] = row + jnp.where(lane == z, weight, 0.0)

    scan(mon, hit, add)
    rows = field[...].reshape(3 * RX * RY, NZ).astype(BF16)
    modes = jnp.dot(rows, table[...], preferred_element_type=F32)
    modes = modes.reshape(3, RX, 2, 8, LANES)
    tiles = exchange([modes[:, x].reshape(6, 8, LANES) for x in range(RX)], 1, 1)
    tiles = [t.reshape(3, 2, 8, LANES) for t in tiles]
    tiles = exchange([tiles[y % 8][:, y // 8] for y in range(RY)], 8, 2)
    out[...] = jnp.concatenate([t.reshape(24, LANES) for t in tiles], 0).astype(BF16)


def share_kernel(
    src_in, perm_in, field, magnetic_in, material_in,
    taken, inverse,
    src, perm, magnetic, material, scaled, held, sems,
):
    b, w = own_block()
    copies = fetch(
        (
            (src_in, src), (perm_in, perm), (magnetic_in, magnetic),
            (material_in, material),
        ),
        sems,
    )
    zero = jnp.zeros((12, 32, NZ), F32)
    for c in range(3):
        scaled[c] = zero
        held[c] = zero
    for copy in copies:
        copy.wait()
    eps = jnp.zeros((RX, RY, NZ), F32)
    cells = material[...]
    for level in range(8):
        eps = jnp.where(cells == level, perm[level], eps)
    inv = 1.0 / eps
    inverse[...] = inv
    lane = iota((1, NZ), 1)
    for c in range(3):
        scaled[c, 2:10, 8:24, :] = 0.5 * inv * field[c]
        held[c, 2:10, 8:24, :] = magnetic[c]
    taken[...] = jnp.zeros((8, LANES), F32)
    spot_row, spot_lane = iota((8, LANES), 0), iota((8, LANES), 1)

    def hit(x, y, z):
        lx, ly = x - b * RX, y - w * RY
        return (lx >= -1) & (lx <= RX) & (ly >= -1) & (ly <= RY)

    def take(i, flat):
        x, y, z = place_of(flat)
        lx, ly = x - b * RX, y - w * RY

        def a(c, dx, dy):
            return scaled[c, lx + 2 + dx, pl.ds(ly + 8 + dy, 1), :]

        def h(c, dx, dy):
            old = held[c, lx + 2 + dx, pl.ds(ly + 8 + dy, 1), :]
            if c == 0:
                near = a(1, dx, dy)
                turn = (a(2, dx, dy + 1) - a(2, dx, dy)) - (z_ahead(near) - near)
            elif c == 1:
                near = a(0, dx, dy)
                turn = (z_ahead(near) - near) - (a(2, dx + 1, dy) - a(2, dx, dy))
            else:
                turn = (a(1, dx + 1, dy) - a(1, dx, dy)) - (a(0, dx, dy + 1) - a(0, dx, dy))
            return old + turn

        left = jnp.where(x > 0, 1.0, 0.0)
        down = jnp.where(y > 0, 1.0, 0.0)
        hx, hy, hz = h(0, 0, 0), h(1, 0, 0), h(2, 0, 0)
        hx_y, hz_y = down * h(0, 0, -1), down * h(2, 0, -1)
        hy_x, hz_x = left * h(1, -1, 0), left * h(2, -1, 0)
        curls = (
            (hz - hz_y) - (hy - z_behind(hy)),
            (hx - z_behind(hx)) - (hz - hz_x),
            (hy - hy_x) - (hx - hx_y),
        )
        mine = jnp.where((lx >= 0) & (lx < RX) & (ly >= 0) & (ly < RY), 1.0, 0.0)
        cx, cy = jnp.clip(lx, 0, RX - 1), jnp.clip(ly, 0, RY - 1)
        got = taken[...]
        for c in range(3):
            old = mine * field[c, cx, pl.ds(cy, 1), :]
            for n, row in ((0, old - 0.5 * curls[c]), (1, old)):
                value = jnp.sum(jnp.where(lane == z, row, 0.0), axis=1, keepdims=True)
                spot = (spot_row == n * 3 + c) & (spot_lane == i)
                got = got + jnp.where(spot, value, 0.0)
        taken[...] = got

    scan(src, hit, take)


def middle_kernel(lines, taken, table, out):
    got = lines[...].astype(F32).reshape(WIDE, 24, LANES)
    halves = [exchange([got[h * 8 + i] for i in range(8)], 1, 1) for h in range(2)]
    rows = [
        jnp.concatenate([halves[0][k], halves[1][k], halves[0][OWN + k], halves[1][OWN + k]], 1)
        for k in range(OWN)
    ]
    lhs = jnp.concatenate(rows, 0).astype(BF16)
    found = jnp.dot(lhs, table[...], preferred_element_type=F32)
    lane = iota((8, LANES), 1)
    parts = [[jnp.zeros((8, LANES), F32) for _ in range(2)] for _ in range(NEAR)]
    split = LANES - (NEAR - 1) * SHARE
    for part in range(2):
        for d in range(3):
            piece = [
                found[(k * 3 + d) * 8 : (k * 3 + d) * 8 + 8, part * LANES : (part + 1) * LANES]
                for k in range(OWN)
            ]
            last = pltpu.roll(piece[2], 2 * K, 1)
            first = piece[0] + pltpu.roll(piece[1], K, 1) + jnp.where(lane >= 2 * K, last, 0.0)
            rest = jnp.where(lane < 16, last, 0.0)
            to = d * SHARE
            for n in range(NEAR):
                shift = (to - n * SHARE) % LANES
                moved = pltpu.roll(first, shift, 1) if shift else first
                if n == NEAR - 1:
                    moved = jnp.where(lane < to + split, moved, pltpu.roll(rest, to + split, 1))
                within = (lane >= to) & (lane < to + SHARE)
                parts[n][part] = parts[n][part] + jnp.where(within, moved, 0.0)
    src = jnp.concatenate([taken[...], jnp.zeros((LANES - 8, LANES), F32)], 0).T
    src = jnp.where(iota((LANES, LANES), 1) < 6, src, 0.0)
    high = src.astype(BF16).astype(F32)
    at = 3 * SHARE
    rows = []
    for n in range(NEAR):
        for part, value in enumerate((high, src - high)):
            for i in range(2):
                start = n * 16 + i * 8
                parts[n][part] = parts[n][part] + pltpu.roll(
                    value[start : start + 8], at + i * 6, 1
                )
        rows.append(jnp.concatenate(parts[n], 1))
    deal = jnp.concatenate(rows, 0).astype(BF16)
    for f in range(DEPTH // NEAR):
        out[f * NEAR * 8 : (f + 1) * NEAR * 8, :] = deal


def param_kernel(
    mon, weights, lift, cells, project, gain_x, gain_y, mix, at_x, at_y, at_z, after,
    coef_a, coef_b, phase_x, phase_yz, injected,
):
    b, w = own_block()
    n = b // HALVES % NEAR
    flat = cells[...]
    x, y, z = place_of(flat)
    first = iota((1, LANES), 1) < 64
    hot_x = jnp.where(iota((NX, LANES), 0) == x, 1.0, 0.0)
    real = jnp.where(first, hot_x, 0.0).astype(BF16)
    imag = jnp.where(first, 0.0, hot_x).astype(BF16)
    phase_x[...] = (
        jnp.dot(at_x[0], real, preferred_element_type=F32)
        + jnp.dot(at_x[1], imag, preferred_element_type=F32)
    ).astype(BF16)
    hot_y = jnp.where(iota((NY, LANES), 0) == y, 1.0, 0.0).astype(BF16)
    hot_z = jnp.where(iota((NZ, LANES), 0) == z, 1.0, 0.0).astype(BF16)
    cy = jnp.dot(at_y[n, 0], hot_y, preferred_element_type=F32)[:PAD]
    sy = jnp.dot(at_y[n, 1], hot_y, preferred_element_type=F32)[:PAD]
    cz = jnp.dot(at_z[w, 0], hot_z, preferred_element_type=F32)
    sz = jnp.dot(at_z[w, 1], hot_z, preferred_element_type=F32)
    mode = n * SHARE + iota((PAD, 1), 0)
    ck = jnp.where(mode < K, cz[0:1], jnp.where(mode < 2 * K, cz[1:2], cz[2:3]))
    sk = jnp.where(mode < K, sz[0:1], jnp.where(mode < 2 * K, sz[1:2], sz[2:3]))
    phase_yz[...] = jnp.where(first, cy * ck - sy * sk, -(sy * ck + cy * sk))

    place = iota((K, PAD), 1)
    mode = n * SHARE + place
    depth = jnp.where(mode < K, 0, jnp.where(mode < 2 * K, 1, 2))
    live = place < SHARE
    hot_j = jnp.where((iota((K, PAD), 0) == mode - depth * K) & live, 1.0, 0.0)
    hot_k = jnp.where((iota((K, PAD), 0) == w * OWN + depth) & live, 1.0, 0.0)
    gains = jnp.dot(gain_y[...], hot_j, precision=HIGHEST, preferred_element_type=F32)
    diagonal = iota((16, 16), 0) == iota((16, 16), 1)
    columns = [
        jnp.sum(jnp.where(diagonal, project[e : e + 1, :], 0.0), axis=1, keepdims=True)
        for e in range(3)
    ]
    blank = jnp.zeros((16, 16), F32)
    along = gain_x[...]
    for part, to in ((0, coef_a), (1, coef_b)):
        joined = []
        for d in range(3):
            total = jnp.zeros((16, K), F32)
            for c in range(16):
                total = total + lift[d, c] * mix[part, c].astype(F32)
            joined.append(
                gains * jnp.dot(total, hot_k, precision=HIGHEST, preferred_element_type=F32)
            )
        sign = 1.0 if part == 0 else -1.0
        right = jnp.concatenate([sign * along, blank, along, blank], 1)
        for e in range(3):
            for d in range(3):
                left = (columns[e] * joined[d]).T
                to[(e * 3 + d) * PAD : (e * 3 + d + 1) * PAD, :] = jnp.dot(
                    left, right, precision=HIGHEST, preferred_element_type=F32
                )
    row = iota((8, LANES), 0)
    total = jnp.zeros((8, LANES), F32)
    for i in range(64):
        given = jnp.where(
            row == 0, weights[0, 0, i], jnp.where(row == 1, weights[1, 0, i], weights[2, 0, i])
        )
        total = total + jnp.where((flat == mon[i]) & (row < 3), given, 0.0)
    injected[...] = jnp.where(iota((8, LANES), 1) < 64, total, 0.0)


def filter_kernel(
    own, other, coef_a, coef_b, fwd_x, inv_x, phase_x, phase_yz, after, out
):
    b, w = own_block()
    half, near = b % HALVES, b // HALVES % NEAR
    lane = iota((1, LANES), 1)
    mine, theirs = own[...], other[...]
    both = jnp.dot(fwd_x[half], mine, preferred_element_type=F32) + jnp.dot(
        fwd_x[1 - half], theirs, preferred_element_type=F32
    )
    full = (both[:LANES, :LANES] + both[LANES:, LANES:]).T
    field = [full[d * SHARE : d * SHARE + PAD] for d in range(3)]
    turned = [pltpu.roll(f, 64, 1) for f in field]
    sign = jnp.where(lane < 64, 1.0, -1.0)
    real = []
    for e in range(3):
        q = jnp.zeros((PAD, LANES), F32)
        for d in range(3):
            at = (e * 3 + d) * PAD
            q = q + coef_a[at : at + PAD] * field[d] + coef_b[at : at + PAD] * turned[d]
        real.append(q)
    gap = jnp.zeros((LANES - 3 * SHARE, LANES), F32)
    packed = jnp.concatenate([q[:SHARE] for q in real] + [gap], 0)
    right = jnp.concatenate([packed, pltpu.roll(packed, 64, 1) * sign], 0).astype(BF16)
    back = lax.dot_general(
        inv_x[b // (HALVES * NEAR), half], right, (((1,), (1,)), ((), ())),
        preferred_element_type=F32,
    ).reshape(NEAR, 2, 8, 2 * LANES)

    total = mine.astype(F32).reshape(DEPTH, 8, 2 * LANES).sum(0)
    total = total + theirs.astype(F32).reshape(DEPTH, 8, 2 * LANES).sum(0)
    total = pltpu.roll(total[:, :LANES] + total[:, LANES:], LANES - 3 * SHARE, 1)
    second = pltpu.roll(total, LANES - 6, 1)
    gap = jnp.zeros((LANES - 16, LANES), F32)
    total = jnp.concatenate([total, second, gap], 0)
    total = jnp.where(iota((LANES, LANES), 1) < 6, total, 0.0).T[:8]
    total = pltpu.roll(total, near * 16, 1)
    near = jnp.dot(
        jnp.concatenate(real, 0).astype(BF16), phase_x[...], preferred_element_type=F32
    )
    row = iota((8, LANES), 0)
    for e in range(3):
        line = jnp.sum(near[e * PAD : (e + 1) * PAD] * phase_yz[...], axis=0, keepdims=True)
        line = line + pltpu.roll(line, 64, 1)
        total = total + jnp.where((row == e) & (lane < 64), line, 0.0)
    high = total.astype(BF16).astype(F32)
    extra = pltpu.roll(high + pltpu.roll(total - high, 64, 1), 2, 0)
    extra = jnp.concatenate([extra, jnp.zeros((8, LANES), F32)], 1)
    tiles = []
    for n in range(NEAR):
        tiles += [back[n, 0], back[n, 1] + extra]
    out[...] = jnp.concatenate(tiles, 0).astype(BF16)


def spread_kernel(shares, inv_y, after_low, after_high, out, rows):
    lane = iota((1, LANES), 1)
    got = shares[...].astype(F32).reshape(NEAR, 16, 2 * LANES)
    rows[...] = jnp.zeros((32, 8, LANES), F32)
    for e in range(3):
        flat = []
        for part in range(2):
            start = e * SHARE
            first, rest = jnp.zeros((16, LANES), F32), None
            for n in range(NEAR):
                moved = got[n][:, part * LANES : (part + 1) * LANES]
                if n != e:
                    moved = pltpu.roll(moved, (n * SHARE - start) % LANES, 1)
                within = (lane >= n * SHARE) & (lane < (n + 1) * SHARE)
                first = first + jnp.where(within, moved, 0.0)
                if n == NEAR - 1:
                    rest = jnp.where(lane < 16, moved, 0.0)
            flat.append((first, rest))

        def mode_rows(part, k, to):
            first, rest = flat[part]
            moved = pltpu.roll(first, (to - k * K) % LANES, 1)
            if k < 2:
                return jnp.where((lane >= to) & (lane < to + K), moved, 0.0)
            tail = pltpu.roll(rest, to + 32, 1)
            return jnp.where((lane >= to) & (lane < to + 32), moved, 0.0) + jnp.where(
                (lane >= to + 32) & (lane < to + K), tail, 0.0
            )

        for k in range(OWN):
            real = mode_rows(0, k, 0) + mode_rows(1, k, 64)
            imag = mode_rows(1, k, 0) - mode_rows(0, k, 64)
            for x in range(10):
                rows[e * 10 + x, k : k + 1, :] = real[x : x + 1]
                rows[e * 10 + x, OWN + k : OWN + k + 1, :] = imag[x : x + 1]
    lhs = rows[...].reshape(256, LANES).astype(BF16)
    wide = jnp.dot(lhs, inv_y[...], preferred_element_type=F32).reshape(32, 8, 384)
    near = []
    for low in range(8):
        group = [wide[high * 8 + low, :, c * LANES : (c + 1) * LANES] for high in range(4) for c in range(2)]
        near.append(jnp.stack(group))
    near = exchange(near, 16, 2)
    edge = []
    for low in range(16):
        edge.append(jnp.stack([wide[high * 16 + low, :, 256:384] for high in range(2)]))
    edge = exchange(edge, 2, 2)
    row = iota((8, LANES), 0)
    total = pltpu.roll(got[:, 8:16, :LANES].sum(0), 6, 0)
    total = jnp.where((row < 6) & (lane < 64), total + pltpu.roll(total, 64, 1), 0.0)
    high = total.astype(BF16).astype(F32)
    other = pltpu.roll(total - high, 64, 1)
    moved = pltpu.roll(high, 64, 1)
    low = total - high
    extra = []
    for t in range(3):
        first = jnp.where(lane < 64, high[2 * t : 2 * t + 1], moved[2 * t + 1 : 2 * t + 2])
        second = jnp.where(lane < 64, low[2 * t : 2 * t + 1], other[2 * t + 1 : 2 * t + 2])
        extra.append(jnp.where(row == 6, first, jnp.where(row == 7, second, 0.0)))
    blocks = []
    for w in range(WIDE):
        tiles = [near[w % 8][high_x * 2 + w // 8] for high_x in range(4)]
        for t in range(3):
            tiles[t] = tiles[t] + extra[t]
        pair = jnp.where(lane < 32, edge[w], 0.0)
        tiles.append(pair[0] + pltpu.roll(pair[1], 32, 1))
        blocks.append(jnp.concatenate(tiles, 1))
    out[...] = jnp.concatenate(blocks, 0).astype(BF16)


def high_planes(across):
    first, second = [c for c in range(3) if c != across]
    planes = [(c, 0) for c in range(3)] + [(first, 1), (second, 1), (6, 0), (6, 1)]
    return planes + [(3 + c, 0) for c in range(3)]


def low_planes(across):
    first, second = [c for c in range(3) if c != across]
    planes = [(c, i) for i in range(2) for c in range(3)] + [(6, 0), (6, 1)]
    return planes + [(3 + first, 0), (3 + second, 0)] + [(3 + c, 1) for c in range(3)]


def edge_kernel(electric, magnetic, inverse, saved, after, to_low, to_high):
    def own(f):
        return electric.at[f] if f < 3 else (magnetic.at[f - 3] if f < 6 else inverse)

    for p, (f, i) in enumerate(low_planes(0)):
        to_low[p] = own(f)[6 + i].astype(BF16)
    for n in range(2):
        for c in range(2):
            to_low[13 + 2 * n + c] = saved[n, 1 + c, 7]
    for p, (f, i) in enumerate(high_planes(0)):
        to_high[p] = own(f)[i].astype(BF16)


def corner_kernel(
    electric, magnetic, inverse, saved, x_low, x_high, after, to_low, to_high, low, high
):
    x_of = [{}, {}]
    for p, key in enumerate(low_planes(0)):
        x_of[0][key] = x_low[p].astype(F32)
    for p, key in enumerate(high_planes(0)):
        x_of[1][key] = x_high[p].astype(F32)
    low[...] = jnp.zeros(low.shape, F32)
    high[...] = jnp.zeros(high.shape, F32)
    for to, planes, start in ((low, low_planes(1), 14), (high, high_planes(1), 0)):
        for p, (f, i) in enumerate(planes):
            own = electric.at[f] if f < 3 else (magnetic.at[f - 3] if f < 6 else inverse)
            row = start + i
            to[p, 0:8, :] = own[:, row, :]
            for side, at in ((1, 8), (0, 10)):
                for layer in range(2):
                    if (f, layer) in x_of[side]:
                        got = x_of[side][(f, layer)]
                        to[p, at + layer : at + layer + 1, :] = got[row : row + 1]
    for n in range(2):
        for i, c in enumerate((0, 2)):
            low[13 + 2 * n + i, 0:8, :] = saved[n, c].astype(F32)[:, RY - 1, :]
    to_low[...] = low[...].astype(BF16)
    to_high[...] = high[...].astype(BF16)


def first_kernel(
    mon, weights, electric, magnetic, inverse, saved, x_low, x_high, y_low, y_high, after,
    early, curled, factor, grad, ready, e_ext, h_ext, g_ext,
):
    b, w = own_block()
    lane = iota((1, NZ), 1)
    zero = jnp.zeros((12, 24, NZ), F32)
    for c in range(7):
        to = e_ext.at[c] if c < 3 else (h_ext.at[c - 3] if c < 6 else g_ext)
        to[...] = zero
        own = electric[c] if c < 3 else (magnetic[c - 3] if c < 6 else inverse[...])
        to[0:8, 0:16, :] = own
        for planes, ref, at in ((high_planes(0), x_high, 8), (low_planes(0), x_low, 10)):
            for p, (f, i) in enumerate(planes):
                if f == c:
                    to[at + i, 0:16, :] = ref[p].astype(F32)
        for planes, ref, at in ((high_planes(1), y_high, 16), (low_planes(1), y_low, 22)):
            for p, (f, i) in enumerate(planes):
                if f == c:
                    to[:, at + i : at + i + 1, :] = ref[p].astype(F32)[0:12][:, None, :]

    g = g_ext[...]
    half = 0.5 * g
    a = [half * e_ext[c] for c in range(3)]
    spot_x = iota((12, 24, 1), 0)
    spot_y = iota((12, 24, 1), 1)
    outside = ((spot_x >= 10) & (b == 0)) | ((spot_y >= 22) & (w == 0))
    inside = jnp.where(outside, 0.0, 1.0)
    turned = curl_ahead(*a)
    h = [h_ext[c] + inside * turned[c] for c in range(3)]
    back = curl_behind(*h)
    for c in range(3):
        e_ext[c] = e_ext[c] - 0.5 * back[c]

    def hit(x, y, z):
        lx, ly = x - b * RX, y - w * RY
        return (lx >= -2) & (lx < RX + 2) & (ly >= -2) & (ly < RY + 2)

    def add(i, flat):
        x, y, z = place_of(flat)
        lx, ly = x - b * RX, y - w * RY
        px = jnp.where(lx < 0, lx + 12, lx)
        py = jnp.where(ly < 0, ly + 24, ly)
        for c in range(3):
            row = e_ext[c, px, pl.ds(py, 1), :]
            e_ext[c, px, pl.ds(py, 1), :] = row + jnp.where(lane == z, weights[c, 0, i], 0.0)

    scan(mon, hit, add)
    for c in range(3):
        early[c, 0:9] = e_ext[c, 0:9]
        early[c, 9:10] = e_ext[c, 11:12]
        curled[c, 0:9] = h[c][0:9]
        curled[c, 9:10] = h[c][11:12]
    factor[0:9] = half[0:9]
    factor[9:10] = half[11:12]

    near = inverse[...]
    for step in range(2):
        s = [saved[step, c].astype(F32) for c in range(3)]
        before_x = {c: jnp.concatenate([x_low[12 + 2 * step + c].astype(F32)[None], s[c][:-1]], 0) for c in (1, 2)}
        before_y = {}
        for c in (0, 2):
            edge = y_low[13 + 2 * step + c // 2].astype(F32)[0:8][:, None, :]
            first = iota((RX, RY, NZ), 1) == 0
            before_y[c] = jnp.where(first, edge, pltpu.roll(s[c], 1, 1))
        curls = (
            (s[2] - before_y[2]) - (s[1] - z_behind(s[1])),
            (s[0] - z_behind(s[0])) - (s[2] - before_x[2]),
            (s[1] - before_x[1]) - (s[0] - before_y[0]),
        )
        if step == 0:
            for c in range(3):
                ready[c] = near * curls[c]
        else:
            total = jnp.zeros((RX, RY, NZ), F32)
            for c in range(3):
                total = total + a[c][0:8, 0:16] * near * curls[c]
            grad[...] = -total


def second_kernel(
    lines, table, apart, early, curled, factor, first_grad, ready, injected,
    grad_e, grad_h, grad_eps, sources,
):
    b, w = own_block()
    turn = (((0,), (0,)), ((), ()))
    main = lax.dot_general(lines[:, 0:512], table[...], turn, preferred_element_type=F32)
    main = main.reshape(32, 16, NZ)
    edge = jnp.dot(lines[:, 512:640], apart[...], preferred_element_type=F32).astype(BF16)
    edge = lax.dot_general(edge, table[...], turn, preferred_element_type=F32)
    edge = edge.reshape(32, 8, NZ)
    half = factor[...]
    e1 = []
    for c in range(3):
        at = slice(c * 10, c * 10 + 10)
        e1.append(early[c] + jnp.concatenate([main[at], edge[at]], 1))
    a = [half * e for e in e1]
    spot_x = iota((10, 24, 1), 0)
    spot_y = iota((10, 24, 1), 1)
    outside = ((spot_x == 9) & (b == 0)) | ((spot_y == 23) & (w == 0))
    inside = jnp.where(outside, 0.0, 1.0)
    turned = curl_ahead(*a)
    h = [curled[c] + inside * turned[c] for c in range(3)]
    backed = curl_behind(*h)
    total = first_grad[...]
    for c in range(3):
        grad_h[c] = h[c][0:8, 0:16]
        grad_e[c] = e1[c][0:8, 0:16] - 0.5 * backed[c][0:8, 0:16]
        total = total - a[c][0:8, 0:16] * ready[c]
    grad_eps[...] = total
    got = lines[:, 0:384].astype(F32).reshape(WIDE, 8, 384).sum(0)
    got = got[6:7] + got[7:8]
    moved = pltpu.roll(got, 384 - 64, 1)
    for n in range(2):
        for c in range(3):
            at = n * 3 + c
            line = got if at % 2 == 0 else moved
            line = line[:, at // 2 * LANES : (at // 2 + 1) * LANES]
            if n == 0:
                line = line + injected[c : c + 1, :]
            sources[c, n : n + 1, :] = line[:, 0:64]


def call(kernel, outs, places, scratch=(), flops=0, moved=0, params=PARAMS):
    spaces = {"s": pltpu.SMEM, "v": pltpu.VMEM, "a": pl.ANY}
    return pl.pallas_call(
        kernel,
        out_shape=outs,
        in_specs=[pl.BlockSpec(memory_space=spaces[p]) for p in places],
        out_specs=jax.tree.map(lambda _: pl.BlockSpec(memory_space=pltpu.VMEM), outs),
        scratch_shapes=list(scratch),
        compiler_params=params,
        cost_estimate=pl.CostEstimate(flops=flops, bytes_accessed=moved, transcendentals=0),
    )


def shape(*dims, dtype=F32):
    return jax.ShapeDtypeStruct(dims, dtype)


def passed_along(block, axis, distance):
    devices = range(lax.axis_size(axis))
    route = [(i - distance, i) for i in devices if i - distance in devices]
    return lax.ppermute(block, axis, route)


def dealt_near(block):
    groups = [
        [(f * NEAR + n) * HALVES + half for n in range(NEAR)]
        for f in range(DEPTH // NEAR)
        for half in range(HALVES)
    ]
    return lax.all_to_all(
        block, "bulk", split_axis=0, concat_axis=0, axis_index_groups=groups, tiled=True
    )


def dealt_along(block):
    groups = [[z * HALVES + half for z in range(DEPTH)] for half in range(HALVES)]
    return lax.all_to_all(
        block, "bulk", split_axis=0, concat_axis=0, axis_index_groups=groups, tiled=True
    )


def tables_of(name):
    return jnp.asarray(TABLES[name])


def body(
    seed_electric, seed_magnetic, saved_magnetic, material, permittivity, source_cells,
    monitor_cells, monitor_weights, lift_weight, project_weight, mode_mix, gain_first, gain_second,
):
    weights = monitor_weights.transpose(2, 0, 1)
    big, dma = pltpu.CompilerParams(vmem_limit_bytes=56 * 1024 * 1024), pltpu.SemaphoreType.DMA
    block = (RX, RY, NZ)

    payload, field = call(
        lift_kernel,
        (shape(384, LANES, dtype=BF16), shape(3, *block)),
        "aaaa",
        [
            pltpu.SMEM((64,), jnp.int32), pltpu.VMEM((3, 2, 64), F32),
            pltpu.VMEM((LANES, LANES), BF16), dma((4,)),
        ],
        13_000_000,
        500_000,
        big,
    )(monitor_cells, weights, seed_electric, tables_of("lift_z"))
    lines = lax.all_to_all(payload, "wide", split_axis=0, concat_axis=0, tiled=True)

    taken, inverse = call(
        share_kernel,
        (shape(8, LANES), shape(*block)),
        "aavaa",
        [
            pltpu.SMEM((64,), jnp.int32), pltpu.SMEM((8,), F32), pltpu.VMEM((3, *block), F32),
            pltpu.VMEM(block, jnp.int32), pltpu.VMEM((3, 12, 32, NZ), F32),
            pltpu.VMEM((3, 12, 32, NZ), F32), dma((4,)),
        ],
        3_000_000,
        1_500_000,
    )(source_cells, permittivity, field, seed_magnetic, material)

    dealt = call(
        middle_kernel, shape(DEPTH * 8, 2 * LANES, dtype=BF16), "vvv", (), 20_000_000, 400_000
    )(lines, taken, tables_of("fwd_y"))
    mine = dealt_along(dealt)
    theirs = lax.ppermute(mine, "bulk", [(i, i ^ 1) for i in range(BULK)])

    cells = jnp.concatenate([source_cells, source_cells]).reshape(1, LANES)
    coef_a, coef_b, phase_x, phase_yz, injected = call(
        param_kernel,
        (
            shape(9 * PAD, LANES), shape(9 * PAD, LANES), shape(LANES, LANES, dtype=BF16),
            shape(PAD, LANES), shape(8, LANES),
        ),
        "sssvvvvvvvva",
        (),
        20_000_000,
        1_000_000,
    )(
        monitor_cells, weights, lift_weight.T, cells, project_weight, gain_first, gain_second,
        mode_mix.transpose(0, 2, 3, 1), tables_of("at_x"), tables_of("at_y"), tables_of("at_z"),
        dealt,
    )

    to_low, to_high = call(
        edge_kernel,
        (shape(17, RY, NZ, dtype=BF16), shape(10, RY, NZ, dtype=BF16)),
        "vvvva",
        (),
        0,
        500_000,
    )(field, seed_magnetic, inverse, saved_magnetic, dealt)
    x_low = passed_along(to_low, "bulk", 1)
    x_high = passed_along(to_high, "bulk", -1)

    low_part, high_part = call(
        corner_kernel,
        (shape(17, 16, NZ, dtype=BF16), shape(10, 16, NZ, dtype=BF16)),
        "vvvvvva",
        [pltpu.VMEM((17, 16, NZ), F32), pltpu.VMEM((10, 16, NZ), F32)],
        0,
        1_000_000,
    )(field, seed_magnetic, inverse, saved_magnetic, x_low, x_high, coef_a)
    shares = call(
        filter_kernel, shape(NEAR * 16, 2 * LANES, dtype=BF16), "vvvvvvvva", (), 40_000_000, 600_000
    )(
        mine, theirs, coef_a, coef_b, tables_of("fwd_x"), tables_of("inv_x"), phase_x, phase_yz,
        low_part,
    )
    back = dealt_near(shares)

    y_low = passed_along(low_part, "wide", 1)
    y_high = passed_along(high_part, "wide", -1)

    sent = call(
        spread_kernel,
        shape(128, 640, dtype=BF16),
        "vvaa",
        [pltpu.VMEM((32, 8, LANES), F32)],
        40_000_000,
        600_000,
    )(back, tables_of("inv_y"), y_low, y_high)
    returned = lax.all_to_all(sent, "wide", split_axis=0, concat_axis=0, tiled=True)
    early, curled, factor, first_grad, ready = call(
        first_kernel,
        (
            shape(3, 10, 24, NZ), shape(3, 10, 24, NZ), shape(10, 24, NZ), shape(*block),
            shape(3, *block),
        ),
        "ssvvvvvvvva",
        [pltpu.VMEM((3, 12, 24, NZ), F32)] * 2 + [pltpu.VMEM((12, 24, NZ), F32)],
        10_000_000,
        3_000_000,
    )(
        monitor_cells, weights, field, seed_magnetic, inverse, saved_magnetic,
        x_low, x_high, y_low, y_high, sent,
    )

    grad_e, grad_h, grad_eps, sources = call(
        second_kernel,
        (shape(3, *block), shape(3, *block), shape(*block), shape(3, 2, 64)),
        "vvvvvvvvv",
        (),
        40_000_000,
        4_000_000,
    )(
        returned, tables_of("back_z"), tables_of("apart"), early, curled, factor, first_grad,
        ready, injected,
    )
    return grad_e, grad_h, grad_eps, sources.transpose(1, 2, 0)


def solution(mesh):
    field = P(None, "bulk", "wide", None)
    return jax.shard_map(
        body,
        mesh=mesh,
        in_specs=(
            field, field, P(None, None, "bulk", "wide", None), P("bulk", "wide", None),
            P(), P(), P(), P(), P(), P(), P(), P(), P(),
        ),
        out_specs=(field, field, P("bulk", "wide", None), P()),
        check_vma=False,
    )
```

```python
import functools
import math

import jax
import jax.numpy as jnp
import ml_dtypes
import numpy as np
from jax import lax
from jax.experimental import pallas as pl
from jax.experimental.pallas import tpu as pltpu
from jax.sharding import PartitionSpec as P

NX, NY, NZ = 256, 256, 128
K = 48
OWN = 3
WIDE, BULK = 16, 32
RX, RY = 8, 16
NEAR, DEPTH, HALVES = 4, 16, 2
SHARE = OWN * K // NEAR
PAD = 40
LANES = 128
F32, BF16 = jnp.float32, jnp.bfloat16
PARAMS = pltpu.CompilerParams(vmem_limit_bytes=40 * 1024 * 1024)
HIGHEST = lax.Precision.HIGHEST


def waves(freqs, places, total):
    phase = np.mod(np.asarray(freqs)[:, None] * np.asarray(places)[None, :], total)
    angle = phase.astype(np.float32) * np.float32(2.0 * math.pi / total)
    return np.cos(angle).astype(np.float32), np.sin(angle).astype(np.float32)


def rounded(table):
    return np.asarray(table, np.float32).astype(ml_dtypes.bfloat16)


def make_tables():
    mode = np.arange(K)
    plane = np.where(mode < K // 2, mode, mode - K)
    cz, sz = waves(mode, np.arange(NZ), NZ)
    cx, sx = (rounded(t) for t in waves(plane, np.arange(NX), NX))
    cy, sy = (rounded(t) for t in waves(plane, np.arange(NY), NY))
    scale = np.float32(1.0 / math.sqrt(NX * NY * NZ))
    back = np.float32(1.0 / math.sqrt(K**3))
    fz, gz = rounded(cz * scale), rounded(-sz * scale)
    bz, hz = rounded(cz * back), rounded(sz * back)
    out = {}
    lift_z = np.zeros((LANES, LANES), ml_dtypes.bfloat16)
    back_z = np.zeros((LANES, LANES), ml_dtypes.bfloat16)
    for w in range(WIDE):
        for i in range(OWN):
            lift_z[:, w * 8 + i] = fz[w * OWN + i]
            lift_z[:, w * 8 + OWN + i] = gz[w * OWN + i]
            back_z[w * 8 + i] = bz[w * OWN + i]
            back_z[w * 8 + OWN + i] = -hz[w * OWN + i]
    out["lift_z"], out["back_z"] = lift_z, back_z

    lane = np.arange(LANES)
    y_of = np.concatenate([(h * 8 + lane % 8) * RY + lane // 8 for h in range(2)])
    fwd_y = np.zeros((512, 256), ml_dtypes.bfloat16)
    fwd_y[:256, :K] = cy[:, y_of].T
    fwd_y[256:, :K] = sy[:, y_of].T
    fwd_y[:256, 128 : 128 + K] = -sy[:, y_of].T
    fwd_y[256:, 128 : 128 + K] = cy[:, y_of].T
    out["fwd_y"] = fwd_y

    fwd_x = np.zeros((2 * LANES, NX), ml_dtypes.bfloat16)
    fwd_x[:K], fwd_x[64 : 64 + K] = cx, -sx
    fwd_x[128 : 128 + K], fwd_x[192 : 192 + K] = sx, cx
    inv_x = np.zeros((DEPTH // NEAR, HALVES, NEAR * 16, LANES), ml_dtypes.bfloat16)
    for half in range(HALVES):
        for z in range(DEPTH):
            start = (z * HALVES + half) * RX
            x_of = (start + np.array([0, 1, 2, 3, 4, 5, 6, 7, 8, -1])) % NX
            at = slice(z % NEAR * 16, z % NEAR * 16 + 10)
            inv_x[z // NEAR, half, at, :K] = cx[:, x_of].T
            inv_x[z // NEAR, half, at, 64 : 64 + K] = -sx[:, x_of].T
    out["fwd_x"], out["inv_x"] = fwd_x, inv_x

    inv_y = np.zeros((LANES, 384), ml_dtypes.bfloat16)
    inv_y[:K, :256], inv_y[64 : 64 + K, :256] = cy, -sy
    for w in range(WIDE):
        for h, y in enumerate((w * RY + RY, w * RY - 1)):
            inv_y[:K, 256 + w * 2 + h] = cy[:, y % NY]
            inv_y[64 : 64 + K, 256 + w * 2 + h] = -sy[:, y % NY]
    out["inv_y"] = inv_y
    apart = np.zeros((LANES, 256), ml_dtypes.bfloat16)
    for cell in range(32):
        apart[cell * 2, cell * 8] = 1
        apart[cell * 2 + 1, cell * 8 + 7] = 1
    out["apart"] = apart

    at_x = np.zeros((2, LANES, NX), ml_dtypes.bfloat16)
    at_x[0, :K], at_x[0, 64 : 64 + K] = cx, -sx
    at_x[1, :K], at_x[1, 64 : 64 + K] = sx, cx
    out["at_x"] = at_x
    at_y = np.zeros((NEAR, 2, 48, NY), ml_dtypes.bfloat16)
    for n in range(NEAR):
        j_of = np.arange(n * SHARE, (n + 1) * SHARE) % K
        at_y[n, 0, :SHARE], at_y[n, 1, :SHARE] = cy[j_of], sy[j_of]
    out["at_y"] = at_y
    at_z = np.zeros((WIDE, 2, 16, NZ), ml_dtypes.bfloat16)
    for w in range(WIDE):
        at_z[w, 0, :OWN] = bz[w * OWN : (w + 1) * OWN]
        at_z[w, 1, :OWN] = hz[w * OWN : (w + 1) * OWN]
    out["at_z"] = at_z
    return out


TABLES = make_tables()


def iota(shape, axis):
    return lax.broadcasted_iota(jnp.int32, shape, axis)


def exchange(tiles, block, axis):
    tiles = list(tiles)
    shape = tiles[0].shape
    size = shape[axis]
    place = iota(shape, axis) // block
    step = 1
    while step < len(tiles):
        high = (place // step) % 2 == 1
        new = list(tiles)
        for low in range(len(tiles)):
            if low & step:
                continue
            u, v = tiles[low], tiles[low + step]
            new[low] = jnp.where(high, pltpu.roll(v, step * block, axis), u)
            new[low + step] = jnp.where(high, v, pltpu.roll(u, size - step * block, axis))
        tiles = new
        step *= 2
    return tiles


def z_ahead(v):
    axis = v.ndim - 1
    return jnp.where(iota(v.shape, axis) < NZ - 1, pltpu.roll(v, NZ - 1, axis), 0.0)


def z_behind(v):
    axis = v.ndim - 1
    return jnp.where(iota(v.shape, axis) > 0, pltpu.roll(v, 1, axis), 0.0)


def x_ahead(v):
    return jnp.concatenate([v[1:], v[:1]], 0)


def x_behind(v):
    return jnp.concatenate([v[-1:], v[:-1]], 0)


def y_ahead(v):
    return pltpu.roll(v, v.shape[1] - 1, 1)


def y_behind(v):
    return pltpu.roll(v, 1, 1)


def curl_ahead(fx, fy, fz):
    return (
        (y_ahead(fz) - fz) - (z_ahead(fy) - fy),
        (z_ahead(fx) - fx) - (x_ahead(fz) - fz),
        (x_ahead(fy) - fy) - (y_ahead(fx) - fx),
    )


def curl_behind(fx, fy, fz):
    return (
        (fz - y_behind(fz)) - (fy - z_behind(fy)),
        (fx - z_behind(fx)) - (fz - x_behind(fz)),
        (fy - x_behind(fy)) - (fx - y_behind(fx)),
    )


def place_of(flat):
    return flat >> 15, (flat >> 7) & (NY - 1), flat & (NZ - 1)


def own_block():
    return lax.axis_index("bulk"), lax.axis_index("wide")


def fetch(pairs, sems):
    copies = [pltpu.make_async_copy(a, b, sems.at[i]) for i, (a, b) in enumerate(pairs)]
    for copy in copies:
        copy.start()
    return copies


def scan(cells, hit, act):
    def group(g, carry):
        found = [cells[g * 8 + i] for i in range(8)]
        hits = [hit(*place_of(f)) for f in found]
        some = functools.reduce(jnp.logical_or, hits)

        @pl.when(some)
        def _():
            for i in range(8):
                pl.when(hits[i])(functools.partial(act, g * 8 + i, found[i]))

        return carry

    lax.fori_loop(0, 8, group, 0)


def lift_kernel(mon_in, weights_in, electric, table_in, out, field, mon, weights, table, sems):
    b, w = own_block()
    copies = fetch(
        ((mon_in, mon), (electric, field), (weights_in, weights), (table_in, table)), sems
    )
    for copy in copies:
        copy.wait()
    lane = iota((1, NZ), 1)
    spot = iota((1, 64), 1)

    def hit(x, y, z):
        return ((x >> 3) == b) & ((y >> 4) == w)

    def add(i, flat):
        x, y, z = place_of(flat)
        lx, ly = x & (RX - 1), y & (RY - 1)
        for c in range(3):
            row = field[c, lx, pl.ds(ly, 1), :]
            given = jnp.where(spot == i, weights[c, 1:2, :], 0.0)
            weight = jnp.sum(given, axis=1, keepdims=True)
            field[c, lx, pl.ds(ly, 1), :] = row + jnp.where(lane == z, weight, 0.0)

    scan(mon, hit, add)
    rows = field[...].reshape(3 * RX * RY, NZ).astype(BF16)
    modes = jnp.dot(rows, table[...], preferred_element_type=F32)
    modes = modes.reshape(3, RX, 2, 8, LANES)
    tiles = exchange([modes[:, x].reshape(6, 8, LANES) for x in range(RX)], 1, 1)
    tiles = [t.reshape(3, 2, 8, LANES) for t in tiles]
    tiles = exchange([tiles[y % 8][:, y // 8] for y in range(RY)], 8, 2)
    out[...] = jnp.concatenate([t.reshape(24, LANES) for t in tiles], 0).astype(BF16)


def share_kernel(
    src_in, perm_in, field, magnetic_in, material_in,
    taken, inverse,
    src, perm, magnetic, material, scaled, held, sems,
):
    b, w = own_block()
    copies = fetch(
        (
            (src_in, src), (perm_in, perm), (magnetic_in, magnetic),
            (material_in, material),
        ),
        sems,
    )
    zero = jnp.zeros((12, 32, NZ), F32)
    for c in range(3):
        scaled[c] = zero
        held[c] = zero
    for copy in copies:
        copy.wait()
    eps = jnp.zeros((RX, RY, NZ), F32)
    cells = material[...]
    for level in range(8):
        eps = jnp.where(cells == level, perm[level], eps)
    inv = 1.0 / eps
    inverse[...] = inv
    lane = iota((1, NZ), 1)
    for c in range(3):
        scaled[c, 2:10, 8:24, :] = 0.5 * inv * field[c]
        held[c, 2:10, 8:24, :] = magnetic[c]
    taken[...] = jnp.zeros((8, LANES), F32)
    spot_row, spot_lane = iota((8, LANES), 0), iota((8, LANES), 1)

    def hit(x, y, z):
        lx, ly = x - b * RX, y - w * RY
        return (lx >= -1) & (lx <= RX) & (ly >= -1) & (ly <= RY)

    def take(i, flat):
        x, y, z = place_of(flat)
        lx, ly = x - b * RX, y - w * RY

        def a(c, dx, dy):
            return scaled[c, lx + 2 + dx, pl.ds(ly + 8 + dy, 1), :]

        def h(c, dx, dy):
            old = held[c, lx + 2 + dx, pl.ds(ly + 8 + dy, 1), :]
            if c == 0:
                near = a(1, dx, dy)
                turn = (a(2, dx, dy + 1) - a(2, dx, dy)) - (z_ahead(near) - near)
            elif c == 1:
                near = a(0, dx, dy)
                turn = (z_ahead(near) - near) - (a(2, dx + 1, dy) - a(2, dx, dy))
            else:
                turn = (a(1, dx + 1, dy) - a(1, dx, dy)) - (a(0, dx, dy + 1) - a(0, dx, dy))
            return old + turn

        left = jnp.where(x > 0, 1.0, 0.0)
        down = jnp.where(y > 0, 1.0, 0.0)
        hx, hy, hz = h(0, 0, 0), h(1, 0, 0), h(2, 0, 0)
        hx_y, hz_y = down * h(0, 0, -1), down * h(2, 0, -1)
        hy_x, hz_x = left * h(1, -1, 0), left * h(2, -1, 0)
        curls = (
            (hz - hz_y) - (hy - z_behind(hy)),
            (hx - z_behind(hx)) - (hz - hz_x),
            (hy - hy_x) - (hx - hx_y),
        )
        mine = jnp.where((lx >= 0) & (lx < RX) & (ly >= 0) & (ly < RY), 1.0, 0.0)
        cx, cy = jnp.clip(lx, 0, RX - 1), jnp.clip(ly, 0, RY - 1)
        got = taken[...]
        for c in range(3):
            old = mine * field[c, cx, pl.ds(cy, 1), :]
            for n, row in ((0, old - 0.5 * curls[c]), (1, old)):
                value = jnp.sum(jnp.where(lane == z, row, 0.0), axis=1, keepdims=True)
                spot = (spot_row == n * 3 + c) & (spot_lane == i)
                got = got + jnp.where(spot, value, 0.0)
        taken[...] = got

    scan(src, hit, take)


def middle_kernel(lines, taken, table, out):
    got = lines[...].astype(F32).reshape(WIDE, 24, LANES)
    halves = [exchange([got[h * 8 + i] for i in range(8)], 1, 1) for h in range(2)]
    rows = [
        jnp.concatenate([halves[0][k], halves[1][k], halves[0][OWN + k], halves[1][OWN + k]], 1)
        for k in range(OWN)
    ]
    lhs = jnp.concatenate(rows, 0).astype(BF16)
    found = jnp.dot(lhs, table[...], preferred_element_type=F32)
    lane = iota((8, LANES), 1)
    parts = [[jnp.zeros((8, LANES), F32) for _ in range(2)] for _ in range(NEAR)]
    split = LANES - (NEAR - 1) * SHARE
    for part in range(2):
        for d in range(3):
            piece = [
                found[(k * 3 + d) * 8 : (k * 3 + d) * 8 + 8, part * LANES : (part + 1) * LANES]
                for k in range(OWN)
            ]
            last = pltpu.roll(piece[2], 2 * K, 1)
            first = piece[0] + pltpu.roll(piece[1], K, 1) + jnp.where(lane >= 2 * K, last, 0.0)
            rest = jnp.where(lane < 16, last, 0.0)
            to = d * SHARE
            for n in range(NEAR):
                shift = (to - n * SHARE) % LANES
                moved = pltpu.roll(first, shift, 1) if shift else first
                if n == NEAR - 1:
                    moved = jnp.where(lane < to + split, moved, pltpu.roll(rest, to + split, 1))
                within = (lane >= to) & (lane < to + SHARE)
                parts[n][part] = parts[n][part] + jnp.where(within, moved, 0.0)
    src = jnp.concatenate([taken[...], jnp.zeros((LANES - 8, LANES), F32)], 0).T
    src = jnp.where(iota((LANES, LANES), 1) < 6, src, 0.0)
    high = src.astype(BF16).astype(F32)
    at = 3 * SHARE
    rows = []
    for n in range(NEAR):
        for part, value in enumerate((high, src - high)):
            for i in range(2):
                start = n * 16 + i * 8
                parts[n][part] = parts[n][part] + pltpu.roll(
                    value[start : start + 8], at + i * 6, 1
                )
        rows.append(jnp.concatenate(parts[n], 1))
    deal = jnp.concatenate([r for r in rows for _ in range(HALVES)], 0).astype(BF16)
    size = NEAR * HALVES * 8
    for f in range(DEPTH // NEAR):
        out[f * size : (f + 1) * size, :] = deal


def param_kernel(
    mon, weights, lift, cells, project, gain_x, gain_y, mix, at_x, at_y, at_z, after,
    coef_a, coef_b, phase_x, phase_yz, injected,
):
    b, w = own_block()
    n = b // HALVES % NEAR
    flat = cells[...]
    x, y, z = place_of(flat)
    first = iota((1, LANES), 1) < 64
    hot_x = jnp.where(iota((NX, LANES), 0) == x, 1.0, 0.0)
    real = jnp.where(first, hot_x, 0.0).astype(BF16)
    imag = jnp.where(first, 0.0, hot_x).astype(BF16)
    phase_x[...] = (
        jnp.dot(at_x[0], real, preferred_element_type=F32)
        + jnp.dot(at_x[1], imag, preferred_element_type=F32)
    ).astype(BF16)
    hot_y = jnp.where(iota((NY, LANES), 0) == y, 1.0, 0.0).astype(BF16)
    hot_z = jnp.where(iota((NZ, LANES), 0) == z, 1.0, 0.0).astype(BF16)
    cy = jnp.dot(at_y[n, 0], hot_y, preferred_element_type=F32)[:PAD]
    sy = jnp.dot(at_y[n, 1], hot_y, preferred_element_type=F32)[:PAD]
    cz = jnp.dot(at_z[w, 0], hot_z, preferred_element_type=F32)
    sz = jnp.dot(at_z[w, 1], hot_z, preferred_element_type=F32)
    mode = n * SHARE + iota((PAD, 1), 0)
    ck = jnp.where(mode < K, cz[0:1], jnp.where(mode < 2 * K, cz[1:2], cz[2:3]))
    sk = jnp.where(mode < K, sz[0:1], jnp.where(mode < 2 * K, sz[1:2], sz[2:3]))
    phase_yz[...] = jnp.where(first, cy * ck - sy * sk, -(sy * ck + cy * sk))

    place = iota((K, PAD), 1)
    mode = n * SHARE + place
    depth = jnp.where(mode < K, 0, jnp.where(mode < 2 * K, 1, 2))
    live = place < SHARE
    hot_j = jnp.where((iota((K, PAD), 0) == mode - depth * K) & live, 1.0, 0.0)
    hot_k = jnp.where((iota((K, PAD), 0) == w * OWN + depth) & live, 1.0, 0.0)
    gains = jnp.dot(gain_y[...], hot_j, precision=HIGHEST, preferred_element_type=F32)
    diagonal = iota((16, 16), 0) == iota((16, 16), 1)
    columns = [
        jnp.sum(jnp.where(diagonal, project[e : e + 1, :], 0.0), axis=1, keepdims=True)
        for e in range(3)
    ]
    blank = jnp.zeros((16, 16), F32)
    along = gain_x[...]
    for part, to in ((0, coef_a), (1, coef_b)):
        joined = []
        for d in range(3):
            total = jnp.zeros((16, K), F32)
            for c in range(16):
                total = total + lift[d, c] * mix[part, c].astype(F32)
            joined.append(
                gains * jnp.dot(total, hot_k, precision=HIGHEST, preferred_element_type=F32)
            )
        sign = 1.0 if part == 0 else -1.0
        right = jnp.concatenate([sign * along, blank, along, blank], 1)
        for e in range(3):
            for d in range(3):
                left = (columns[e] * joined[d]).T
                to[(e * 3 + d) * PAD : (e * 3 + d + 1) * PAD, :] = jnp.dot(
                    left, right, precision=HIGHEST, preferred_element_type=F32
                )
    row = iota((8, LANES), 0)
    total = jnp.zeros((8, LANES), F32)
    for i in range(64):
        given = jnp.where(
            row == 0, weights[0, 0, i], jnp.where(row == 1, weights[1, 0, i], weights[2, 0, i])
        )
        total = total + jnp.where((flat == mon[i]) & (row < 3), given, 0.0)
    injected[...] = jnp.where(iota((8, LANES), 1) < 64, total, 0.0)


def filter_kernel(
    gathered, coef_a, coef_b, fwd_x, inv_x, phase_x, phase_yz, after, out
):
    b, w = own_block()
    half, near = b % HALVES, b // HALVES % NEAR
    lane = iota((1, LANES), 1)
    got = gathered[...]
    both = jnp.dot(fwd_x[...], got, preferred_element_type=F32)
    full = (both[:LANES, :LANES] + both[LANES:, LANES:]).T
    field = [full[d * SHARE : d * SHARE + PAD] for d in range(3)]
    turned = [pltpu.roll(f, 64, 1) for f in field]
    sign = jnp.where(lane < 64, 1.0, -1.0)
    real = []
    for e in range(3):
        q = jnp.zeros((PAD, LANES), F32)
        for d in range(3):
            at = (e * 3 + d) * PAD
            q = q + coef_a[at : at + PAD] * field[d] + coef_b[at : at + PAD] * turned[d]
        real.append(q)
    gap = jnp.zeros((LANES - 3 * SHARE, LANES), F32)
    packed = jnp.concatenate([q[:SHARE] for q in real] + [gap], 0)
    right = jnp.concatenate([packed, pltpu.roll(packed, 64, 1) * sign], 0).astype(BF16)
    back = lax.dot_general(
        inv_x[b // (HALVES * NEAR), half], right, (((1,), (1,)), ((), ())),
        preferred_element_type=F32,
    ).reshape(NEAR, 2, 8, 2 * LANES)

    total = got.astype(F32).reshape(BULK, 8, 2 * LANES).sum(0)
    total = pltpu.roll(total[:, :LANES] + total[:, LANES:], LANES - 3 * SHARE, 1)
    second = pltpu.roll(total, LANES - 6, 1)
    gap = jnp.zeros((LANES - 16, LANES), F32)
    total = jnp.concatenate([total, second, gap], 0)
    total = jnp.where(iota((LANES, LANES), 1) < 6, total, 0.0).T[:8]
    total = pltpu.roll(total, near * 16, 1)
    near = jnp.dot(
        jnp.concatenate(real, 0).astype(BF16), phase_x[...], preferred_element_type=F32
    )
    row = iota((8, LANES), 0)
    for e in range(3):
        line = jnp.sum(near[e * PAD : (e + 1) * PAD] * phase_yz[...], axis=0, keepdims=True)
        line = line + pltpu.roll(line, 64, 1)
        total = total + jnp.where((row == e) & (lane < 64), line, 0.0)
    high = total.astype(BF16).astype(F32)
    extra = pltpu.roll(high + pltpu.roll(total - high, 64, 1), 2, 0)
    extra = jnp.concatenate([extra, jnp.zeros((8, LANES), F32)], 1)
    tiles = []
    for n in range(NEAR):
        tiles += [back[n, 0], back[n, 1] + extra]
    out[...] = jnp.concatenate(tiles, 0).astype(BF16)


def spread_kernel(shares, inv_y, out, rows):
    lane = iota((1, LANES), 1)
    got = shares[...].astype(F32).reshape(NEAR, 16, 2 * LANES)
    rows[...] = jnp.zeros((32, 8, LANES), F32)
    for e in range(3):
        flat = []
        for part in range(2):
            start = e * SHARE
            first, rest = jnp.zeros((16, LANES), F32), None
            for n in range(NEAR):
                moved = got[n][:, part * LANES : (part + 1) * LANES]
                if n != e:
                    moved = pltpu.roll(moved, (n * SHARE - start) % LANES, 1)
                within = (lane >= n * SHARE) & (lane < (n + 1) * SHARE)
                first = first + jnp.where(within, moved, 0.0)
                if n == NEAR - 1:
                    rest = jnp.where(lane < 16, moved, 0.0)
            flat.append((first, rest))

        def mode_rows(part, k, to):
            first, rest = flat[part]
            moved = pltpu.roll(first, (to - k * K) % LANES, 1)
            if k < 2:
                return jnp.where((lane >= to) & (lane < to + K), moved, 0.0)
            tail = pltpu.roll(rest, to + 32, 1)
            return jnp.where((lane >= to) & (lane < to + 32), moved, 0.0) + jnp.where(
                (lane >= to + 32) & (lane < to + K), tail, 0.0
            )

        for k in range(OWN):
            real = mode_rows(0, k, 0) + mode_rows(1, k, 64)
            imag = mode_rows(1, k, 0) - mode_rows(0, k, 64)
            for x in range(10):
                rows[e * 10 + x, k : k + 1, :] = real[x : x + 1]
                rows[e * 10 + x, OWN + k : OWN + k + 1, :] = imag[x : x + 1]
    lhs = rows[...].reshape(256, LANES).astype(BF16)
    wide = jnp.dot(lhs, inv_y[...], preferred_element_type=F32).reshape(32, 8, 384)
    near = []
    for low in range(8):
        group = [wide[high * 8 + low, :, c * LANES : (c + 1) * LANES] for high in range(4) for c in range(2)]
        near.append(jnp.stack(group))
    near = exchange(near, 16, 2)
    edge = []
    for low in range(16):
        edge.append(jnp.stack([wide[high * 16 + low, :, 256:384] for high in range(2)]))
    edge = exchange(edge, 2, 2)
    row = iota((8, LANES), 0)
    total = pltpu.roll(got[:, 8:16, :LANES].sum(0), 6, 0)
    total = jnp.where((row < 6) & (lane < 64), total + pltpu.roll(total, 64, 1), 0.0)
    high = total.astype(BF16).astype(F32)
    other = pltpu.roll(total - high, 64, 1)
    moved = pltpu.roll(high, 64, 1)
    low = total - high
    extra = []
    for t in range(3):
        first = jnp.where(lane < 64, high[2 * t : 2 * t + 1], moved[2 * t + 1 : 2 * t + 2])
        second = jnp.where(lane < 64, low[2 * t : 2 * t + 1], other[2 * t + 1 : 2 * t + 2])
        extra.append(jnp.where(row == 6, first, jnp.where(row == 7, second, 0.0)))
    blocks = []
    for w in range(WIDE):
        tiles = [near[w % 8][high_x * 2 + w // 8] for high_x in range(4)]
        for t in range(3):
            tiles[t] = tiles[t] + extra[t]
        pair = jnp.where(lane < 32, edge[w], 0.0)
        tiles.append(pair[0] + pltpu.roll(pair[1], 32, 1))
        blocks.append(jnp.concatenate(tiles, 1))
    out[...] = jnp.concatenate(blocks, 0).astype(BF16)


def high_planes(across):
    first, second = [c for c in range(3) if c != across]
    planes = [(c, 0) for c in range(3)] + [(first, 1), (second, 1), (6, 0), (6, 1)]
    return planes + [(3 + c, 0) for c in range(3)]


def low_planes(across):
    first, second = [c for c in range(3) if c != across]
    planes = [(c, i) for i in range(2) for c in range(3)] + [(6, 0), (6, 1)]
    return planes + [(3 + first, 0), (3 + second, 0)] + [(3 + c, 1) for c in range(3)]


def edge_kernel(electric, magnetic, inverse, saved, after, to_low, to_high):
    def own(f):
        return electric.at[f] if f < 3 else (magnetic.at[f - 3] if f < 6 else inverse)

    for p, (f, i) in enumerate(low_planes(0)):
        to_low[p] = own(f)[6 + i].astype(BF16)
    for n in range(2):
        for c in range(2):
            to_low[13 + 2 * n + c] = saved[n, 1 + c, 7]
    for p, (f, i) in enumerate(high_planes(0)):
        to_high[p] = own(f)[i].astype(BF16)


def corner_kernel(
    electric, magnetic, inverse, saved, x_low, x_high, after, to_low, to_high, low, high
):
    x_of = [{}, {}]
    for p, key in enumerate(low_planes(0)):
        x_of[0][key] = x_low[p].astype(F32)
    for p, key in enumerate(high_planes(0)):
        x_of[1][key] = x_high[p].astype(F32)
    low[...] = jnp.zeros(low.shape, F32)
    high[...] = jnp.zeros(high.shape, F32)
    for to, planes, start in ((low, low_planes(1), 14), (high, high_planes(1), 0)):
        for p, (f, i) in enumerate(planes):
            own = electric.at[f] if f < 3 else (magnetic.at[f - 3] if f < 6 else inverse)
            row = start + i
            to[p, 0:8, :] = own[:, row, :]
            for side, at in ((1, 8), (0, 10)):
                for layer in range(2):
                    if (f, layer) in x_of[side]:
                        got = x_of[side][(f, layer)]
                        to[p, at + layer : at + layer + 1, :] = got[row : row + 1]
    for n in range(2):
        for i, c in enumerate((0, 2)):
            low[13 + 2 * n + i, 0:8, :] = saved[n, c].astype(F32)[:, RY - 1, :]
    to_low[...] = low[...].astype(BF16)
    to_high[...] = high[...].astype(BF16)


def first_kernel(
    mon, weights, electric, magnetic, inverse, saved, x_low, x_high, y_low, y_high, after,
    early, curled, factor, grad, ready, e_ext, h_ext, g_ext,
):
    b, w = own_block()
    lane = iota((1, NZ), 1)
    zero = jnp.zeros((12, 24, NZ), F32)
    for c in range(7):
        to = e_ext.at[c] if c < 3 else (h_ext.at[c - 3] if c < 6 else g_ext)
        to[...] = zero
        own = electric[c] if c < 3 else (magnetic[c - 3] if c < 6 else inverse[...])
        to[0:8, 0:16, :] = own
        for planes, ref, at in ((high_planes(0), x_high, 8), (low_planes(0), x_low, 10)):
            for p, (f, i) in enumerate(planes):
                if f == c:
                    to[at + i, 0:16, :] = ref[p].astype(F32)
        for planes, ref, at in ((high_planes(1), y_high, 16), (low_planes(1), y_low, 22)):
            for p, (f, i) in enumerate(planes):
                if f == c:
                    to[:, at + i : at + i + 1, :] = ref[p].astype(F32)[0:12][:, None, :]

    g = g_ext[...]
    half = 0.5 * g
    a = [half * e_ext[c] for c in range(3)]
    spot_x = iota((12, 24, 1), 0)
    spot_y = iota((12, 24, 1), 1)
    outside = ((spot_x >= 10) & (b == 0)) | ((spot_y >= 22) & (w == 0))
    inside = jnp.where(outside, 0.0, 1.0)
    turned = curl_ahead(*a)
    h = [h_ext[c] + inside * turned[c] for c in range(3)]
    back = curl_behind(*h)
    for c in range(3):
        e_ext[c] = e_ext[c] - 0.5 * back[c]

    def hit(x, y, z):
        lx, ly = x - b * RX, y - w * RY
        return (lx >= -2) & (lx < RX + 2) & (ly >= -2) & (ly < RY + 2)

    def add(i, flat):
        x, y, z = place_of(flat)
        lx, ly = x - b * RX, y - w * RY
        px = jnp.where(lx < 0, lx + 12, lx)
        py = jnp.where(ly < 0, ly + 24, ly)
        for c in range(3):
            row = e_ext[c, px, pl.ds(py, 1), :]
            e_ext[c, px, pl.ds(py, 1), :] = row + jnp.where(lane == z, weights[c, 0, i], 0.0)

    scan(mon, hit, add)
    for c in range(3):
        early[c, 0:9] = e_ext[c, 0:9]
        early[c, 9:10] = e_ext[c, 11:12]
        curled[c, 0:9] = h[c][0:9]
        curled[c, 9:10] = h[c][11:12]
    factor[0:9] = half[0:9]
    factor[9:10] = half[11:12]

    near = inverse[...]
    for step in range(2):
        s = [saved[step, c].astype(F32) for c in range(3)]
        before_x = {c: jnp.concatenate([x_low[12 + 2 * step + c].astype(F32)[None], s[c][:-1]], 0) for c in (1, 2)}
        before_y = {}
        for c in (0, 2):
            edge = y_low[13 + 2 * step + c // 2].astype(F32)[0:8][:, None, :]
            first = iota((RX, RY, NZ), 1) == 0
            before_y[c] = jnp.where(first, edge, pltpu.roll(s[c], 1, 1))
        curls = (
            (s[2] - before_y[2]) - (s[1] - z_behind(s[1])),
            (s[0] - z_behind(s[0])) - (s[2] - before_x[2]),
            (s[1] - before_x[1]) - (s[0] - before_y[0]),
        )
        if step == 0:
            for c in range(3):
                ready[c] = near * curls[c]
        else:
            total = jnp.zeros((RX, RY, NZ), F32)
            for c in range(3):
                total = total + a[c][0:8, 0:16] * near * curls[c]
            grad[...] = -total


def second_kernel(
    lines, table, apart, early, curled, factor, first_grad, ready, injected,
    grad_e, grad_h, grad_eps, sources,
):
    b, w = own_block()
    turn = (((0,), (0,)), ((), ()))
    main = lax.dot_general(lines[:, 0:512], table[...], turn, preferred_element_type=F32)
    main = main.reshape(32, 16, NZ)
    edge = jnp.dot(lines[:, 512:640], apart[...], preferred_element_type=F32).astype(BF16)
    edge = lax.dot_general(edge, table[...], turn, preferred_element_type=F32)
    edge = edge.reshape(32, 8, NZ)
    half = factor[...]
    e1 = []
    for c in range(3):
        at = slice(c * 10, c * 10 + 10)
        e1.append(early[c] + jnp.concatenate([main[at], edge[at]], 1))
    a = [half * e for e in e1]
    spot_x = iota((10, 24, 1), 0)
    spot_y = iota((10, 24, 1), 1)
    outside = ((spot_x == 9) & (b == 0)) | ((spot_y == 23) & (w == 0))
    inside = jnp.where(outside, 0.0, 1.0)
    turned = curl_ahead(*a)
    h = [curled[c] + inside * turned[c] for c in range(3)]
    backed = curl_behind(*h)
    total = first_grad[...]
    for c in range(3):
        grad_h[c] = h[c][0:8, 0:16]
        grad_e[c] = e1[c][0:8, 0:16] - 0.5 * backed[c][0:8, 0:16]
        total = total - a[c][0:8, 0:16] * ready[c]
    grad_eps[...] = total
    got = lines[:, 0:384].astype(F32).reshape(WIDE, 8, 384).sum(0)
    got = got[6:7] + got[7:8]
    moved = pltpu.roll(got, 384 - 64, 1)
    for n in range(2):
        for c in range(3):
            at = n * 3 + c
            line = got if at % 2 == 0 else moved
            line = line[:, at // 2 * LANES : (at // 2 + 1) * LANES]
            if n == 0:
                line = line + injected[c : c + 1, :]
            sources[c, n : n + 1, :] = line[:, 0:64]


def call(kernel, outs, places, scratch=(), flops=0, moved=0, params=PARAMS):
    spaces = {"s": pltpu.SMEM, "v": pltpu.VMEM, "a": pl.ANY}
    return pl.pallas_call(
        kernel,
        out_shape=outs,
        in_specs=[pl.BlockSpec(memory_space=spaces[p]) for p in places],
        out_specs=jax.tree.map(lambda _: pl.BlockSpec(memory_space=pltpu.VMEM), outs),
        scratch_shapes=list(scratch),
        compiler_params=params,
        cost_estimate=pl.CostEstimate(flops=flops, bytes_accessed=moved, transcendentals=0),
    )


def shape(*dims, dtype=F32):
    return jax.ShapeDtypeStruct(dims, dtype)


def passed_along(block, axis, distance):
    devices = range(lax.axis_size(axis))
    route = [(i - distance, i) for i in devices if i - distance in devices]
    return lax.ppermute(block, axis, route)


def dealt_near(block):
    groups = [
        [(f * NEAR + n) * HALVES + half for n in range(NEAR)]
        for f in range(DEPTH // NEAR)
        for half in range(HALVES)
    ]
    return lax.all_to_all(
        block, "bulk", split_axis=0, concat_axis=0, axis_index_groups=groups, tiled=True
    )


def tables_of(name):
    return jnp.asarray(TABLES[name])


def body(
    seed_electric, seed_magnetic, saved_magnetic, material, permittivity, source_cells,
    monitor_cells, monitor_weights, lift_weight, project_weight, mode_mix, gain_first, gain_second,
):
    weights = monitor_weights.transpose(2, 0, 1)
    big, dma = pltpu.CompilerParams(vmem_limit_bytes=56 * 1024 * 1024), pltpu.SemaphoreType.DMA
    block = (RX, RY, NZ)

    payload, field = call(
        lift_kernel,
        (shape(384, LANES, dtype=BF16), shape(3, *block)),
        "aaaa",
        [
            pltpu.SMEM((64,), jnp.int32), pltpu.VMEM((3, 2, 64), F32),
            pltpu.VMEM((LANES, LANES), BF16), dma((4,)),
        ],
        13_000_000,
        500_000,
        big,
    )(monitor_cells, weights, seed_electric, tables_of("lift_z"))
    lines = lax.all_to_all(payload, "wide", split_axis=0, concat_axis=0, tiled=True)

    taken, inverse = call(
        share_kernel,
        (shape(8, LANES), shape(*block)),
        "aavaa",
        [
            pltpu.SMEM((64,), jnp.int32), pltpu.SMEM((8,), F32), pltpu.VMEM((3, *block), F32),
            pltpu.VMEM(block, jnp.int32), pltpu.VMEM((3, 12, 32, NZ), F32),
            pltpu.VMEM((3, 12, 32, NZ), F32), dma((4,)),
        ],
        3_000_000,
        1_500_000,
    )(source_cells, permittivity, field, seed_magnetic, material)

    dealt = call(
        middle_kernel, shape(BULK * 8, 2 * LANES, dtype=BF16), "vvv", (), 20_000_000, 400_000
    )(lines, taken, tables_of("fwd_y"))
    gathered = lax.all_to_all(dealt, "bulk", split_axis=0, concat_axis=0, tiled=True)

    cells = jnp.concatenate([source_cells, source_cells]).reshape(1, LANES)
    coef_a, coef_b, phase_x, phase_yz, injected = call(
        param_kernel,
        (
            shape(9 * PAD, LANES), shape(9 * PAD, LANES), shape(LANES, LANES, dtype=BF16),
            shape(PAD, LANES), shape(8, LANES),
        ),
        "sssvvvvvvvva",
        (),
        20_000_000,
        1_000_000,
    )(
        monitor_cells, weights, lift_weight.T, cells, project_weight, gain_first, gain_second,
        mode_mix.transpose(0, 2, 3, 1), tables_of("at_x"), tables_of("at_y"), tables_of("at_z"),
        dealt,
    )

    to_low, to_high = call(
        edge_kernel,
        (shape(17, RY, NZ, dtype=BF16), shape(10, RY, NZ, dtype=BF16)),
        "vvvva",
        (),
        0,
        500_000,
    )(field, seed_magnetic, inverse, saved_magnetic, dealt)
    x_low = passed_along(to_low, "bulk", 1)
    x_high = passed_along(to_high, "bulk", -1)

    low_part, high_part = call(
        corner_kernel,
        (shape(17, 16, NZ, dtype=BF16), shape(10, 16, NZ, dtype=BF16)),
        "vvvvvva",
        [pltpu.VMEM((17, 16, NZ), F32), pltpu.VMEM((10, 16, NZ), F32)],
        0,
        1_000_000,
    )(field, seed_magnetic, inverse, saved_magnetic, x_low, x_high, coef_a)
    shares = call(
        filter_kernel, shape(NEAR * 16, 2 * LANES, dtype=BF16), "vvvvvvva", (), 40_000_000, 600_000
    )(
        gathered, coef_a, coef_b, tables_of("fwd_x"), tables_of("inv_x"), phase_x, phase_yz,
        low_part,
    )
    back = dealt_near(shares)

    y_low = passed_along(low_part, "wide", 1)
    y_high = passed_along(high_part, "wide", -1)

    sent = call(
        spread_kernel,
        shape(128, 640, dtype=BF16),
        "vv",
        [pltpu.VMEM((32, 8, LANES), F32)],
        40_000_000,
        600_000,
    )(back, tables_of("inv_y"))
    returned = lax.all_to_all(sent, "wide", split_axis=0, concat_axis=0, tiled=True)
    early, curled, factor, first_grad, ready = call(
        first_kernel,
        (
            shape(3, 10, 24, NZ), shape(3, 10, 24, NZ), shape(10, 24, NZ), shape(*block),
            shape(3, *block),
        ),
        "ssvvvvvvvva",
        [pltpu.VMEM((3, 12, 24, NZ), F32)] * 2 + [pltpu.VMEM((12, 24, NZ), F32)],
        10_000_000,
        3_000_000,
    )(
        monitor_cells, weights, field, seed_magnetic, inverse, saved_magnetic,
        x_low, x_high, y_low, y_high, sent,
    )

    grad_e, grad_h, grad_eps, sources = call(
        second_kernel,
        (shape(3, *block), shape(3, *block), shape(*block), shape(3, 2, 64)),
        "vvvvvvvvv",
        (),
        40_000_000,
        4_000_000,
    )(
        returned, tables_of("back_z"), tables_of("apart"), early, curled, factor, first_grad,
        ready, injected,
    )
    return grad_e, grad_h, grad_eps, sources.transpose(1, 2, 0)


def solution(mesh):
    field = P(None, "bulk", "wide", None)
    return jax.shard_map(
        body,
        mesh=mesh,
        in_specs=(
            field, field, P(None, None, "bulk", "wide", None), P("bulk", "wide", None),
            P(), P(), P(), P(), P(), P(), P(), P(), P(),
        ),
        out_specs=(field, field, P("bulk", "wide", None), P()),
        check_vma=False,
    )
```

```python
import functools
import math

import jax
import jax.numpy as jnp
import ml_dtypes
import numpy as np
from jax import lax
from jax.experimental import pallas as pl
from jax.experimental.pallas import tpu as pltpu
from jax.sharding import PartitionSpec as P

NX, NY, NZ = 256, 256, 128
K = 48
OWN = 3
WIDE, BULK = 16, 32
RX, RY = 8, 16
NEAR, DEPTH, HALVES = 4, 16, 2
SHARE = OWN * K // NEAR
PAD = 40
LANES = 128
F32, BF16 = jnp.float32, jnp.bfloat16
PARAMS = pltpu.CompilerParams(vmem_limit_bytes=40 * 1024 * 1024)
HIGHEST = lax.Precision.HIGHEST


def waves(freqs, places, total):
    phase = np.mod(np.asarray(freqs)[:, None] * np.asarray(places)[None, :], total)
    angle = phase.astype(np.float32) * np.float32(2.0 * math.pi / total)
    return np.cos(angle).astype(np.float32), np.sin(angle).astype(np.float32)


def rounded(table):
    return np.asarray(table, np.float32).astype(ml_dtypes.bfloat16)


def make_tables():
    mode = np.arange(K)
    plane = np.where(mode < K // 2, mode, mode - K)
    cz, sz = waves(mode, np.arange(NZ), NZ)
    cx, sx = (rounded(t) for t in waves(plane, np.arange(NX), NX))
    cy, sy = (rounded(t) for t in waves(plane, np.arange(NY), NY))
    scale = np.float32(1.0 / math.sqrt(NX * NY * NZ))
    back = np.float32(1.0 / math.sqrt(K**3))
    fz, gz = rounded(cz * scale), rounded(-sz * scale)
    bz, hz = rounded(cz * back), rounded(sz * back)
    out = {}
    lift_z = np.zeros((LANES, LANES), ml_dtypes.bfloat16)
    back_z = np.zeros((LANES, LANES), ml_dtypes.bfloat16)
    for w in range(WIDE):
        for i in range(OWN):
            lift_z[:, w * 8 + i] = fz[w * OWN + i]
            lift_z[:, w * 8 + OWN + i] = gz[w * OWN + i]
            back_z[w * 8 + i] = bz[w * OWN + i]
            back_z[w * 8 + OWN + i] = -hz[w * OWN + i]
    out["lift_z"], out["back_z"] = lift_z, back_z

    lane = np.arange(LANES)
    y_of = np.concatenate([(h * 8 + lane % 8) * RY + lane // 8 for h in range(2)])
    fwd_y = np.zeros((512, 256), ml_dtypes.bfloat16)
    fwd_y[:256, :K] = cy[:, y_of].T
    fwd_y[256:, :K] = sy[:, y_of].T
    fwd_y[:256, 128 : 128 + K] = -sy[:, y_of].T
    fwd_y[256:, 128 : 128 + K] = cy[:, y_of].T
    out["fwd_y"] = fwd_y

    fwd_x = np.zeros((2 * LANES, NX), ml_dtypes.bfloat16)
    fwd_x[:K], fwd_x[64 : 64 + K] = cx, -sx
    fwd_x[128 : 128 + K], fwd_x[192 : 192 + K] = sx, cx
    inv_x = np.zeros((DEPTH // NEAR, HALVES, NEAR * 16, LANES), ml_dtypes.bfloat16)
    for half in range(HALVES):
        for z in range(DEPTH):
            start = (z * HALVES + half) * RX
            x_of = (start + np.array([0, 1, 2, 3, 4, 5, 6, 7, 8, -1])) % NX
            at = slice(z % NEAR * 16, z % NEAR * 16 + 10)
            inv_x[z // NEAR, half, at, :K] = cx[:, x_of].T
            inv_x[z // NEAR, half, at, 64 : 64 + K] = -sx[:, x_of].T
    out["fwd_x"], out["inv_x"] = fwd_x, inv_x

    inv_y = np.zeros((LANES, 384), ml_dtypes.bfloat16)
    inv_y[:K, :256], inv_y[64 : 64 + K, :256] = cy, -sy
    for w in range(WIDE):
        for h, y in enumerate((w * RY + RY, w * RY - 1)):
            inv_y[:K, 256 + w * 2 + h] = cy[:, y % NY]
            inv_y[64 : 64 + K, 256 + w * 2 + h] = -sy[:, y % NY]
    out["inv_y"] = inv_y
    apart = np.zeros((LANES, 256), ml_dtypes.bfloat16)
    for cell in range(32):
        apart[cell * 2, cell * 8] = 1
        apart[cell * 2 + 1, cell * 8 + 7] = 1
    out["apart"] = apart

    at_x = np.zeros((2, LANES, NX), ml_dtypes.bfloat16)
    at_x[0, :K], at_x[0, 64 : 64 + K] = cx, -sx
    at_x[1, :K], at_x[1, 64 : 64 + K] = sx, cx
    out["at_x"] = at_x
    at_y = np.zeros((NEAR, 2, 48, NY), ml_dtypes.bfloat16)
    for n in range(NEAR):
        j_of = np.arange(n * SHARE, (n + 1) * SHARE) % K
        at_y[n, 0, :SHARE], at_y[n, 1, :SHARE] = cy[j_of], sy[j_of]
    out["at_y"] = at_y
    at_z = np.zeros((WIDE, 2, 16, NZ), ml_dtypes.bfloat16)
    for w in range(WIDE):
        at_z[w, 0, :OWN] = bz[w * OWN : (w + 1) * OWN]
        at_z[w, 1, :OWN] = hz[w * OWN : (w + 1) * OWN]
    out["at_z"] = at_z
    return out


TABLES = make_tables()


def iota(shape, axis):
    return lax.broadcasted_iota(jnp.int32, shape, axis)


def exchange(tiles, block, axis):
    tiles = list(tiles)
    shape = tiles[0].shape
    size = shape[axis]
    place = iota(shape, axis) // block
    step = 1
    while step < len(tiles):
        high = (place // step) % 2 == 1
        new = list(tiles)
        for low in range(len(tiles)):
            if low & step:
                continue
            u, v = tiles[low], tiles[low + step]
            new[low] = jnp.where(high, pltpu.roll(v, step * block, axis), u)
            new[low + step] = jnp.where(high, v, pltpu.roll(u, size - step * block, axis))
        tiles = new
        step *= 2
    return tiles


def z_ahead(v):
    axis = v.ndim - 1
    return jnp.where(iota(v.shape, axis) < NZ - 1, pltpu.roll(v, NZ - 1, axis), 0.0)


def z_behind(v):
    axis = v.ndim - 1
    return jnp.where(iota(v.shape, axis) > 0, pltpu.roll(v, 1, axis), 0.0)


def x_ahead(v):
    return jnp.concatenate([v[1:], v[:1]], 0)


def x_behind(v):
    return jnp.concatenate([v[-1:], v[:-1]], 0)


def y_ahead(v):
    return pltpu.roll(v, v.shape[1] - 1, 1)


def y_behind(v):
    return pltpu.roll(v, 1, 1)


def curl_ahead(fx, fy, fz):
    return (
        (y_ahead(fz) - fz) - (z_ahead(fy) - fy),
        (z_ahead(fx) - fx) - (x_ahead(fz) - fz),
        (x_ahead(fy) - fy) - (y_ahead(fx) - fx),
    )


def curl_behind(fx, fy, fz):
    return (
        (fz - y_behind(fz)) - (fy - z_behind(fy)),
        (fx - z_behind(fx)) - (fz - x_behind(fz)),
        (fy - x_behind(fy)) - (fx - y_behind(fx)),
    )


def place_of(flat):
    return flat >> 15, (flat >> 7) & (NY - 1), flat & (NZ - 1)


def own_block():
    return lax.axis_index("bulk"), lax.axis_index("wide")


def fetch(pairs, sems):
    copies = [pltpu.make_async_copy(a, b, sems.at[i]) for i, (a, b) in enumerate(pairs)]
    for copy in copies:
        copy.start()
    return copies


def scan(cells, hit, act):
    def group(g, carry):
        found = [cells[g * 8 + i] for i in range(8)]
        hits = [hit(*place_of(f)) for f in found]
        some = functools.reduce(jnp.logical_or, hits)

        @pl.when(some)
        def _():
            for i in range(8):
                pl.when(hits[i])(functools.partial(act, g * 8 + i, found[i]))

        return carry

    lax.fori_loop(0, 8, group, 0)


def lift_kernel(mon_in, weights_in, electric, table_in, out, field, mon, weights, table, sems):
    b, w = own_block()
    copies = fetch(
        ((mon_in, mon), (electric, field), (weights_in, weights), (table_in, table)), sems
    )
    for copy in copies:
        copy.wait()
    lane = iota((1, NZ), 1)
    spot = iota((1, 64), 1)

    def hit(x, y, z):
        return ((x >> 3) == b) & ((y >> 4) == w)

    def add(i, flat):
        x, y, z = place_of(flat)
        lx, ly = x & (RX - 1), y & (RY - 1)
        for c in range(3):
            row = field[c, lx, pl.ds(ly, 1), :]
            given = jnp.where(spot == i, weights[c, 1:2, :], 0.0)
            weight = jnp.sum(given, axis=1, keepdims=True)
            field[c, lx, pl.ds(ly, 1), :] = row + jnp.where(lane == z, weight, 0.0)

    scan(mon, hit, add)
    rows = field[...].reshape(3 * RX * RY, NZ).astype(BF16)
    modes = jnp.dot(rows, table[...], preferred_element_type=F32)
    modes = modes.reshape(3, RX, 2, 8, LANES)
    tiles = exchange([modes[:, x].reshape(6, 8, LANES) for x in range(RX)], 1, 1)
    tiles = [t.reshape(3, 2, 8, LANES) for t in tiles]
    tiles = exchange([tiles[y % 8][:, y // 8] for y in range(RY)], 8, 2)
    out[...] = jnp.concatenate([t.reshape(24, LANES) for t in tiles], 0).astype(BF16)


def share_kernel(
    src_in, perm_in, field, magnetic_in, material_in,
    taken, inverse,
    src, perm, magnetic, material, scaled, held, sems,
):
    b, w = own_block()
    copies = fetch(
        (
            (src_in, src), (perm_in, perm), (magnetic_in, magnetic),
            (material_in, material),
        ),
        sems,
    )
    zero = jnp.zeros((12, 32, NZ), F32)
    for c in range(3):
        scaled[c] = zero
        held[c] = zero
    for copy in copies:
        copy.wait()
    eps = jnp.zeros((RX, RY, NZ), F32)
    cells = material[...]
    for level in range(8):
        eps = jnp.where(cells == level, perm[level], eps)
    inv = 1.0 / eps
    inverse[...] = inv
    lane = iota((1, NZ), 1)
    for c in range(3):
        scaled[c, 2:10, 8:24, :] = 0.5 * inv * field[c]
        held[c, 2:10, 8:24, :] = magnetic[c]
    taken[...] = jnp.zeros((8, LANES), F32)
    spot_row, spot_lane = iota((8, LANES), 0), iota((8, LANES), 1)

    def hit(x, y, z):
        lx, ly = x - b * RX, y - w * RY
        return (lx >= -1) & (lx <= RX) & (ly >= -1) & (ly <= RY)

    def take(i, flat):
        x, y, z = place_of(flat)
        lx, ly = x - b * RX, y - w * RY

        def a(c, dx, dy):
            return scaled[c, lx + 2 + dx, pl.ds(ly + 8 + dy, 1), :]

        def h(c, dx, dy):
            old = held[c, lx + 2 + dx, pl.ds(ly + 8 + dy, 1), :]
            if c == 0:
                near = a(1, dx, dy)
                turn = (a(2, dx, dy + 1) - a(2, dx, dy)) - (z_ahead(near) - near)
            elif c == 1:
                near = a(0, dx, dy)
                turn = (z_ahead(near) - near) - (a(2, dx + 1, dy) - a(2, dx, dy))
            else:
                turn = (a(1, dx + 1, dy) - a(1, dx, dy)) - (a(0, dx, dy + 1) - a(0, dx, dy))
            return old + turn

        left = jnp.where(x > 0, 1.0, 0.0)
        down = jnp.where(y > 0, 1.0, 0.0)
        hx, hy, hz = h(0, 0, 0), h(1, 0, 0), h(2, 0, 0)
        hx_y, hz_y = down * h(0, 0, -1), down * h(2, 0, -1)
        hy_x, hz_x = left * h(1, -1, 0), left * h(2, -1, 0)
        curls = (
            (hz - hz_y) - (hy - z_behind(hy)),
            (hx - z_behind(hx)) - (hz - hz_x),
            (hy - hy_x) - (hx - hx_y),
        )
        mine = jnp.where((lx >= 0) & (lx < RX) & (ly >= 0) & (ly < RY), 1.0, 0.0)
        cx, cy = jnp.clip(lx, 0, RX - 1), jnp.clip(ly, 0, RY - 1)
        got = taken[...]
        for c in range(3):
            old = mine * field[c, cx, pl.ds(cy, 1), :]
            for n, row in ((0, old - 0.5 * curls[c]), (1, old)):
                value = jnp.sum(jnp.where(lane == z, row, 0.0), axis=1, keepdims=True)
                spot = (spot_row == n * 3 + c) & (spot_lane == i)
                got = got + jnp.where(spot, value, 0.0)
        taken[...] = got

    scan(src, hit, take)


def middle_kernel(lines, taken, table, out):
    got = lines[...].astype(F32).reshape(WIDE, 24, LANES)
    halves = [exchange([got[h * 8 + i] for i in range(8)], 1, 1) for h in range(2)]
    rows = [
        jnp.concatenate([halves[0][k], halves[1][k], halves[0][OWN + k], halves[1][OWN + k]], 1)
        for k in range(OWN)
    ]
    lhs = jnp.concatenate(rows, 0).astype(BF16)
    found = jnp.dot(lhs, table[...], preferred_element_type=F32)
    lane = iota((8, LANES), 1)
    parts = [[jnp.zeros((8, LANES), F32) for _ in range(2)] for _ in range(NEAR)]
    split = LANES - (NEAR - 1) * SHARE
    for part in range(2):
        for d in range(3):
            piece = [
                found[(k * 3 + d) * 8 : (k * 3 + d) * 8 + 8, part * LANES : (part + 1) * LANES]
                for k in range(OWN)
            ]
            last = pltpu.roll(piece[2], 2 * K, 1)
            first = piece[0] + pltpu.roll(piece[1], K, 1) + jnp.where(lane >= 2 * K, last, 0.0)
            rest = jnp.where(lane < 16, last, 0.0)
            to = d * SHARE
            for n in range(NEAR):
                shift = (to - n * SHARE) % LANES
                moved = pltpu.roll(first, shift, 1) if shift else first
                if n == NEAR - 1:
                    moved = jnp.where(lane < to + split, moved, pltpu.roll(rest, to + split, 1))
                within = (lane >= to) & (lane < to + SHARE)
                parts[n][part] = parts[n][part] + jnp.where(within, moved, 0.0)
    src = jnp.concatenate([taken[...], jnp.zeros((LANES - 8, LANES), F32)], 0).T
    src = jnp.where(iota((LANES, LANES), 1) < 6, src, 0.0)
    high = src.astype(BF16).astype(F32)
    at = 3 * SHARE
    rows = []
    for n in range(NEAR):
        for part, value in enumerate((high, src - high)):
            for i in range(2):
                start = n * 16 + i * 8
                parts[n][part] = parts[n][part] + pltpu.roll(
                    value[start : start + 8], at + i * 6, 1
                )
        rows.append(jnp.concatenate(parts[n], 1))
    deal = jnp.concatenate([r for r in rows for _ in range(HALVES)], 0).astype(BF16)
    size = NEAR * HALVES * 8
    for f in range(DEPTH // NEAR):
        out[f * size : (f + 1) * size, :] = deal


def param_kernel(
    mon, weights, lift, cells, project, gain_x, gain_y, mix, at_x, at_y, at_z, after,
    coef_a, coef_b, phase_x, phase_yz, injected,
):
    b, w = own_block()
    n = b // HALVES % NEAR
    flat = cells[...]
    x, y, z = place_of(flat)
    first = iota((1, LANES), 1) < 64
    hot_x = jnp.where(iota((NX, LANES), 0) == x, 1.0, 0.0)
    real = jnp.where(first, hot_x, 0.0).astype(BF16)
    imag = jnp.where(first, 0.0, hot_x).astype(BF16)
    phase_x[...] = (
        jnp.dot(at_x[0], real, preferred_element_type=F32)
        + jnp.dot(at_x[1], imag, preferred_element_type=F32)
    ).astype(BF16)
    hot_y = jnp.where(iota((NY, LANES), 0) == y, 1.0, 0.0).astype(BF16)
    hot_z = jnp.where(iota((NZ, LANES), 0) == z, 1.0, 0.0).astype(BF16)
    cy = jnp.dot(at_y[n, 0], hot_y, preferred_element_type=F32)[:PAD]
    sy = jnp.dot(at_y[n, 1], hot_y, preferred_element_type=F32)[:PAD]
    cz = jnp.dot(at_z[w, 0], hot_z, preferred_element_type=F32)
    sz = jnp.dot(at_z[w, 1], hot_z, preferred_element_type=F32)
    mode = n * SHARE + iota((PAD, 1), 0)
    ck = jnp.where(mode < K, cz[0:1], jnp.where(mode < 2 * K, cz[1:2], cz[2:3]))
    sk = jnp.where(mode < K, sz[0:1], jnp.where(mode < 2 * K, sz[1:2], sz[2:3]))
    phase_yz[...] = jnp.where(first, cy * ck - sy * sk, -(sy * ck + cy * sk))

    place = iota((K, PAD), 1)
    mode = n * SHARE + place
    depth = jnp.where(mode < K, 0, jnp.where(mode < 2 * K, 1, 2))
    live = place < SHARE
    hot_j = jnp.where((iota((K, PAD), 0) == mode - depth * K) & live, 1.0, 0.0)
    hot_k = jnp.where((iota((K, PAD), 0) == w * OWN + depth) & live, 1.0, 0.0)
    gains = jnp.dot(gain_y[...], hot_j, precision=HIGHEST, preferred_element_type=F32)
    diagonal = iota((16, 16), 0) == iota((16, 16), 1)
    columns = [
        jnp.sum(jnp.where(diagonal, project[e : e + 1, :], 0.0), axis=1, keepdims=True)
        for e in range(3)
    ]
    blank = jnp.zeros((16, 16), F32)
    along = gain_x[...]
    totals = []
    for part in range(2):
        rows = [mix[part, c].astype(F32) for c in range(16)]
        for d in range(3):
            total = lift[d, 0] * rows[0]
            for c in range(1, 16):
                total = total + lift[d, c] * rows[c]
            totals.append(total)
    joined = jnp.dot(
        jnp.concatenate(totals, 0), hot_k, precision=HIGHEST, preferred_element_type=F32
    )
    joined = [joined[i * 16 : (i + 1) * 16] * gains for i in range(6)]
    for part, to in ((0, coef_a), (1, coef_b)):
        sign = 1.0 if part == 0 else -1.0
        right = jnp.concatenate([sign * along, blank, along, blank], 1)
        right = jnp.concatenate([columns[e] * right for e in range(3)], 1)
        left = jnp.concatenate([j.T for j in joined[part * 3 : part * 3 + 3]], 0)
        found = jnp.dot(left, right, precision=HIGHEST, preferred_element_type=F32)
        for e in range(3):
            for d in range(3):
                to[(e * 3 + d) * PAD : (e * 3 + d + 1) * PAD, :] = found[
                    d * PAD : (d + 1) * PAD, e * LANES : (e + 1) * LANES
                ]
    row = iota((8, LANES), 0)
    total = jnp.zeros((8, LANES), F32)
    for i in range(64):
        given = jnp.where(
            row == 0, weights[0, 0, i], jnp.where(row == 1, weights[1, 0, i], weights[2, 0, i])
        )
        total = total + jnp.where((flat == mon[i]) & (row < 3), given, 0.0)
    injected[...] = jnp.where(iota((8, LANES), 1) < 64, total, 0.0)


def filter_kernel(
    gathered, coef_a, coef_b, fwd_x, inv_x, phase_x, phase_yz, after, out
):
    b, w = own_block()
    half, near = b % HALVES, b // HALVES % NEAR
    lane = iota((1, LANES), 1)
    got = gathered[...]
    both = jnp.dot(fwd_x[...], got, preferred_element_type=F32)
    full = (both[:LANES, :LANES] + both[LANES:, LANES:]).T
    field = [full[d * SHARE : d * SHARE + PAD] for d in range(3)]
    turned = [pltpu.roll(f, 64, 1) for f in field]
    sign = jnp.where(lane < 64, 1.0, -1.0)
    real = []
    for e in range(3):
        q = jnp.zeros((PAD, LANES), F32)
        for d in range(3):
            at = (e * 3 + d) * PAD
            q = q + coef_a[at : at + PAD] * field[d] + coef_b[at : at + PAD] * turned[d]
        real.append(q)
    gap = jnp.zeros((LANES - 3 * SHARE, LANES), F32)
    packed = jnp.concatenate([q[:SHARE] for q in real] + [gap], 0)
    right = jnp.concatenate([packed, pltpu.roll(packed, 64, 1) * sign], 0).astype(BF16)
    back = lax.dot_general(
        inv_x[b // (HALVES * NEAR), half], right, (((1,), (1,)), ((), ())),
        preferred_element_type=F32,
    ).reshape(NEAR, 2, 8, 2 * LANES)

    total = got.astype(F32).reshape(BULK, 8, 2 * LANES).sum(0)
    total = pltpu.roll(total[:, :LANES] + total[:, LANES:], LANES - 3 * SHARE, 1)
    second = pltpu.roll(total, LANES - 6, 1)
    gap = jnp.zeros((LANES - 16, LANES), F32)
    total = jnp.concatenate([total, second, gap], 0)
    total = jnp.where(iota((LANES, LANES), 1) < 6, total, 0.0).T[:8]
    total = pltpu.roll(total, near * 16, 1)
    near = jnp.dot(
        jnp.concatenate(real, 0).astype(BF16), phase_x[...], preferred_element_type=F32
    )
    row = iota((8, LANES), 0)
    for e in range(3):
        line = jnp.sum(near[e * PAD : (e + 1) * PAD] * phase_yz[...], axis=0, keepdims=True)
        line = line + pltpu.roll(line, 64, 1)
        total = total + jnp.where((row == e) & (lane < 64), line, 0.0)
    high = total.astype(BF16).astype(F32)
    extra = pltpu.roll(high + pltpu.roll(total - high, 64, 1), 2, 0)
    extra = jnp.concatenate([extra, jnp.zeros((8, LANES), F32)], 1)
    tiles = []
    for n in range(NEAR):
        tiles += [back[n, 0], back[n, 1] + extra]
    out[...] = jnp.concatenate(tiles, 0).astype(BF16)


def spread_kernel(shares, inv_y, after, out, rows):
    lane = iota((1, LANES), 1)
    got = shares[...].astype(F32).reshape(NEAR, 16, 2 * LANES)
    rows[...] = jnp.zeros((32, 8, LANES), F32)
    for e in range(3):
        flat = []
        for part in range(2):
            start = e * SHARE
            first, rest = jnp.zeros((16, LANES), F32), None
            for n in range(NEAR):
                moved = got[n][:, part * LANES : (part + 1) * LANES]
                if n != e:
                    moved = pltpu.roll(moved, (n * SHARE - start) % LANES, 1)
                within = (lane >= n * SHARE) & (lane < (n + 1) * SHARE)
                first = first + jnp.where(within, moved, 0.0)
                if n == NEAR - 1:
                    rest = jnp.where(lane < 16, moved, 0.0)
            flat.append((first, rest))

        def mode_rows(part, k, to):
            first, rest = flat[part]
            moved = pltpu.roll(first, (to - k * K) % LANES, 1)
            if k < 2:
                return jnp.where((lane >= to) & (lane < to + K), moved, 0.0)
            tail = pltpu.roll(rest, to + 32, 1)
            return jnp.where((lane >= to) & (lane < to + 32), moved, 0.0) + jnp.where(
                (lane >= to + 32) & (lane < to + K), tail, 0.0
            )

        for k in range(OWN):
            real = mode_rows(0, k, 0) + mode_rows(1, k, 64)
            imag = mode_rows(1, k, 0) - mode_rows(0, k, 64)
            for x in range(10):
                rows[e * 10 + x, k : k + 1, :] = real[x : x + 1]
                rows[e * 10 + x, OWN + k : OWN + k + 1, :] = imag[x : x + 1]
    lhs = rows[...].reshape(256, LANES).astype(BF16)
    wide = jnp.dot(lhs, inv_y[...], preferred_element_type=F32).reshape(32, 8, 384)
    near = []
    for low in range(8):
        group = [wide[high * 8 + low, :, c * LANES : (c + 1) * LANES] for high in range(4) for c in range(2)]
        near.append(jnp.stack(group))
    near = exchange(near, 16, 2)
    edge = []
    for low in range(16):
        edge.append(jnp.stack([wide[high * 16 + low, :, 256:384] for high in range(2)]))
    edge = exchange(edge, 2, 2)
    row = iota((8, LANES), 0)
    total = pltpu.roll(got[:, 8:16, :LANES].sum(0), 6, 0)
    total = jnp.where((row < 6) & (lane < 64), total + pltpu.roll(total, 64, 1), 0.0)
    high = total.astype(BF16).astype(F32)
    other = pltpu.roll(total - high, 64, 1)
    moved = pltpu.roll(high, 64, 1)
    low = total - high
    extra = []
    for t in range(3):
        first = jnp.where(lane < 64, high[2 * t : 2 * t + 1], moved[2 * t + 1 : 2 * t + 2])
        second = jnp.where(lane < 64, low[2 * t : 2 * t + 1], other[2 * t + 1 : 2 * t + 2])
        extra.append(jnp.where(row == 6, first, jnp.where(row == 7, second, 0.0)))
    blocks = []
    for w in range(WIDE):
        tiles = [near[w % 8][high_x * 2 + w // 8] for high_x in range(4)]
        for t in range(3):
            tiles[t] = tiles[t] + extra[t]
        pair = jnp.where(lane < 32, edge[w], 0.0)
        tiles.append(pair[0] + pltpu.roll(pair[1], 32, 1))
        blocks.append(jnp.concatenate(tiles, 1))
    out[...] = jnp.concatenate(blocks, 0).astype(BF16)


def high_planes(across):
    first, second = [c for c in range(3) if c != across]
    planes = [(c, 0) for c in range(3)] + [(first, 1), (second, 1), (6, 0), (6, 1)]
    return planes + [(3 + c, 0) for c in range(3)]


def low_planes(across):
    first, second = [c for c in range(3) if c != across]
    planes = [(c, i) for i in range(2) for c in range(3)] + [(6, 0), (6, 1)]
    return planes + [(3 + first, 0), (3 + second, 0)] + [(3 + c, 1) for c in range(3)]


def edge_kernel(electric, magnetic, inverse, saved, after, to_low, to_high):
    def own(f):
        return electric.at[f] if f < 3 else (magnetic.at[f - 3] if f < 6 else inverse)

    for p, (f, i) in enumerate(low_planes(0)):
        to_low[p] = own(f)[6 + i].astype(BF16)
    for n in range(2):
        for c in range(2):
            to_low[13 + 2 * n + c] = saved[n, 1 + c, 7]
    for p, (f, i) in enumerate(high_planes(0)):
        to_high[p] = own(f)[i].astype(BF16)


def corner_kernel(
    electric, magnetic, inverse, saved, x_low, x_high, after, to_low, to_high, low, high
):
    x_of = [{}, {}]
    for p, key in enumerate(low_planes(0)):
        x_of[0][key] = x_low[p].astype(F32)
    for p, key in enumerate(high_planes(0)):
        x_of[1][key] = x_high[p].astype(F32)
    low[...] = jnp.zeros(low.shape, F32)
    high[...] = jnp.zeros(high.shape, F32)
    for to, planes, start in ((low, low_planes(1), 14), (high, high_planes(1), 0)):
        for p, (f, i) in enumerate(planes):
            own = electric.at[f] if f < 3 else (magnetic.at[f - 3] if f < 6 else inverse)
            row = start + i
            to[p, 0:8, :] = own[:, row, :]
            for side, at in ((1, 8), (0, 10)):
                for layer in range(2):
                    if (f, layer) in x_of[side]:
                        got = x_of[side][(f, layer)]
                        to[p, at + layer : at + layer + 1, :] = got[row : row + 1]
    for n in range(2):
        for i, c in enumerate((0, 2)):
            low[13 + 2 * n + i, 0:8, :] = saved[n, c].astype(F32)[:, RY - 1, :]
    to_low[...] = low[...].astype(BF16)
    to_high[...] = high[...].astype(BF16)


def first_kernel(
    mon, weights, electric, magnetic, inverse, saved, x_low, x_high, y_low, y_high, after,
    early, curled, factor, grad, ready, e_ext, h_ext, g_ext,
):
    b, w = own_block()
    lane = iota((1, NZ), 1)
    zero = jnp.zeros((12, 24, NZ), F32)
    for c in range(7):
        to = e_ext.at[c] if c < 3 else (h_ext.at[c - 3] if c < 6 else g_ext)
        to[...] = zero
        own = electric[c] if c < 3 else (magnetic[c - 3] if c < 6 else inverse[...])
        to[0:8, 0:16, :] = own
        for planes, ref, at in ((high_planes(0), x_high, 8), (low_planes(0), x_low, 10)):
            for p, (f, i) in enumerate(planes):
                if f == c:
                    to[at + i, 0:16, :] = ref[p].astype(F32)
        for planes, ref, at in ((high_planes(1), y_high, 16), (low_planes(1), y_low, 22)):
            for p, (f, i) in enumerate(planes):
                if f == c:
                    to[:, at + i : at + i + 1, :] = ref[p].astype(F32)[0:12][:, None, :]

    g = g_ext[...]
    half = 0.5 * g
    a = [half * e_ext[c] for c in range(3)]
    spot_x = iota((12, 24, 1), 0)
    spot_y = iota((12, 24, 1), 1)
    outside = ((spot_x >= 10) & (b == 0)) | ((spot_y >= 22) & (w == 0))
    inside = jnp.where(outside, 0.0, 1.0)
    turned = curl_ahead(*a)
    h = [h_ext[c] + inside * turned[c] for c in range(3)]
    back = curl_behind(*h)
    for c in range(3):
        e_ext[c] = e_ext[c] - 0.5 * back[c]

    def hit(x, y, z):
        lx, ly = x - b * RX, y - w * RY
        return (lx >= -2) & (lx < RX + 2) & (ly >= -2) & (ly < RY + 2)

    def add(i, flat):
        x, y, z = place_of(flat)
        lx, ly = x - b * RX, y - w * RY
        px = jnp.where(lx < 0, lx + 12, lx)
        py = jnp.where(ly < 0, ly + 24, ly)
        for c in range(3):
            row = e_ext[c, px, pl.ds(py, 1), :]
            e_ext[c, px, pl.ds(py, 1), :] = row + jnp.where(lane == z, weights[c, 0, i], 0.0)

    scan(mon, hit, add)
    for c in range(3):
        early[c, 0:9] = e_ext[c, 0:9]
        early[c, 9:10] = e_ext[c, 11:12]
        curled[c, 0:9] = h[c][0:9]
        curled[c, 9:10] = h[c][11:12]
    factor[0:9] = half[0:9]
    factor[9:10] = half[11:12]

    near = inverse[...]
    for step in range(2):
        s = [saved[step, c].astype(F32) for c in range(3)]
        before_x = {c: jnp.concatenate([x_low[12 + 2 * step + c].astype(F32)[None], s[c][:-1]], 0) for c in (1, 2)}
        before_y = {}
        for c in (0, 2):
            edge = y_low[13 + 2 * step + c // 2].astype(F32)[0:8][:, None, :]
            first = iota((RX, RY, NZ), 1) == 0
            before_y[c] = jnp.where(first, edge, pltpu.roll(s[c], 1, 1))
        curls = (
            (s[2] - before_y[2]) - (s[1] - z_behind(s[1])),
            (s[0] - z_behind(s[0])) - (s[2] - before_x[2]),
            (s[1] - before_x[1]) - (s[0] - before_y[0]),
        )
        if step == 0:
            for c in range(3):
                ready[c] = near * curls[c]
        else:
            total = jnp.zeros((RX, RY, NZ), F32)
            for c in range(3):
                total = total + a[c][0:8, 0:16] * near * curls[c]
            grad[...] = -total


def second_kernel(
    lines, table, apart, early, curled, factor, first_grad, ready, injected,
    grad_e, grad_h, grad_eps, sources,
):
    b, w = own_block()
    turn = (((0,), (0,)), ((), ()))
    main = lax.dot_general(lines[:, 0:512], table[...], turn, preferred_element_type=F32)
    main = main.reshape(32, 16, NZ)
    edge = jnp.dot(lines[:, 512:640], apart[...], preferred_element_type=F32).astype(BF16)
    edge = lax.dot_general(edge, table[...], turn, preferred_element_type=F32)
    edge = edge.reshape(32, 8, NZ)
    half = factor[...]
    e1 = []
    for c in range(3):
        at = slice(c * 10, c * 10 + 10)
        e1.append(early[c] + jnp.concatenate([main[at], edge[at]], 1))
    a = [half * e for e in e1]
    spot_x = iota((10, 24, 1), 0)
    spot_y = iota((10, 24, 1), 1)
    outside = ((spot_x == 9) & (b == 0)) | ((spot_y == 23) & (w == 0))
    inside = jnp.where(outside, 0.0, 1.0)
    turned = curl_ahead(*a)
    h = [curled[c] + inside * turned[c] for c in range(3)]
    backed = curl_behind(*h)
    total = first_grad[...]
    for c in range(3):
        grad_h[c] = h[c][0:8, 0:16]
        grad_e[c] = e1[c][0:8, 0:16] - 0.5 * backed[c][0:8, 0:16]
        total = total - a[c][0:8, 0:16] * ready[c]
    grad_eps[...] = total
    got = lines[:, 0:384].astype(F32).reshape(WIDE, 8, 384).sum(0)
    got = got[6:7] + got[7:8]
    moved = pltpu.roll(got, 384 - 64, 1)
    for n in range(2):
        for c in range(3):
            at = n * 3 + c
            line = got if at % 2 == 0 else moved
            line = line[:, at // 2 * LANES : (at // 2 + 1) * LANES]
            if n == 0:
                line = line + injected[c : c + 1, :]
            sources[c, n : n + 1, :] = line[:, 0:64]


def call(kernel, outs, places, scratch=(), flops=0, moved=0, params=PARAMS):
    spaces = {"s": pltpu.SMEM, "v": pltpu.VMEM, "a": pl.ANY}
    return pl.pallas_call(
        kernel,
        out_shape=outs,
        in_specs=[pl.BlockSpec(memory_space=spaces[p]) for p in places],
        out_specs=jax.tree.map(lambda _: pl.BlockSpec(memory_space=pltpu.VMEM), outs),
        scratch_shapes=list(scratch),
        compiler_params=params,
        cost_estimate=pl.CostEstimate(flops=flops, bytes_accessed=moved, transcendentals=0),
    )


def shape(*dims, dtype=F32):
    return jax.ShapeDtypeStruct(dims, dtype)


def passed_along(block, axis, distance):
    devices = range(lax.axis_size(axis))
    route = [(i - distance, i) for i in devices if i - distance in devices]
    return lax.ppermute(block, axis, route)


def dealt_near(block):
    groups = [
        [(f * NEAR + n) * HALVES + half for n in range(NEAR)]
        for f in range(DEPTH // NEAR)
        for half in range(HALVES)
    ]
    return lax.all_to_all(
        block, "bulk", split_axis=0, concat_axis=0, axis_index_groups=groups, tiled=True
    )


def tables_of(name):
    return jnp.asarray(TABLES[name])


def body(
    seed_electric, seed_magnetic, saved_magnetic, material, permittivity, source_cells,
    monitor_cells, monitor_weights, lift_weight, project_weight, mode_mix, gain_first, gain_second,
):
    weights = monitor_weights.transpose(2, 0, 1)
    big, dma = pltpu.CompilerParams(vmem_limit_bytes=56 * 1024 * 1024), pltpu.SemaphoreType.DMA
    block = (RX, RY, NZ)

    payload, field = call(
        lift_kernel,
        (shape(384, LANES, dtype=BF16), shape(3, *block)),
        "aaaa",
        [
            pltpu.SMEM((64,), jnp.int32), pltpu.VMEM((3, 2, 64), F32),
            pltpu.VMEM((LANES, LANES), BF16), dma((4,)),
        ],
        13_000_000,
        500_000,
        big,
    )(monitor_cells, weights, seed_electric, tables_of("lift_z"))
    lines = lax.all_to_all(payload, "wide", split_axis=0, concat_axis=0, tiled=True)

    taken, inverse = call(
        share_kernel,
        (shape(8, LANES), shape(*block)),
        "aavaa",
        [
            pltpu.SMEM((64,), jnp.int32), pltpu.SMEM((8,), F32), pltpu.VMEM((3, *block), F32),
            pltpu.VMEM(block, jnp.int32), pltpu.VMEM((3, 12, 32, NZ), F32),
            pltpu.VMEM((3, 12, 32, NZ), F32), dma((4,)),
        ],
        3_000_000,
        1_500_000,
    )(source_cells, permittivity, field, seed_magnetic, material)

    dealt = call(
        middle_kernel, shape(BULK * 8, 2 * LANES, dtype=BF16), "vvv", (), 20_000_000, 400_000
    )(lines, taken, tables_of("fwd_y"))
    gathered = lax.all_to_all(dealt, "bulk", split_axis=0, concat_axis=0, tiled=True)

    cells = jnp.concatenate([source_cells, source_cells]).reshape(1, LANES)
    coef_a, coef_b, phase_x, phase_yz, injected = call(
        param_kernel,
        (
            shape(9 * PAD, LANES), shape(9 * PAD, LANES), shape(LANES, LANES, dtype=BF16),
            shape(PAD, LANES), shape(8, LANES),
        ),
        "sssvvvvvvvva",
        (),
        20_000_000,
        1_000_000,
    )(
        monitor_cells, weights, lift_weight.T, cells, project_weight, gain_first, gain_second,
        mode_mix.transpose(0, 2, 3, 1), tables_of("at_x"), tables_of("at_y"), tables_of("at_z"),
        dealt,
    )

    to_low, to_high = call(
        edge_kernel,
        (shape(17, RY, NZ, dtype=BF16), shape(10, RY, NZ, dtype=BF16)),
        "vvvva",
        (),
        0,
        500_000,
    )(field, seed_magnetic, inverse, saved_magnetic, dealt)
    x_low = passed_along(to_low, "bulk", 1)
    x_high = passed_along(to_high, "bulk", -1)

    low_part, high_part = call(
        corner_kernel,
        (shape(17, 16, NZ, dtype=BF16), shape(10, 16, NZ, dtype=BF16)),
        "vvvvvva",
        [pltpu.VMEM((17, 16, NZ), F32), pltpu.VMEM((10, 16, NZ), F32)],
        0,
        1_000_000,
    )(field, seed_magnetic, inverse, saved_magnetic, x_low, x_high, coef_a)
    shares = call(
        filter_kernel, shape(NEAR * 16, 2 * LANES, dtype=BF16), "vvvvvvva", (), 40_000_000, 600_000
    )(
        gathered, coef_a, coef_b, tables_of("fwd_x"), tables_of("inv_x"), phase_x, phase_yz,
        low_part,
    )
    back = dealt_near(shares)

    y_low = passed_along(low_part, "wide", 1)
    y_high = passed_along(high_part, "wide", -1)

    sent = call(
        spread_kernel,
        shape(128, 640, dtype=BF16),
        "vva",
        [pltpu.VMEM((32, 8, LANES), F32)],
        40_000_000,
        600_000,
    )(back, tables_of("inv_y"), y_low)
    returned = lax.all_to_all(sent, "wide", split_axis=0, concat_axis=0, tiled=True)
    early, curled, factor, first_grad, ready = call(
        first_kernel,
        (
            shape(3, 10, 24, NZ), shape(3, 10, 24, NZ), shape(10, 24, NZ), shape(*block),
            shape(3, *block),
        ),
        "ssvvvvvvvva",
        [pltpu.VMEM((3, 12, 24, NZ), F32)] * 2 + [pltpu.VMEM((12, 24, NZ), F32)],
        10_000_000,
        3_000_000,
    )(
        monitor_cells, weights, field, seed_magnetic, inverse, saved_magnetic,
        x_low, x_high, y_low, y_high, sent,
    )

    grad_e, grad_h, grad_eps, sources = call(
        second_kernel,
        (shape(3, *block), shape(3, *block), shape(*block), shape(3, 2, 64)),
        "vvvvvvvvv",
        (),
        40_000_000,
        4_000_000,
    )(
        returned, tables_of("back_z"), tables_of("apart"), early, curled, factor, first_grad,
        ready, injected,
    )
    return grad_e, grad_h, grad_eps, sources.transpose(1, 2, 0)


def solution(mesh):
    field = P(None, "bulk", "wide", None)
    return jax.shard_map(
        body,
        mesh=mesh,
        in_specs=(
            field, field, P(None, None, "bulk", "wide", None), P("bulk", "wide", None),
            P(), P(), P(), P(), P(), P(), P(), P(), P(),
        ),
        out_specs=(field, field, P("bulk", "wide", None), P()),
        check_vma=False,
    )
```

```python
import functools
import math

import jax
import jax.numpy as jnp
import ml_dtypes
import numpy as np
from jax import lax
from jax.experimental import pallas as pl
from jax.experimental.pallas import tpu as pltpu
from jax.sharding import PartitionSpec as P

NX, NY, NZ = 256, 256, 128
K = 48
OWN = 3
WIDE, BULK = 16, 32
RX, RY = 8, 16
NEAR, FAR = 8, 4
SHARE = OWN * K // NEAR
PAD = 24
LANES = 128
F32, BF16 = jnp.float32, jnp.bfloat16
PARAMS = pltpu.CompilerParams(vmem_limit_bytes=40 * 1024 * 1024)
HIGHEST = lax.Precision.HIGHEST


def waves(freqs, places, total):
    phase = np.mod(np.asarray(freqs)[:, None] * np.asarray(places)[None, :], total)
    angle = phase.astype(np.float32) * np.float32(2.0 * math.pi / total)
    return np.cos(angle).astype(np.float32), np.sin(angle).astype(np.float32)


def rounded(table):
    return np.asarray(table, np.float32).astype(ml_dtypes.bfloat16)


def make_tables():
    mode = np.arange(K)
    plane = np.where(mode < K // 2, mode, mode - K)
    cz, sz = waves(mode, np.arange(NZ), NZ)
    cx, sx = (rounded(t) for t in waves(plane, np.arange(NX), NX))
    cy, sy = (rounded(t) for t in waves(plane, np.arange(NY), NY))
    scale = np.float32(1.0 / math.sqrt(NX * NY * NZ))
    back = np.float32(1.0 / math.sqrt(K**3))
    fz, gz = rounded(cz * scale), rounded(-sz * scale)
    bz, hz = rounded(cz * back), rounded(sz * back)
    out = {}
    lift_z = np.zeros((LANES, LANES), ml_dtypes.bfloat16)
    back_z = np.zeros((LANES, LANES), ml_dtypes.bfloat16)
    for w in range(WIDE):
        for i in range(OWN):
            lift_z[:, w * 8 + i] = fz[w * OWN + i]
            lift_z[:, w * 8 + OWN + i] = gz[w * OWN + i]
            back_z[w * 8 + i] = bz[w * OWN + i]
            back_z[w * 8 + OWN + i] = -hz[w * OWN + i]
    out["lift_z"], out["back_z"] = lift_z, back_z

    lane = np.arange(LANES)
    y_of = np.concatenate([(h * 8 + lane % 8) * RY + lane // 8 for h in range(2)])
    fwd_y = np.zeros((512, 256), ml_dtypes.bfloat16)
    fwd_y[:256, :K] = cy[:, y_of].T
    fwd_y[256:, :K] = sy[:, y_of].T
    fwd_y[:256, 128 : 128 + K] = -sy[:, y_of].T
    fwd_y[256:, 128 : 128 + K] = cy[:, y_of].T
    out["fwd_y"] = fwd_y

    inv_x = np.zeros((FAR, LANES, LANES), ml_dtypes.bfloat16)
    for far in range(FAR):
        for n in range(NEAR):
            start = (far * NEAR + n) * RX
            x_of = (start + np.array([0, 1, 2, 3, 4, 5, 6, 7, 8, -1])) % NX
            inv_x[far, n * 16 : n * 16 + 10, :K] = cx[:, x_of].T
            inv_x[far, n * 16 : n * 16 + 10, 64 : 64 + K] = -sx[:, x_of].T
    out["inv_x"] = inv_x

    inv_y = np.zeros((LANES, 384), ml_dtypes.bfloat16)
    inv_y[:K, :256], inv_y[64 : 64 + K, :256] = cy, -sy
    for w in range(WIDE):
        for h, y in enumerate((w * RY + RY, w * RY - 1)):
            inv_y[:K, 256 + w * 2 + h] = cy[:, y % NY]
            inv_y[64 : 64 + K, 256 + w * 2 + h] = -sy[:, y % NY]
    out["inv_y"] = inv_y
    apart = np.zeros((LANES, 256), ml_dtypes.bfloat16)
    for cell in range(32):
        apart[cell * 2, cell * 8] = 1
        apart[cell * 2 + 1, cell * 8 + 7] = 1
    out["apart"] = apart

    at_x = np.zeros((2, LANES, NX), ml_dtypes.bfloat16)
    at_x[0, :K], at_x[0, 64 : 64 + K] = cx, -sx
    at_x[1, :K], at_x[1, 64 : 64 + K] = sx, cx
    out["at_x"] = at_x
    at_y = np.zeros((NEAR, 2, 32, NY), ml_dtypes.bfloat16)
    for n in range(NEAR):
        j_of = np.arange(n * SHARE, (n + 1) * SHARE) % K
        at_y[n, 0, :SHARE], at_y[n, 1, :SHARE] = cy[j_of], sy[j_of]
    out["at_y"] = at_y
    at_z = np.zeros((WIDE, 2, 16, NZ), ml_dtypes.bfloat16)
    for w in range(WIDE):
        at_z[w, 0, :OWN] = bz[w * OWN : (w + 1) * OWN]
        at_z[w, 1, :OWN] = hz[w * OWN : (w + 1) * OWN]
    out["at_z"] = at_z
    return out


TABLES = make_tables()


def iota(shape, axis):
    return lax.broadcasted_iota(jnp.int32, shape, axis)


def exchange(tiles, block, axis):
    tiles = list(tiles)
    shape = tiles[0].shape
    size = shape[axis]
    place = iota(shape, axis) // block
    step = 1
    while step < len(tiles):
        high = (place // step) % 2 == 1
        new = list(tiles)
        for low in range(len(tiles)):
            if low & step:
                continue
            u, v = tiles[low], tiles[low + step]
            new[low] = jnp.where(high, pltpu.roll(v, step * block, axis), u)
            new[low + step] = jnp.where(high, v, pltpu.roll(u, size - step * block, axis))
        tiles = new
        step *= 2
    return tiles


def z_ahead(v):
    axis = v.ndim - 1
    return jnp.where(iota(v.shape, axis) < NZ - 1, pltpu.roll(v, NZ - 1, axis), 0.0)


def z_behind(v):
    axis = v.ndim - 1
    return jnp.where(iota(v.shape, axis) > 0, pltpu.roll(v, 1, axis), 0.0)


def x_ahead(v):
    return jnp.concatenate([v[1:], v[:1]], 0)


def x_behind(v):
    return jnp.concatenate([v[-1:], v[:-1]], 0)


def y_ahead(v):
    return pltpu.roll(v, v.shape[1] - 1, 1)


def y_behind(v):
    return pltpu.roll(v, 1, 1)


def curl_ahead(fx, fy, fz):
    return (
        (y_ahead(fz) - fz) - (z_ahead(fy) - fy),
        (z_ahead(fx) - fx) - (x_ahead(fz) - fz),
        (x_ahead(fy) - fy) - (y_ahead(fx) - fx),
    )


def curl_behind(fx, fy, fz):
    return (
        (fz - y_behind(fz)) - (fy - z_behind(fy)),
        (fx - z_behind(fx)) - (fz - x_behind(fz)),
        (fy - x_behind(fy)) - (fx - y_behind(fx)),
    )


def place_of(flat):
    return flat >> 15, (flat >> 7) & (NY - 1), flat & (NZ - 1)


def own_block():
    return lax.axis_index("bulk"), lax.axis_index("wide")


def fetch(pairs, sems):
    copies = [pltpu.make_async_copy(a, b, sems.at[i]) for i, (a, b) in enumerate(pairs)]
    for copy in copies:
        copy.start()
    return copies


def scan(cells, hit, act):
    def group(g, carry):
        found = [cells[g * 8 + i] for i in range(8)]
        hits = [hit(*place_of(f)) for f in found]
        some = functools.reduce(jnp.logical_or, hits)

        @pl.when(some)
        def _():
            for i in range(8):
                pl.when(hits[i])(functools.partial(act, g * 8 + i, found[i]))

        return carry

    lax.fori_loop(0, 8, group, 0)


def lift_kernel(mon_in, weights_in, electric, table_in, out, field, mon, weights, table, sems):
    b, w = own_block()
    copies = fetch(
        ((mon_in, mon), (electric, field), (weights_in, weights), (table_in, table)), sems
    )
    for copy in copies:
        copy.wait()
    lane = iota((1, NZ), 1)
    spot = iota((1, 64), 1)

    def hit(x, y, z):
        return ((x >> 3) == b) & ((y >> 4) == w)

    def add(i, flat):
        x, y, z = place_of(flat)
        lx, ly = x & (RX - 1), y & (RY - 1)
        for c in range(3):
            row = field[c, lx, pl.ds(ly, 1), :]
            given = jnp.where(spot == i, weights[c, 1:2, :], 0.0)
            weight = jnp.sum(given, axis=1, keepdims=True)
            field[c, lx, pl.ds(ly, 1), :] = row + jnp.where(lane == z, weight, 0.0)

    scan(mon, hit, add)
    rows = field[...].reshape(3 * RX * RY, NZ).astype(BF16)
    modes = jnp.dot(rows, table[...], preferred_element_type=F32)
    modes = modes.reshape(3, RX, 2, 8, LANES)
    tiles = exchange([modes[:, x].reshape(6, 8, LANES) for x in range(RX)], 1, 1)
    tiles = [t.reshape(3, 2, 8, LANES) for t in tiles]
    tiles = exchange([tiles[y % 8][:, y // 8] for y in range(RY)], 8, 2)
    out[...] = jnp.concatenate([t.reshape(24, LANES) for t in tiles], 0).astype(BF16)


def share_kernel(
    src_in, perm_in, field, magnetic_in, material_in,
    taken, inverse,
    src, perm, magnetic, material, scaled, held, sems,
):
    b, w = own_block()
    copies = fetch(
        (
            (src_in, src), (perm_in, perm), (magnetic_in, magnetic),
            (material_in, material),
        ),
        sems,
    )
    zero = jnp.zeros((12, 32, NZ), F32)
    for c in range(3):
        scaled[c] = zero
        held[c] = zero
    for copy in copies:
        copy.wait()
    eps = jnp.zeros((RX, RY, NZ), F32)
    cells = material[...]
    for level in range(8):
        eps = jnp.where(cells == level, perm[level], eps)
    inv = 1.0 / eps
    inverse[...] = inv
    lane = iota((1, NZ), 1)
    for c in range(3):
        scaled[c, 2:10, 8:24, :] = 0.5 * inv * field[c]
        held[c, 2:10, 8:24, :] = magnetic[c]
    taken[...] = jnp.zeros((8, LANES), F32)
    spot_row, spot_lane = iota((8, LANES), 0), iota((8, LANES), 1)

    def hit(x, y, z):
        lx, ly = x - b * RX, y - w * RY
        return (lx >= -1) & (lx <= RX) & (ly >= -1) & (ly <= RY)

    def take(i, flat):
        x, y, z = place_of(flat)
        lx, ly = x - b * RX, y - w * RY

        def a(c, dx, dy):
            return scaled[c, lx + 2 + dx, pl.ds(ly + 8 + dy, 1), :]

        def h(c, dx, dy):
            old = held[c, lx + 2 + dx, pl.ds(ly + 8 + dy, 1), :]
            if c == 0:
                near = a(1, dx, dy)
                turn = (a(2, dx, dy + 1) - a(2, dx, dy)) - (z_ahead(near) - near)
            elif c == 1:
                near = a(0, dx, dy)
                turn = (z_ahead(near) - near) - (a(2, dx + 1, dy) - a(2, dx, dy))
            else:
                turn = (a(1, dx + 1, dy) - a(1, dx, dy)) - (a(0, dx, dy + 1) - a(0, dx, dy))
            return old + turn

        left = jnp.where(x > 0, 1.0, 0.0)
        down = jnp.where(y > 0, 1.0, 0.0)
        hx, hy, hz = h(0, 0, 0), h(1, 0, 0), h(2, 0, 0)
        hx_y, hz_y = down * h(0, 0, -1), down * h(2, 0, -1)
        hy_x, hz_x = left * h(1, -1, 0), left * h(2, -1, 0)
        curls = (
            (hz - hz_y) - (hy - z_behind(hy)),
            (hx - z_behind(hx)) - (hz - hz_x),
            (hy - hy_x) - (hx - hx_y),
        )
        mine = jnp.where((lx >= 0) & (lx < RX) & (ly >= 0) & (ly < RY), 1.0, 0.0)
        cx, cy = jnp.clip(lx, 0, RX - 1), jnp.clip(ly, 0, RY - 1)
        got = taken[...]
        for c in range(3):
            old = mine * field[c, cx, pl.ds(cy, 1), :]
            for n, row in ((0, old - 0.5 * curls[c]), (1, old)):
                value = jnp.sum(jnp.where(lane == z, row, 0.0), axis=1, keepdims=True)
                spot = (spot_row == n * 3 + c) & (spot_lane == i)
                got = got + jnp.where(spot, value, 0.0)
        taken[...] = got

    scan(src, hit, take)


def middle_kernel(lines, taken, table, out):
    got = lines[...].astype(F32).reshape(WIDE, 24, LANES)
    halves = [exchange([got[h * 8 + i] for i in range(8)], 1, 1) for h in range(2)]
    rows = [
        jnp.concatenate([halves[0][k], halves[1][k], halves[0][OWN + k], halves[1][OWN + k]], 1)
        for k in range(OWN)
    ]
    lhs = jnp.concatenate(rows, 0).astype(BF16)
    found = jnp.dot(lhs, table[...], preferred_element_type=F32)
    lane = iota((8, LANES), 1)
    parts = [jnp.zeros((8, LANES), F32) for _ in range(NEAR)]
    for part in range(2):
        for d in range(3):
            piece = [
                found[(k * 3 + d) * 8 : (k * 3 + d) * 8 + 8, part * LANES : (part + 1) * LANES]
                for k in range(OWN)
            ]
            last = pltpu.roll(piece[2], 2 * K, 1)
            first = piece[0] + pltpu.roll(piece[1], K, 1) + jnp.where(lane >= 2 * K, last, 0.0)
            rest = jnp.where(lane < 16, last, 0.0)
            to = part * 64 + d * SHARE
            for n in range(NEAR):
                moved = pltpu.roll(first, (to - n * SHARE) % LANES, 1)
                if n == NEAR - 1:
                    moved = jnp.where(lane < to + 2, moved, pltpu.roll(rest, to + 2, 1))
                within = (lane >= to) & (lane < to + SHARE)
                parts[n] = parts[n] + jnp.where(within, moved, 0.0)
    src = jnp.concatenate([taken[...], jnp.zeros((LANES - 8, LANES), F32)], 0).T
    high = src.astype(BF16).astype(F32)
    extra = pltpu.roll(high, 54, 1) + pltpu.roll(src - high, 118, 1)
    deal = (jnp.concatenate(parts, 0) + extra[: NEAR * 8]).astype(BF16)
    for f in range(FAR):
        out[f * NEAR * 8 : (f + 1) * NEAR * 8, :] = deal


def param_kernel(
    mon, weights, lift, cells, project, gain_x, gain_y, mix, at_x, at_y, at_z, inv_x,
    after, coef_a, coef_b, phase_x, phase_yz, injected, back_x,
):
    b, w = own_block()
    n = b % NEAR
    back_x[...] = inv_x[b // NEAR]
    flat = cells[...]
    x, y, z = place_of(flat)
    first = iota((1, LANES), 1) < 64
    hot_x = jnp.where(iota((NX, LANES), 0) == x, 1.0, 0.0)
    real = jnp.where(first, hot_x, 0.0).astype(BF16)
    imag = jnp.where(first, 0.0, hot_x).astype(BF16)
    phase_x[...] = (
        jnp.dot(at_x[0], real, preferred_element_type=F32)
        + jnp.dot(at_x[1], imag, preferred_element_type=F32)
    ).astype(BF16)
    hot_y = jnp.where(iota((NY, LANES), 0) == y, 1.0, 0.0).astype(BF16)
    hot_z = jnp.where(iota((NZ, LANES), 0) == z, 1.0, 0.0).astype(BF16)
    cy = jnp.dot(at_y[n, 0], hot_y, preferred_element_type=F32)[:PAD]
    sy = jnp.dot(at_y[n, 1], hot_y, preferred_element_type=F32)[:PAD]
    cz = jnp.dot(at_z[w, 0], hot_z, preferred_element_type=F32)
    sz = jnp.dot(at_z[w, 1], hot_z, preferred_element_type=F32)
    mode = n * SHARE + iota((PAD, 1), 0)
    ck = jnp.where(mode < K, cz[0:1], jnp.where(mode < 2 * K, cz[1:2], cz[2:3]))
    sk = jnp.where(mode < K, sz[0:1], jnp.where(mode < 2 * K, sz[1:2], sz[2:3]))
    phase_yz[...] = jnp.where(first, cy * ck - sy * sk, -(sy * ck + cy * sk))

    place = iota((K, PAD), 1)
    mode = n * SHARE + place
    depth = jnp.where(mode < K, 0, jnp.where(mode < 2 * K, 1, 2))
    live = place < SHARE
    hot_j = jnp.where((iota((K, PAD), 0) == mode - depth * K) & live, 1.0, 0.0)
    hot_k = jnp.where((iota((K, PAD), 0) == w * OWN + depth) & live, 1.0, 0.0)
    gains = jnp.dot(gain_y[...], hot_j, precision=HIGHEST, preferred_element_type=F32)
    diagonal = iota((16, 16), 0) == iota((16, 16), 1)
    columns = [
        jnp.sum(jnp.where(diagonal, project[e : e + 1, :], 0.0), axis=1, keepdims=True)
        for e in range(3)
    ]
    blank = jnp.zeros((16, 16), F32)
    along = gain_x[...]
    totals = []
    for part in range(2):
        rows = [mix[part, c].astype(F32) for c in range(16)]
        for d in range(3):
            total = lift[d, 0] * rows[0]
            for c in range(1, 16):
                total = total + lift[d, c] * rows[c]
            totals.append(total)
    joined = jnp.dot(
        jnp.concatenate(totals, 0), hot_k, precision=HIGHEST, preferred_element_type=F32
    )
    joined = [joined[i * 16 : (i + 1) * 16] * gains for i in range(6)]
    for part, to in ((0, coef_a), (1, coef_b)):
        sign = 1.0 if part == 0 else -1.0
        right = jnp.concatenate([sign * along, blank, along, blank], 1)
        right = jnp.concatenate([columns[e] * right for e in range(3)], 1)
        left = jnp.concatenate([j.T for j in joined[part * 3 : part * 3 + 3]], 0)
        found = jnp.dot(left, right, precision=HIGHEST, preferred_element_type=F32)
        for e in range(3):
            for d in range(3):
                to[(e * 3 + d) * PAD : (e * 3 + d + 1) * PAD, :] = found[
                    d * PAD : (d + 1) * PAD, e * LANES : (e + 1) * LANES
                ]
    row = iota((8, LANES), 0)
    total = jnp.zeros((8, LANES), F32)
    for i in range(64):
        given = jnp.where(
            row == 0, weights[0, 0, i], jnp.where(row == 1, weights[1, 0, i], weights[2, 0, i])
        )
        total = total + jnp.where((flat == mon[i]) & (row < 3), given, 0.0)
    injected[...] = jnp.where(iota((8, LANES), 1) < 64, total, 0.0)


def filter_kernel(
    gathered, coef_a, coef_b, at_x, back_x, phase_x, phase_yz, after, out
):
    b, w = own_block()
    lane = iota((1, LANES), 1)
    got = gathered[...]
    real = jnp.dot(at_x[0], got, preferred_element_type=F32)
    imag = jnp.dot(at_x[1], got, preferred_element_type=F32)
    total = got.astype(F32).reshape(BULK, 8, LANES).sum(0)
    total = total + pltpu.roll(total, 64, 1)
    total = jnp.where(lane < 6, pltpu.roll(total, LANES - 54, 1), 0.0)
    total = jnp.concatenate([total, jnp.zeros((LANES - 8, LANES), F32)], 0).T[:8]
    total = pltpu.roll(total, (b % NEAR) * 8, 1)
    full = (real + pltpu.roll(imag, 64, 1)).T
    field = [full[d * SHARE : d * SHARE + 24] for d in range(3)]
    turned = [pltpu.roll(f, 64, 1) for f in field]
    sign = jnp.where(lane < 64, 1.0, -1.0)
    real = []
    for e in range(3):
        q = jnp.zeros((24, LANES), F32)
        for d in range(3):
            at = (e * 3 + d) * 24
            q = q + coef_a[at : at + 24] * field[d] + coef_b[at : at + 24] * turned[d]
        real.append(q)
    near = jnp.dot(
        jnp.concatenate(real, 0).astype(BF16), phase_x[...], preferred_element_type=F32
    )
    gap = jnp.zeros((10, LANES), F32)
    packed = jnp.concatenate([q[:SHARE] for q in real] + [gap], 0)
    right = jnp.concatenate([packed, pltpu.roll(packed, 64, 1) * sign], 0).astype(BF16)
    back = lax.dot_general(
        back_x[...], right, (((1,), (1,)), ((), ())), preferred_element_type=F32
    ).reshape(NEAR, 2, 8, LANES)
    row = iota((8, LANES), 0)
    for e in range(3):
        line = jnp.sum(near[e * 24 : (e + 1) * 24] * phase_yz[...], axis=0, keepdims=True)
        line = line + pltpu.roll(line, 64, 1)
        total = total + jnp.where((row == e) & (lane < 64), line, 0.0)
    high = total.astype(BF16).astype(F32)
    extra = pltpu.roll(high + pltpu.roll(total - high, 64, 1), 2, 0)
    tiles = []
    for n in range(NEAR):
        tiles += [back[n, 0], back[n, 1] + extra]
    out[...] = jnp.concatenate(tiles, 0).astype(BF16)


def spread_kernel(shares, inv_y, after, out, rows):
    lane = iota((1, LANES), 1)
    got = shares[...].astype(F32).reshape(NEAR, 16, LANES)
    rows[...] = jnp.zeros((32, 8, LANES), F32)
    for e in range(3):
        flat = []
        for part in range(2):
            start = part * 64 + e * SHARE
            first, rest = jnp.zeros((16, LANES), F32), None
            for n in range(NEAR):
                moved = pltpu.roll(got[n], (n * SHARE - start) % LANES, 1)
                within = (lane >= n * SHARE) & (lane < (n + 1) * SHARE)
                first = first + jnp.where(within, moved, 0.0)
                if n == NEAR - 1:
                    rest = jnp.where(lane < 16, moved, 0.0)
            flat.append((first, rest))

        def mode_rows(part, k, to):
            first, rest = flat[part]
            moved = pltpu.roll(first, (to - k * K) % LANES, 1)
            if k < 2:
                return jnp.where((lane >= to) & (lane < to + K), moved, 0.0)
            tail = pltpu.roll(rest, to + 32, 1)
            return jnp.where((lane >= to) & (lane < to + 32), moved, 0.0) + jnp.where(
                (lane >= to + 32) & (lane < to + K), tail, 0.0
            )

        for k in range(OWN):
            real = mode_rows(0, k, 0) + mode_rows(1, k, 64)
            imag = mode_rows(1, k, 0) - mode_rows(0, k, 64)
            for x in range(10):
                rows[e * 10 + x, k : k + 1, :] = real[x : x + 1]
                rows[e * 10 + x, OWN + k : OWN + k + 1, :] = imag[x : x + 1]
    lhs = rows[...].reshape(256, LANES).astype(BF16)
    wide = jnp.dot(lhs, inv_y[...], preferred_element_type=F32).reshape(32, 8, 384)
    near = []
    for low in range(8):
        group = [wide[high * 8 + low, :, c * LANES : (c + 1) * LANES] for high in range(4) for c in range(2)]
        near.append(jnp.stack(group))
    near = exchange(near, 16, 2)
    edge = []
    for low in range(16):
        edge.append(jnp.stack([wide[high * 16 + low, :, 256:384] for high in range(2)]))
    edge = exchange(edge, 2, 2)
    row = iota((8, LANES), 0)
    total = pltpu.roll(got[:, 8:16].sum(0), 6, 0)
    total = jnp.where((row < 6) & (lane < 64), total + pltpu.roll(total, 64, 1), 0.0)
    high = total.astype(BF16).astype(F32)
    other = pltpu.roll(total - high, 64, 1)
    moved = pltpu.roll(high, 64, 1)
    low = total - high
    extra = []
    for t in range(3):
        first = jnp.where(lane < 64, high[2 * t : 2 * t + 1], moved[2 * t + 1 : 2 * t + 2])
        second = jnp.where(lane < 64, low[2 * t : 2 * t + 1], other[2 * t + 1 : 2 * t + 2])
        extra.append(jnp.where(row == 6, first, jnp.where(row == 7, second, 0.0)))
    blocks = []
    for w in range(WIDE):
        tiles = [near[w % 8][high_x * 2 + w // 8] for high_x in range(4)]
        for t in range(3):
            tiles[t] = tiles[t] + extra[t]
        pair = jnp.where(lane < 32, edge[w], 0.0)
        tiles.append(pair[0] + pltpu.roll(pair[1], 32, 1))
        blocks.append(jnp.concatenate(tiles, 1))
    out[...] = jnp.concatenate(blocks, 0).astype(BF16)


def high_planes(across):
    first, second = [c for c in range(3) if c != across]
    planes = [(c, 0) for c in range(3)] + [(first, 1), (second, 1), (6, 0), (6, 1)]
    return planes + [(3 + c, 0) for c in range(3)]


def low_planes(across):
    first, second = [c for c in range(3) if c != across]
    planes = [(c, i) for i in range(2) for c in range(3)] + [(6, 0), (6, 1)]
    return planes + [(3 + first, 0), (3 + second, 0)] + [(3 + c, 1) for c in range(3)]


def edge_kernel(electric, magnetic, inverse, saved, after, to_low, to_high):
    def own(f):
        return electric.at[f] if f < 3 else (magnetic.at[f - 3] if f < 6 else inverse)

    for p, (f, i) in enumerate(low_planes(0)):
        to_low[p] = own(f)[6 + i].astype(BF16)
    for n in range(2):
        for c in range(2):
            to_low[13 + 2 * n + c] = saved[n, 1 + c, 7]
    for p, (f, i) in enumerate(high_planes(0)):
        to_high[p] = own(f)[i].astype(BF16)


def corner_kernel(
    electric, magnetic, inverse, saved, x_low, x_high, after, to_low, to_high, low, high
):
    x_of = [{}, {}]
    for p, key in enumerate(low_planes(0)):
        x_of[0][key] = x_low[p].astype(F32)
    for p, key in enumerate(high_planes(0)):
        x_of[1][key] = x_high[p].astype(F32)
    low[...] = jnp.zeros(low.shape, F32)
    high[...] = jnp.zeros(high.shape, F32)
    for to, planes, start in ((low, low_planes(1), 14), (high, high_planes(1), 0)):
        for p, (f, i) in enumerate(planes):
            own = electric.at[f] if f < 3 else (magnetic.at[f - 3] if f < 6 else inverse)
            row = start + i
            to[p, 0:8, :] = own[:, row, :]
            for side, at in ((1, 8), (0, 10)):
                for layer in range(2):
                    if (f, layer) in x_of[side]:
                        got = x_of[side][(f, layer)]
                        to[p, at + layer : at + layer + 1, :] = got[row : row + 1]
    for n in range(2):
        for i, c in enumerate((0, 2)):
            low[13 + 2 * n + i, 0:8, :] = saved[n, c].astype(F32)[:, RY - 1, :]
    to_low[...] = low[...].astype(BF16)
    to_high[...] = high[...].astype(BF16)


def first_kernel(
    mon, weights, electric, magnetic, inverse, x_low, x_high, y_low, y_high, after,
    early, curled, factor, e_ext, h_ext, g_ext,
):
    b, w = own_block()
    lane = iota((1, NZ), 1)
    zero = jnp.zeros((12, 24, NZ), F32)
    for c in range(7):
        to = e_ext.at[c] if c < 3 else (h_ext.at[c - 3] if c < 6 else g_ext)
        to[...] = zero
        own = electric[c] if c < 3 else (magnetic[c - 3] if c < 6 else inverse[...])
        to[0:8, 0:16, :] = own
        for planes, ref, at in ((high_planes(0), x_high, 8), (low_planes(0), x_low, 10)):
            for p, (f, i) in enumerate(planes):
                if f == c:
                    to[at + i, 0:16, :] = ref[p].astype(F32)
        for planes, ref, at in ((high_planes(1), y_high, 16), (low_planes(1), y_low, 22)):
            for p, (f, i) in enumerate(planes):
                if f == c:
                    to[:, at + i : at + i + 1, :] = ref[p].astype(F32)[0:12][:, None, :]

    g = g_ext[...]
    half = 0.5 * g
    a = [half * e_ext[c] for c in range(3)]
    spot_x = iota((12, 24, 1), 0)
    spot_y = iota((12, 24, 1), 1)
    outside = ((spot_x >= 10) & (b == 0)) | ((spot_y >= 22) & (w == 0))
    inside = jnp.where(outside, 0.0, 1.0)
    turned = curl_ahead(*a)
    h = [h_ext[c] + inside * turned[c] for c in range(3)]
    back = curl_behind(*h)
    for c in range(3):
        e_ext[c] = e_ext[c] - 0.5 * back[c]

    def hit(x, y, z):
        lx, ly = x - b * RX, y - w * RY
        return (lx >= -2) & (lx < RX + 2) & (ly >= -2) & (ly < RY + 2)

    def add(i, flat):
        x, y, z = place_of(flat)
        lx, ly = x - b * RX, y - w * RY
        px = jnp.where(lx < 0, lx + 12, lx)
        py = jnp.where(ly < 0, ly + 24, ly)
        for c in range(3):
            row = e_ext[c, px, pl.ds(py, 1), :]
            e_ext[c, px, pl.ds(py, 1), :] = row + jnp.where(lane == z, weights[c, 0, i], 0.0)

    scan(mon, hit, add)
    for c in range(3):
        early[c, 0:9] = e_ext[c, 0:9]
        early[c, 9:10] = e_ext[c, 11:12]
        curled[c, 0:9] = h[c][0:9]
        curled[c, 9:10] = h[c][11:12]
    factor[0:9] = half[0:9]
    factor[9:10] = half[11:12]


def saved_kernel(electric, inverse, saved, x_low, y_low, after, grad, ready):
    near = inverse[...]
    for step in range(2):
        s = [saved[step, c].astype(F32) for c in range(3)]
        before_x = {c: jnp.concatenate([x_low[12 + 2 * step + c].astype(F32)[None], s[c][:-1]], 0) for c in (1, 2)}
        before_y = {}
        for c in (0, 2):
            edge = y_low[13 + 2 * step + c // 2].astype(F32)[0:8][:, None, :]
            first = iota((RX, RY, NZ), 1) == 0
            before_y[c] = jnp.where(first, edge, pltpu.roll(s[c], 1, 1))
        curls = (
            (s[2] - before_y[2]) - (s[1] - z_behind(s[1])),
            (s[0] - z_behind(s[0])) - (s[2] - before_x[2]),
            (s[1] - before_x[1]) - (s[0] - before_y[0]),
        )
        if step == 0:
            for c in range(3):
                ready[c] = near * curls[c]
        else:
            total = jnp.zeros((RX, RY, NZ), F32)
            for c in range(3):
                total = total + 0.5 * near * electric[c] * near * curls[c]
            grad[...] = -total


def second_kernel(
    lines, table, apart, early, curled, factor, first_grad, ready, injected,
    grad_e, grad_h, grad_eps, sources,
):
    b, w = own_block()
    turn = (((0,), (0,)), ((), ()))
    main = lax.dot_general(lines[:, 0:512], table[...], turn, preferred_element_type=F32)
    main = main.reshape(32, 16, NZ)
    edge = jnp.dot(lines[:, 512:640], apart[...], preferred_element_type=F32).astype(BF16)
    edge = lax.dot_general(edge, table[...], turn, preferred_element_type=F32)
    edge = edge.reshape(32, 8, NZ)
    half = factor[...]
    e1 = []
    for c in range(3):
        at = slice(c * 10, c * 10 + 10)
        e1.append(early[c] + jnp.concatenate([main[at], edge[at]], 1))
    a = [half * e for e in e1]
    spot_x = iota((10, 24, 1), 0)
    spot_y = iota((10, 24, 1), 1)
    outside = ((spot_x == 9) & (b == 0)) | ((spot_y == 23) & (w == 0))
    inside = jnp.where(outside, 0.0, 1.0)
    turned = curl_ahead(*a)
    h = [curled[c] + inside * turned[c] for c in range(3)]
    backed = curl_behind(*h)
    total = first_grad[...]
    for c in range(3):
        grad_h[c] = h[c][0:8, 0:16]
        grad_e[c] = e1[c][0:8, 0:16] - 0.5 * backed[c][0:8, 0:16]
        total = total - a[c][0:8, 0:16] * ready[c]
    grad_eps[...] = total
    got = lines[:, 0:384].astype(F32).reshape(WIDE, 8, 384).sum(0)
    got = got[6:7] + got[7:8]
    moved = pltpu.roll(got, 384 - 64, 1)
    for n in range(2):
        for c in range(3):
            at = n * 3 + c
            line = got if at % 2 == 0 else moved
            line = line[:, at // 2 * LANES : (at // 2 + 1) * LANES]
            if n == 0:
                line = line + injected[c : c + 1, :]
            sources[c, n : n + 1, :] = line[:, 0:64]


def call(kernel, outs, places, scratch=(), flops=0, moved=0, params=PARAMS):
    spaces = {"s": pltpu.SMEM, "v": pltpu.VMEM, "a": pl.ANY}
    return pl.pallas_call(
        kernel,
        out_shape=outs,
        in_specs=[pl.BlockSpec(memory_space=spaces[p]) for p in places],
        out_specs=jax.tree.map(lambda _: pl.BlockSpec(memory_space=pltpu.VMEM), outs),
        scratch_shapes=list(scratch),
        compiler_params=params,
        cost_estimate=pl.CostEstimate(flops=flops, bytes_accessed=moved, transcendentals=0),
    )


def shape(*dims, dtype=F32):
    return jax.ShapeDtypeStruct(dims, dtype)


def passed_along(block, axis, distance):
    devices = range(lax.axis_size(axis))
    route = [(i - distance, i) for i in devices if i - distance in devices]
    return lax.ppermute(block, axis, route)


def dealt_near(block):
    groups = [[f * NEAR + n for n in range(NEAR)] for f in range(FAR)]
    return lax.all_to_all(
        block, "bulk", split_axis=0, concat_axis=0, axis_index_groups=groups, tiled=True
    )


def tables_of(name):
    return jnp.asarray(TABLES[name])


def body(
    seed_electric, seed_magnetic, saved_magnetic, material, permittivity, source_cells,
    monitor_cells, monitor_weights, lift_weight, project_weight, mode_mix, gain_first, gain_second,
):
    weights = monitor_weights.transpose(2, 0, 1)
    big, dma = pltpu.CompilerParams(vmem_limit_bytes=56 * 1024 * 1024), pltpu.SemaphoreType.DMA
    block = (RX, RY, NZ)

    payload, field = call(
        lift_kernel,
        (shape(384, LANES, dtype=BF16), shape(3, *block)),
        "aaaa",
        [
            pltpu.SMEM((64,), jnp.int32), pltpu.VMEM((3, 2, 64), F32),
            pltpu.VMEM((LANES, LANES), BF16), dma((4,)),
        ],
        13_000_000,
        500_000,
        big,
    )(monitor_cells, weights, seed_electric, tables_of("lift_z"))
    lines = lax.all_to_all(payload, "wide", split_axis=0, concat_axis=0, tiled=True)

    taken, inverse = call(
        share_kernel,
        (shape(8, LANES), shape(*block)),
        "aavaa",
        [
            pltpu.SMEM((64,), jnp.int32), pltpu.SMEM((8,), F32), pltpu.VMEM((3, *block), F32),
            pltpu.VMEM(block, jnp.int32), pltpu.VMEM((3, 12, 32, NZ), F32),
            pltpu.VMEM((3, 12, 32, NZ), F32), dma((4,)),
        ],
        3_000_000,
        1_500_000,
    )(source_cells, permittivity, field, seed_magnetic, material)

    dealt = call(
        middle_kernel, shape(BULK * 8, LANES, dtype=BF16), "vvv", (), 20_000_000, 400_000
    )(lines, taken, tables_of("fwd_y"))
    gathered = lax.all_to_all(dealt, "bulk", split_axis=0, concat_axis=0, tiled=True)

    cells = jnp.concatenate([source_cells, source_cells]).reshape(1, LANES)
    coef_a, coef_b, phase_x, phase_yz, injected, back_x = call(
        param_kernel,
        (
            shape(216, LANES), shape(216, LANES), shape(LANES, LANES, dtype=BF16),
            shape(PAD, LANES), shape(8, LANES), shape(LANES, LANES, dtype=BF16),
        ),
        "sssvvvvvvvvva",
        (),
        20_000_000,
        1_000_000,
    )(
        monitor_cells, weights, lift_weight.T, cells, project_weight, gain_first, gain_second,
        mode_mix.transpose(0, 2, 3, 1), tables_of("at_x"), tables_of("at_y"), tables_of("at_z"),
        tables_of("inv_x"), dealt,
    )

    to_low, to_high = call(
        edge_kernel,
        (shape(17, RY, NZ, dtype=BF16), shape(10, RY, NZ, dtype=BF16)),
        "vvvva",
        (),
        0,
        500_000,
    )(field, seed_magnetic, inverse, saved_magnetic, dealt)
    x_low = passed_along(to_low, "bulk", 1)
    x_high = passed_along(to_high, "bulk", -1)

    low_part, high_part = call(
        corner_kernel,
        (shape(17, 16, NZ, dtype=BF16), shape(10, 16, NZ, dtype=BF16)),
        "vvvvvva",
        [pltpu.VMEM((17, 16, NZ), F32), pltpu.VMEM((10, 16, NZ), F32)],
        0,
        1_000_000,
    )(field, seed_magnetic, inverse, saved_magnetic, x_low, x_high, coef_a)
    shares = call(
        filter_kernel, shape(LANES, LANES, dtype=BF16), "vvvvvvva", (), 40_000_000, 600_000
    )(
        gathered, coef_a, coef_b, tables_of("at_x"), back_x, phase_x, phase_yz,
        low_part,
    )
    back = dealt_near(shares)

    y_low = passed_along(low_part, "wide", 1)
    y_high = passed_along(high_part, "wide", -1)

    sent = call(
        spread_kernel,
        shape(128, 640, dtype=BF16),
        "vva",
        [pltpu.VMEM((32, 8, LANES), F32)],
        40_000_000,
        600_000,
    )(back, tables_of("inv_y"), y_low)
    returned = lax.all_to_all(sent, "wide", split_axis=0, concat_axis=0, tiled=True)
    first_grad, ready = call(
        saved_kernel, (shape(*block), shape(3, *block)), "vvvvva", (), 3_000_000, 1_000_000
    )(field, inverse, saved_magnetic, x_low, y_low, sent)
    early, curled, factor = call(
        first_kernel,
        (shape(3, 10, 24, NZ), shape(3, 10, 24, NZ), shape(10, 24, NZ)),
        "ssvvvvvvva",
        [pltpu.VMEM((3, 12, 24, NZ), F32)] * 2 + [pltpu.VMEM((12, 24, NZ), F32)],
        10_000_000,
        3_000_000,
    )(
        monitor_cells, weights, field, seed_magnetic, inverse, x_low, x_high, y_low, y_high,
        sent,
    )
    grad_e, grad_h, grad_eps, sources = call(
        second_kernel,
        (shape(3, *block), shape(3, *block), shape(*block), shape(3, 2, 64)),
        "vvvvvvvvv",
        (),
        40_000_000,
        4_000_000,
    )(
        returned, tables_of("back_z"), tables_of("apart"), early, curled, factor, first_grad,
        ready, injected,
    )
    return grad_e, grad_h, grad_eps, sources.transpose(1, 2, 0)


def solution(mesh):
    field = P(None, "bulk", "wide", None)
    return jax.shard_map(
        body,
        mesh=mesh,
        in_specs=(
            field, field, P(None, None, "bulk", "wide", None), P("bulk", "wide", None),
            P(), P(), P(), P(), P(), P(), P(), P(), P(),
        ),
        out_specs=(field, field, P("bulk", "wide", None), P()),
        check_vma=False,
    )
```

```python
import functools
import math

import jax
import jax.numpy as jnp
import ml_dtypes
import numpy as np
from jax import lax
from jax.experimental import pallas as pl
from jax.experimental.pallas import tpu as pltpu
from jax.sharding import PartitionSpec as P

NX, NY, NZ = 256, 256, 128
K = 48
OWN = 3
WIDE, BULK = 16, 32
RX, RY = 8, 16
NEAR, DEPTH, HALVES = 4, 16, 2
SHARE = OWN * K // NEAR
PAD = 40
LANES = 128
F32, BF16 = jnp.float32, jnp.bfloat16
PARAMS = pltpu.CompilerParams(vmem_limit_bytes=40 * 1024 * 1024)
HIGHEST = lax.Precision.HIGHEST


def waves(freqs, places, total):
    phase = np.mod(np.asarray(freqs)[:, None] * np.asarray(places)[None, :], total)
    angle = phase.astype(np.float32) * np.float32(2.0 * math.pi / total)
    return np.cos(angle).astype(np.float32), np.sin(angle).astype(np.float32)


def rounded(table):
    return np.asarray(table, np.float32).astype(ml_dtypes.bfloat16)


def make_tables():
    mode = np.arange(K)
    plane = np.where(mode < K // 2, mode, mode - K)
    cz, sz = waves(mode, np.arange(NZ), NZ)
    cx, sx = (rounded(t) for t in waves(plane, np.arange(NX), NX))
    cy, sy = (rounded(t) for t in waves(plane, np.arange(NY), NY))
    scale = np.float32(1.0 / math.sqrt(NX * NY * NZ))
    back = np.float32(1.0 / math.sqrt(K**3))
    fz, gz = rounded(cz * scale), rounded(-sz * scale)
    bz, hz = rounded(cz * back), rounded(sz * back)
    out = {}
    lift_z = np.zeros((LANES, LANES), ml_dtypes.bfloat16)
    back_z = np.zeros((LANES, LANES), ml_dtypes.bfloat16)
    for w in range(WIDE):
        for i in range(OWN):
            lift_z[:, w * 8 + i] = fz[w * OWN + i]
            lift_z[:, w * 8 + OWN + i] = gz[w * OWN + i]
            back_z[w * 8 + i] = bz[w * OWN + i]
            back_z[w * 8 + OWN + i] = -hz[w * OWN + i]
    out["lift_z"], out["back_z"] = lift_z, back_z

    lane = np.arange(LANES)
    y_of = np.concatenate([(h * 8 + lane % 8) * RY + lane // 8 for h in range(2)])
    fwd_y = np.zeros((512, 256), ml_dtypes.bfloat16)
    fwd_y[:256, :K] = cy[:, y_of].T
    fwd_y[256:, :K] = sy[:, y_of].T
    fwd_y[:256, 128 : 128 + K] = -sy[:, y_of].T
    fwd_y[256:, 128 : 128 + K] = cy[:, y_of].T
    out["fwd_y"] = fwd_y

    inv_x = np.zeros((DEPTH // NEAR, HALVES, NEAR * 16, LANES), ml_dtypes.bfloat16)
    for half in range(HALVES):
        for z in range(DEPTH):
            start = (z * HALVES + half) * RX
            x_of = (start + np.array([0, 1, 2, 3, 4, 5, 6, 7, 8, -1])) % NX
            at = slice(z % NEAR * 16, z % NEAR * 16 + 10)
            inv_x[z // NEAR, half, at, :K] = cx[:, x_of].T
            inv_x[z // NEAR, half, at, 64 : 64 + K] = -sx[:, x_of].T
    out["inv_x"] = inv_x

    inv_y = np.zeros((LANES, 384), ml_dtypes.bfloat16)
    inv_y[:K, :256], inv_y[64 : 64 + K, :256] = cy, -sy
    for w in range(WIDE):
        for h, y in enumerate((w * RY + RY, w * RY - 1)):
            inv_y[:K, 256 + w * 2 + h] = cy[:, y % NY]
            inv_y[64 : 64 + K, 256 + w * 2 + h] = -sy[:, y % NY]
    out["inv_y"] = inv_y
    apart = np.zeros((LANES, 256), ml_dtypes.bfloat16)
    for cell in range(32):
        apart[cell * 2, cell * 8] = 1
        apart[cell * 2 + 1, cell * 8 + 7] = 1
    out["apart"] = apart

    at_x = np.zeros((2, LANES, NX), ml_dtypes.bfloat16)
    at_x[0, :K], at_x[0, 64 : 64 + K] = cx, -sx
    at_x[1, :K], at_x[1, 64 : 64 + K] = sx, cx
    out["at_x"] = at_x
    at_y = np.zeros((NEAR, 2, 48, NY), ml_dtypes.bfloat16)
    for n in range(NEAR):
        j_of = np.arange(n * SHARE, (n + 1) * SHARE) % K
        at_y[n, 0, :SHARE], at_y[n, 1, :SHARE] = cy[j_of], sy[j_of]
    out["at_y"] = at_y
    at_z = np.zeros((WIDE, 2, 16, NZ), ml_dtypes.bfloat16)
    for w in range(WIDE):
        at_z[w, 0, :OWN] = bz[w * OWN : (w + 1) * OWN]
        at_z[w, 1, :OWN] = hz[w * OWN : (w + 1) * OWN]
    out["at_z"] = at_z
    return out


TABLES = make_tables()


def iota(shape, axis):
    return lax.broadcasted_iota(jnp.int32, shape, axis)


def exchange(tiles, block, axis):
    tiles = list(tiles)
    shape = tiles[0].shape
    size = shape[axis]
    place = iota(shape, axis) // block
    step = 1
    while step < len(tiles):
        high = (place // step) % 2 == 1
        new = list(tiles)
        for low in range(len(tiles)):
            if low & step:
                continue
            u, v = tiles[low], tiles[low + step]
            new[low] = jnp.where(high, pltpu.roll(v, step * block, axis), u)
            new[low + step] = jnp.where(high, v, pltpu.roll(u, size - step * block, axis))
        tiles = new
        step *= 2
    return tiles


def z_ahead(v):
    axis = v.ndim - 1
    return jnp.where(iota(v.shape, axis) < NZ - 1, pltpu.roll(v, NZ - 1, axis), 0.0)


def z_behind(v):
    axis = v.ndim - 1
    return jnp.where(iota(v.shape, axis) > 0, pltpu.roll(v, 1, axis), 0.0)


def x_ahead(v):
    return jnp.concatenate([v[1:], v[:1]], 0)


def x_behind(v):
    return jnp.concatenate([v[-1:], v[:-1]], 0)


def y_ahead(v):
    return pltpu.roll(v, v.shape[1] - 1, 1)


def y_behind(v):
    return pltpu.roll(v, 1, 1)


def curl_ahead(fx, fy, fz):
    return (
        (y_ahead(fz) - fz) - (z_ahead(fy) - fy),
        (z_ahead(fx) - fx) - (x_ahead(fz) - fz),
        (x_ahead(fy) - fy) - (y_ahead(fx) - fx),
    )


def curl_behind(fx, fy, fz):
    return (
        (fz - y_behind(fz)) - (fy - z_behind(fy)),
        (fx - z_behind(fx)) - (fz - x_behind(fz)),
        (fy - x_behind(fy)) - (fx - y_behind(fx)),
    )


def place_of(flat):
    return flat >> 15, (flat >> 7) & (NY - 1), flat & (NZ - 1)


def own_block():
    return lax.axis_index("bulk"), lax.axis_index("wide")


def fetch(pairs, sems):
    copies = [pltpu.make_async_copy(a, b, sems.at[i]) for i, (a, b) in enumerate(pairs)]
    for copy in copies:
        copy.start()
    return copies


def scan(cells, hit, act):
    def group(g, carry):
        found = [cells[g * 8 + i] for i in range(8)]
        hits = [hit(*place_of(f)) for f in found]
        some = functools.reduce(jnp.logical_or, hits)

        @pl.when(some)
        def _():
            for i in range(8):
                pl.when(hits[i])(functools.partial(act, g * 8 + i, found[i]))

        return carry

    lax.fori_loop(0, 8, group, 0)


def lift_kernel(mon_in, weights_in, electric, table_in, out, field, mon, weights, table, sems):
    b, w = own_block()
    copies = fetch(
        ((mon_in, mon), (electric, field), (weights_in, weights), (table_in, table)), sems
    )
    for copy in copies:
        copy.wait()
    lane = iota((1, NZ), 1)
    spot = iota((1, 64), 1)

    def hit(x, y, z):
        return ((x >> 3) == b) & ((y >> 4) == w)

    def add(i, flat):
        x, y, z = place_of(flat)
        lx, ly = x & (RX - 1), y & (RY - 1)
        for c in range(3):
            row = field[c, lx, pl.ds(ly, 1), :]
            given = jnp.where(spot == i, weights[c, 1:2, :], 0.0)
            weight = jnp.sum(given, axis=1, keepdims=True)
            field[c, lx, pl.ds(ly, 1), :] = row + jnp.where(lane == z, weight, 0.0)

    scan(mon, hit, add)
    rows = field[...].reshape(3 * RX * RY, NZ).astype(BF16)
    modes = jnp.dot(rows, table[...], preferred_element_type=F32)
    modes = modes.reshape(3, RX, 2, 8, LANES)
    tiles = exchange([modes[:, x].reshape(6, 8, LANES) for x in range(RX)], 1, 1)
    tiles = [t.reshape(3, 2, 8, LANES) for t in tiles]
    tiles = exchange([tiles[y % 8][:, y // 8] for y in range(RY)], 8, 2)
    out[...] = jnp.concatenate([t.reshape(24, LANES) for t in tiles], 0).astype(BF16)


def share_kernel(
    src_in, perm_in, field, magnetic_in, material_in,
    taken, inverse,
    src, perm, magnetic, material, scaled, held, sems,
):
    b, w = own_block()
    copies = fetch(
        (
            (src_in, src), (perm_in, perm), (magnetic_in, magnetic),
            (material_in, material),
        ),
        sems,
    )
    zero = jnp.zeros((12, 32, NZ), F32)
    for c in range(3):
        scaled[c] = zero
        held[c] = zero
    for copy in copies:
        copy.wait()
    eps = jnp.zeros((RX, RY, NZ), F32)
    cells = material[...]
    for level in range(8):
        eps = jnp.where(cells == level, perm[level], eps)
    inv = 1.0 / eps
    inverse[...] = inv
    lane = iota((1, NZ), 1)
    for c in range(3):
        scaled[c, 2:10, 8:24, :] = 0.5 * inv * field[c]
        held[c, 2:10, 8:24, :] = magnetic[c]
    taken[...] = jnp.zeros((8, LANES), F32)
    spot_row, spot_lane = iota((8, LANES), 0), iota((8, LANES), 1)

    def hit(x, y, z):
        lx, ly = x - b * RX, y - w * RY
        return (lx >= -1) & (lx <= RX) & (ly >= -1) & (ly <= RY)

    def take(i, flat):
        x, y, z = place_of(flat)
        lx, ly = x - b * RX, y - w * RY

        def a(c, dx, dy):
            return scaled[c, lx + 2 + dx, pl.ds(ly + 8 + dy, 1), :]

        def h(c, dx, dy):
            old = held[c, lx + 2 + dx, pl.ds(ly + 8 + dy, 1), :]
            if c == 0:
                near = a(1, dx, dy)
                turn = (a(2, dx, dy + 1) - a(2, dx, dy)) - (z_ahead(near) - near)
            elif c == 1:
                near = a(0, dx, dy)
                turn = (z_ahead(near) - near) - (a(2, dx + 1, dy) - a(2, dx, dy))
            else:
                turn = (a(1, dx + 1, dy) - a(1, dx, dy)) - (a(0, dx, dy + 1) - a(0, dx, dy))
            return old + turn

        left = jnp.where(x > 0, 1.0, 0.0)
        down = jnp.where(y > 0, 1.0, 0.0)
        hx, hy, hz = h(0, 0, 0), h(1, 0, 0), h(2, 0, 0)
        hx_y, hz_y = down * h(0, 0, -1), down * h(2, 0, -1)
        hy_x, hz_x = left * h(1, -1, 0), left * h(2, -1, 0)
        curls = (
            (hz - hz_y) - (hy - z_behind(hy)),
            (hx - z_behind(hx)) - (hz - hz_x),
            (hy - hy_x) - (hx - hx_y),
        )
        mine = jnp.where((lx >= 0) & (lx < RX) & (ly >= 0) & (ly < RY), 1.0, 0.0)
        cx, cy = jnp.clip(lx, 0, RX - 1), jnp.clip(ly, 0, RY - 1)
        got = taken[...]
        for c in range(3):
            old = mine * field[c, cx, pl.ds(cy, 1), :]
            for n, row in ((0, old - 0.5 * curls[c]), (1, old)):
                value = jnp.sum(jnp.where(lane == z, row, 0.0), axis=1, keepdims=True)
                spot = (spot_row == n * 3 + c) & (spot_lane == i)
                got = got + jnp.where(spot, value, 0.0)
        taken[...] = got

    scan(src, hit, take)


def middle_kernel(lines, taken, table, out):
    got = lines[...].astype(F32).reshape(WIDE, 24, LANES)
    halves = [exchange([got[h * 8 + i] for i in range(8)], 1, 1) for h in range(2)]
    rows = [
        jnp.concatenate([halves[0][k], halves[1][k], halves[0][OWN + k], halves[1][OWN + k]], 1)
        for k in range(OWN)
    ]
    lhs = jnp.concatenate(rows, 0).astype(BF16)
    found = jnp.dot(lhs, table[...], preferred_element_type=F32)
    lane = iota((8, LANES), 1)
    parts = [[jnp.zeros((8, LANES), F32) for _ in range(2)] for _ in range(NEAR)]
    split = LANES - (NEAR - 1) * SHARE
    for part in range(2):
        for d in range(3):
            piece = [
                found[(k * 3 + d) * 8 : (k * 3 + d) * 8 + 8, part * LANES : (part + 1) * LANES]
                for k in range(OWN)
            ]
            last = pltpu.roll(piece[2], 2 * K, 1)
            first = piece[0] + pltpu.roll(piece[1], K, 1) + jnp.where(lane >= 2 * K, last, 0.0)
            rest = jnp.where(lane < 16, last, 0.0)
            to = d * SHARE
            for n in range(NEAR):
                shift = (to - n * SHARE) % LANES
                moved = pltpu.roll(first, shift, 1) if shift else first
                if n == NEAR - 1:
                    moved = jnp.where(lane < to + split, moved, pltpu.roll(rest, to + split, 1))
                within = (lane >= to) & (lane < to + SHARE)
                parts[n][part] = parts[n][part] + jnp.where(within, moved, 0.0)
    src = jnp.concatenate([taken[...], jnp.zeros((LANES - 8, LANES), F32)], 0).T
    src = jnp.where(iota((LANES, LANES), 1) < 6, src, 0.0)
    high = src.astype(BF16).astype(F32)
    at = 3 * SHARE
    rows = []
    for n in range(NEAR):
        for part, value in enumerate((high, src - high)):
            for i in range(2):
                start = n * 16 + i * 8
                parts[n][part] = parts[n][part] + pltpu.roll(
                    value[start : start + 8], at + i * 6, 1
                )
        rows.append(jnp.concatenate(parts[n], 1))
    deal = jnp.concatenate([r for r in rows for _ in range(HALVES)], 0).astype(BF16)
    size = NEAR * HALVES * 8
    for f in range(DEPTH // NEAR):
        out[f * size : (f + 1) * size, :] = deal


def param_kernel(
    mon, weights, lift, cells, project, gain_x, gain_y, mix, at_x, at_y, at_z, inv_x,
    after, coef_a, coef_b, phase_x, phase_yz, injected, back_x,
):
    b, w = own_block()
    n = b // HALVES % NEAR
    back_x[...] = inv_x[b // (HALVES * NEAR), b % HALVES]
    flat = cells[...]
    x, y, z = place_of(flat)
    first = iota((1, LANES), 1) < 64
    hot_x = jnp.where(iota((NX, LANES), 0) == x, 1.0, 0.0)
    real = jnp.where(first, hot_x, 0.0).astype(BF16)
    imag = jnp.where(first, 0.0, hot_x).astype(BF16)
    phase_x[...] = (
        jnp.dot(at_x[0], real, preferred_element_type=F32)
        + jnp.dot(at_x[1], imag, preferred_element_type=F32)
    ).astype(BF16)
    hot_y = jnp.where(iota((NY, LANES), 0) == y, 1.0, 0.0).astype(BF16)
    hot_z = jnp.where(iota((NZ, LANES), 0) == z, 1.0, 0.0).astype(BF16)
    cy = jnp.dot(at_y[n, 0], hot_y, preferred_element_type=F32)[:PAD]
    sy = jnp.dot(at_y[n, 1], hot_y, preferred_element_type=F32)[:PAD]
    cz = jnp.dot(at_z[w, 0], hot_z, preferred_element_type=F32)
    sz = jnp.dot(at_z[w, 1], hot_z, preferred_element_type=F32)
    mode = n * SHARE + iota((PAD, 1), 0)
    ck = jnp.where(mode < K, cz[0:1], jnp.where(mode < 2 * K, cz[1:2], cz[2:3]))
    sk = jnp.where(mode < K, sz[0:1], jnp.where(mode < 2 * K, sz[1:2], sz[2:3]))
    phase_yz[...] = jnp.where(first, cy * ck - sy * sk, -(sy * ck + cy * sk))

    place = iota((K, PAD), 1)
    mode = n * SHARE + place
    depth = jnp.where(mode < K, 0, jnp.where(mode < 2 * K, 1, 2))
    live = place < SHARE
    hot_j = jnp.where((iota((K, PAD), 0) == mode - depth * K) & live, 1.0, 0.0)
    hot_k = jnp.where((iota((K, PAD), 0) == w * OWN + depth) & live, 1.0, 0.0)
    gains = jnp.dot(gain_y[...], hot_j, precision=HIGHEST, preferred_element_type=F32)
    diagonal = iota((16, 16), 0) == iota((16, 16), 1)
    columns = [
        jnp.sum(jnp.where(diagonal, project[e : e + 1, :], 0.0), axis=1, keepdims=True)
        for e in range(3)
    ]
    blank = jnp.zeros((16, 16), F32)
    along = gain_x[...]
    totals = []
    for part in range(2):
        rows = [mix[part, c].astype(F32) for c in range(16)]
        for d in range(3):
            total = lift[d, 0] * rows[0]
            for c in range(1, 16):
                total = total + lift[d, c] * rows[c]
            totals.append(total)
    joined = jnp.dot(
        jnp.concatenate(totals, 0), hot_k, precision=HIGHEST, preferred_element_type=F32
    )
    joined = [joined[i * 16 : (i + 1) * 16] * gains for i in range(6)]
    for part, to in ((0, coef_a), (1, coef_b)):
        sign = 1.0 if part == 0 else -1.0
        right = jnp.concatenate([sign * along, blank, along, blank], 1)
        right = jnp.concatenate([columns[e] * right for e in range(3)], 1)
        left = jnp.concatenate([j.T for j in joined[part * 3 : part * 3 + 3]], 0)
        found = jnp.dot(left, right, precision=HIGHEST, preferred_element_type=F32)
        for e in range(3):
            for d in range(3):
                to[(e * 3 + d) * PAD : (e * 3 + d + 1) * PAD, :] = found[
                    d * PAD : (d + 1) * PAD, e * LANES : (e + 1) * LANES
                ]
    row = iota((8, LANES), 0)
    total = jnp.zeros((8, LANES), F32)
    for i in range(64):
        given = jnp.where(
            row == 0, weights[0, 0, i], jnp.where(row == 1, weights[1, 0, i], weights[2, 0, i])
        )
        total = total + jnp.where((flat == mon[i]) & (row < 3), given, 0.0)
    injected[...] = jnp.where(iota((8, LANES), 1) < 64, total, 0.0)


def filter_kernel(
    gathered, coef_a, coef_b, at_x, back_x, phase_x, phase_yz, after, out
):
    b, w = own_block()
    near = b // HALVES % NEAR
    lane = iota((1, LANES), 1)
    got = gathered[...]
    real = jnp.dot(at_x[0], got[:, :LANES], preferred_element_type=F32)
    imag = jnp.dot(at_x[1], got[:, LANES:], preferred_element_type=F32)
    full = (real + imag).T
    field = [full[d * SHARE : d * SHARE + PAD] for d in range(3)]
    turned = [pltpu.roll(f, 64, 1) for f in field]
    sign = jnp.where(lane < 64, 1.0, -1.0)
    real = []
    for e in range(3):
        q = jnp.zeros((PAD, LANES), F32)
        for d in range(3):
            at = (e * 3 + d) * PAD
            q = q + coef_a[at : at + PAD] * field[d] + coef_b[at : at + PAD] * turned[d]
        real.append(q)
    gap = jnp.zeros((LANES - 3 * SHARE, LANES), F32)
    packed = jnp.concatenate([q[:SHARE] for q in real] + [gap], 0)
    right = jnp.concatenate([packed, pltpu.roll(packed, 64, 1) * sign], 0).astype(BF16)
    back = lax.dot_general(
        back_x[...], right, (((1,), (1,)), ((), ())),
        preferred_element_type=F32,
    ).reshape(NEAR, 2, 8, 2 * LANES)

    total = got.astype(F32).reshape(BULK, 8, 2 * LANES).sum(0)
    total = pltpu.roll(total[:, :LANES] + total[:, LANES:], LANES - 3 * SHARE, 1)
    second = pltpu.roll(total, LANES - 6, 1)
    gap = jnp.zeros((LANES - 16, LANES), F32)
    total = jnp.concatenate([total, second, gap], 0)
    total = jnp.where(iota((LANES, LANES), 1) < 6, total, 0.0).T[:8]
    total = pltpu.roll(total, near * 16, 1)
    near = jnp.dot(
        jnp.concatenate(real, 0).astype(BF16), phase_x[...], preferred_element_type=F32
    )
    row = iota((8, LANES), 0)
    for e in range(3):
        line = jnp.sum(near[e * PAD : (e + 1) * PAD] * phase_yz[...], axis=0, keepdims=True)
        line = line + pltpu.roll(line, 64, 1)
        total = total + jnp.where((row == e) & (lane < 64), line, 0.0)
    high = total.astype(BF16).astype(F32)
    extra = pltpu.roll(high + pltpu.roll(total - high, 64, 1), 2, 0)
    extra = jnp.concatenate([extra, jnp.zeros((8, LANES), F32)], 1)
    tiles = []
    for n in range(NEAR):
        tiles += [back[n, 0], back[n, 1] + extra]
    out[...] = jnp.concatenate(tiles, 0).astype(BF16)


def spread_kernel(shares, inv_y, after, out, rows):
    lane = iota((1, LANES), 1)
    got = shares[...].astype(F32).reshape(NEAR, 16, 2 * LANES)
    rows[...] = jnp.zeros((32, 8, LANES), F32)
    for e in range(3):
        flat = []
        for part in range(2):
            start = e * SHARE
            first, rest = jnp.zeros((16, LANES), F32), None
            for n in range(NEAR):
                moved = got[n][:, part * LANES : (part + 1) * LANES]
                if n != e:
                    moved = pltpu.roll(moved, (n * SHARE - start) % LANES, 1)
                within = (lane >= n * SHARE) & (lane < (n + 1) * SHARE)
                first = first + jnp.where(within, moved, 0.0)
                if n == NEAR - 1:
                    rest = jnp.where(lane < 16, moved, 0.0)
            flat.append((first, rest))

        def mode_rows(part, k, to):
            first, rest = flat[part]
            moved = pltpu.roll(first, (to - k * K) % LANES, 1)
            if k < 2:
                return jnp.where((lane >= to) & (lane < to + K), moved, 0.0)
            tail = pltpu.roll(rest, to + 32, 1)
            return jnp.where((lane >= to) & (lane < to + 32), moved, 0.0) + jnp.where(
                (lane >= to + 32) & (lane < to + K), tail, 0.0
            )

        for k in range(OWN):
            real = mode_rows(0, k, 0) + mode_rows(1, k, 64)
            imag = mode_rows(1, k, 0) - mode_rows(0, k, 64)
            for x in range(10):
                rows[e * 10 + x, k : k + 1, :] = real[x : x + 1]
                rows[e * 10 + x, OWN + k : OWN + k + 1, :] = imag[x : x + 1]
    lhs = rows[...].reshape(256, LANES).astype(BF16)
    wide = jnp.dot(lhs, inv_y[...], preferred_element_type=F32).reshape(32, 8, 384)
    near = []
    for low in range(8):
        group = [wide[high * 8 + low, :, c * LANES : (c + 1) * LANES] for high in range(4) for c in range(2)]
        near.append(jnp.stack(group))
    near = exchange(near, 16, 2)
    edge = []
    for low in range(16):
        edge.append(jnp.stack([wide[high * 16 + low, :, 256:384] for high in range(2)]))
    edge = exchange(edge, 2, 2)
    row = iota((8, LANES), 0)
    total = pltpu.roll(got[:, 8:16, :LANES].sum(0), 6, 0)
    total = jnp.where((row < 6) & (lane < 64), total + pltpu.roll(total, 64, 1), 0.0)
    high = total.astype(BF16).astype(F32)
    other = pltpu.roll(total - high, 64, 1)
    moved = pltpu.roll(high, 64, 1)
    low = total - high
    extra = []
    for t in range(3):
        first = jnp.where(lane < 64, high[2 * t : 2 * t + 1], moved[2 * t + 1 : 2 * t + 2])
        second = jnp.where(lane < 64, low[2 * t : 2 * t + 1], other[2 * t + 1 : 2 * t + 2])
        extra.append(jnp.where(row == 6, first, jnp.where(row == 7, second, 0.0)))
    blocks = []
    for w in range(WIDE):
        tiles = [near[w % 8][high_x * 2 + w // 8] for high_x in range(4)]
        for t in range(3):
            tiles[t] = tiles[t] + extra[t]
        pair = jnp.where(lane < 32, edge[w], 0.0)
        tiles.append(pair[0] + pltpu.roll(pair[1], 32, 1))
        blocks.append(jnp.concatenate(tiles, 1))
    out[...] = jnp.concatenate(blocks, 0).astype(BF16)


def high_planes(across):
    first, second = [c for c in range(3) if c != across]
    planes = [(c, 0) for c in range(3)] + [(first, 1), (second, 1), (6, 0), (6, 1)]
    return planes + [(3 + c, 0) for c in range(3)]


def low_planes(across):
    first, second = [c for c in range(3) if c != across]
    planes = [(c, i) for i in range(2) for c in range(3)] + [(6, 0), (6, 1)]
    return planes + [(3 + first, 0), (3 + second, 0)] + [(3 + c, 1) for c in range(3)]


def edge_kernel(electric, magnetic, inverse, saved, after, to_low, to_high):
    def own(f):
        return electric.at[f] if f < 3 else (magnetic.at[f - 3] if f < 6 else inverse)

    for p, (f, i) in enumerate(low_planes(0)):
        to_low[p] = own(f)[6 + i].astype(BF16)
    for n in range(2):
        for c in range(2):
            to_low[13 + 2 * n + c] = saved[n, 1 + c, 7]
    for p, (f, i) in enumerate(high_planes(0)):
        to_high[p] = own(f)[i].astype(BF16)


def corner_kernel(
    electric, magnetic, inverse, saved, x_low, x_high, after, to_first, to_second, low, high
):
    x_of = [{}, {}]
    for p, key in enumerate(low_planes(0)):
        x_of[0][key] = x_low[p].astype(F32)
    for p, key in enumerate(high_planes(0)):
        x_of[1][key] = x_high[p].astype(F32)
    low[...] = jnp.zeros(low.shape, F32)
    high[...] = jnp.zeros(high.shape, F32)
    for to, planes, start in ((low, low_planes(1), 14), (high, high_planes(1), 0)):
        for p, (f, i) in enumerate(planes):
            own = electric.at[f] if f < 3 else (magnetic.at[f - 3] if f < 6 else inverse)
            row = start + i
            to[p, 0:8, :] = own[:, row, :]
            for side, at in ((1, 8), (0, 10)):
                for layer in range(2):
                    if (f, layer) in x_of[side]:
                        got = x_of[side][(f, layer)]
                        to[p, at + layer : at + layer + 1, :] = got[row : row + 1]
    for n in range(2):
        for i, c in enumerate((0, 2)):
            low[13 + 2 * n + i, 0:8, :] = saved[n, c].astype(F32)[:, RY - 1, :]
    even = jnp.where(lax.axis_index("wide") % 2 == 0, 1.0, 0.0)
    a, b = low[...], high[...]
    to_first[...] = (even * a + (1.0 - even) * b).astype(BF16)
    to_second[...] = (even * b + (1.0 - even) * a).astype(BF16)


def first_kernel(
    mon, weights, electric, magnetic, inverse, saved, x_low, x_high, y_first, y_second, after,
    early, curled, factor, grad, ready, e_ext, h_ext, g_ext,
):
    b, w = own_block()
    lane = iota((1, NZ), 1)
    even = jnp.where(w % 2 == 0, 1.0, 0.0)
    first, second = y_first[...].astype(F32), y_second[...].astype(F32)
    y_low = even * second + (1.0 - even) * first
    y_high = even * first + (1.0 - even) * second
    zero = jnp.zeros((12, 24, NZ), F32)
    for c in range(7):
        to = e_ext.at[c] if c < 3 else (h_ext.at[c - 3] if c < 6 else g_ext)
        to[...] = zero
        own = electric[c] if c < 3 else (magnetic[c - 3] if c < 6 else inverse[...])
        to[0:8, 0:16, :] = own
        for planes, ref, at in ((high_planes(0), x_high, 8), (low_planes(0), x_low, 10)):
            for p, (f, i) in enumerate(planes):
                if f == c:
                    to[at + i, 0:16, :] = ref[p].astype(F32)
        for planes, ref, at in ((high_planes(1), y_high, 16), (low_planes(1), y_low, 22)):
            for p, (f, i) in enumerate(planes):
                if f == c:
                    to[:, at + i : at + i + 1, :] = ref[p][0:12][:, None, :]

    g = g_ext[...]
    half = 0.5 * g
    a = [half * e_ext[c] for c in range(3)]
    spot_x = iota((12, 24, 1), 0)
    spot_y = iota((12, 24, 1), 1)
    outside = ((spot_x >= 10) & (b == 0)) | ((spot_y >= 22) & (w == 0))
    inside = jnp.where(outside, 0.0, 1.0)
    turned = curl_ahead(*a)
    h = [h_ext[c] + inside * turned[c] for c in range(3)]
    back = curl_behind(*h)
    for c in range(3):
        e_ext[c] = e_ext[c] - 0.5 * back[c]

    def hit(x, y, z):
        lx, ly = x - b * RX, y - w * RY
        return (lx >= -2) & (lx < RX + 2) & (ly >= -2) & (ly < RY + 2)

    def add(i, flat):
        x, y, z = place_of(flat)
        lx, ly = x - b * RX, y - w * RY
        px = jnp.where(lx < 0, lx + 12, lx)
        py = jnp.where(ly < 0, ly + 24, ly)
        for c in range(3):
            row = e_ext[c, px, pl.ds(py, 1), :]
            e_ext[c, px, pl.ds(py, 1), :] = row + jnp.where(lane == z, weights[c, 0, i], 0.0)

    scan(mon, hit, add)
    for c in range(3):
        early[c, 0:9] = e_ext[c, 0:9]
        early[c, 9:10] = e_ext[c, 11:12]
        curled[c, 0:9] = h[c][0:9]
        curled[c, 9:10] = h[c][11:12]
    factor[0:9] = half[0:9]
    factor[9:10] = half[11:12]

    near = inverse[...]
    for step in range(2):
        s = [saved[step, c].astype(F32) for c in range(3)]
        before_x = {c: jnp.concatenate([x_low[12 + 2 * step + c].astype(F32)[None], s[c][:-1]], 0) for c in (1, 2)}
        before_y = {}
        for c in (0, 2):
            edge = y_low[13 + 2 * step + c // 2][0:8][:, None, :]
            first = iota((RX, RY, NZ), 1) == 0
            before_y[c] = jnp.where(first, edge, pltpu.roll(s[c], 1, 1))
        curls = (
            (s[2] - before_y[2]) - (s[1] - z_behind(s[1])),
            (s[0] - z_behind(s[0])) - (s[2] - before_x[2]),
            (s[1] - before_x[1]) - (s[0] - before_y[0]),
        )
        if step == 0:
            for c in range(3):
                ready[c] = near * curls[c]
        else:
            total = jnp.zeros((RX, RY, NZ), F32)
            for c in range(3):
                total = total + a[c][0:8, 0:16] * near * curls[c]
            grad[...] = -total


def second_kernel(
    lines, table, apart, early, curled, factor, first_grad, ready, injected,
    grad_e, grad_h, grad_eps, sources,
):
    b, w = own_block()
    turn = (((0,), (0,)), ((), ()))
    main = lax.dot_general(lines[:, 0:512], table[...], turn, preferred_element_type=F32)
    main = main.reshape(32, 16, NZ)
    edge = jnp.dot(lines[:, 512:640], apart[...], preferred_element_type=F32).astype(BF16)
    edge = lax.dot_general(edge, table[...], turn, preferred_element_type=F32)
    edge = edge.reshape(32, 8, NZ)
    half = factor[...]
    e1 = []
    for c in range(3):
        at = slice(c * 10, c * 10 + 10)
        e1.append(early[c] + jnp.concatenate([main[at], edge[at]], 1))
    a = [half * e for e in e1]
    spot_x = iota((10, 24, 1), 0)
    spot_y = iota((10, 24, 1), 1)
    outside = ((spot_x == 9) & (b == 0)) | ((spot_y == 23) & (w == 0))
    inside = jnp.where(outside, 0.0, 1.0)
    turned = curl_ahead(*a)
    h = [curled[c] + inside * turned[c] for c in range(3)]
    backed = curl_behind(*h)
    total = first_grad[...]
    for c in range(3):
        grad_h[c] = h[c][0:8, 0:16]
        grad_e[c] = e1[c][0:8, 0:16] - 0.5 * backed[c][0:8, 0:16]
        total = total - a[c][0:8, 0:16] * ready[c]
    grad_eps[...] = total
    got = lines[:, 0:384].astype(F32).reshape(WIDE, 8, 384).sum(0)
    got = got[6:7] + got[7:8]
    moved = pltpu.roll(got, 384 - 64, 1)
    for n in range(2):
        for c in range(3):
            at = n * 3 + c
            line = got if at % 2 == 0 else moved
            line = line[:, at // 2 * LANES : (at // 2 + 1) * LANES]
            if n == 0:
                line = line + injected[c : c + 1, :]
            sources[c, n : n + 1, :] = line[:, 0:64]


def call(kernel, outs, places, scratch=(), flops=0, moved=0, params=PARAMS):
    spaces = {"s": pltpu.SMEM, "v": pltpu.VMEM, "a": pl.ANY}
    return pl.pallas_call(
        kernel,
        out_shape=outs,
        in_specs=[pl.BlockSpec(memory_space=spaces[p]) for p in places],
        out_specs=jax.tree.map(lambda _: pl.BlockSpec(memory_space=pltpu.VMEM), outs),
        scratch_shapes=list(scratch),
        compiler_params=params,
        cost_estimate=pl.CostEstimate(flops=flops, bytes_accessed=moved, transcendentals=0),
    )


def shape(*dims, dtype=F32):
    return jax.ShapeDtypeStruct(dims, dtype)


def passed_along(block, axis, distance):
    devices = range(lax.axis_size(axis))
    route = [(i - distance, i) for i in devices if i - distance in devices]
    return lax.ppermute(block, axis, route)


def dealt_near(block):
    groups = [
        [(f * NEAR + n) * HALVES + half for n in range(NEAR)]
        for f in range(DEPTH // NEAR)
        for half in range(HALVES)
    ]
    return lax.all_to_all(
        block, "bulk", split_axis=0, concat_axis=0, axis_index_groups=groups, tiled=True
    )


def tables_of(name):
    return jnp.asarray(TABLES[name])


def body(
    seed_electric, seed_magnetic, saved_magnetic, material, permittivity, source_cells,
    monitor_cells, monitor_weights, lift_weight, project_weight, mode_mix, gain_first, gain_second,
):
    weights = monitor_weights.transpose(2, 0, 1)
    big, dma = pltpu.CompilerParams(vmem_limit_bytes=56 * 1024 * 1024), pltpu.SemaphoreType.DMA
    block = (RX, RY, NZ)

    payload, field = call(
        lift_kernel,
        (shape(384, LANES, dtype=BF16), shape(3, *block)),
        "aaaa",
        [
            pltpu.SMEM((64,), jnp.int32), pltpu.VMEM((3, 2, 64), F32),
            pltpu.VMEM((LANES, LANES), BF16), dma((4,)),
        ],
        13_000_000,
        500_000,
        big,
    )(monitor_cells, weights, seed_electric, tables_of("lift_z"))
    lines = lax.all_to_all(payload, "wide", split_axis=0, concat_axis=0, tiled=True)

    taken, inverse = call(
        share_kernel,
        (shape(8, LANES), shape(*block)),
        "aavaa",
        [
            pltpu.SMEM((64,), jnp.int32), pltpu.SMEM((8,), F32), pltpu.VMEM((3, *block), F32),
            pltpu.VMEM(block, jnp.int32), pltpu.VMEM((3, 12, 32, NZ), F32),
            pltpu.VMEM((3, 12, 32, NZ), F32), dma((4,)),
        ],
        3_000_000,
        1_500_000,
    )(source_cells, permittivity, field, seed_magnetic, material)

    dealt = call(
        middle_kernel, shape(BULK * 8, 2 * LANES, dtype=BF16), "vvv", (), 20_000_000, 400_000
    )(lines, taken, tables_of("fwd_y"))
    gathered = lax.all_to_all(dealt, "bulk", split_axis=0, concat_axis=0, tiled=True)

    cells = jnp.concatenate([source_cells, source_cells]).reshape(1, LANES)
    coef_a, coef_b, phase_x, phase_yz, injected, back_x = call(
        param_kernel,
        (
            shape(9 * PAD, LANES), shape(9 * PAD, LANES), shape(LANES, LANES, dtype=BF16),
            shape(PAD, LANES), shape(8, LANES), shape(NEAR * 16, LANES, dtype=BF16),
        ),
        "sssvvvvvvvvva",
        (),
        20_000_000,
        1_000_000,
    )(
        monitor_cells, weights, lift_weight.T, cells, project_weight, gain_first, gain_second,
        mode_mix.transpose(0, 2, 3, 1), tables_of("at_x"), tables_of("at_y"), tables_of("at_z"),
        tables_of("inv_x"), dealt,
    )

    to_low, to_high = call(
        edge_kernel,
        (shape(17, RY, NZ, dtype=BF16), shape(10, RY, NZ, dtype=BF16)),
        "vvvva",
        (),
        0,
        500_000,
    )(field, seed_magnetic, inverse, saved_magnetic, dealt)
    x_low = passed_along(to_low, "bulk", 1)
    x_high = passed_along(to_high, "bulk", -1)

    first_part, second_part = call(
        corner_kernel,
        (shape(17, 16, NZ, dtype=BF16), shape(17, 16, NZ, dtype=BF16)),
        "vvvvvva",
        [pltpu.VMEM((17, 16, NZ), F32)] * 2,
        0,
        1_000_000,
    )(field, seed_magnetic, inverse, saved_magnetic, x_low, x_high, coef_a)
    shares = call(
        filter_kernel, shape(NEAR * 16, 2 * LANES, dtype=BF16), "vvvvvvva", (), 40_000_000, 600_000
    )(
        gathered, coef_a, coef_b, tables_of("at_x"), back_x, phase_x, phase_yz,
        first_part,
    )
    back = dealt_near(shares)

    y_first = lax.ppermute(first_part, "wide", [(i, i ^ 1) for i in range(WIDE)])
    pairs = [(i, i + 1) for i in range(1, WIDE - 1, 2)]
    y_second = lax.ppermute(second_part, "wide", pairs + [(j, i) for i, j in pairs])

    sent = call(
        spread_kernel,
        shape(128, 640, dtype=BF16),
        "vva",
        [pltpu.VMEM((32, 8, LANES), F32)],
        40_000_000,
        600_000,
    )(back, tables_of("inv_y"), y_second)
    returned = lax.all_to_all(sent, "wide", split_axis=0, concat_axis=0, tiled=True)
    early, curled, factor, first_grad, ready = call(
        first_kernel,
        (
            shape(3, 10, 24, NZ), shape(3, 10, 24, NZ), shape(10, 24, NZ), shape(*block),
            shape(3, *block),
        ),
        "ssvvvvvvvva",
        [pltpu.VMEM((3, 12, 24, NZ), F32)] * 2 + [pltpu.VMEM((12, 24, NZ), F32)],
        10_000_000,
        3_000_000,
    )(
        monitor_cells, weights, field, seed_magnetic, inverse, saved_magnetic,
        x_low, x_high, y_first, y_second, sent,
    )

    grad_e, grad_h, grad_eps, sources = call(
        second_kernel,
        (shape(3, *block), shape(3, *block), shape(*block), shape(3, 2, 64)),
        "vvvvvvvvv",
        (),
        40_000_000,
        4_000_000,
    )(
        returned, tables_of("back_z"), tables_of("apart"), early, curled, factor, first_grad,
        ready, injected,
    )
    return grad_e, grad_h, grad_eps, sources.transpose(1, 2, 0)


def solution(mesh):
    field = P(None, "bulk", "wide", None)
    return jax.shard_map(
        body,
        mesh=mesh,
        in_specs=(
            field, field, P(None, None, "bulk", "wide", None), P("bulk", "wide", None),
            P(), P(), P(), P(), P(), P(), P(), P(), P(),
        ),
        out_specs=(field, field, P("bulk", "wide", None), P()),
        check_vma=False,
    )
```

```python
import functools
import math

import jax
import jax.numpy as jnp
import ml_dtypes
import numpy as np
from jax import lax
from jax.experimental import pallas as pl
from jax.experimental.pallas import tpu as pltpu
from jax.sharding import PartitionSpec as P

NX, NY, NZ = 256, 256, 128
K = 48
OWN = 3
WIDE, BULK = 16, 32
RX, RY = 8, 16
NEAR, DEPTH, HALVES = 4, 16, 2
SHARE = OWN * K // NEAR
PAD = 40
LANES = 128
F32, BF16 = jnp.float32, jnp.bfloat16
PARAMS = pltpu.CompilerParams(vmem_limit_bytes=40 * 1024 * 1024)
HIGHEST = lax.Precision.HIGHEST


def waves(freqs, places, total):
    phase = np.mod(np.asarray(freqs)[:, None] * np.asarray(places)[None, :], total)
    angle = phase.astype(np.float32) * np.float32(2.0 * math.pi / total)
    return np.cos(angle).astype(np.float32), np.sin(angle).astype(np.float32)


def rounded(table):
    return np.asarray(table, np.float32).astype(ml_dtypes.bfloat16)


def make_tables():
    mode = np.arange(K)
    plane = np.where(mode < K // 2, mode, mode - K)
    cz, sz = waves(mode, np.arange(NZ), NZ)
    cx, sx = (rounded(t) for t in waves(plane, np.arange(NX), NX))
    cy, sy = (rounded(t) for t in waves(plane, np.arange(NY), NY))
    scale = np.float32(1.0 / math.sqrt(NX * NY * NZ))
    back = np.float32(1.0 / math.sqrt(K**3))
    fz, gz = rounded(cz * scale), rounded(-sz * scale)
    bz, hz = rounded(cz * back), rounded(sz * back)
    out = {}
    lift_z = np.zeros((LANES, LANES), ml_dtypes.bfloat16)
    back_z = np.zeros((LANES, LANES), ml_dtypes.bfloat16)
    for w in range(WIDE):
        for i in range(OWN):
            lift_z[:, w * 8 + i] = fz[w * OWN + i]
            lift_z[:, w * 8 + OWN + i] = gz[w * OWN + i]
            back_z[w * 8 + i] = bz[w * OWN + i]
            back_z[w * 8 + OWN + i] = -hz[w * OWN + i]
    out["lift_z"], out["back_z"] = lift_z, back_z

    lane = np.arange(LANES)
    y_of = np.concatenate([(h * 8 + lane % 8) * RY + lane // 8 for h in range(2)])
    fwd_y = np.zeros((512, 256), ml_dtypes.bfloat16)
    fwd_y[:256, :K] = cy[:, y_of].T
    fwd_y[256:, :K] = sy[:, y_of].T
    fwd_y[:256, 128 : 128 + K] = -sy[:, y_of].T
    fwd_y[256:, 128 : 128 + K] = cy[:, y_of].T
    out["fwd_y"] = fwd_y

    inv_x = np.zeros((DEPTH // NEAR, HALVES, NEAR * 16, LANES), ml_dtypes.bfloat16)
    for half in range(HALVES):
        for z in range(DEPTH):
            start = (z * HALVES + half) * RX
            x_of = (start + np.array([0, 1, 2, 3, 4, 5, 6, 7, 8, -1])) % NX
            at = slice(z % NEAR * 16, z % NEAR * 16 + 10)
            inv_x[z // NEAR, half, at, :K] = cx[:, x_of].T
            inv_x[z // NEAR, half, at, 64 : 64 + K] = -sx[:, x_of].T
    out["inv_x"] = inv_x

    inv_y = np.zeros((LANES, 384), ml_dtypes.bfloat16)
    inv_y[:K, :256], inv_y[64 : 64 + K, :256] = cy, -sy
    for w in range(WIDE):
        for h, y in enumerate((w * RY + RY, w * RY - 1)):
            inv_y[:K, 256 + w * 2 + h] = cy[:, y % NY]
            inv_y[64 : 64 + K, 256 + w * 2 + h] = -sy[:, y % NY]
    out["inv_y"] = inv_y
    apart = np.zeros((LANES, 256), ml_dtypes.bfloat16)
    for cell in range(32):
        apart[cell * 2, cell * 8] = 1
        apart[cell * 2 + 1, cell * 8 + 7] = 1
    out["apart"] = apart

    at_x = np.zeros((2, LANES, NX), ml_dtypes.bfloat16)
    at_x[0, :K], at_x[0, 64 : 64 + K] = cx, -sx
    at_x[1, :K], at_x[1, 64 : 64 + K] = sx, cx
    out["at_x"] = at_x
    at_y = np.zeros((NEAR, 2, 48, NY), ml_dtypes.bfloat16)
    for n in range(NEAR):
        j_of = np.arange(n * SHARE, (n + 1) * SHARE) % K
        at_y[n, 0, :SHARE], at_y[n, 1, :SHARE] = cy[j_of], sy[j_of]
    out["at_y"] = at_y
    at_z = np.zeros((WIDE, 2, 16, NZ), ml_dtypes.bfloat16)
    for w in range(WIDE):
        at_z[w, 0, :OWN] = bz[w * OWN : (w + 1) * OWN]
        at_z[w, 1, :OWN] = hz[w * OWN : (w + 1) * OWN]
    out["at_z"] = at_z
    return out


TABLES = make_tables()


def iota(shape, axis):
    return lax.broadcasted_iota(jnp.int32, shape, axis)


def exchange(tiles, block, axis):
    tiles = list(tiles)
    shape = tiles[0].shape
    size = shape[axis]
    place = iota(shape, axis) // block
    step = 1
    while step < len(tiles):
        high = (place // step) % 2 == 1
        new = list(tiles)
        for low in range(len(tiles)):
            if low & step:
                continue
            u, v = tiles[low], tiles[low + step]
            new[low] = jnp.where(high, pltpu.roll(v, step * block, axis), u)
            new[low + step] = jnp.where(high, v, pltpu.roll(u, size - step * block, axis))
        tiles = new
        step *= 2
    return tiles


def z_ahead(v):
    axis = v.ndim - 1
    return jnp.where(iota(v.shape, axis) < NZ - 1, pltpu.roll(v, NZ - 1, axis), 0.0)


def z_behind(v):
    axis = v.ndim - 1
    return jnp.where(iota(v.shape, axis) > 0, pltpu.roll(v, 1, axis), 0.0)


def x_ahead(v):
    return jnp.concatenate([v[1:], v[:1]], 0)


def x_behind(v):
    return jnp.concatenate([v[-1:], v[:-1]], 0)


def y_ahead(v):
    return pltpu.roll(v, v.shape[1] - 1, 1)


def y_behind(v):
    return pltpu.roll(v, 1, 1)


def curl_ahead(fx, fy, fz):
    return (
        (y_ahead(fz) - fz) - (z_ahead(fy) - fy),
        (z_ahead(fx) - fx) - (x_ahead(fz) - fz),
        (x_ahead(fy) - fy) - (y_ahead(fx) - fx),
    )


def curl_behind(fx, fy, fz):
    return (
        (fz - y_behind(fz)) - (fy - z_behind(fy)),
        (fx - z_behind(fx)) - (fz - x_behind(fz)),
        (fy - x_behind(fy)) - (fx - y_behind(fx)),
    )


def place_of(flat):
    return flat >> 15, (flat >> 7) & (NY - 1), flat & (NZ - 1)


def own_block():
    return lax.axis_index("bulk"), lax.axis_index("wide")


def fetch(pairs, sems):
    copies = [pltpu.make_async_copy(a, b, sems.at[i]) for i, (a, b) in enumerate(pairs)]
    for copy in copies:
        copy.start()
    return copies


def scan(cells, hit, act):
    def group(g, carry):
        found = [cells[g * 8 + i] for i in range(8)]
        hits = [hit(*place_of(f)) for f in found]
        some = functools.reduce(jnp.logical_or, hits)

        @pl.when(some)
        def _():
            for i in range(8):
                pl.when(hits[i])(functools.partial(act, g * 8 + i, found[i]))

        return carry

    lax.fori_loop(0, 8, group, 0)


def lift_kernel(mon_in, weights_in, electric, table_in, out, field, mon, weights, table, sems):
    b, w = own_block()
    copies = fetch(
        ((mon_in, mon), (electric, field), (weights_in, weights), (table_in, table)), sems
    )
    for copy in copies:
        copy.wait()
    lane = iota((1, NZ), 1)
    spot = iota((1, 64), 1)

    def hit(x, y, z):
        return ((x >> 3) == b) & ((y >> 4) == w)

    def add(i, flat):
        x, y, z = place_of(flat)
        lx, ly = x & (RX - 1), y & (RY - 1)
        for c in range(3):
            row = field[c, lx, pl.ds(ly, 1), :]
            given = jnp.where(spot == i, weights[c, 1:2, :], 0.0)
            weight = jnp.sum(given, axis=1, keepdims=True)
            field[c, lx, pl.ds(ly, 1), :] = row + jnp.where(lane == z, weight, 0.0)

    scan(mon, hit, add)
    rows = field[...].reshape(3 * RX * RY, NZ).astype(BF16)
    modes = jnp.dot(rows, table[...], preferred_element_type=F32)
    modes = modes.reshape(3, RX, 2, 8, LANES)
    tiles = exchange([modes[:, x].reshape(6, 8, LANES) for x in range(RX)], 1, 1)
    tiles = [t.reshape(3, 2, 8, LANES) for t in tiles]
    tiles = exchange([tiles[y % 8][:, y // 8] for y in range(RY)], 8, 2)
    out[...] = jnp.concatenate([t.reshape(24, LANES) for t in tiles], 0).astype(BF16)


def share_kernel(
    src_in, perm_in, field, magnetic_in, material_in,
    taken, inverse,
    src, perm, magnetic, material, scaled, held, sems,
):
    b, w = own_block()
    copies = fetch(
        (
            (src_in, src), (perm_in, perm), (magnetic_in, magnetic),
            (material_in, material),
        ),
        sems,
    )
    zero = jnp.zeros((12, 32, NZ), F32)
    for c in range(3):
        scaled[c] = zero
        held[c] = zero
    for copy in copies:
        copy.wait()
    eps = jnp.zeros((RX, RY, NZ), F32)
    cells = material[...]
    for level in range(8):
        eps = jnp.where(cells == level, perm[level], eps)
    inv = 1.0 / eps
    inverse[...] = inv
    lane = iota((1, NZ), 1)
    for c in range(3):
        scaled[c, 2:10, 8:24, :] = 0.5 * inv * field[c]
        held[c, 2:10, 8:24, :] = magnetic[c]
    taken[...] = jnp.zeros((8, LANES), F32)
    spot_row, spot_lane = iota((8, LANES), 0), iota((8, LANES), 1)

    def hit(x, y, z):
        lx, ly = x - b * RX, y - w * RY
        return (lx >= -1) & (lx <= RX) & (ly >= -1) & (ly <= RY)

    def take(i, flat):
        x, y, z = place_of(flat)
        lx, ly = x - b * RX, y - w * RY

        def a(c, dx, dy):
            return scaled[c, lx + 2 + dx, pl.ds(ly + 8 + dy, 1), :]

        def h(c, dx, dy):
            old = held[c, lx + 2 + dx, pl.ds(ly + 8 + dy, 1), :]
            if c == 0:
                near = a(1, dx, dy)
                turn = (a(2, dx, dy + 1) - a(2, dx, dy)) - (z_ahead(near) - near)
            elif c == 1:
                near = a(0, dx, dy)
                turn = (z_ahead(near) - near) - (a(2, dx + 1, dy) - a(2, dx, dy))
            else:
                turn = (a(1, dx + 1, dy) - a(1, dx, dy)) - (a(0, dx, dy + 1) - a(0, dx, dy))
            return old + turn

        left = jnp.where(x > 0, 1.0, 0.0)
        down = jnp.where(y > 0, 1.0, 0.0)
        hx, hy, hz = h(0, 0, 0), h(1, 0, 0), h(2, 0, 0)
        hx_y, hz_y = down * h(0, 0, -1), down * h(2, 0, -1)
        hy_x, hz_x = left * h(1, -1, 0), left * h(2, -1, 0)
        curls = (
            (hz - hz_y) - (hy - z_behind(hy)),
            (hx - z_behind(hx)) - (hz - hz_x),
            (hy - hy_x) - (hx - hx_y),
        )
        mine = jnp.where((lx >= 0) & (lx < RX) & (ly >= 0) & (ly < RY), 1.0, 0.0)
        cx, cy = jnp.clip(lx, 0, RX - 1), jnp.clip(ly, 0, RY - 1)
        got = taken[...]
        for c in range(3):
            old = mine * field[c, cx, pl.ds(cy, 1), :]
            for n, row in ((0, old - 0.5 * curls[c]), (1, old)):
                value = jnp.sum(jnp.where(lane == z, row, 0.0), axis=1, keepdims=True)
                spot = (spot_row == n * 3 + c) & (spot_lane == i)
                got = got + jnp.where(spot, value, 0.0)
        taken[...] = got

    scan(src, hit, take)


def middle_kernel(lines, taken, table, out):
    got = lines[...].astype(F32).reshape(WIDE, 24, LANES)
    halves = [exchange([got[h * 8 + i] for i in range(8)], 1, 1) for h in range(2)]
    rows = [
        jnp.concatenate([halves[0][k], halves[1][k], halves[0][OWN + k], halves[1][OWN + k]], 1)
        for k in range(OWN)
    ]
    lhs = jnp.concatenate(rows, 0).astype(BF16)
    found = jnp.dot(lhs, table[...], preferred_element_type=F32)
    lane = iota((8, LANES), 1)
    parts = [[jnp.zeros((8, LANES), F32) for _ in range(2)] for _ in range(NEAR)]
    split = LANES - (NEAR - 1) * SHARE
    for part in range(2):
        for d in range(3):
            piece = [
                found[(k * 3 + d) * 8 : (k * 3 + d) * 8 + 8, part * LANES : (part + 1) * LANES]
                for k in range(OWN)
            ]
            last = pltpu.roll(piece[2], 2 * K, 1)
            first = piece[0] + pltpu.roll(piece[1], K, 1) + jnp.where(lane >= 2 * K, last, 0.0)
            rest = jnp.where(lane < 16, last, 0.0)
            to = d * SHARE
            for n in range(NEAR):
                shift = (to - n * SHARE) % LANES
                moved = pltpu.roll(first, shift, 1) if shift else first
                if n == NEAR - 1:
                    moved = jnp.where(lane < to + split, moved, pltpu.roll(rest, to + split, 1))
                within = (lane >= to) & (lane < to + SHARE)
                parts[n][part] = parts[n][part] + jnp.where(within, moved, 0.0)
    src = jnp.concatenate([taken[...], jnp.zeros((LANES - 8, LANES), F32)], 0).T
    src = jnp.where(iota((LANES, LANES), 1) < 6, src, 0.0)
    high = src.astype(BF16).astype(F32)
    at = 3 * SHARE
    rows = []
    for n in range(NEAR):
        for part, value in enumerate((high, src - high)):
            for i in range(2):
                start = n * 16 + i * 8
                parts[n][part] = parts[n][part] + pltpu.roll(
                    value[start : start + 8], at + i * 6, 1
                )
        rows.append(jnp.concatenate(parts[n], 1))
    deal = jnp.concatenate([r for r in rows for _ in range(HALVES)], 0).astype(BF16)
    size = NEAR * HALVES * 8
    for f in range(DEPTH // NEAR):
        out[f * size : (f + 1) * size, :] = deal


def param_kernel(
    mon, weights, lift, cells, project, gain_x, gain_y, mix, at_x, at_y, at_z, inv_x,
    after, coef_a, coef_b, phase_x, phase_yz, injected, back_x,
):
    b, w = own_block()
    n = b // HALVES % NEAR
    back_x[...] = inv_x[b // (HALVES * NEAR), b % HALVES]
    flat = cells[...]
    x, y, z = place_of(flat)
    first = iota((1, LANES), 1) < 64
    hot_x = jnp.where(iota((NX, LANES), 0) == x, 1.0, 0.0)
    real = jnp.where(first, hot_x, 0.0).astype(BF16)
    imag = jnp.where(first, 0.0, hot_x).astype(BF16)
    phase_x[...] = (
        jnp.dot(at_x[0], real, preferred_element_type=F32)
        + jnp.dot(at_x[1], imag, preferred_element_type=F32)
    ).astype(BF16)
    hot_y = jnp.where(iota((NY, LANES), 0) == y, 1.0, 0.0).astype(BF16)
    hot_z = jnp.where(iota((NZ, LANES), 0) == z, 1.0, 0.0).astype(BF16)
    cy = jnp.dot(at_y[n, 0], hot_y, preferred_element_type=F32)[:PAD]
    sy = jnp.dot(at_y[n, 1], hot_y, preferred_element_type=F32)[:PAD]
    cz = jnp.dot(at_z[w, 0], hot_z, preferred_element_type=F32)
    sz = jnp.dot(at_z[w, 1], hot_z, preferred_element_type=F32)
    mode = n * SHARE + iota((PAD, 1), 0)
    ck = jnp.where(mode < K, cz[0:1], jnp.where(mode < 2 * K, cz[1:2], cz[2:3]))
    sk = jnp.where(mode < K, sz[0:1], jnp.where(mode < 2 * K, sz[1:2], sz[2:3]))
    phase_yz[...] = jnp.where(first, cy * ck - sy * sk, -(sy * ck + cy * sk))

    place = iota((K, PAD), 1)
    mode = n * SHARE + place
    depth = jnp.where(mode < K, 0, jnp.where(mode < 2 * K, 1, 2))
    live = place < SHARE
    hot_j = jnp.where((iota((K, PAD), 0) == mode - depth * K) & live, 1.0, 0.0)
    hot_k = jnp.where((iota((K, PAD), 0) == w * OWN + depth) & live, 1.0, 0.0)
    gains = jnp.dot(gain_y[...], hot_j, precision=HIGHEST, preferred_element_type=F32)
    diagonal = iota((16, 16), 0) == iota((16, 16), 1)
    columns = [
        jnp.sum(jnp.where(diagonal, project[e : e + 1, :], 0.0), axis=1, keepdims=True)
        for e in range(3)
    ]
    blank = jnp.zeros((16, 16), F32)
    along = gain_x[...]
    totals = []
    for part in range(2):
        rows = [mix[part, c].astype(F32) for c in range(16)]
        for d in range(3):
            total = lift[d, 0] * rows[0]
            for c in range(1, 16):
                total = total + lift[d, c] * rows[c]
            totals.append(total)
    joined = jnp.dot(
        jnp.concatenate(totals, 0), hot_k, precision=HIGHEST, preferred_element_type=F32
    )
    joined = [joined[i * 16 : (i + 1) * 16] * gains for i in range(6)]
    for part, to in ((0, coef_a), (1, coef_b)):
        sign = 1.0 if part == 0 else -1.0
        right = jnp.concatenate([sign * along, blank, along, blank], 1)
        right = jnp.concatenate([columns[e] * right for e in range(3)], 1)
        left = jnp.concatenate([j.T for j in joined[part * 3 : part * 3 + 3]], 0)
        found = jnp.dot(left, right, precision=HIGHEST, preferred_element_type=F32)
        for e in range(3):
            for d in range(3):
                to[(e * 3 + d) * PAD : (e * 3 + d + 1) * PAD, :] = found[
                    d * PAD : (d + 1) * PAD, e * LANES : (e + 1) * LANES
                ]
    row = iota((8, LANES), 0)
    total = jnp.zeros((8, LANES), F32)
    for i in range(64):
        given = jnp.where(
            row == 0, weights[0, 0, i], jnp.where(row == 1, weights[1, 0, i], weights[2, 0, i])
        )
        total = total + jnp.where((flat == mon[i]) & (row < 3), given, 0.0)
    injected[...] = jnp.where(iota((8, LANES), 1) < 64, total, 0.0)


def filter_kernel(
    gathered, coef_a, coef_b, at_x, back_x, phase_x, phase_yz, after, out
):
    b, w = own_block()
    near = b // HALVES % NEAR
    lane = iota((1, LANES), 1)
    got = gathered[...]
    real = jnp.dot(at_x[0], got[:, :LANES], preferred_element_type=F32)
    imag = jnp.dot(at_x[1], got[:, LANES:], preferred_element_type=F32)
    full = (real + imag).T
    field = [full[d * SHARE : d * SHARE + PAD] for d in range(3)]
    turned = [pltpu.roll(f, 64, 1) for f in field]
    sign = jnp.where(lane < 64, 1.0, -1.0)
    real = []
    for e in range(3):
        q = jnp.zeros((PAD, LANES), F32)
        for d in range(3):
            at = (e * 3 + d) * PAD
            q = q + coef_a[at : at + PAD] * field[d] + coef_b[at : at + PAD] * turned[d]
        real.append(q)
    gap = jnp.zeros((LANES - 3 * SHARE, LANES), F32)
    packed = jnp.concatenate([q[:SHARE] for q in real] + [gap], 0)
    right = jnp.concatenate([packed, pltpu.roll(packed, 64, 1) * sign], 0).astype(BF16)
    back = lax.dot_general(
        back_x[...], right, (((1,), (1,)), ((), ())),
        preferred_element_type=F32,
    ).reshape(NEAR, 2, 8, 2 * LANES)

    total = got.astype(F32).reshape(BULK, 8, 2 * LANES).sum(0)
    total = pltpu.roll(total[:, :LANES] + total[:, LANES:], LANES - 3 * SHARE, 1)
    second = pltpu.roll(total, LANES - 6, 1)
    gap = jnp.zeros((LANES - 16, LANES), F32)
    total = jnp.concatenate([total, second, gap], 0)
    total = jnp.where(iota((LANES, LANES), 1) < 6, total, 0.0).T[:8]
    total = pltpu.roll(total, near * 16, 1)
    near = jnp.dot(
        jnp.concatenate(real, 0).astype(BF16), phase_x[...], preferred_element_type=F32
    )
    row = iota((8, LANES), 0)
    for e in range(3):
        line = jnp.sum(near[e * PAD : (e + 1) * PAD] * phase_yz[...], axis=0, keepdims=True)
        line = line + pltpu.roll(line, 64, 1)
        total = total + jnp.where((row == e) & (lane < 64), line, 0.0)
    high = total.astype(BF16).astype(F32)
    extra = pltpu.roll(high + pltpu.roll(total - high, 64, 1), 2, 0)
    extra = jnp.concatenate([extra, jnp.zeros((8, LANES), F32)], 1)
    tiles = []
    for n in range(NEAR):
        tiles += [back[n, 0], back[n, 1] + extra]
    out[...] = jnp.concatenate(tiles, 0).astype(BF16)


def spread_kernel(shares, inv_y, after_first, after_second, out, rows):
    lane = iota((1, LANES), 1)
    got = shares[...].astype(F32).reshape(NEAR, 16, 2 * LANES)
    rows[...] = jnp.zeros((32, 8, LANES), F32)
    for e in range(3):
        flat = []
        for part in range(2):
            start = e * SHARE
            first, rest = jnp.zeros((16, LANES), F32), None
            for n in range(NEAR):
                moved = got[n][:, part * LANES : (part + 1) * LANES]
                if n != e:
                    moved = pltpu.roll(moved, (n * SHARE - start) % LANES, 1)
                within = (lane >= n * SHARE) & (lane < (n + 1) * SHARE)
                first = first + jnp.where(within, moved, 0.0)
                if n == NEAR - 1:
                    rest = jnp.where(lane < 16, moved, 0.0)
            flat.append((first, rest))

        def mode_rows(part, k, to):
            first, rest = flat[part]
            moved = pltpu.roll(first, (to - k * K) % LANES, 1)
            if k < 2:
                return jnp.where((lane >= to) & (lane < to + K), moved, 0.0)
            tail = pltpu.roll(rest, to + 32, 1)
            return jnp.where((lane >= to) & (lane < to + 32), moved, 0.0) + jnp.where(
                (lane >= to + 32) & (lane < to + K), tail, 0.0
            )

        for k in range(OWN):
            real = mode_rows(0, k, 0) + mode_rows(1, k, 64)
            imag = mode_rows(1, k, 0) - mode_rows(0, k, 64)
            for x in range(10):
                rows[e * 10 + x, k : k + 1, :] = real[x : x + 1]
                rows[e * 10 + x, OWN + k : OWN + k + 1, :] = imag[x : x + 1]
    lhs = rows[...].reshape(256, LANES).astype(BF16)
    wide = jnp.dot(lhs, inv_y[...], preferred_element_type=F32).reshape(32, 8, 384)
    near = []
    for low in range(8):
        group = [wide[high * 8 + low, :, c * LANES : (c + 1) * LANES] for high in range(4) for c in range(2)]
        near.append(jnp.stack(group))
    near = exchange(near, 16, 2)
    edge = []
    for low in range(16):
        edge.append(jnp.stack([wide[high * 16 + low, :, 256:384] for high in range(2)]))
    edge = exchange(edge, 2, 2)
    row = iota((8, LANES), 0)
    total = pltpu.roll(got[:, 8:16, :LANES].sum(0), 6, 0)
    total = jnp.where((row < 6) & (lane < 64), total + pltpu.roll(total, 64, 1), 0.0)
    high = total.astype(BF16).astype(F32)
    other = pltpu.roll(total - high, 64, 1)
    moved = pltpu.roll(high, 64, 1)
    low = total - high
    extra = []
    for t in range(3):
        first = jnp.where(lane < 64, high[2 * t : 2 * t + 1], moved[2 * t + 1 : 2 * t + 2])
        second = jnp.where(lane < 64, low[2 * t : 2 * t + 1], other[2 * t + 1 : 2 * t + 2])
        extra.append(jnp.where(row == 6, first, jnp.where(row == 7, second, 0.0)))
    blocks = []
    for w in range(WIDE):
        tiles = [near[w % 8][high_x * 2 + w // 8] for high_x in range(4)]
        for t in range(3):
            tiles[t] = tiles[t] + extra[t]
        pair = jnp.where(lane < 32, edge[w], 0.0)
        tiles.append(pair[0] + pltpu.roll(pair[1], 32, 1))
        blocks.append(jnp.concatenate(tiles, 1))
    out[...] = jnp.concatenate(blocks, 0).astype(BF16)


def high_planes(across):
    first, second = [c for c in range(3) if c != across]
    planes = [(c, 0) for c in range(3)] + [(first, 1), (second, 1), (6, 0), (6, 1)]
    return planes + [(3 + c, 0) for c in range(3)]


def low_planes(across):
    first, second = [c for c in range(3) if c != across]
    planes = [(c, i) for i in range(2) for c in range(3)] + [(6, 0), (6, 1)]
    return planes + [(3 + first, 0), (3 + second, 0)] + [(3 + c, 1) for c in range(3)]


def swapped(axis, for_next, for_previous):
    even = jnp.where(lax.axis_index(axis) % 2 == 0, 1.0, 0.0)
    first = even * for_next + (1.0 - even) * for_previous
    return first, even * for_previous + (1.0 - even) * for_next


def edge_kernel(electric, magnetic, inverse, saved, after, to_first, to_second, to_low, to_high):
    def own(f):
        return electric.at[f] if f < 3 else (magnetic.at[f - 3] if f < 6 else inverse)

    for p, (f, i) in enumerate(low_planes(0)):
        to_low[p] = own(f)[6 + i]
    for n in range(2):
        for c in range(2):
            to_low[13 + 2 * n + c] = saved[n, 1 + c, 7].astype(F32)
    to_high[...] = jnp.zeros(to_high.shape, F32)
    for p, (f, i) in enumerate(high_planes(0)):
        to_high[p] = own(f)[i]
    first, second = swapped("bulk", to_low[...], to_high[...])
    to_first[...], to_second[...] = first.astype(BF16), second.astype(BF16)


def corner_kernel(
    electric, magnetic, inverse, saved, x_first, x_second, after, to_first, to_second, low, high
):
    x_high, x_low = swapped("bulk", x_first[...].astype(F32), x_second[...].astype(F32))
    x_of = [{}, {}]
    for p, key in enumerate(low_planes(0)):
        x_of[0][key] = x_low[p]
    for p, key in enumerate(high_planes(0)):
        x_of[1][key] = x_high[p]
    low[...] = jnp.zeros(low.shape, F32)
    high[...] = jnp.zeros(high.shape, F32)
    for to, planes, start in ((low, low_planes(1), 14), (high, high_planes(1), 0)):
        for p, (f, i) in enumerate(planes):
            own = electric.at[f] if f < 3 else (magnetic.at[f - 3] if f < 6 else inverse)
            row = start + i
            to[p, 0:8, :] = own[:, row, :]
            for side, at in ((1, 8), (0, 10)):
                for layer in range(2):
                    if (f, layer) in x_of[side]:
                        got = x_of[side][(f, layer)]
                        to[p, at + layer : at + layer + 1, :] = got[row : row + 1]
    for n in range(2):
        for i, c in enumerate((0, 2)):
            low[13 + 2 * n + i, 0:8, :] = saved[n, c].astype(F32)[:, RY - 1, :]
    first, second = swapped("wide", low[...], high[...])
    to_first[...], to_second[...] = first.astype(BF16), second.astype(BF16)


def first_kernel(
    mon, weights, electric, magnetic, inverse, saved, x_first, x_second, y_first, y_second, after,
    early, curled, factor, grad, ready, e_ext, h_ext, g_ext,
):
    b, w = own_block()
    lane = iota((1, NZ), 1)
    x_high, x_low = swapped("bulk", x_first[...].astype(F32), x_second[...].astype(F32))
    y_high, y_low = swapped("wide", y_first[...].astype(F32), y_second[...].astype(F32))
    zero = jnp.zeros((12, 24, NZ), F32)
    for c in range(7):
        to = e_ext.at[c] if c < 3 else (h_ext.at[c - 3] if c < 6 else g_ext)
        to[...] = zero
        own = electric[c] if c < 3 else (magnetic[c - 3] if c < 6 else inverse[...])
        to[0:8, 0:16, :] = own
        for planes, ref, at in ((high_planes(0), x_high, 8), (low_planes(0), x_low, 10)):
            for p, (f, i) in enumerate(planes):
                if f == c:
                    to[at + i, 0:16, :] = ref[p]
        for planes, ref, at in ((high_planes(1), y_high, 16), (low_planes(1), y_low, 22)):
            for p, (f, i) in enumerate(planes):
                if f == c:
                    to[:, at + i : at + i + 1, :] = ref[p][0:12][:, None, :]

    g = g_ext[...]
    half = 0.5 * g
    a = [half * e_ext[c] for c in range(3)]
    spot_x = iota((12, 24, 1), 0)
    spot_y = iota((12, 24, 1), 1)
    outside = ((spot_x >= 10) & (b == 0)) | ((spot_y >= 22) & (w == 0))
    inside = jnp.where(outside, 0.0, 1.0)
    turned = curl_ahead(*a)
    h = [h_ext[c] + inside * turned[c] for c in range(3)]
    back = curl_behind(*h)
    for c in range(3):
        e_ext[c] = e_ext[c] - 0.5 * back[c]

    def hit(x, y, z):
        lx, ly = x - b * RX, y - w * RY
        return (lx >= -2) & (lx < RX + 2) & (ly >= -2) & (ly < RY + 2)

    def add(i, flat):
        x, y, z = place_of(flat)
        lx, ly = x - b * RX, y - w * RY
        px = jnp.where(lx < 0, lx + 12, lx)
        py = jnp.where(ly < 0, ly + 24, ly)
        for c in range(3):
            row = e_ext[c, px, pl.ds(py, 1), :]
            e_ext[c, px, pl.ds(py, 1), :] = row + jnp.where(lane == z, weights[c, 0, i], 0.0)

    scan(mon, hit, add)
    for c in range(3):
        early[c, 0:9] = e_ext[c, 0:9]
        early[c, 9:10] = e_ext[c, 11:12]
        curled[c, 0:9] = h[c][0:9]
        curled[c, 9:10] = h[c][11:12]
    factor[0:9] = half[0:9]
    factor[9:10] = half[11:12]

    near = inverse[...]
    for step in range(2):
        s = [saved[step, c].astype(F32) for c in range(3)]
        before_x = {c: jnp.concatenate([x_low[12 + 2 * step + c][None], s[c][:-1]], 0) for c in (1, 2)}
        before_y = {}
        for c in (0, 2):
            edge = y_low[13 + 2 * step + c // 2][0:8][:, None, :]
            first = iota((RX, RY, NZ), 1) == 0
            before_y[c] = jnp.where(first, edge, pltpu.roll(s[c], 1, 1))
        curls = (
            (s[2] - before_y[2]) - (s[1] - z_behind(s[1])),
            (s[0] - z_behind(s[0])) - (s[2] - before_x[2]),
            (s[1] - before_x[1]) - (s[0] - before_y[0]),
        )
        if step == 0:
            for c in range(3):
                ready[c] = near * curls[c]
        else:
            total = jnp.zeros((RX, RY, NZ), F32)
            for c in range(3):
                total = total + a[c][0:8, 0:16] * near * curls[c]
            grad[...] = -total


def second_kernel(
    lines, table, apart, early, curled, factor, first_grad, ready, injected,
    grad_e, grad_h, grad_eps, sources,
):
    b, w = own_block()
    turn = (((0,), (0,)), ((), ()))
    main = lax.dot_general(lines[:, 0:512], table[...], turn, preferred_element_type=F32)
    main = main.reshape(32, 16, NZ)
    edge = jnp.dot(lines[:, 512:640], apart[...], preferred_element_type=F32).astype(BF16)
    edge = lax.dot_general(edge, table[...], turn, preferred_element_type=F32)
    edge = edge.reshape(32, 8, NZ)
    half = factor[...]
    e1 = []
    for c in range(3):
        at = slice(c * 10, c * 10 + 10)
        e1.append(early[c] + jnp.concatenate([main[at], edge[at]], 1))
    a = [half * e for e in e1]
    spot_x = iota((10, 24, 1), 0)
    spot_y = iota((10, 24, 1), 1)
    outside = ((spot_x == 9) & (b == 0)) | ((spot_y == 23) & (w == 0))
    inside = jnp.where(outside, 0.0, 1.0)
    turned = curl_ahead(*a)
    h = [curled[c] + inside * turned[c] for c in range(3)]
    backed = curl_behind(*h)
    total = first_grad[...]
    for c in range(3):
        grad_h[c] = h[c][0:8, 0:16]
        grad_e[c] = e1[c][0:8, 0:16] - 0.5 * backed[c][0:8, 0:16]
        total = total - a[c][0:8, 0:16] * ready[c]
    grad_eps[...] = total
    got = lines[:, 0:384].astype(F32).reshape(WIDE, 8, 384).sum(0)
    got = got[6:7] + got[7:8]
    moved = pltpu.roll(got, 384 - 64, 1)
    for n in range(2):
        for c in range(3):
            at = n * 3 + c
            line = got if at % 2 == 0 else moved
            line = line[:, at // 2 * LANES : (at // 2 + 1) * LANES]
            if n == 0:
                line = line + injected[c : c + 1, :]
            sources[c, n : n + 1, :] = line[:, 0:64]


def call(kernel, outs, places, scratch=(), flops=0, moved=0, params=PARAMS):
    spaces = {"s": pltpu.SMEM, "v": pltpu.VMEM, "a": pl.ANY}
    return pl.pallas_call(
        kernel,
        out_shape=outs,
        in_specs=[pl.BlockSpec(memory_space=spaces[p]) for p in places],
        out_specs=jax.tree.map(lambda _: pl.BlockSpec(memory_space=pltpu.VMEM), outs),
        scratch_shapes=list(scratch),
        compiler_params=params,
        cost_estimate=pl.CostEstimate(flops=flops, bytes_accessed=moved, transcendentals=0),
    )


def shape(*dims, dtype=F32):
    return jax.ShapeDtypeStruct(dims, dtype)


def swaps(first, second, axis):
    size = lax.axis_size(axis)
    pairs = [(i, i + 1) for i in range(1, size - 1, 2)]
    return (
        lax.ppermute(first, axis, [(i, i ^ 1) for i in range(size)]),
        lax.ppermute(second, axis, pairs + [(j, i) for i, j in pairs]),
    )


def dealt_near(block):
    groups = [
        [(f * NEAR + n) * HALVES + half for n in range(NEAR)]
        for f in range(DEPTH // NEAR)
        for half in range(HALVES)
    ]
    return lax.all_to_all(
        block, "bulk", split_axis=0, concat_axis=0, axis_index_groups=groups, tiled=True
    )


def tables_of(name):
    return jnp.asarray(TABLES[name])


def body(
    seed_electric, seed_magnetic, saved_magnetic, material, permittivity, source_cells,
    monitor_cells, monitor_weights, lift_weight, project_weight, mode_mix, gain_first, gain_second,
):
    weights = monitor_weights.transpose(2, 0, 1)
    big, dma = pltpu.CompilerParams(vmem_limit_bytes=56 * 1024 * 1024), pltpu.SemaphoreType.DMA
    block = (RX, RY, NZ)

    payload, field = call(
        lift_kernel,
        (shape(384, LANES, dtype=BF16), shape(3, *block)),
        "aaaa",
        [
            pltpu.SMEM((64,), jnp.int32), pltpu.VMEM((3, 2, 64), F32),
            pltpu.VMEM((LANES, LANES), BF16), dma((4,)),
        ],
        13_000_000,
        500_000,
        big,
    )(monitor_cells, weights, seed_electric, tables_of("lift_z"))
    lines = lax.all_to_all(payload, "wide", split_axis=0, concat_axis=0, tiled=True)

    taken, inverse = call(
        share_kernel,
        (shape(8, LANES), shape(*block)),
        "aavaa",
        [
            pltpu.SMEM((64,), jnp.int32), pltpu.SMEM((8,), F32), pltpu.VMEM((3, *block), F32),
            pltpu.VMEM(block, jnp.int32), pltpu.VMEM((3, 12, 32, NZ), F32),
            pltpu.VMEM((3, 12, 32, NZ), F32), dma((4,)),
        ],
        3_000_000,
        1_500_000,
    )(source_cells, permittivity, field, seed_magnetic, material)

    dealt = call(
        middle_kernel, shape(BULK * 8, 2 * LANES, dtype=BF16), "vvv", (), 20_000_000, 400_000
    )(lines, taken, tables_of("fwd_y"))
    gathered = lax.all_to_all(dealt, "bulk", split_axis=0, concat_axis=0, tiled=True)

    cells = jnp.concatenate([source_cells, source_cells]).reshape(1, LANES)
    coef_a, coef_b, phase_x, phase_yz, injected, back_x = call(
        param_kernel,
        (
            shape(9 * PAD, LANES), shape(9 * PAD, LANES), shape(LANES, LANES, dtype=BF16),
            shape(PAD, LANES), shape(8, LANES), shape(NEAR * 16, LANES, dtype=BF16),
        ),
        "sssvvvvvvvvva",
        (),
        20_000_000,
        1_000_000,
    )(
        monitor_cells, weights, lift_weight.T, cells, project_weight, gain_first, gain_second,
        mode_mix.transpose(0, 2, 3, 1), tables_of("at_x"), tables_of("at_y"), tables_of("at_z"),
        tables_of("inv_x"), dealt,
    )

    x_first_part, x_second_part = call(
        edge_kernel,
        (shape(17, RY, NZ, dtype=BF16), shape(17, RY, NZ, dtype=BF16)),
        "vvvva",
        [pltpu.VMEM((17, RY, NZ), F32)] * 2,
        0,
        500_000,
    )(field, seed_magnetic, inverse, saved_magnetic, dealt)
    x_first, x_second = swaps(x_first_part, x_second_part, "bulk")

    first_part, second_part = call(
        corner_kernel,
        (shape(17, 16, NZ, dtype=BF16), shape(17, 16, NZ, dtype=BF16)),
        "vvvvvva",
        [pltpu.VMEM((17, 16, NZ), F32)] * 2,
        0,
        1_000_000,
    )(field, seed_magnetic, inverse, saved_magnetic, x_first, x_second, coef_a)
    shares = call(
        filter_kernel, shape(NEAR * 16, 2 * LANES, dtype=BF16), "vvvvvvva", (), 40_000_000, 600_000
    )(
        gathered, coef_a, coef_b, tables_of("at_x"), back_x, phase_x, phase_yz,
        first_part,
    )
    back = dealt_near(shares)

    y_first, y_second = swaps(first_part, second_part, "wide")

    sent = call(
        spread_kernel,
        shape(128, 640, dtype=BF16),
        "vvaa",
        [pltpu.VMEM((32, 8, LANES), F32)],
        40_000_000,
        600_000,
    )(back, tables_of("inv_y"), y_first, y_second)
    returned = lax.all_to_all(sent, "wide", split_axis=0, concat_axis=0, tiled=True)
    early, curled, factor, first_grad, ready = call(
        first_kernel,
        (
            shape(3, 10, 24, NZ), shape(3, 10, 24, NZ), shape(10, 24, NZ), shape(*block),
            shape(3, *block),
        ),
        "ssvvvvvvvva",
        [pltpu.VMEM((3, 12, 24, NZ), F32)] * 2 + [pltpu.VMEM((12, 24, NZ), F32)],
        10_000_000,
        3_000_000,
    )(
        monitor_cells, weights, field, seed_magnetic, inverse, saved_magnetic,
        x_first, x_second, y_first, y_second, sent,
    )

    grad_e, grad_h, grad_eps, sources = call(
        second_kernel,
        (shape(3, *block), shape(3, *block), shape(*block), shape(3, 2, 64)),
        "vvvvvvvvv",
        (),
        40_000_000,
        4_000_000,
    )(
        returned, tables_of("back_z"), tables_of("apart"), early, curled, factor, first_grad,
        ready, injected,
    )
    return grad_e, grad_h, grad_eps, sources.transpose(1, 2, 0)


def solution(mesh):
    field = P(None, "bulk", "wide", None)
    return jax.shard_map(
        body,
        mesh=mesh,
        in_specs=(
            field, field, P(None, None, "bulk", "wide", None), P("bulk", "wide", None),
            P(), P(), P(), P(), P(), P(), P(), P(), P(),
        ),
        out_specs=(field, field, P("bulk", "wide", None), P()),
        check_vma=False,
    )
```

```python
import functools
import math

import jax
import jax.numpy as jnp
import ml_dtypes
import numpy as np
from jax import lax
from jax.experimental import pallas as pl
from jax.experimental.pallas import tpu as pltpu
from jax.sharding import PartitionSpec as P

NX, NY, NZ = 256, 256, 128
K = 48
OWN = 3
WIDE, BULK = 16, 32
RX, RY = 8, 16
NEAR, DEPTH, HALVES = 4, 16, 2
SHARE = OWN * K // NEAR
PAD = 40
LANES = 128
F32, BF16 = jnp.float32, jnp.bfloat16
PARAMS = pltpu.CompilerParams(vmem_limit_bytes=40 * 1024 * 1024)
HIGHEST = lax.Precision.HIGHEST


def waves(freqs, places, total):
    phase = np.mod(np.asarray(freqs)[:, None] * np.asarray(places)[None, :], total)
    angle = phase.astype(np.float32) * np.float32(2.0 * math.pi / total)
    return np.cos(angle).astype(np.float32), np.sin(angle).astype(np.float32)


def rounded(table):
    return np.asarray(table, np.float32).astype(ml_dtypes.bfloat16)


def make_tables():
    mode = np.arange(K)
    plane = np.where(mode < K // 2, mode, mode - K)
    cz, sz = waves(mode, np.arange(NZ), NZ)
    cx, sx = (rounded(t) for t in waves(plane, np.arange(NX), NX))
    cy, sy = (rounded(t) for t in waves(plane, np.arange(NY), NY))
    scale = np.float32(1.0 / math.sqrt(NX * NY * NZ))
    back = np.float32(1.0 / math.sqrt(K**3))
    fz, gz = rounded(cz * scale), rounded(-sz * scale)
    bz, hz = rounded(cz * back), rounded(sz * back)
    out = {}
    lift_z = np.zeros((LANES, LANES), ml_dtypes.bfloat16)
    back_z = np.zeros((LANES, LANES), ml_dtypes.bfloat16)
    for w in range(WIDE):
        for i in range(OWN):
            lift_z[:, w * 8 + i] = fz[w * OWN + i]
            lift_z[:, w * 8 + OWN + i] = gz[w * OWN + i]
            back_z[w * 8 + i] = bz[w * OWN + i]
            back_z[w * 8 + OWN + i] = -hz[w * OWN + i]
    out["lift_z"], out["back_z"] = lift_z, back_z

    lane = np.arange(LANES)
    y_of = np.concatenate([(h * 8 + lane % 8) * RY + lane // 8 for h in range(2)])
    fwd_y = np.zeros((512, 256), ml_dtypes.bfloat16)
    fwd_y[:256, :K] = cy[:, y_of].T
    fwd_y[256:, :K] = sy[:, y_of].T
    fwd_y[:256, 128 : 128 + K] = -sy[:, y_of].T
    fwd_y[256:, 128 : 128 + K] = cy[:, y_of].T
    out["fwd_y"] = fwd_y

    inv_x = np.zeros((DEPTH // NEAR, HALVES, NEAR * 16, LANES), ml_dtypes.bfloat16)
    for half in range(HALVES):
        for z in range(DEPTH):
            start = (z * HALVES + half) * RX
            x_of = (start + np.array([0, 1, 2, 3, 4, 5, 6, 7, 8, -1])) % NX
            at = slice(z % NEAR * 16, z % NEAR * 16 + 10)
            inv_x[z // NEAR, half, at, :K] = cx[:, x_of].T
            inv_x[z // NEAR, half, at, 64 : 64 + K] = -sx[:, x_of].T
    out["inv_x"] = inv_x

    inv_y = np.zeros((LANES, 384), ml_dtypes.bfloat16)
    inv_y[:K, :256], inv_y[64 : 64 + K, :256] = cy, -sy
    for w in range(WIDE):
        for h, y in enumerate((w * RY + RY, w * RY - 1)):
            inv_y[:K, 256 + w * 2 + h] = cy[:, y % NY]
            inv_y[64 : 64 + K, 256 + w * 2 + h] = -sy[:, y % NY]
    out["inv_y"] = inv_y
    apart = np.zeros((LANES, 256), ml_dtypes.bfloat16)
    for cell in range(32):
        apart[cell * 2, cell * 8] = 1
        apart[cell * 2 + 1, cell * 8 + 7] = 1
    out["apart"] = apart

    at_x = np.zeros((2, LANES, NX), ml_dtypes.bfloat16)
    at_x[0, :K], at_x[0, 64 : 64 + K] = cx, -sx
    at_x[1, :K], at_x[1, 64 : 64 + K] = sx, cx
    out["at_x"] = at_x
    at_y = np.zeros((NEAR, 2, 48, NY), ml_dtypes.bfloat16)
    for n in range(NEAR):
        j_of = np.arange(n * SHARE, (n + 1) * SHARE) % K
        at_y[n, 0, :SHARE], at_y[n, 1, :SHARE] = cy[j_of], sy[j_of]
    out["at_y"] = at_y
    at_z = np.zeros((WIDE, 2, 16, NZ), ml_dtypes.bfloat16)
    for w in range(WIDE):
        at_z[w, 0, :OWN] = bz[w * OWN : (w + 1) * OWN]
        at_z[w, 1, :OWN] = hz[w * OWN : (w + 1) * OWN]
    out["at_z"] = at_z
    return out


TABLES = make_tables()


def iota(shape, axis):
    return lax.broadcasted_iota(jnp.int32, shape, axis)


def exchange(tiles, block, axis):
    tiles = list(tiles)
    shape = tiles[0].shape
    size = shape[axis]
    place = iota(shape, axis) // block
    step = 1
    while step < len(tiles):
        high = (place // step) % 2 == 1
        new = list(tiles)
        for low in range(len(tiles)):
            if low & step:
                continue
            u, v = tiles[low], tiles[low + step]
            new[low] = jnp.where(high, pltpu.roll(v, step * block, axis), u)
            new[low + step] = jnp.where(high, v, pltpu.roll(u, size - step * block, axis))
        tiles = new
        step *= 2
    return tiles


def z_ahead(v):
    axis = v.ndim - 1
    return jnp.where(iota(v.shape, axis) < NZ - 1, pltpu.roll(v, NZ - 1, axis), 0.0)


def z_behind(v):
    axis = v.ndim - 1
    return jnp.where(iota(v.shape, axis) > 0, pltpu.roll(v, 1, axis), 0.0)


def x_ahead(v):
    return jnp.concatenate([v[1:], v[:1]], 0)


def x_behind(v):
    return jnp.concatenate([v[-1:], v[:-1]], 0)


def y_ahead(v):
    return pltpu.roll(v, v.shape[1] - 1, 1)


def y_behind(v):
    return pltpu.roll(v, 1, 1)


def curl_ahead(fx, fy, fz):
    return (
        (y_ahead(fz) - fz) - (z_ahead(fy) - fy),
        (z_ahead(fx) - fx) - (x_ahead(fz) - fz),
        (x_ahead(fy) - fy) - (y_ahead(fx) - fx),
    )


def curl_behind(fx, fy, fz):
    return (
        (fz - y_behind(fz)) - (fy - z_behind(fy)),
        (fx - z_behind(fx)) - (fz - x_behind(fz)),
        (fy - x_behind(fy)) - (fx - y_behind(fx)),
    )


def place_of(flat):
    return flat >> 15, (flat >> 7) & (NY - 1), flat & (NZ - 1)


def own_block():
    return lax.axis_index("bulk"), lax.axis_index("wide")


def fetch(pairs, sems):
    copies = [pltpu.make_async_copy(a, b, sems.at[i]) for i, (a, b) in enumerate(pairs)]
    for copy in copies:
        copy.start()
    return copies


def scan(cells, hit, act):
    def group(g, carry):
        found = [cells[g * 8 + i] for i in range(8)]
        hits = [hit(*place_of(f)) for f in found]
        some = functools.reduce(jnp.logical_or, hits)

        @pl.when(some)
        def _():
            for i in range(8):
                pl.when(hits[i])(functools.partial(act, g * 8 + i, found[i]))

        return carry

    lax.fori_loop(0, 8, group, 0)


def lift_kernel(mon_in, weights_in, electric, table_in, out, field, mon, weights, table, sems):
    b, w = own_block()
    copies = fetch(
        ((mon_in, mon), (electric, field), (weights_in, weights), (table_in, table)), sems
    )
    for copy in copies:
        copy.wait()
    lane = iota((1, NZ), 1)
    spot = iota((1, 64), 1)

    def hit(x, y, z):
        return ((x >> 3) == b) & ((y >> 4) == w)

    def add(i, flat):
        x, y, z = place_of(flat)
        lx, ly = x & (RX - 1), y & (RY - 1)
        for c in range(3):
            row = field[c, lx, pl.ds(ly, 1), :]
            given = jnp.where(spot == i, weights[c, 1:2, :], 0.0)
            weight = jnp.sum(given, axis=1, keepdims=True)
            field[c, lx, pl.ds(ly, 1), :] = row + jnp.where(lane == z, weight, 0.0)

    scan(mon, hit, add)
    rows = field[...].reshape(3 * RX * RY, NZ).astype(BF16)
    modes = jnp.dot(rows, table[...], preferred_element_type=F32)
    modes = modes.reshape(3, RX, 2, 8, LANES)
    tiles = exchange([modes[:, x].reshape(6, 8, LANES) for x in range(RX)], 1, 1)
    tiles = [t.reshape(3, 2, 8, LANES) for t in tiles]
    tiles = exchange([tiles[y % 8][:, y // 8] for y in range(RY)], 8, 2)
    out[...] = jnp.concatenate([t.reshape(24, LANES) for t in tiles], 0).astype(BF16)


def share_kernel(
    src_in, perm_in, field, magnetic_in, material_in,
    taken, inverse,
    src, perm, magnetic, material, scaled, held, sems,
):
    b, w = own_block()
    copies = fetch(
        (
            (src_in, src), (perm_in, perm), (magnetic_in, magnetic),
            (material_in, material),
        ),
        sems,
    )
    zero = jnp.zeros((12, 32, NZ), F32)
    for c in range(3):
        scaled[c] = zero
        held[c] = zero
    for copy in copies:
        copy.wait()
    eps = jnp.zeros((RX, RY, NZ), F32)
    cells = material[...]
    for level in range(8):
        eps = jnp.where(cells == level, perm[level], eps)
    inv = 1.0 / eps
    inverse[...] = inv
    lane = iota((1, NZ), 1)
    for c in range(3):
        scaled[c, 2:10, 8:24, :] = 0.5 * inv * field[c]
        held[c, 2:10, 8:24, :] = magnetic[c]
    taken[...] = jnp.zeros((8, LANES), F32)
    spot_row, spot_lane = iota((8, LANES), 0), iota((8, LANES), 1)

    def hit(x, y, z):
        lx, ly = x - b * RX, y - w * RY
        return (lx >= -1) & (lx <= RX) & (ly >= -1) & (ly <= RY)

    def take(i, flat):
        x, y, z = place_of(flat)
        lx, ly = x - b * RX, y - w * RY

        def a(c, dx, dy):
            return scaled[c, lx + 2 + dx, pl.ds(ly + 8 + dy, 1), :]

        def h(c, dx, dy):
            old = held[c, lx + 2 + dx, pl.ds(ly + 8 + dy, 1), :]
            if c == 0:
                near = a(1, dx, dy)
                turn = (a(2, dx, dy + 1) - a(2, dx, dy)) - (z_ahead(near) - near)
            elif c == 1:
                near = a(0, dx, dy)
                turn = (z_ahead(near) - near) - (a(2, dx + 1, dy) - a(2, dx, dy))
            else:
                turn = (a(1, dx + 1, dy) - a(1, dx, dy)) - (a(0, dx, dy + 1) - a(0, dx, dy))
            return old + turn

        left = jnp.where(x > 0, 1.0, 0.0)
        down = jnp.where(y > 0, 1.0, 0.0)
        hx, hy, hz = h(0, 0, 0), h(1, 0, 0), h(2, 0, 0)
        hx_y, hz_y = down * h(0, 0, -1), down * h(2, 0, -1)
        hy_x, hz_x = left * h(1, -1, 0), left * h(2, -1, 0)
        curls = (
            (hz - hz_y) - (hy - z_behind(hy)),
            (hx - z_behind(hx)) - (hz - hz_x),
            (hy - hy_x) - (hx - hx_y),
        )
        mine = jnp.where((lx >= 0) & (lx < RX) & (ly >= 0) & (ly < RY), 1.0, 0.0)
        cx, cy = jnp.clip(lx, 0, RX - 1), jnp.clip(ly, 0, RY - 1)
        got = taken[...]
        for c in range(3):
            old = mine * field[c, cx, pl.ds(cy, 1), :]
            for n, row in ((0, old - 0.5 * curls[c]), (1, old)):
                value = jnp.sum(jnp.where(lane == z, row, 0.0), axis=1, keepdims=True)
                spot = (spot_row == n * 3 + c) & (spot_lane == i)
                got = got + jnp.where(spot, value, 0.0)
        taken[...] = got

    scan(src, hit, take)


def middle_kernel(lines, taken, table, out):
    got = lines[...].astype(F32).reshape(WIDE, 24, LANES)
    halves = [exchange([got[h * 8 + i] for i in range(8)], 1, 1) for h in range(2)]
    rows = [
        jnp.concatenate([halves[0][k], halves[1][k], halves[0][OWN + k], halves[1][OWN + k]], 1)
        for k in range(OWN)
    ]
    lhs = jnp.concatenate(rows, 0).astype(BF16)
    found = jnp.dot(lhs, table[...], preferred_element_type=F32)
    lane = iota((8, LANES), 1)
    parts = [[jnp.zeros((8, LANES), F32) for _ in range(2)] for _ in range(NEAR)]
    split = LANES - (NEAR - 1) * SHARE
    for part in range(2):
        for d in range(3):
            piece = [
                found[(k * 3 + d) * 8 : (k * 3 + d) * 8 + 8, part * LANES : (part + 1) * LANES]
                for k in range(OWN)
            ]
            last = pltpu.roll(piece[2], 2 * K, 1)
            first = piece[0] + pltpu.roll(piece[1], K, 1) + jnp.where(lane >= 2 * K, last, 0.0)
            rest = jnp.where(lane < 16, last, 0.0)
            to = d * SHARE
            for n in range(NEAR):
                shift = (to - n * SHARE) % LANES
                moved = pltpu.roll(first, shift, 1) if shift else first
                if n == NEAR - 1:
                    moved = jnp.where(lane < to + split, moved, pltpu.roll(rest, to + split, 1))
                within = (lane >= to) & (lane < to + SHARE)
                parts[n][part] = parts[n][part] + jnp.where(within, moved, 0.0)
    src = jnp.concatenate([taken[...], jnp.zeros((LANES - 8, LANES), F32)], 0).T
    src = jnp.where(iota((LANES, LANES), 1) < 6, src, 0.0)
    high = src.astype(BF16).astype(F32)
    at = 3 * SHARE
    rows = []
    for n in range(NEAR):
        for part, value in enumerate((high, src - high)):
            for i in range(2):
                start = n * 16 + i * 8
                parts[n][part] = parts[n][part] + pltpu.roll(
                    value[start : start + 8], at + i * 6, 1
                )
        rows.append(jnp.concatenate(parts[n], 1))
    deal = jnp.concatenate([r for r in rows for _ in range(HALVES)], 0).astype(BF16)
    size = NEAR * HALVES * 8
    for f in range(DEPTH // NEAR):
        out[f * size : (f + 1) * size, :] = deal


def param_kernel(
    mon, weights, lift, cells, project, gain_x, gain_y, mix, at_x, at_y, at_z, inv_x,
    after, coef_a, coef_b, phase_x, phase_yz, injected, back_x,
):
    b, w = own_block()
    n = b // HALVES % NEAR
    back_x[...] = inv_x[b // (HALVES * NEAR), b % HALVES]
    flat = cells[...]
    x, y, z = place_of(flat)
    first = iota((1, LANES), 1) < 64
    hot_x = jnp.where(iota((NX, LANES), 0) == x, 1.0, 0.0)
    real = jnp.where(first, hot_x, 0.0).astype(BF16)
    imag = jnp.where(first, 0.0, hot_x).astype(BF16)
    phase_x[...] = (
        jnp.dot(at_x[0], real, preferred_element_type=F32)
        + jnp.dot(at_x[1], imag, preferred_element_type=F32)
    ).astype(BF16)
    hot_y = jnp.where(iota((NY, LANES), 0) == y, 1.0, 0.0).astype(BF16)
    hot_z = jnp.where(iota((NZ, LANES), 0) == z, 1.0, 0.0).astype(BF16)
    cy = jnp.dot(at_y[n, 0], hot_y, preferred_element_type=F32)[:PAD]
    sy = jnp.dot(at_y[n, 1], hot_y, preferred_element_type=F32)[:PAD]
    cz = jnp.dot(at_z[w, 0], hot_z, preferred_element_type=F32)
    sz = jnp.dot(at_z[w, 1], hot_z, preferred_element_type=F32)
    mode = n * SHARE + iota((PAD, 1), 0)
    ck = jnp.where(mode < K, cz[0:1], jnp.where(mode < 2 * K, cz[1:2], cz[2:3]))
    sk = jnp.where(mode < K, sz[0:1], jnp.where(mode < 2 * K, sz[1:2], sz[2:3]))
    phase_yz[...] = jnp.where(first, cy * ck - sy * sk, -(sy * ck + cy * sk))

    place = iota((K, PAD), 1)
    mode = n * SHARE + place
    depth = jnp.where(mode < K, 0, jnp.where(mode < 2 * K, 1, 2))
    live = place < SHARE
    hot_j = jnp.where((iota((K, PAD), 0) == mode - depth * K) & live, 1.0, 0.0)
    hot_k = jnp.where((iota((K, PAD), 0) == w * OWN + depth) & live, 1.0, 0.0)
    gains = jnp.dot(gain_y[...], hot_j, precision=HIGHEST, preferred_element_type=F32)
    diagonal = iota((16, 16), 0) == iota((16, 16), 1)
    columns = [
        jnp.sum(jnp.where(diagonal, project[e : e + 1, :], 0.0), axis=1, keepdims=True)
        for e in range(3)
    ]
    blank = jnp.zeros((16, 16), F32)
    along = gain_x[...]
    totals = []
    for part in range(2):
        rows = [mix[part, c].astype(F32) for c in range(16)]
        for d in range(3):
            total = lift[d, 0] * rows[0]
            for c in range(1, 16):
                total = total + lift[d, c] * rows[c]
            totals.append(total)
    joined = jnp.dot(
        jnp.concatenate(totals, 0), hot_k, precision=HIGHEST, preferred_element_type=F32
    )
    joined = [joined[i * 16 : (i + 1) * 16] * gains for i in range(6)]
    for part, to in ((0, coef_a), (1, coef_b)):
        sign = 1.0 if part == 0 else -1.0
        right = jnp.concatenate([sign * along, blank, along, blank], 1)
        right = jnp.concatenate([columns[e] * right for e in range(3)], 1)
        left = jnp.concatenate([j.T for j in joined[part * 3 : part * 3 + 3]], 0)
        found = jnp.dot(left, right, precision=HIGHEST, preferred_element_type=F32)
        for e in range(3):
            for d in range(3):
                to[(e * 3 + d) * PAD : (e * 3 + d + 1) * PAD, :] = found[
                    d * PAD : (d + 1) * PAD, e * LANES : (e + 1) * LANES
                ]
    row = iota((8, LANES), 0)
    total = jnp.zeros((8, LANES), F32)
    for i in range(64):
        given = jnp.where(
            row == 0, weights[0, 0, i], jnp.where(row == 1, weights[1, 0, i], weights[2, 0, i])
        )
        total = total + jnp.where((flat == mon[i]) & (row < 3), given, 0.0)
    injected[...] = jnp.where(iota((8, LANES), 1) < 64, total, 0.0)


def filter_kernel(
    gathered, coef_a, coef_b, at_x, back_x, phase_x, phase_yz, after, out
):
    b, w = own_block()
    near = b // HALVES % NEAR
    lane = iota((1, LANES), 1)
    got = gathered[...]
    real = jnp.dot(at_x[0], got[:, :LANES], preferred_element_type=F32)
    imag = jnp.dot(at_x[1], got[:, LANES:], preferred_element_type=F32)
    full = (real + imag).T
    field = [full[d * SHARE : d * SHARE + PAD] for d in range(3)]
    turned = [pltpu.roll(f, 64, 1) for f in field]
    sign = jnp.where(lane < 64, 1.0, -1.0)
    real = []
    for e in range(3):
        q = jnp.zeros((PAD, LANES), F32)
        for d in range(3):
            at = (e * 3 + d) * PAD
            q = q + coef_a[at : at + PAD] * field[d] + coef_b[at : at + PAD] * turned[d]
        real.append(q)
    gap = jnp.zeros((LANES - 3 * SHARE, LANES), F32)
    packed = jnp.concatenate([q[:SHARE] for q in real] + [gap], 0)
    right = jnp.concatenate([packed, pltpu.roll(packed, 64, 1) * sign], 0).astype(BF16)
    back = lax.dot_general(
        back_x[...], right, (((1,), (1,)), ((), ())),
        preferred_element_type=F32,
    ).reshape(NEAR, 2, 8, 2 * LANES)

    total = got.astype(F32).reshape(BULK, 8, 2 * LANES).sum(0)
    total = pltpu.roll(total[:, :LANES] + total[:, LANES:], LANES - 3 * SHARE, 1)
    second = pltpu.roll(total, LANES - 6, 1)
    gap = jnp.zeros((LANES - 16, LANES), F32)
    total = jnp.concatenate([total, second, gap], 0)
    total = jnp.where(iota((LANES, LANES), 1) < 6, total, 0.0).T[:8]
    total = pltpu.roll(total, near * 16, 1)
    near = jnp.dot(
        jnp.concatenate(real, 0).astype(BF16), phase_x[...], preferred_element_type=F32
    )
    row = iota((8, LANES), 0)
    for e in range(3):
        line = jnp.sum(near[e * PAD : (e + 1) * PAD] * phase_yz[...], axis=0, keepdims=True)
        line = line + pltpu.roll(line, 64, 1)
        total = total + jnp.where((row == e) & (lane < 64), line, 0.0)
    high = total.astype(BF16).astype(F32)
    extra = pltpu.roll(high + pltpu.roll(total - high, 64, 1), 2, 0)
    extra = jnp.concatenate([extra, jnp.zeros((8, LANES), F32)], 1)
    tiles = []
    for n in range(NEAR):
        tiles += [back[n, 0], back[n, 1] + extra]
    out[...] = jnp.concatenate(tiles, 0).astype(BF16)


def spread_kernel(shares, inv_y, after, out, rows):
    lane = iota((1, LANES), 1)
    got = shares[...].astype(F32).reshape(NEAR, 16, 2 * LANES)
    rows[...] = jnp.zeros((32, 8, LANES), F32)
    for e in range(3):
        flat = []
        for part in range(2):
            start = e * SHARE
            first, rest = jnp.zeros((16, LANES), F32), None
            for n in range(NEAR):
                moved = got[n][:, part * LANES : (part + 1) * LANES]
                if n != e:
                    moved = pltpu.roll(moved, (n * SHARE - start) % LANES, 1)
                within = (lane >= n * SHARE) & (lane < (n + 1) * SHARE)
                first = first + jnp.where(within, moved, 0.0)
                if n == NEAR - 1:
                    rest = jnp.where(lane < 16, moved, 0.0)
            flat.append((first, rest))

        def mode_rows(part, k, to):
            first, rest = flat[part]
            moved = pltpu.roll(first, (to - k * K) % LANES, 1)
            if k < 2:
                return jnp.where((lane >= to) & (lane < to + K), moved, 0.0)
            tail = pltpu.roll(rest, to + 32, 1)
            return jnp.where((lane >= to) & (lane < to + 32), moved, 0.0) + jnp.where(
                (lane >= to + 32) & (lane < to + K), tail, 0.0
            )

        for k in range(OWN):
            real = mode_rows(0, k, 0) + mode_rows(1, k, 64)
            imag = mode_rows(1, k, 0) - mode_rows(0, k, 64)
            for x in range(10):
                rows[e * 10 + x, k : k + 1, :] = real[x : x + 1]
                rows[e * 10 + x, OWN + k : OWN + k + 1, :] = imag[x : x + 1]
    lhs = rows[...].reshape(256, LANES).astype(BF16)
    wide = jnp.dot(lhs, inv_y[...], preferred_element_type=F32).reshape(32, 8, 384)
    near = []
    for low in range(8):
        group = [wide[high * 8 + low, :, c * LANES : (c + 1) * LANES] for high in range(4) for c in range(2)]
        near.append(jnp.stack(group))
    near = exchange(near, 16, 2)
    edge = []
    for low in range(16):
        edge.append(jnp.stack([wide[high * 16 + low, :, 256:384] for high in range(2)]))
    edge = exchange(edge, 2, 2)
    row = iota((8, LANES), 0)
    total = pltpu.roll(got[:, 8:16, :LANES].sum(0), 6, 0)
    total = jnp.where((row < 6) & (lane < 64), total + pltpu.roll(total, 64, 1), 0.0)
    high = total.astype(BF16).astype(F32)
    other = pltpu.roll(total - high, 64, 1)
    moved = pltpu.roll(high, 64, 1)
    low = total - high
    extra = []
    for t in range(3):
        first = jnp.where(lane < 64, high[2 * t : 2 * t + 1], moved[2 * t + 1 : 2 * t + 2])
        second = jnp.where(lane < 64, low[2 * t : 2 * t + 1], other[2 * t + 1 : 2 * t + 2])
        extra.append(jnp.where(row == 6, first, jnp.where(row == 7, second, 0.0)))
    blocks = []
    for w in range(WIDE):
        tiles = [near[w % 8][high_x * 2 + w // 8] for high_x in range(4)]
        for t in range(3):
            tiles[t] = tiles[t] + extra[t]
        pair = jnp.where(lane < 32, edge[w], 0.0)
        tiles.append(pair[0] + pltpu.roll(pair[1], 32, 1))
        blocks.append(jnp.concatenate(tiles, 1))
    out[...] = jnp.concatenate(blocks, 0).astype(BF16)


def high_planes(across):
    first, second = [c for c in range(3) if c != across]
    planes = [(c, 0) for c in range(3)] + [(first, 1), (second, 1), (6, 0), (6, 1)]
    return planes + [(3 + c, 0) for c in range(3)]


def low_planes(across):
    first, second = [c for c in range(3) if c != across]
    planes = [(c, i) for i in range(2) for c in range(3)] + [(6, 0), (6, 1)]
    return planes + [(3 + first, 0), (3 + second, 0)] + [(3 + c, 1) for c in range(3)]


def edge_kernel(electric, magnetic, inverse, saved, after, to_low, to_high):
    def own(f):
        return electric.at[f] if f < 3 else (magnetic.at[f - 3] if f < 6 else inverse)

    for p, (f, i) in enumerate(low_planes(0)):
        to_low[p] = own(f)[6 + i].astype(BF16)
    for n in range(2):
        for c in range(2):
            to_low[13 + 2 * n + c] = saved[n, 1 + c, 7]
    for p, (f, i) in enumerate(high_planes(0)):
        to_high[p] = own(f)[i].astype(BF16)


def corner_kernel(
    electric, magnetic, inverse, saved, x_low, x_high, after, to_first, to_second, low, high
):
    x_of = [{}, {}]
    for p, key in enumerate(low_planes(0)):
        x_of[0][key] = x_low[p].astype(F32)
    for p, key in enumerate(high_planes(0)):
        x_of[1][key] = x_high[p].astype(F32)
    low[...] = jnp.zeros(low.shape, F32)
    high[...] = jnp.zeros(high.shape, F32)
    for to, planes, start in ((low, low_planes(1), 14), (high, high_planes(1), 0)):
        for p, (f, i) in enumerate(planes):
            own = electric.at[f] if f < 3 else (magnetic.at[f - 3] if f < 6 else inverse)
            row = start + i
            to[p, 0:8, :] = own[:, row, :]
            for side, at in ((1, 8), (0, 10)):
                for layer in range(2):
                    if (f, layer) in x_of[side]:
                        got = x_of[side][(f, layer)]
                        to[p, at + layer : at + layer + 1, :] = got[row : row + 1]
    for n in range(2):
        for i, c in enumerate((0, 2)):
            low[13 + 2 * n + i, 0:8, :] = saved[n, c].astype(F32)[:, RY - 1, :]
    even = jnp.where(lax.axis_index("wide") % 2 == 0, 1.0, 0.0)
    a, b = low[...], high[...]
    to_first[...] = (even * a + (1.0 - even) * b).astype(BF16)
    to_second[...] = (even * b + (1.0 - even) * a).astype(BF16)


def first_kernel(
    mon, weights, electric, magnetic, inverse, saved, x_low, x_high, y_first, y_second, after,
    early, curled, factor, grad, ready, e_ext, h_ext, g_ext,
):
    b, w = own_block()
    lane = iota((1, NZ), 1)
    even = jnp.where(w % 2 == 0, 1.0, 0.0)
    first, second = y_first[...].astype(F32), y_second[...].astype(F32)
    y_low = even * second + (1.0 - even) * first
    y_high = even * first + (1.0 - even) * second
    zero = jnp.zeros((12, 24, NZ), F32)
    for c in range(7):
        to = e_ext.at[c] if c < 3 else (h_ext.at[c - 3] if c < 6 else g_ext)
        to[...] = zero
        own = electric[c] if c < 3 else (magnetic[c - 3] if c < 6 else inverse[...])
        to[0:8, 0:16, :] = own
        for planes, ref, at in ((high_planes(0), x_high, 8), (low_planes(0), x_low, 10)):
            for p, (f, i) in enumerate(planes):
                if f == c:
                    to[at + i, 0:16, :] = ref[p].astype(F32)
        for planes, ref, at in ((high_planes(1), y_high, 16), (low_planes(1), y_low, 22)):
            for p, (f, i) in enumerate(planes):
                if f == c:
                    to[:, at + i : at + i + 1, :] = ref[p][0:12][:, None, :]

    g = g_ext[...]
    half = 0.5 * g
    a = [half * e_ext[c] for c in range(3)]
    spot_x = iota((12, 24, 1), 0)
    spot_y = iota((12, 24, 1), 1)
    outside = ((spot_x >= 10) & (b == 0)) | ((spot_y >= 22) & (w == 0))
    inside = jnp.where(outside, 0.0, 1.0)
    turned = curl_ahead(*a)
    h = [h_ext[c] + inside * turned[c] for c in range(3)]
    back = curl_behind(*h)
    for c in range(3):
        e_ext[c] = e_ext[c] - 0.5 * back[c]

    def hit(x, y, z):
        lx, ly = x - b * RX, y - w * RY
        return (lx >= -2) & (lx < RX + 2) & (ly >= -2) & (ly < RY + 2)

    def add(i, flat):
        x, y, z = place_of(flat)
        lx, ly = x - b * RX, y - w * RY
        px = jnp.where(lx < 0, lx + 12, lx)
        py = jnp.where(ly < 0, ly + 24, ly)
        for c in range(3):
            row = e_ext[c, px, pl.ds(py, 1), :]
            e_ext[c, px, pl.ds(py, 1), :] = row + jnp.where(lane == z, weights[c, 0, i], 0.0)

    scan(mon, hit, add)
    for c in range(3):
        early[c, 0:9] = e_ext[c, 0:9]
        early[c, 9:10] = e_ext[c, 11:12]
        curled[c, 0:9] = h[c][0:9]
        curled[c, 9:10] = h[c][11:12]
    factor[0:9] = half[0:9]
    factor[9:10] = half[11:12]

    near = inverse[...]
    for step in range(2):
        s = [saved[step, c].astype(F32) for c in range(3)]
        before_x = {c: jnp.concatenate([x_low[12 + 2 * step + c].astype(F32)[None], s[c][:-1]], 0) for c in (1, 2)}
        before_y = {}
        for c in (0, 2):
            edge = y_low[13 + 2 * step + c // 2][0:8][:, None, :]
            first = iota((RX, RY, NZ), 1) == 0
            before_y[c] = jnp.where(first, edge, pltpu.roll(s[c], 1, 1))
        curls = (
            (s[2] - before_y[2]) - (s[1] - z_behind(s[1])),
            (s[0] - z_behind(s[0])) - (s[2] - before_x[2]),
            (s[1] - before_x[1]) - (s[0] - before_y[0]),
        )
        if step == 0:
            for c in range(3):
                ready[c] = near * curls[c]
        else:
            total = jnp.zeros((RX, RY, NZ), F32)
            for c in range(3):
                total = total + a[c][0:8, 0:16] * near * curls[c]
            grad[...] = -total


def second_kernel(
    lines, table, apart, early, curled, factor, first_grad, ready, injected,
    grad_e, grad_h, grad_eps, sources,
):
    b, w = own_block()
    turn = (((0,), (0,)), ((), ()))
    main = lax.dot_general(lines[:, 0:512], table[...], turn, preferred_element_type=F32)
    main = main.reshape(32, 16, NZ)
    edge = jnp.dot(lines[:, 512:640], apart[...], preferred_element_type=F32).astype(BF16)
    edge = lax.dot_general(edge, table[...], turn, preferred_element_type=F32)
    edge = edge.reshape(32, 8, NZ)
    half = factor[...]
    e1 = []
    for c in range(3):
        at = slice(c * 10, c * 10 + 10)
        e1.append(early[c] + jnp.concatenate([main[at], edge[at]], 1))
    a = [half * e for e in e1]
    spot_x = iota((10, 24, 1), 0)
    spot_y = iota((10, 24, 1), 1)
    outside = ((spot_x == 9) & (b == 0)) | ((spot_y == 23) & (w == 0))
    inside = jnp.where(outside, 0.0, 1.0)
    turned = curl_ahead(*a)
    h = [curled[c] + inside * turned[c] for c in range(3)]
    backed = curl_behind(*h)
    total = first_grad[...]
    for c in range(3):
        grad_h[c] = h[c][0:8, 0:16]
        grad_e[c] = e1[c][0:8, 0:16] - 0.5 * backed[c][0:8, 0:16]
        total = total - a[c][0:8, 0:16] * ready[c]
    grad_eps[...] = total
    got = lines[:, 0:384].astype(F32).reshape(WIDE, 8, 384).sum(0)
    got = got[6:7] + got[7:8]
    moved = pltpu.roll(got, 384 - 64, 1)
    for n in range(2):
        for c in range(3):
            at = n * 3 + c
            line = got if at % 2 == 0 else moved
            line = line[:, at // 2 * LANES : (at // 2 + 1) * LANES]
            if n == 0:
                line = line + injected[c : c + 1, :]
            sources[c, n : n + 1, :] = line[:, 0:64]


def call(kernel, outs, places, scratch=(), flops=0, moved=0, params=PARAMS):
    spaces = {"s": pltpu.SMEM, "v": pltpu.VMEM, "a": pl.ANY}
    return pl.pallas_call(
        kernel,
        out_shape=outs,
        in_specs=[pl.BlockSpec(memory_space=spaces[p]) for p in places],
        out_specs=jax.tree.map(lambda _: pl.BlockSpec(memory_space=pltpu.VMEM), outs),
        scratch_shapes=list(scratch),
        compiler_params=params,
        cost_estimate=pl.CostEstimate(flops=flops, bytes_accessed=moved, transcendentals=0),
    )


def shape(*dims, dtype=F32):
    return jax.ShapeDtypeStruct(dims, dtype)


def passed_along(block, axis, distance):
    devices = range(lax.axis_size(axis))
    route = [(i - distance, i) for i in devices if i - distance in devices]
    return lax.ppermute(block, axis, route)


def dealt_near(block):
    groups = [
        [(f * NEAR + n) * HALVES + half for n in range(NEAR)]
        for f in range(DEPTH // NEAR)
        for half in range(HALVES)
    ]
    return lax.all_to_all(
        block, "bulk", split_axis=0, concat_axis=0, axis_index_groups=groups, tiled=True
    )


def tables_of(name):
    return jnp.asarray(TABLES[name])


def body(
    seed_electric, seed_magnetic, saved_magnetic, material, permittivity, source_cells,
    monitor_cells, monitor_weights, lift_weight, project_weight, mode_mix, gain_first, gain_second,
):
    weights = monitor_weights.transpose(2, 0, 1)
    big, dma = pltpu.CompilerParams(vmem_limit_bytes=56 * 1024 * 1024), pltpu.SemaphoreType.DMA
    block = (RX, RY, NZ)

    payload, field = call(
        lift_kernel,
        (shape(384, LANES, dtype=BF16), shape(3, *block)),
        "aaaa",
        [
            pltpu.SMEM((64,), jnp.int32), pltpu.VMEM((3, 2, 64), F32),
            pltpu.VMEM((LANES, LANES), BF16), dma((4,)),
        ],
        13_000_000,
        500_000,
        big,
    )(monitor_cells, weights, seed_electric, tables_of("lift_z"))
    lines = lax.all_to_all(payload, "wide", split_axis=0, concat_axis=0, tiled=True)

    taken, inverse = call(
        share_kernel,
        (shape(8, LANES), shape(*block)),
        "aavaa",
        [
            pltpu.SMEM((64,), jnp.int32), pltpu.SMEM((8,), F32), pltpu.VMEM((3, *block), F32),
            pltpu.VMEM(block, jnp.int32), pltpu.VMEM((3, 12, 32, NZ), F32),
            pltpu.VMEM((3, 12, 32, NZ), F32), dma((4,)),
        ],
        3_000_000,
        1_500_000,
    )(source_cells, permittivity, field, seed_magnetic, material)

    dealt = call(
        middle_kernel, shape(BULK * 8, 2 * LANES, dtype=BF16), "vvv", (), 20_000_000, 400_000
    )(lines, taken, tables_of("fwd_y"))
    gathered = lax.all_to_all(dealt, "bulk", split_axis=0, concat_axis=0, tiled=True)

    cells = jnp.concatenate([source_cells, source_cells]).reshape(1, LANES)
    coef_a, coef_b, phase_x, phase_yz, injected, back_x = call(
        param_kernel,
        (
            shape(9 * PAD, LANES), shape(9 * PAD, LANES), shape(LANES, LANES, dtype=BF16),
            shape(PAD, LANES), shape(8, LANES), shape(NEAR * 16, LANES, dtype=BF16),
        ),
        "sssvvvvvvvvva",
        (),
        20_000_000,
        1_000_000,
    )(
        monitor_cells, weights, lift_weight.T, cells, project_weight, gain_first, gain_second,
        mode_mix.transpose(0, 2, 3, 1), tables_of("at_x"), tables_of("at_y"), tables_of("at_z"),
        tables_of("inv_x"), dealt,
    )

    to_low, to_high = call(
        edge_kernel,
        (shape(17, RY, NZ, dtype=BF16), shape(10, RY, NZ, dtype=BF16)),
        "vvvva",
        (),
        0,
        500_000,
    )(field, seed_magnetic, inverse, saved_magnetic, dealt)
    x_low = passed_along(to_low, "bulk", 1)
    x_high = passed_along(to_high, "bulk", -1)

    first_part, second_part = call(
        corner_kernel,
        (shape(17, 16, NZ, dtype=BF16), shape(17, 16, NZ, dtype=BF16)),
        "vvvvvva",
        [pltpu.VMEM((17, 16, NZ), F32)] * 2,
        0,
        1_000_000,
    )(field, seed_magnetic, inverse, saved_magnetic, x_low, x_high, coef_a)
    shares = call(
        filter_kernel, shape(NEAR * 16, 2 * LANES, dtype=BF16), "vvvvvvva", (), 40_000_000, 600_000
    )(
        gathered, coef_a, coef_b, tables_of("at_x"), back_x, phase_x, phase_yz,
        first_part,
    )
    back = dealt_near(shares)

    y_first = lax.ppermute(first_part, "wide", [(i, i ^ 1) for i in range(WIDE)])
    pairs = [(i, i + 1) for i in range(1, WIDE - 1, 2)]
    y_second = lax.ppermute(second_part, "wide", pairs + [(j, i) for i, j in pairs])

    sent = call(
        spread_kernel,
        shape(128, 640, dtype=BF16),
        "vva",
        [pltpu.VMEM((32, 8, LANES), F32)],
        40_000_000,
        600_000,
    )(back, tables_of("inv_y"), y_second)
    returned = lax.all_to_all(sent, "wide", split_axis=0, concat_axis=0, tiled=True)
    early, curled, factor, first_grad, ready = call(
        first_kernel,
        (
            shape(3, 10, 24, NZ), shape(3, 10, 24, NZ), shape(10, 24, NZ), shape(*block),
            shape(3, *block),
        ),
        "ssvvvvvvvva",
        [pltpu.VMEM((3, 12, 24, NZ), F32)] * 2 + [pltpu.VMEM((12, 24, NZ), F32)],
        10_000_000,
        60_000_000,
    )(
        monitor_cells, weights, field, seed_magnetic, inverse, saved_magnetic,
        x_low, x_high, y_first, y_second, sent,
    )

    grad_e, grad_h, grad_eps, sources = call(
        second_kernel,
        (shape(3, *block), shape(3, *block), shape(*block), shape(3, 2, 64)),
        "vvvvvvvvv",
        (),
        40_000_000,
        4_000_000,
    )(
        returned, tables_of("back_z"), tables_of("apart"), early, curled, factor, first_grad,
        ready, injected,
    )
    return grad_e, grad_h, grad_eps, sources.transpose(1, 2, 0)


def solution(mesh):
    field = P(None, "bulk", "wide", None)
    return jax.shard_map(
        body,
        mesh=mesh,
        in_specs=(
            field, field, P(None, None, "bulk", "wide", None), P("bulk", "wide", None),
            P(), P(), P(), P(), P(), P(), P(), P(), P(),
        ),
        out_specs=(field, field, P("bulk", "wide", None), P()),
        check_vma=False,
    )
```

```python
import functools
import math

import jax
import jax.numpy as jnp
import ml_dtypes
import numpy as np
from jax import lax
from jax.experimental import pallas as pl
from jax.experimental.pallas import tpu as pltpu
from jax.sharding import PartitionSpec as P

NX, NY, NZ = 256, 256, 128
K = 48
OWN = 3
WIDE, BULK = 16, 32
RX, RY = 8, 16
NEAR, DEPTH, HALVES = 4, 16, 2
SHARE = OWN * K // NEAR
PAD = 40
LANES = 128
F32, BF16 = jnp.float32, jnp.bfloat16
PARAMS = pltpu.CompilerParams(vmem_limit_bytes=40 * 1024 * 1024)
HIGHEST = lax.Precision.HIGHEST


def waves(freqs, places, total):
    phase = np.mod(np.asarray(freqs)[:, None] * np.asarray(places)[None, :], total)
    angle = phase.astype(np.float32) * np.float32(2.0 * math.pi / total)
    return np.cos(angle).astype(np.float32), np.sin(angle).astype(np.float32)


def rounded(table):
    return np.asarray(table, np.float32).astype(ml_dtypes.bfloat16)


def make_tables():
    mode = np.arange(K)
    plane = np.where(mode < K // 2, mode, mode - K)
    cz, sz = waves(mode, np.arange(NZ), NZ)
    cx, sx = (rounded(t) for t in waves(plane, np.arange(NX), NX))
    cy, sy = (rounded(t) for t in waves(plane, np.arange(NY), NY))
    scale = np.float32(1.0 / math.sqrt(NX * NY * NZ))
    back = np.float32(1.0 / math.sqrt(K**3))
    fz, gz = rounded(cz * scale), rounded(-sz * scale)
    bz, hz = rounded(cz * back), rounded(sz * back)
    out = {}
    lift_z = np.zeros((LANES, LANES), ml_dtypes.bfloat16)
    back_z = np.zeros((LANES, LANES), ml_dtypes.bfloat16)
    for w in range(WIDE):
        for i in range(OWN):
            lift_z[:, w * 8 + i] = fz[w * OWN + i]
            lift_z[:, w * 8 + OWN + i] = gz[w * OWN + i]
            back_z[w * 8 + i] = bz[w * OWN + i]
            back_z[w * 8 + OWN + i] = -hz[w * OWN + i]
    out["lift_z"], out["back_z"] = lift_z, back_z

    lane = np.arange(LANES)
    y_of = np.concatenate([(h * 8 + lane % 8) * RY + lane // 8 for h in range(2)])
    fwd_y = np.zeros((512, 256), ml_dtypes.bfloat16)
    fwd_y[:256, :K] = cy[:, y_of].T
    fwd_y[256:, :K] = sy[:, y_of].T
    fwd_y[:256, 128 : 128 + K] = -sy[:, y_of].T
    fwd_y[256:, 128 : 128 + K] = cy[:, y_of].T
    out["fwd_y"] = fwd_y

    inv_x = np.zeros((DEPTH // NEAR, HALVES, NEAR * 16, LANES), ml_dtypes.bfloat16)
    for half in range(HALVES):
        for z in range(DEPTH):
            start = (z * HALVES + half) * RX
            x_of = (start + np.array([0, 1, 2, 3, 4, 5, 6, 7, 8, -1])) % NX
            at = slice(z % NEAR * 16, z % NEAR * 16 + 10)
            inv_x[z // NEAR, half, at, :K] = cx[:, x_of].T
            inv_x[z // NEAR, half, at, 64 : 64 + K] = -sx[:, x_of].T
    out["inv_x"] = inv_x

    inv_y = np.zeros((LANES, 384), ml_dtypes.bfloat16)
    inv_y[:K, :256], inv_y[64 : 64 + K, :256] = cy, -sy
    for w in range(WIDE):
        for h, y in enumerate((w * RY + RY, w * RY - 1)):
            inv_y[:K, 256 + w * 2 + h] = cy[:, y % NY]
            inv_y[64 : 64 + K, 256 + w * 2 + h] = -sy[:, y % NY]
    out["inv_y"] = inv_y
    apart = np.zeros((LANES, 256), ml_dtypes.bfloat16)
    for cell in range(32):
        apart[cell * 2, cell * 8] = 1
        apart[cell * 2 + 1, cell * 8 + 7] = 1
    out["apart"] = apart

    at_x = np.zeros((2, LANES, NX), ml_dtypes.bfloat16)
    at_x[0, :K], at_x[0, 64 : 64 + K] = cx, -sx
    at_x[1, :K], at_x[1, 64 : 64 + K] = sx, cx
    out["at_x"] = at_x
    at_y = np.zeros((NEAR, 2, 48, NY), ml_dtypes.bfloat16)
    for n in range(NEAR):
        j_of = np.arange(n * SHARE, (n + 1) * SHARE) % K
        at_y[n, 0, :SHARE], at_y[n, 1, :SHARE] = cy[j_of], sy[j_of]
    out["at_y"] = at_y
    at_z = np.zeros((WIDE, 2, 16, NZ), ml_dtypes.bfloat16)
    for w in range(WIDE):
        at_z[w, 0, :OWN] = bz[w * OWN : (w + 1) * OWN]
        at_z[w, 1, :OWN] = hz[w * OWN : (w + 1) * OWN]
    out["at_z"] = at_z
    return out


TABLES = make_tables()


def iota(shape, axis):
    return lax.broadcasted_iota(jnp.int32, shape, axis)


def exchange(tiles, block, axis):
    tiles = list(tiles)
    shape = tiles[0].shape
    size = shape[axis]
    place = iota(shape, axis) // block
    step = 1
    while step < len(tiles):
        high = (place // step) % 2 == 1
        new = list(tiles)
        for low in range(len(tiles)):
            if low & step:
                continue
            u, v = tiles[low], tiles[low + step]
            new[low] = jnp.where(high, pltpu.roll(v, step * block, axis), u)
            new[low + step] = jnp.where(high, v, pltpu.roll(u, size - step * block, axis))
        tiles = new
        step *= 2
    return tiles


def z_ahead(v):
    axis = v.ndim - 1
    return jnp.where(iota(v.shape, axis) < NZ - 1, pltpu.roll(v, NZ - 1, axis), 0.0)


def z_behind(v):
    axis = v.ndim - 1
    return jnp.where(iota(v.shape, axis) > 0, pltpu.roll(v, 1, axis), 0.0)


def x_ahead(v):
    return jnp.concatenate([v[1:], v[:1]], 0)


def x_behind(v):
    return jnp.concatenate([v[-1:], v[:-1]], 0)


def y_ahead(v):
    return pltpu.roll(v, v.shape[1] - 1, 1)


def y_behind(v):
    return pltpu.roll(v, 1, 1)


def curl_ahead(fx, fy, fz):
    return (
        (y_ahead(fz) - fz) - (z_ahead(fy) - fy),
        (z_ahead(fx) - fx) - (x_ahead(fz) - fz),
        (x_ahead(fy) - fy) - (y_ahead(fx) - fx),
    )


def curl_behind(fx, fy, fz):
    return (
        (fz - y_behind(fz)) - (fy - z_behind(fy)),
        (fx - z_behind(fx)) - (fz - x_behind(fz)),
        (fy - x_behind(fy)) - (fx - y_behind(fx)),
    )


def place_of(flat):
    return flat >> 15, (flat >> 7) & (NY - 1), flat & (NZ - 1)


def own_block():
    return lax.axis_index("bulk"), lax.axis_index("wide")


def fetch(pairs, sems):
    copies = [pltpu.make_async_copy(a, b, sems.at[i]) for i, (a, b) in enumerate(pairs)]
    for copy in copies:
        copy.start()
    return copies


def scan(cells, hit, act):
    def group(g, carry):
        found = [cells[g * 8 + i] for i in range(8)]
        hits = [hit(*place_of(f)) for f in found]
        some = functools.reduce(jnp.logical_or, hits)

        @pl.when(some)
        def _():
            for i in range(8):
                pl.when(hits[i])(functools.partial(act, g * 8 + i, found[i]))

        return carry

    lax.fori_loop(0, 8, group, 0)


def lift_kernel(mon_in, weights_in, electric, table_in, out, field, mon, weights, table, sems):
    b, w = own_block()
    copies = fetch(
        ((mon_in, mon), (electric, field), (weights_in, weights), (table_in, table)), sems
    )
    for copy in copies:
        copy.wait()
    lane = iota((1, NZ), 1)
    spot = iota((1, 64), 1)

    def hit(x, y, z):
        return ((x >> 3) == b) & ((y >> 4) == w)

    def add(i, flat):
        x, y, z = place_of(flat)
        lx, ly = x & (RX - 1), y & (RY - 1)
        for c in range(3):
            row = field[c, lx, pl.ds(ly, 1), :]
            given = jnp.where(spot == i, weights[c, 1:2, :], 0.0)
            weight = jnp.sum(given, axis=1, keepdims=True)
            field[c, lx, pl.ds(ly, 1), :] = row + jnp.where(lane == z, weight, 0.0)

    scan(mon, hit, add)
    rows = field[...].reshape(3 * RX * RY, NZ).astype(BF16)
    modes = jnp.dot(rows, table[...], preferred_element_type=F32)
    modes = modes.reshape(3, RX, 2, 8, LANES)
    tiles = exchange([modes[:, x].reshape(6, 8, LANES) for x in range(RX)], 1, 1)
    tiles = [t.reshape(3, 2, 8, LANES) for t in tiles]
    tiles = exchange([tiles[y % 8][:, y // 8] for y in range(RY)], 8, 2)
    out[...] = jnp.concatenate([t.reshape(24, LANES) for t in tiles], 0).astype(BF16)


def share_kernel(
    src_in, perm_in, field, magnetic_in, material_in,
    taken, inverse,
    src, perm, magnetic, material, scaled, held, sems,
):
    b, w = own_block()
    copies = fetch(
        (
            (src_in, src), (perm_in, perm), (magnetic_in, magnetic),
            (material_in, material),
        ),
        sems,
    )
    zero = jnp.zeros((12, 32, NZ), F32)
    for c in range(3):
        scaled[c] = zero
        held[c] = zero
    for copy in copies:
        copy.wait()
    eps = jnp.zeros((RX, RY, NZ), F32)
    cells = material[...]
    for level in range(8):
        eps = jnp.where(cells == level, perm[level], eps)
    inv = 1.0 / eps
    inverse[...] = inv
    lane = iota((1, NZ), 1)
    for c in range(3):
        scaled[c, 2:10, 8:24, :] = 0.5 * inv * field[c]
        held[c, 2:10, 8:24, :] = magnetic[c]
    taken[...] = jnp.zeros((8, LANES), F32)
    spot_row, spot_lane = iota((8, LANES), 0), iota((8, LANES), 1)

    def hit(x, y, z):
        lx, ly = x - b * RX, y - w * RY
        return (lx >= -1) & (lx <= RX) & (ly >= -1) & (ly <= RY)

    def take(i, flat):
        x, y, z = place_of(flat)
        lx, ly = x - b * RX, y - w * RY

        def a(c, dx, dy):
            return scaled[c, lx + 2 + dx, pl.ds(ly + 8 + dy, 1), :]

        def h(c, dx, dy):
            old = held[c, lx + 2 + dx, pl.ds(ly + 8 + dy, 1), :]
            if c == 0:
                near = a(1, dx, dy)
                turn = (a(2, dx, dy + 1) - a(2, dx, dy)) - (z_ahead(near) - near)
            elif c == 1:
                near = a(0, dx, dy)
                turn = (z_ahead(near) - near) - (a(2, dx + 1, dy) - a(2, dx, dy))
            else:
                turn = (a(1, dx + 1, dy) - a(1, dx, dy)) - (a(0, dx, dy + 1) - a(0, dx, dy))
            return old + turn

        left = jnp.where(x > 0, 1.0, 0.0)
        down = jnp.where(y > 0, 1.0, 0.0)
        hx, hy, hz = h(0, 0, 0), h(1, 0, 0), h(2, 0, 0)
        hx_y, hz_y = down * h(0, 0, -1), down * h(2, 0, -1)
        hy_x, hz_x = left * h(1, -1, 0), left * h(2, -1, 0)
        curls = (
            (hz - hz_y) - (hy - z_behind(hy)),
            (hx - z_behind(hx)) - (hz - hz_x),
            (hy - hy_x) - (hx - hx_y),
        )
        mine = jnp.where((lx >= 0) & (lx < RX) & (ly >= 0) & (ly < RY), 1.0, 0.0)
        cx, cy = jnp.clip(lx, 0, RX - 1), jnp.clip(ly, 0, RY - 1)
        got = taken[...]
        for c in range(3):
            old = mine * field[c, cx, pl.ds(cy, 1), :]
            for n, row in ((0, old - 0.5 * curls[c]), (1, old)):
                value = jnp.sum(jnp.where(lane == z, row, 0.0), axis=1, keepdims=True)
                spot = (spot_row == n * 3 + c) & (spot_lane == i)
                got = got + jnp.where(spot, value, 0.0)
        taken[...] = got

    scan(src, hit, take)


def middle_kernel(lines, taken, table, out):
    got = lines[...].astype(F32).reshape(WIDE, 24, LANES)
    halves = [exchange([got[h * 8 + i] for i in range(8)], 1, 1) for h in range(2)]
    rows = [
        jnp.concatenate([halves[0][k], halves[1][k], halves[0][OWN + k], halves[1][OWN + k]], 1)
        for k in range(OWN)
    ]
    lhs = jnp.concatenate(rows, 0).astype(BF16)
    found = jnp.dot(lhs, table[...], preferred_element_type=F32)
    lane = iota((8, LANES), 1)
    parts = [[jnp.zeros((8, LANES), F32) for _ in range(2)] for _ in range(NEAR)]
    split = LANES - (NEAR - 1) * SHARE
    for part in range(2):
        for d in range(3):
            piece = [
                found[(k * 3 + d) * 8 : (k * 3 + d) * 8 + 8, part * LANES : (part + 1) * LANES]
                for k in range(OWN)
            ]
            last = pltpu.roll(piece[2], 2 * K, 1)
            first = piece[0] + pltpu.roll(piece[1], K, 1) + jnp.where(lane >= 2 * K, last, 0.0)
            rest = jnp.where(lane < 16, last, 0.0)
            to = d * SHARE
            for n in range(NEAR):
                shift = (to - n * SHARE) % LANES
                moved = pltpu.roll(first, shift, 1) if shift else first
                if n == NEAR - 1:
                    moved = jnp.where(lane < to + split, moved, pltpu.roll(rest, to + split, 1))
                within = (lane >= to) & (lane < to + SHARE)
                parts[n][part] = parts[n][part] + jnp.where(within, moved, 0.0)
    src = jnp.concatenate([taken[...], jnp.zeros((LANES - 8, LANES), F32)], 0).T
    src = jnp.where(iota((LANES, LANES), 1) < 6, src, 0.0)
    high = src.astype(BF16).astype(F32)
    at = 3 * SHARE
    rows = []
    for n in range(NEAR):
        for part, value in enumerate((high, src - high)):
            for i in range(2):
                start = n * 16 + i * 8
                parts[n][part] = parts[n][part] + pltpu.roll(
                    value[start : start + 8], at + i * 6, 1
                )
        rows.append(jnp.concatenate(parts[n], 1))
    deal = jnp.concatenate([r for r in rows for _ in range(HALVES)], 0).astype(BF16)
    size = NEAR * HALVES * 8
    for f in range(DEPTH // NEAR):
        out[f * size : (f + 1) * size, :] = deal


def param_kernel(
    mon, weights, lift, cells, project, gain_x, gain_y, mix, at_x, at_y, at_z, inv_x,
    after, coef_a, coef_b, phase_x, phase_yz, injected, back_x,
):
    b, w = own_block()
    n = b // HALVES % NEAR
    back_x[...] = inv_x[b // (HALVES * NEAR), b % HALVES]
    flat = cells[...]
    x, y, z = place_of(flat)
    first = iota((1, LANES), 1) < 64
    hot_x = jnp.where(iota((NX, LANES), 0) == x, 1.0, 0.0)
    real = jnp.where(first, hot_x, 0.0).astype(BF16)
    imag = jnp.where(first, 0.0, hot_x).astype(BF16)
    phase_x[...] = (
        jnp.dot(at_x[0], real, preferred_element_type=F32)
        + jnp.dot(at_x[1], imag, preferred_element_type=F32)
    ).astype(BF16)
    hot_y = jnp.where(iota((NY, LANES), 0) == y, 1.0, 0.0).astype(BF16)
    hot_z = jnp.where(iota((NZ, LANES), 0) == z, 1.0, 0.0).astype(BF16)
    cy = jnp.dot(at_y[n, 0], hot_y, preferred_element_type=F32)[:PAD]
    sy = jnp.dot(at_y[n, 1], hot_y, preferred_element_type=F32)[:PAD]
    cz = jnp.dot(at_z[w, 0], hot_z, preferred_element_type=F32)
    sz = jnp.dot(at_z[w, 1], hot_z, preferred_element_type=F32)
    mode = n * SHARE + iota((PAD, 1), 0)
    ck = jnp.where(mode < K, cz[0:1], jnp.where(mode < 2 * K, cz[1:2], cz[2:3]))
    sk = jnp.where(mode < K, sz[0:1], jnp.where(mode < 2 * K, sz[1:2], sz[2:3]))
    phase_yz[...] = jnp.where(first, cy * ck - sy * sk, -(sy * ck + cy * sk))

    place = iota((K, PAD), 1)
    mode = n * SHARE + place
    depth = jnp.where(mode < K, 0, jnp.where(mode < 2 * K, 1, 2))
    live = place < SHARE
    hot_j = jnp.where((iota((K, PAD), 0) == mode - depth * K) & live, 1.0, 0.0)
    hot_k = jnp.where((iota((K, PAD), 0) == w * OWN + depth) & live, 1.0, 0.0)
    gains = jnp.dot(gain_y[...], hot_j, precision=HIGHEST, preferred_element_type=F32)
    diagonal = iota((16, 16), 0) == iota((16, 16), 1)
    columns = [
        jnp.sum(jnp.where(diagonal, project[e : e + 1, :], 0.0), axis=1, keepdims=True)
        for e in range(3)
    ]
    blank = jnp.zeros((16, 16), F32)
    along = gain_x[...]
    totals = []
    for part in range(2):
        rows = [mix[part, c].astype(F32) for c in range(16)]
        for d in range(3):
            total = lift[d, 0] * rows[0]
            for c in range(1, 16):
                total = total + lift[d, c] * rows[c]
            totals.append(total)
    joined = jnp.dot(
        jnp.concatenate(totals, 0), hot_k, precision=HIGHEST, preferred_element_type=F32
    )
    joined = [joined[i * 16 : (i + 1) * 16] * gains for i in range(6)]
    for part, to in ((0, coef_a), (1, coef_b)):
        sign = 1.0 if part == 0 else -1.0
        right = jnp.concatenate([sign * along, blank, along, blank], 1)
        right = jnp.concatenate([columns[e] * right for e in range(3)], 1)
        left = jnp.concatenate([j.T for j in joined[part * 3 : part * 3 + 3]], 0)
        found = jnp.dot(left, right, precision=HIGHEST, preferred_element_type=F32)
        for e in range(3):
            for d in range(3):
                to[(e * 3 + d) * PAD : (e * 3 + d + 1) * PAD, :] = found[
                    d * PAD : (d + 1) * PAD, e * LANES : (e + 1) * LANES
                ]
    row = iota((8, LANES), 0)
    total = jnp.zeros((8, LANES), F32)
    for i in range(64):
        given = jnp.where(
            row == 0, weights[0, 0, i], jnp.where(row == 1, weights[1, 0, i], weights[2, 0, i])
        )
        total = total + jnp.where((flat == mon[i]) & (row < 3), given, 0.0)
    injected[...] = jnp.where(iota((8, LANES), 1) < 64, total, 0.0)


def filter_kernel(
    gathered, coef_a, coef_b, at_x, back_x, phase_x, phase_yz, after, out
):
    b, w = own_block()
    near = b // HALVES % NEAR
    lane = iota((1, LANES), 1)
    got = gathered[...]
    real = jnp.dot(at_x[0], got[:, :LANES], preferred_element_type=F32)
    imag = jnp.dot(at_x[1], got[:, LANES:], preferred_element_type=F32)
    full = (real + imag).T
    field = [full[d * SHARE : d * SHARE + PAD] for d in range(3)]
    turned = [pltpu.roll(f, 64, 1) for f in field]
    sign = jnp.where(lane < 64, 1.0, -1.0)
    real = []
    for e in range(3):
        q = jnp.zeros((PAD, LANES), F32)
        for d in range(3):
            at = (e * 3 + d) * PAD
            q = q + coef_a[at : at + PAD] * field[d] + coef_b[at : at + PAD] * turned[d]
        real.append(q)
    gap = jnp.zeros((LANES - 3 * SHARE, LANES), F32)
    packed = jnp.concatenate([q[:SHARE] for q in real] + [gap], 0)
    right = jnp.concatenate([packed, pltpu.roll(packed, 64, 1) * sign], 0).astype(BF16)
    back = lax.dot_general(
        back_x[...], right, (((1,), (1,)), ((), ())),
        preferred_element_type=F32,
    ).reshape(NEAR, 2, 8, 2 * LANES)

    total = got.astype(F32).reshape(BULK, 8, 2 * LANES).sum(0)
    total = pltpu.roll(total[:, :LANES] + total[:, LANES:], LANES - 3 * SHARE, 1)
    second = pltpu.roll(total, LANES - 6, 1)
    gap = jnp.zeros((LANES - 16, LANES), F32)
    total = jnp.concatenate([total, second, gap], 0)
    total = jnp.where(iota((LANES, LANES), 1) < 6, total, 0.0).T[:8]
    total = pltpu.roll(total, near * 16, 1)
    near = jnp.dot(
        jnp.concatenate(real, 0).astype(BF16), phase_x[...], preferred_element_type=F32
    )
    row = iota((8, LANES), 0)
    for e in range(3):
        line = jnp.sum(near[e * PAD : (e + 1) * PAD] * phase_yz[...], axis=0, keepdims=True)
        line = line + pltpu.roll(line, 64, 1)
        total = total + jnp.where((row == e) & (lane < 64), line, 0.0)
    high = total.astype(BF16).astype(F32)
    extra = pltpu.roll(high + pltpu.roll(total - high, 64, 1), 2, 0)
    extra = jnp.concatenate([extra, jnp.zeros((8, LANES), F32)], 1)
    tiles = []
    for n in range(NEAR):
        tiles += [back[n, 0], back[n, 1] + extra]
    out[...] = jnp.concatenate(tiles, 0).astype(BF16)


def spread_kernel(shares, inv_y, after, out, rows):
    lane = iota((1, LANES), 1)
    got = shares[...].astype(F32).reshape(NEAR, 16, 2 * LANES)
    rows[...] = jnp.zeros((32, 8, LANES), F32)
    for e in range(3):
        flat = []
        for part in range(2):
            start = e * SHARE
            first, rest = jnp.zeros((16, LANES), F32), None
            for n in range(NEAR):
                moved = got[n][:, part * LANES : (part + 1) * LANES]
                if n != e:
                    moved = pltpu.roll(moved, (n * SHARE - start) % LANES, 1)
                within = (lane >= n * SHARE) & (lane < (n + 1) * SHARE)
                first = first + jnp.where(within, moved, 0.0)
                if n == NEAR - 1:
                    rest = jnp.where(lane < 16, moved, 0.0)
            flat.append((first, rest))

        def mode_rows(part, k, to):
            first, rest = flat[part]
            moved = pltpu.roll(first, (to - k * K) % LANES, 1)
            if k < 2:
                return jnp.where((lane >= to) & (lane < to + K), moved, 0.0)
            tail = pltpu.roll(rest, to + 32, 1)
            return jnp.where((lane >= to) & (lane < to + 32), moved, 0.0) + jnp.where(
                (lane >= to + 32) & (lane < to + K), tail, 0.0
            )

        for k in range(OWN):
            real = mode_rows(0, k, 0) + mode_rows(1, k, 64)
            imag = mode_rows(1, k, 0) - mode_rows(0, k, 64)
            for x in range(10):
                rows[e * 10 + x, k : k + 1, :] = real[x : x + 1]
                rows[e * 10 + x, OWN + k : OWN + k + 1, :] = imag[x : x + 1]
    lhs = rows[...].reshape(256, LANES).astype(BF16)
    wide = jnp.dot(lhs, inv_y[...], preferred_element_type=F32).reshape(32, 8, 384)
    near = []
    for low in range(8):
        group = [wide[high * 8 + low, :, c * LANES : (c + 1) * LANES] for high in range(4) for c in range(2)]
        near.append(jnp.stack(group))
    near = exchange(near, 16, 2)
    edge = []
    for low in range(16):
        edge.append(jnp.stack([wide[high * 16 + low, :, 256:384] for high in range(2)]))
    edge = exchange(edge, 2, 2)
    row = iota((8, LANES), 0)
    total = pltpu.roll(got[:, 8:16, :LANES].sum(0), 6, 0)
    total = jnp.where((row < 6) & (lane < 64), total + pltpu.roll(total, 64, 1), 0.0)
    high = total.astype(BF16).astype(F32)
    other = pltpu.roll(total - high, 64, 1)
    moved = pltpu.roll(high, 64, 1)
    low = total - high
    extra = []
    for t in range(3):
        first = jnp.where(lane < 64, high[2 * t : 2 * t + 1], moved[2 * t + 1 : 2 * t + 2])
        second = jnp.where(lane < 64, low[2 * t : 2 * t + 1], other[2 * t + 1 : 2 * t + 2])
        extra.append(jnp.where(row == 6, first, jnp.where(row == 7, second, 0.0)))
    blocks = []
    for w in range(WIDE):
        tiles = [near[w % 8][high_x * 2 + w // 8] for high_x in range(4)]
        for t in range(3):
            tiles[t] = tiles[t] + extra[t]
        pair = jnp.where(lane < 32, edge[w], 0.0)
        tiles.append(pair[0] + pltpu.roll(pair[1], 32, 1))
        blocks.append(jnp.concatenate(tiles, 1))
    out[...] = jnp.concatenate(blocks, 0).astype(BF16)


def high_planes(across):
    first, second = [c for c in range(3) if c != across]
    planes = [(c, 0) for c in range(3)] + [(first, 1), (second, 1), (6, 0), (6, 1)]
    return planes + [(3 + c, 0) for c in range(3)]


def low_planes(across):
    first, second = [c for c in range(3) if c != across]
    planes = [(c, i) for i in range(2) for c in range(3)] + [(6, 0), (6, 1)]
    return planes + [(3 + first, 0), (3 + second, 0)] + [(3 + c, 1) for c in range(3)]


def edge_kernel(electric, magnetic, inverse, saved, after, to_low, to_high):
    def own(f):
        return electric.at[f] if f < 3 else (magnetic.at[f - 3] if f < 6 else inverse)

    for p, (f, i) in enumerate(low_planes(0)):
        to_low[p] = own(f)[6 + i].astype(BF16)
    for n in range(2):
        for c in range(2):
            to_low[13 + 2 * n + c] = saved[n, 1 + c, 7]
    for p, (f, i) in enumerate(high_planes(0)):
        to_high[p] = own(f)[i].astype(BF16)


def corner_kernel(
    electric, magnetic, inverse, saved, x_low, x_high, after, to_first, to_second, low, high
):
    x_of = [{}, {}]
    for p, key in enumerate(low_planes(0)):
        x_of[0][key] = x_low[p].astype(F32)
    for p, key in enumerate(high_planes(0)):
        x_of[1][key] = x_high[p].astype(F32)
    low[...] = jnp.zeros(low.shape, F32)
    high[...] = jnp.zeros(high.shape, F32)
    for to, planes, start in ((low, low_planes(1), 14), (high, high_planes(1), 0)):
        for p, (f, i) in enumerate(planes):
            own = electric.at[f] if f < 3 else (magnetic.at[f - 3] if f < 6 else inverse)
            row = start + i
            to[p, 0:8, :] = own[:, row, :]
            for side, at in ((1, 8), (0, 10)):
                for layer in range(2):
                    if (f, layer) in x_of[side]:
                        got = x_of[side][(f, layer)]
                        to[p, at + layer : at + layer + 1, :] = got[row : row + 1]
    for n in range(2):
        for i, c in enumerate((0, 2)):
            low[13 + 2 * n + i, 0:8, :] = saved[n, c].astype(F32)[:, RY - 1, :]
    even = jnp.where(lax.axis_index("wide") % 2 == 0, 1.0, 0.0)
    a, b = low[...], high[...]
    to_first[...] = (even * a + (1.0 - even) * b).astype(BF16)
    to_second[...] = (even * b + (1.0 - even) * a).astype(BF16)


def first_kernel(
    mon, weights, electric, magnetic, inverse, saved, x_low, x_high, y_first, y_second, after,
    early, curled, factor, grad, ready, e_ext, h_ext, g_ext,
):
    b, w = own_block()
    lane = iota((1, NZ), 1)
    even = jnp.where(w % 2 == 0, 1.0, 0.0)
    first, second = y_first[...].astype(F32), y_second[...].astype(F32)
    y_low = even * second + (1.0 - even) * first
    y_high = even * first + (1.0 - even) * second
    zero = jnp.zeros((12, 24, NZ), F32)
    for c in range(7):
        to = e_ext.at[c] if c < 3 else (h_ext.at[c - 3] if c < 6 else g_ext)
        to[...] = zero
        own = electric[c] if c < 3 else (magnetic[c - 3] if c < 6 else inverse[...])
        to[0:8, 0:16, :] = own
        for planes, ref, at in ((high_planes(0), x_high, 8), (low_planes(0), x_low, 10)):
            for p, (f, i) in enumerate(planes):
                if f == c:
                    to[at + i, 0:16, :] = ref[p].astype(F32)
        for planes, ref, at in ((high_planes(1), y_high, 16), (low_planes(1), y_low, 22)):
            for p, (f, i) in enumerate(planes):
                if f == c:
                    to[:, at + i : at + i + 1, :] = ref[p][0:12][:, None, :]

    g = g_ext[...]
    half = 0.5 * g
    a = [half * e_ext[c] for c in range(3)]
    spot_x = iota((12, 24, 1), 0)
    spot_y = iota((12, 24, 1), 1)
    outside = ((spot_x >= 10) & (b == 0)) | ((spot_y >= 22) & (w == 0))
    inside = jnp.where(outside, 0.0, 1.0)
    turned = curl_ahead(*a)
    h = [h_ext[c] + inside * turned[c] for c in range(3)]
    back = curl_behind(*h)
    for c in range(3):
        e_ext[c] = e_ext[c] - 0.5 * back[c]

    def hit(x, y, z):
        lx, ly = x - b * RX, y - w * RY
        return (lx >= -2) & (lx < RX + 2) & (ly >= -2) & (ly < RY + 2)

    def add(i, flat):
        x, y, z = place_of(flat)
        lx, ly = x - b * RX, y - w * RY
        px = jnp.where(lx < 0, lx + 12, lx)
        py = jnp.where(ly < 0, ly + 24, ly)
        for c in range(3):
            row = e_ext[c, px, pl.ds(py, 1), :]
            e_ext[c, px, pl.ds(py, 1), :] = row + jnp.where(lane == z, weights[c, 0, i], 0.0)

    scan(mon, hit, add)
    for c in range(3):
        early[c, 0:9] = e_ext[c, 0:9]
        early[c, 9:10] = e_ext[c, 11:12]
        curled[c, 0:9] = h[c][0:9]
        curled[c, 9:10] = h[c][11:12]
    factor[0:9] = half[0:9]
    factor[9:10] = half[11:12]

    near = inverse[...]
    for step in range(2):
        s = [saved[step, c].astype(F32) for c in range(3)]
        before_x = {c: jnp.concatenate([x_low[12 + 2 * step + c].astype(F32)[None], s[c][:-1]], 0) for c in (1, 2)}
        before_y = {}
        for c in (0, 2):
            edge = y_low[13 + 2 * step + c // 2][0:8][:, None, :]
            first = iota((RX, RY, NZ), 1) == 0
            before_y[c] = jnp.where(first, edge, pltpu.roll(s[c], 1, 1))
        curls = (
            (s[2] - before_y[2]) - (s[1] - z_behind(s[1])),
            (s[0] - z_behind(s[0])) - (s[2] - before_x[2]),
            (s[1] - before_x[1]) - (s[0] - before_y[0]),
        )
        if step == 0:
            for c in range(3):
                ready[c] = near * curls[c]
        else:
            total = jnp.zeros((RX, RY, NZ), F32)
            for c in range(3):
                total = total + a[c][0:8, 0:16] * near * curls[c]
            grad[...] = -total


def second_kernel(
    lines, table, apart, early, curled, factor, first_grad, ready, injected,
    grad_e, grad_h, grad_eps, sources,
):
    b, w = own_block()
    turn = (((0,), (0,)), ((), ()))
    main = lax.dot_general(lines[:, 0:512], table[...], turn, preferred_element_type=F32)
    main = main.reshape(32, 16, NZ)
    edge = jnp.dot(lines[:, 512:640], apart[...], preferred_element_type=F32).astype(BF16)
    edge = lax.dot_general(edge, table[...], turn, preferred_element_type=F32)
    edge = edge.reshape(32, 8, NZ)
    half = factor[...]
    e1 = []
    for c in range(3):
        at = slice(c * 10, c * 10 + 10)
        e1.append(early[c] + jnp.concatenate([main[at], edge[at]], 1))
    a = [half * e for e in e1]
    spot_x = iota((10, 24, 1), 0)
    spot_y = iota((10, 24, 1), 1)
    outside = ((spot_x == 9) & (b == 0)) | ((spot_y == 23) & (w == 0))
    inside = jnp.where(outside, 0.0, 1.0)
    turned = curl_ahead(*a)
    h = [curled[c] + inside * turned[c] for c in range(3)]
    backed = curl_behind(*h)
    total = first_grad[...]
    for c in range(3):
        grad_h[c] = h[c][0:8, 0:16]
        grad_e[c] = e1[c][0:8, 0:16] - 0.5 * backed[c][0:8, 0:16]
        total = total - a[c][0:8, 0:16] * ready[c]
    grad_eps[...] = total
    got = lines[:, 0:384].astype(F32).reshape(WIDE, 8, 384).sum(0)
    got = got[6:7] + got[7:8]
    moved = pltpu.roll(got, 384 - 64, 1)
    for n in range(2):
        for c in range(3):
            at = n * 3 + c
            line = got if at % 2 == 0 else moved
            line = line[:, at // 2 * LANES : (at // 2 + 1) * LANES]
            if n == 0:
                line = line + injected[c : c + 1, :]
            sources[c, n : n + 1, :] = line[:, 0:64]


def call(kernel, outs, places, scratch=(), flops=0, moved=0, params=PARAMS):
    spaces = {"s": pltpu.SMEM, "v": pltpu.VMEM, "a": pl.ANY}
    return pl.pallas_call(
        kernel,
        out_shape=outs,
        in_specs=[pl.BlockSpec(memory_space=spaces[p]) for p in places],
        out_specs=jax.tree.map(lambda _: pl.BlockSpec(memory_space=pltpu.VMEM), outs),
        scratch_shapes=list(scratch),
        compiler_params=params,
        cost_estimate=pl.CostEstimate(flops=flops, bytes_accessed=moved, transcendentals=0),
    )


def shape(*dims, dtype=F32):
    return jax.ShapeDtypeStruct(dims, dtype)


def passed_along(block, axis, distance):
    devices = range(lax.axis_size(axis))
    route = [(i - distance, i) for i in devices if i - distance in devices]
    return lax.ppermute(block, axis, route)


def dealt_near(block):
    groups = [
        [(f * NEAR + n) * HALVES + half for n in range(NEAR)]
        for f in range(DEPTH // NEAR)
        for half in range(HALVES)
    ]
    return lax.all_to_all(
        block, "bulk", split_axis=0, concat_axis=0, axis_index_groups=groups, tiled=True
    )


def tables_of(name):
    return jnp.asarray(TABLES[name])


def body(
    seed_electric, seed_magnetic, saved_magnetic, material, permittivity, source_cells,
    monitor_cells, monitor_weights, lift_weight, project_weight, mode_mix, gain_first, gain_second,
):
    weights = monitor_weights.transpose(2, 0, 1)
    big, dma = pltpu.CompilerParams(vmem_limit_bytes=56 * 1024 * 1024), pltpu.SemaphoreType.DMA
    block = (RX, RY, NZ)

    payload, field = call(
        lift_kernel,
        (shape(384, LANES, dtype=BF16), shape(3, *block)),
        "aaaa",
        [
            pltpu.SMEM((64,), jnp.int32), pltpu.VMEM((3, 2, 64), F32),
            pltpu.VMEM((LANES, LANES), BF16), dma((4,)),
        ],
        13_000_000,
        500_000,
        big,
    )(monitor_cells, weights, seed_electric, tables_of("lift_z"))
    lines = lax.all_to_all(payload, "wide", split_axis=0, concat_axis=0, tiled=True)

    taken, inverse = call(
        share_kernel,
        (shape(8, LANES), shape(*block)),
        "aavaa",
        [
            pltpu.SMEM((64,), jnp.int32), pltpu.SMEM((8,), F32), pltpu.VMEM((3, *block), F32),
            pltpu.VMEM(block, jnp.int32), pltpu.VMEM((3, 12, 32, NZ), F32),
            pltpu.VMEM((3, 12, 32, NZ), F32), dma((4,)),
        ],
        3_000_000,
        1_500_000,
    )(source_cells, permittivity, field, seed_magnetic, material)

    dealt = call(
        middle_kernel, shape(BULK * 8, 2 * LANES, dtype=BF16), "vvv", (), 20_000_000, 400_000
    )(lines, taken, tables_of("fwd_y"))
    gathered = lax.all_to_all(dealt, "bulk", split_axis=0, concat_axis=0, tiled=True)

    cells = jnp.concatenate([source_cells, source_cells]).reshape(1, LANES)
    coef_a, coef_b, phase_x, phase_yz, injected, back_x = call(
        param_kernel,
        (
            shape(9 * PAD, LANES), shape(9 * PAD, LANES), shape(LANES, LANES, dtype=BF16),
            shape(PAD, LANES), shape(8, LANES), shape(NEAR * 16, LANES, dtype=BF16),
        ),
        "sssvvvvvvvvva",
        (),
        20_000_000,
        1_000_000,
    )(
        monitor_cells, weights, lift_weight.T, cells, project_weight, gain_first, gain_second,
        mode_mix.transpose(0, 2, 3, 1), tables_of("at_x"), tables_of("at_y"), tables_of("at_z"),
        tables_of("inv_x"), dealt,
    )

    to_low, to_high = call(
        edge_kernel,
        (shape(17, RY, NZ, dtype=BF16), shape(10, RY, NZ, dtype=BF16)),
        "vvvva",
        (),
        0,
        500_000,
    )(field, seed_magnetic, inverse, saved_magnetic, dealt)
    x_low = passed_along(to_low, "bulk", 1)
    x_high = passed_along(to_high, "bulk", -1)

    first_part, second_part = call(
        corner_kernel,
        (shape(17, 16, NZ, dtype=BF16), shape(17, 16, NZ, dtype=BF16)),
        "vvvvvva",
        [pltpu.VMEM((17, 16, NZ), F32)] * 2,
        0,
        1_000_000,
    )(field, seed_magnetic, inverse, saved_magnetic, x_low, x_high, coef_a)
    y_first = lax.ppermute(first_part, "wide", [(i, i ^ 1) for i in range(WIDE)])
    shares = call(
        filter_kernel, shape(NEAR * 16, 2 * LANES, dtype=BF16), "vvvvvvva", (), 40_000_000, 600_000
    )(
        gathered, coef_a, coef_b, tables_of("at_x"), back_x, phase_x, phase_yz,
        y_first,
    )
    back = dealt_near(shares)

    pairs = [(i, i + 1) for i in range(1, WIDE - 1, 2)]
    y_second = lax.ppermute(second_part, "wide", pairs + [(j, i) for i, j in pairs])

    sent = call(
        spread_kernel,
        shape(128, 640, dtype=BF16),
        "vva",
        [pltpu.VMEM((32, 8, LANES), F32)],
        40_000_000,
        600_000,
    )(back, tables_of("inv_y"), y_second)
    returned = lax.all_to_all(sent, "wide", split_axis=0, concat_axis=0, tiled=True)
    early, curled, factor, first_grad, ready = call(
        first_kernel,
        (
            shape(3, 10, 24, NZ), shape(3, 10, 24, NZ), shape(10, 24, NZ), shape(*block),
            shape(3, *block),
        ),
        "ssvvvvvvvva",
        [pltpu.VMEM((3, 12, 24, NZ), F32)] * 2 + [pltpu.VMEM((12, 24, NZ), F32)],
        10_000_000,
        3_000_000,
    )(
        monitor_cells, weights, field, seed_magnetic, inverse, saved_magnetic,
        x_low, x_high, y_first, y_second, sent,
    )

    grad_e, grad_h, grad_eps, sources = call(
        second_kernel,
        (shape(3, *block), shape(3, *block), shape(*block), shape(3, 2, 64)),
        "vvvvvvvvv",
        (),
        40_000_000,
        4_000_000,
    )(
        returned, tables_of("back_z"), tables_of("apart"), early, curled, factor, first_grad,
        ready, injected,
    )
    return grad_e, grad_h, grad_eps, sources.transpose(1, 2, 0)


def solution(mesh):
    field = P(None, "bulk", "wide", None)
    return jax.shard_map(
        body,
        mesh=mesh,
        in_specs=(
            field, field, P(None, None, "bulk", "wide", None), P("bulk", "wide", None),
            P(), P(), P(), P(), P(), P(), P(), P(), P(),
        ),
        out_specs=(field, field, P("bulk", "wide", None), P()),
        check_vma=False,
    )
```
